32 devices in a mesh: dp: 4 (over x, core), tensor: 8 (over z, y).
Axes of the slice: x: 2, y: 2, z: 4, core: 2. Of those that a mesh axis runs over, the one named last changes fastest.
Arguments:
- inputs: bfloat16 [2, 4096, 2048], P(None, ('dp', 'tensor')), may hold values from -6 to 6
- lengths: int32 [2, 4, 3], P(None, 'dp'), may hold values from 1 to 897, as said below
- norm_gain: bfloat16 [2048], P('dp'), may hold values from 0.25 to 1.75
- ffn_gain: bfloat16 [2048], P('dp'), may hold values from 0.25 to 1.75
- w_query: bfloat16 [2048, 2048], P(None, 'tensor'), may hold values from -0.125 to 0.125
- w_key: bfloat16 [2048, 2048], P(None, 'tensor'), may hold values from -0.125 to 0.125
- w_value: bfloat16 [2048, 2048], P(None, 'tensor'), may hold values from -0.125 to 0.125
- w_gate_out: bfloat16 [2048, 2048], P(None, 'tensor'), may hold values from -0.125 to 0.125
- w_beta: bfloat16 [2048, 16], P(None, 'tensor'), may hold values from -0.125 to 0.125
- conv_weight: bfloat16 [3, 4, 2048], P(None, None, 'tensor'), may hold values from -3 to 3
- head_gain: bfloat16 [16, 128], P('tensor'), may hold values from 0.25 to 1.75
- w_out: bfloat16 [2048, 2048], P('tensor'), may hold values from -0.1875 to 0.1875
- w_gate: bfloat16 [2048, 5632], P('dp', 'tensor'), may hold values from -0.125 to 0.125
- w_up: bfloat16 [2048, 5632], P('dp', 'tensor'), may hold values from -0.125 to 0.125
- w_down: bfloat16 [5632, 2048], P('tensor', 'dp'), may hold values from -0.109375 to 0.109375
- cotangent: bfloat16 [2, 4096, 2048], P(None, ('dp', 'tensor')), may hold values from -6 to 6
Outputs:
- outputs: float32 [2, 4096, 2048], P(None, ('dp', 'tensor'))
- input_grad: float32 [2, 4096, 2048], P(None, ('dp', 'tensor'))
- norm_gain_grad: float32 [2048], P(('dp', 'tensor'))
- ffn_gain_grad: float32 [2048], P(('dp', 'tensor'))
- w_query_grad: float32 [2048, 2048], P(None, 'tensor')
- w_key_grad: float32 [2048, 2048], P(None, 'tensor')
- w_value_grad: float32 [2048, 2048], P(None, 'tensor')
- w_gate_out_grad: float32 [2048, 2048], P(None, 'tensor')
- w_beta_grad: float32 [2048, 16], P(None, 'tensor')
- conv_weight_grad: float32 [3, 4, 2048], P(None, None, 'tensor')
- head_gain_grad: float32 [16, 128], P('tensor')
- w_out_grad: float32 [2048, 2048], P('tensor')
- w_gate_grad: float32 [2048, 5632], P('dp', 'tensor')
- w_up_grad: float32 [2048, 5632], P('dp', 'tensor')
- w_down_grad: float32 [5632, 2048], P('tensor', 'dp')
The draws below stay inside these ranges and needn't reach their ends.
Inputs may be any that keep to these rules, and one draw needn't show every extreme that they name: `lengths`: each row holds one long sequence of exactly 897 tokens, first or second (drawn from the seed), one short sequence of 102 to 126 tokens, and the padding last; the entries sum to 1024.
All inputs are finite; a program needn't handle non-finite values.
Results may differ from the reference program's by a relative error of at most 0.02.
Values may be sent and summed in bfloat16 or wider, within the bound.
A program may use at most 384 MiB of HBM per device.

```python
from functools import partial
import jax
import jax.numpy as jnp
from jax import lax

D = 2048
HEADS = 16
HEAD_DIM = 128
FF = 5632
CONV = 4
BLOCK = 64
MB = 2
NSEQ = 3
TOK_DEV = 128
GROUP = 1024
TOKENS = 4096
N_DP = 4


def draw_lengths(key, part):
    key = jax.random.fold_in(key, 11)
    first_key, second_key = jax.random.split(key)
    long_first = jax.random.randint(first_key, (MB, N_DP, 1), 0, 2)
    short_len = jax.random.randint(second_key, (MB, N_DP, 1), TOK_DEV * 4 // 5, TOK_DEV - 1)
    pad_len = TOK_DEV - 1 - short_len
    long_len = jnp.full((MB, N_DP, 1), GROUP - TOK_DEV + 1, jnp.int32)
    first_entry = jnp.where(long_first == 1, long_len, short_len)
    second_entry = jnp.where(long_first == 1, short_len, long_len)
    return jnp.concatenate([first_entry, second_entry, pad_len], axis=-1).astype(jnp.int32)


def steps_of(rng, dims, cuts, low, high):
    def one(axis_at, blocks):
        steps = jax.random.uniform(jax.random.fold_in(jax.random.fold_in(rng, 6), axis_at), (blocks,), jnp.float32, low / len(cuts), high / len(cuts))
        return jnp.repeat(jnp.exp(steps), dims[axis_at] // blocks).reshape((-1,) + (1,) * (len(dims) - axis_at - 1))

    factor_of = one(*cuts[0])
    for cut in cuts[1:]:
        factor_of = factor_of * one(*cut)
    return factor_of


def bell_draw(stream_key, shape, scale, bound, cuts=(), held_as=jnp.bfloat16):
    values = jax.random.normal(stream_key, shape, jnp.float32) * scale
    if len(cuts) > 0:
        values = steps_of(stream_key, shape, cuts, -0.22, 0.18) * values
    return jnp.clip(values, min=-bound, max=bound).astype(held_as)


def setup_inputs(seed: int = 0) -> dict:
    arg_keys = jax.random.split(jax.random.key(seed), 17)
    return {
        "inputs": bell_draw(arg_keys[0], (MB, TOKENS, D), 1.0, 6.0, ((1, 32),)),
        "lengths": draw_lengths(jax.random.fold_in(arg_keys[16], 71), 0),
        "norm_gain": jnp.clip(1.0 + 0.15 * jax.random.normal(arg_keys[2], (D,), jnp.float32), 0.25, 1.75).astype(jnp.bfloat16),
        "ffn_gain": jnp.clip(1.0 + 0.15 * jax.random.normal(arg_keys[3], (D,), jnp.float32), 0.25, 1.75).astype(jnp.bfloat16),
        "w_query": bell_draw(arg_keys[4], (D, D), D ** -0.5, 0.125, ((1, 8),)),
        "w_key": bell_draw(arg_keys[5], (D, D), D ** -0.5, 0.125, ((1, 8),)),
        "w_value": bell_draw(arg_keys[6], (D, D), D ** -0.5, 0.125, ((1, 8),)),
        "w_gate_out": bell_draw(arg_keys[7], (D, D), D ** -0.5, 0.125, ((1, 8),)),
        "w_beta": bell_draw(arg_keys[8], (D, HEADS), D ** -0.5, 0.125, ((1, 8),)),
        "conv_weight": bell_draw(arg_keys[9], (3, CONV, D), CONV ** -0.5, 3.0, ((2, 8),)),
        "head_gain": jnp.clip(1.0 + 0.15 * jax.random.normal(arg_keys[10], (HEADS, HEAD_DIM), jnp.float32), 0.25, 1.75).astype(jnp.bfloat16),
        "w_out": bell_draw(arg_keys[11], (D, D), (D // 2) ** -0.5, 0.1875, ((0, 8),)),
        "w_gate": bell_draw(arg_keys[12], (D, FF), D ** -0.5, 0.125, ((0, 4), (1, 8))),
        "w_up": bell_draw(arg_keys[13], (D, FF), D ** -0.5, 0.125, ((0, 4), (1, 8))),
        "w_down": bell_draw(arg_keys[14], (FF, D), (FF // 2) ** -0.5, 0.109375, ((0, 8), (1, 4))),
        "cotangent": bell_draw(arg_keys[15], (MB, TOKENS, D), 1.0, 6.0, ((1, 32),)),
    }


epsilon = 1e-06

@jax.custom_vjp
def low(v):
    return lax.optimization_barrier(v.astype(jnp.bfloat16)).astype(jnp.float32)

@jax.custom_vjp
def low_back(v):
    return v

def low_keep(v):
    return (low(v), None)

def low_pass(kept, grad):
    return (grad,)

def back_keep(v):
    return (v, None)

def back_low(kept, grad):
    return (low(grad),)
low.defvjp(low_keep, low_pass)
low_back.defvjp(back_keep, back_low)

def matmul(left_side, right_side):
    return jnp.dot(left_side.astype(jnp.float32), right_side.astype(jnp.float32), precision=lax.Precision.HIGHEST, preferred_element_type=jnp.float32)

def root_scale(row_values, gain_vector):
    return row_values * lax.rsqrt(lax.optimization_barrier(jnp.mean(row_values * row_values, axis=-1, keepdims=True)) + epsilon) * gain_vector

def delta_rule(queries, key_rows, value_rows, beta_rates, segment, block_rows):
    length_all = queries.shape[0]
    head_width = queries.shape[1]
    blocks = length_all // block_rows
    query_blocks = queries.reshape(blocks, block_rows, head_width)
    key_blocks = key_rows.reshape(blocks, block_rows, head_width)
    value_blocks = value_rows.reshape(blocks, block_rows, head_width)
    beta_blocks = beta_rates.reshape(blocks, block_rows)
    segment_blocks = segment.reshape(blocks, block_rows)
    before = jnp.concatenate([jnp.full((1,), -1, jnp.int32), segment_blocks[:-1, -1].astype(jnp.int32)])
    places = jnp.arange(block_rows, dtype=jnp.int32)
    strict = places[:, None] > places[None, :]
    within = places[:, None] >= places[None, :]
    same_doc = segment_blocks[:, :, None] == segment_blocks[:, None, :]
    key_gram = jnp.einsum('nid,njd->nij', key_blocks, key_blocks, precision=lax.Precision.HIGHEST)
    lower_part = jnp.where(same_doc & strict[None], key_gram * beta_blocks[:, :, None], 0.0)
    system = lower_part + jnp.eye(block_rows, dtype=jnp.float32)
    right_hand = jnp.concatenate([value_blocks, key_blocks], axis=2) * beta_blocks[:, :, None]
    solved = jax.scipy.linalg.solve_triangular(system, right_hand, lower=True, unit_diagonal=True)
    new_values = solved[:, :, :head_width]
    weighted_keys = solved[:, :, head_width:]
    query_gram = jnp.einsum('nid,njd->nij', query_blocks, key_blocks, precision=lax.Precision.HIGHEST)
    attention = jnp.where(same_doc & within[None], query_gram, 0.0)
    carried = (segment_blocks == before[:, None]).astype(jnp.float32)
    closing = (segment_blocks == segment_blocks[:, -1:]).astype(jnp.float32)

    def advance(memory, pieces):
        query_part, key_part, value_part, weight_part, score_part, carry_part, close_part = pieces
        corrected = value_part - carry_part[:, None] * matmul(weight_part, memory)
        output = carry_part[:, None] * matmul(query_part, memory) + matmul(score_part, corrected)
        memory = carry_part[-1] * memory + matmul(key_part.T, close_part[:, None] * corrected)
        return (memory, output)
    _, outputs = lax.scan(jax.checkpoint(advance), jnp.zeros((head_width, head_width), jnp.float32), (query_blocks, key_blocks, new_values, weighted_keys, attention, carried, closing))
    return outputs.reshape(length_all, head_width)

def mixer_block(projected, beta_logits, conv_weight, head_gain, segment, live_mask, block_rows):
    length_all = projected.shape[0]
    head_count = beta_logits.shape[1]
    inner_width = projected.shape[1] // 4
    head_width = inner_width // head_count
    channels = projected[:, :3 * inner_width]
    tap_count = conv_weight.shape[1]
    tap_weights = jnp.transpose(conv_weight, (1, 0, 2)).reshape(tap_count, 3 * inner_width)
    mixed_rows = channels * tap_weights[0]
    for offset in range(1, tap_count):
        shifted = jnp.concatenate([jnp.zeros((offset, 3 * inner_width), jnp.float32), channels[:-offset]], axis=0)
        earlier = jnp.concatenate([jnp.full((offset,), -1, jnp.int32), segment[:-offset]])
        valid_taps = (earlier == segment).astype(jnp.float32)
        mixed_rows = mixed_rows + shifted * tap_weights[offset] * valid_taps[:, None]
    activated = jax.nn.silu(mixed_rows).reshape(length_all, 3, head_count, head_width)
    queries = activated[:, 0]
    queries = queries * lax.rsqrt(lax.optimization_barrier(jnp.sum(queries * queries, axis=-1, keepdims=True)) + epsilon) * head_width ** (-0.5)
    key_rows = activated[:, 1]
    key_rows = key_rows * lax.rsqrt(lax.optimization_barrier(jnp.sum(key_rows * key_rows, axis=-1, keepdims=True)) + epsilon)
    value_rows = activated[:, 2]
    beta_rates = jax.nn.sigmoid(beta_logits) * live_mask[:, None]
    per_head = partial(delta_rule, segment=segment, block_rows=block_rows)
    outputs = jax.vmap(per_head, in_axes=1, out_axes=1)(queries, key_rows, value_rows, beta_rates)
    gate_rows = projected[:, 3 * inner_width:].reshape(length_all, head_count, head_width)
    row_scale = lax.rsqrt(lax.optimization_barrier(jnp.mean(outputs * outputs, axis=-1, keepdims=True)) + epsilon)
    gated_rows = outputs * row_scale * head_gain[None] * jax.nn.silu(gate_rows)
    return gated_rows.reshape(length_all, inner_width)

def slot_forward(params, rows_in, lengths_row):
    norm_gain, ffn_gain, w_query, w_key, w_value, w_gate_out, w_beta, conv_weight, head_gain, w_out, w_gate, w_up, w_down = params
    positions = jnp.arange(GROUP, dtype=jnp.int32)
    seq_ends = jnp.cumsum(lengths_row)[:-1].astype(jnp.int32)
    segment = lax.optimization_barrier(jnp.sum((positions[:, None] >= seq_ends[None, :]).astype(jnp.int32), axis=1)).astype(jnp.int32)
    live_mask = (segment < NSEQ - 1).astype(jnp.float32)
    normed_one = low(root_scale(rows_in, norm_gain))
    projected = low_back(matmul(normed_one, jnp.concatenate([w_query, w_key, w_value, w_gate_out], axis=1)))
    beta_logits = low_back(matmul(normed_one, w_beta))
    mixed_rows = low(mixer_block(projected, beta_logits, conv_weight, head_gain, segment, live_mask, BLOCK))
    hidden = rows_in + low_back(matmul(mixed_rows, w_out))
    normed_two = low(root_scale(hidden, ffn_gain))
    gate_values = low_back(matmul(normed_two, w_gate))
    up_values = low_back(matmul(normed_two, w_up))
    inner_rows = low(jax.nn.silu(gate_values) * up_values)
    return hidden + low_back(matmul(inner_rows, w_down))

def reference(inputs, lengths, norm_gain, ffn_gain, w_query, w_key, w_value, w_gate_out, w_beta, conv_weight, head_gain, w_out, w_gate, w_up, w_down, cotangent):
    params = tuple((weight.astype(jnp.float32) for weight in (norm_gain, ffn_gain, w_query, w_key, w_value, w_gate_out, w_beta, conv_weight, head_gain, w_out, w_gate, w_up, w_down)))
    slot_rows = inputs.astype(jnp.float32).reshape(MB * N_DP, GROUP, D)
    slot_lengths = lengths.reshape(MB * N_DP, NSEQ)

    def forward(weights, rows_all):

        def one_slot(carry_value, pieces):
            return (carry_value, jax.checkpoint(slot_forward)(weights, pieces[0], pieces[1]))
        _, results = lax.scan(one_slot, jnp.zeros((), jnp.float32), (rows_all, slot_lengths))
        return results
    results, pullback = jax.vjp(forward, params, slot_rows)
    weight_grads, rows_grad = pullback(cotangent.astype(jnp.float32).reshape(MB * N_DP, GROUP, D))
    norm_gain_grad, ffn_gain_grad, w_query_grad, w_key_grad, w_value_grad, w_gate_out_grad, w_beta_grad, conv_weight_grad, head_gain_grad, w_out_grad, w_gate_grad, w_up_grad, w_down_grad = weight_grads
    return (results.reshape(MB, TOKENS, D), rows_grad.reshape(MB, TOKENS, D), norm_gain_grad, ffn_gain_grad, w_query_grad, w_key_grad, w_value_grad, w_gate_out_grad, w_beta_grad, conv_weight_grad, head_gain_grad, w_out_grad, w_gate_grad, w_up_grad, w_down_grad)
```

```python
from functools import partial

import jax
import jax.numpy as jnp
from jax import lax
from jax.experimental import pallas as pl
from jax.experimental.pallas import tpu as pltpu
from jax.sharding import PartitionSpec as P


CHUNK = 128
HALO = 8
epsilon = 1e-06
highest = lax.Precision.HIGHEST
f32 = jnp.float32
bf16 = jnp.bfloat16


def product(left, right, left_dim, right_dim, exact=False):
    dims = (((left_dim,), (right_dim,)), ((), ()))
    if exact:
        return lax.dot_general(left, right, dims, precision=highest, preferred_element_type=f32)
    return lax.dot_general(
        left.astype(bf16), right.astype(bf16), dims, preferred_element_type=f32
    )


def sigmoid(x):
    return 1.0 / (1.0 + jnp.exp(-x))


def segment_tools(lengths_ref):
    ends = []
    total = 0
    for i in range(lengths_ref.shape[0] - 1):
        total = total + lengths_ref[i]
        ends.append(total)

    def segment_of(pos):
        result = 0
        for end in ends:
            result = result + (pos >= end).astype(jnp.int32)
        return result

    return segment_of, len(ends)


def chunk_masks(segment_of, base, chunk):
    col = base + lax.broadcasted_iota(jnp.int32, (chunk, 1), 0)
    row = base + lax.broadcasted_iota(jnp.int32, (1, chunk), 1)
    seg_col = segment_of(col)
    seg_row = segment_of(row)
    first = segment_of(base - 1)
    last = segment_of(base + chunk - 1)
    same = seg_col == seg_row
    strict = (same & (col > row)).astype(f32)
    within = (same & (col >= row)).astype(f32)
    has_past = base > 0
    carry = ((seg_col == first) & has_past).astype(f32)
    close = (seg_col == last).astype(f32)
    keep = ((first == last) & has_past).astype(f32)
    return strict, within, carry, close, keep


def level_masks(chunk):
    row = lax.broadcasted_iota(jnp.int32, (chunk, chunk), 0)
    col = lax.broadcasted_iota(jnp.int32, (chunk, chunk), 1)
    masks = []
    width = 1
    while width < chunk:
        mask = (
            (row // (2 * width) == col // (2 * width))
            & ((row // width) % 2 == 1)
            & ((col // width) % 2 == 0)
        )
        masks.append(mask)
        width *= 2
    return masks, (row == col).astype(f32)


def conv_part(proj_ref, tap_ref, segment_of, base, part, width, chunk):
    taps = tap_ref.shape[0] // 3
    cols = pl.ds(part * width, width)
    main = proj_ref[pl.ds(base, chunk), cols]
    prev = proj_ref[pl.ds(pl.multiple_of(jnp.maximum(base - HALO, 0), HALO), HALO), cols]
    full = jnp.concatenate([prev, main], axis=0)
    col = base + lax.broadcasted_iota(jnp.int32, (chunk, 1), 0)
    seg = segment_of(col)
    total = main * tap_ref[part * taps : part * taps + 1, :]
    shifted = [main]
    for s in range(1, taps):
        valid = (segment_of(col - s) == seg) & (col >= s)
        moved = jnp.where(valid, pltpu.roll(full, s, 0)[HALO:], 0.0)
        shifted.append(moved)
        total = total + moved * tap_ref[part * taps + s : part * taps + s + 1, :]
    return total, shifted


def heads_of(x, heads):
    return [x[:, h * 128 : (h + 1) * 128] for h in range(heads)]


def unit_rows(a, scale):
    r = lax.rsqrt(jnp.sum(a * a, axis=-1, keepdims=True) + epsilon)
    return a * (r * scale)


def mixer_forward_kernel(exact, group, lengths_ref, proj_ref, beta_ref, tap_ref, gain_ref,
                         mixed_ref, heads_ref, fixed_ref, delta_ref, state_ref, inverse_ref,
                         query_s, key_s, value_s, score_s):
    rows_all = proj_ref.shape[0]
    width = proj_ref.shape[1] // 4
    heads = width // 128
    chunk = CHUNK
    count = rows_all // chunk
    segment_of, segments = segment_tools(lengths_ref)

    @pl.loop(0, count)
    def _(c):
        base = pl.multiple_of(c * chunk, chunk)
        rows = pl.ds(base, chunk)
        for part, target in enumerate((query_s, key_s, value_s)):
            pre, _ = conv_part(proj_ref, tap_ref, segment_of, base, part, width, chunk)
            act = pre * sigmoid(pre)
            if part == 2:
                target[rows, :] = act
            else:
                scale = 128 ** (-0.5) if part == 0 else 1.0
                for h, a in enumerate(heads_of(act, heads)):
                    target[rows, h * 128 : (h + 1) * 128] = unit_rows(a, scale)

    def beta_of(base, h):
        pos = base + lax.broadcasted_iota(jnp.int32, (chunk, 1), 0)
        live = (segment_of(pos) < segments).astype(f32)
        return sigmoid(beta_ref[pl.ds(base, chunk), h : h + 1]) * live

    masks, eye = level_masks(chunk)

    @pl.loop(0, count // group)
    def _(g):
        lowers, places = [], []
        for i in range(group):
            c = g * group + i
            base = pl.multiple_of(c * chunk, chunk)
            strict, within, _, _, _ = chunk_masks(segment_of, base, chunk)
            for h in range(heads):
                cols = slice(h * 128, (h + 1) * 128)
                k = key_s[pl.ds(base, chunk), cols]
                q = query_s[pl.ds(base, chunk), cols]
                lowers.append(product(k, k, 1, 1, exact) * strict * beta_of(base, h))
                score_s[c * heads + h] = (product(q, k, 1, 1, exact) * within).astype(score_s.dtype)
                places.append(c * heads + h)
        inverses = [eye - jnp.where(masks[0], lower, 0.0) for lower in lowers]
        for mask in masks[1:]:
            steps = [product(jnp.where(mask, lower, 0.0), x, 1, 0, True) for lower, x in zip(lowers, inverses)]
            inverses = [x - product(x, step, 1, 0, True) for x, step in zip(inverses, steps)]
        for place, x in zip(places, inverses):
            inverse_ref[place] = x

    def advance(c, states):
        base = pl.multiple_of(c * chunk, chunk)
        rows = pl.ds(base, chunk)
        _, _, carry, close, keep = chunk_masks(segment_of, base, chunk)
        new_states = []
        for h in range(heads):
            cols = slice(h * 128, (h + 1) * 128)
            state = states[h]
            k = key_s[rows, cols]
            q = query_s[rows, cols]
            delta = value_s[rows, cols] - carry * product(k, state, 1, 0, exact)
            fixed = product(inverse_ref[c * heads + h], beta_of(base, h) * delta, 1, 0, exact)
            out = carry * product(q, state, 1, 0, exact) + product(
                score_s[c * heads + h], fixed, 1, 0, exact)
            state_ref[c * heads + h] = state
            new_states.append(keep * state + product(k, close * fixed, 0, 0, exact))
            delta_ref[rows, cols] = delta
            fixed_ref[rows, cols] = fixed
            heads_ref[rows, cols] = out
            gate = proj_ref[rows, 3 * width + h * 128 : 3 * width + (h + 1) * 128]
            r = lax.rsqrt(jnp.mean(out * out, axis=-1, keepdims=True) + epsilon)
            mixed_ref[rows, cols] = (
                out * r * gain_ref[h : h + 1, :] * (gate * sigmoid(gate))
            ).astype(mixed_ref.dtype)
        return tuple(new_states)

    lax.fori_loop(0, count, advance, tuple(jnp.zeros((128, 128), f32) for _ in range(heads)))


def mixer_backward_kernel(exact, lengths_ref, proj_ref, beta_ref, tap_ref, gain_ref, grad_ref,
                          heads_ref, fixed_ref, delta_ref, state_ref, inverse_ref,
                          dproj_ref, dbeta_ref, dtap_ref, dgain_ref,
                          query_s, key_s, pre_s, dout_s, dpre_s):
    rows_all = proj_ref.shape[0]
    width = proj_ref.shape[1] // 4
    heads = width // 128
    chunk = CHUNK
    count = rows_all // chunk
    taps = tap_ref.shape[0] // 3
    segment_of, segments = segment_tools(lengths_ref)
    dgain_ref[...] = jnp.zeros_like(dgain_ref)
    dtap_ref[...] = jnp.zeros_like(dtap_ref)

    @pl.loop(0, count)
    def _(c):
        base = pl.multiple_of(c * chunk, chunk)
        rows = pl.ds(base, chunk)
        for part in range(3):
            pre, _ = conv_part(proj_ref, tap_ref, segment_of, base, part, width, chunk)
            pre_s[rows, part * width : (part + 1) * width] = pre
            if part < 2:
                act = pre * sigmoid(pre)
                target = (query_s, key_s)[part]
                scale = 128 ** (-0.5) if part == 0 else 1.0
                for h, a in enumerate(heads_of(act, heads)):
                    target[rows, h * 128 : (h + 1) * 128] = unit_rows(a, scale)
        for h in range(heads):
            cols = slice(h * 128, (h + 1) * 128)
            gate_cols = slice(3 * width + h * 128, 3 * width + (h + 1) * 128)
            out = heads_ref[rows, cols]
            gate = proj_ref[rows, gate_cols]
            grad = grad_ref[rows, cols].astype(f32)
            gain = gain_ref[h : h + 1, :]
            sg = sigmoid(gate)
            silu = gate * sg
            r = lax.rsqrt(jnp.mean(out * out, axis=-1, keepdims=True) + epsilon)
            normed = out * r
            dgain_ref[h : h + 1, :] += jnp.sum(grad * normed * silu, axis=0, keepdims=True)
            dproj_ref[rows, gate_cols] = (
                grad * normed * gain * (sg * (1.0 + gate * (1.0 - sg)))
            ).astype(dproj_ref.dtype)
            weighted = grad * gain * silu
            dout_s[rows, cols] = r * weighted - out * (r * r * r) * jnp.mean(
                weighted * out, axis=-1, keepdims=True)

    dpre_s[rows_all : rows_all + HALO, :] = jnp.zeros((HALO, 3 * width), f32)

    def retreat(step, dstates):
        c = count - 1 - step
        base = pl.multiple_of(c * chunk, chunk)
        rows = pl.ds(base, chunk)
        strict, within, carry, close, keep = chunk_masks(segment_of, base, chunk)
        pos = base + lax.broadcasted_iota(jnp.int32, (chunk, 1), 0)
        live = (segment_of(pos) < segments).astype(f32)
        new_dstates = []
        for h in range(heads):
            cols = slice(h * 128, (h + 1) * 128)
            place = c * heads + h
            k = key_s[rows, cols]
            q = query_s[rows, cols]
            dout = dout_s[rows, cols]
            state = state_ref[place]
            inverse = inverse_ref[place]
            fixed = fixed_ref[rows, cols]
            delta = delta_ref[rows, cols]
            dstate = dstates[h]
            rate = sigmoid(beta_ref[rows, h : h + 1])
            beta = rate * live
            scores = product(q, k, 1, 1, exact) * within
            gram = product(k, k, 1, 1, exact) * strict
            dfixed = product(scores, dout, 0, 0, exact) + close * product(k, dstate, 1, 0, exact)
            drhs = product(inverse, dfixed, 0, 0, exact)
            ddelta = beta * drhs
            carried_dout = carry * dout
            carried_ddelta = carry * ddelta
            new_dstates.append(
                keep * dstate
                + product(q, carried_dout, 0, 0, exact)
                - product(k, carried_ddelta, 0, 0, exact)
            )
            dscores = product(dout, fixed, 1, 1, exact) * within
            dlower = -product(drhs, fixed, 1, 1, exact) * strict
            dgram = beta * dlower
            dq = product(carried_dout, state, 1, 1, exact) + product(dscores, k, 1, 0, exact)
            dk = (
                product(dscores, q, 0, 0, exact)
                + close * product(fixed, dstate, 1, 1, exact)
                - product(carried_ddelta, state, 1, 1, exact)
                + product(dgram, k, 1, 0, exact)
                + product(dgram, k, 0, 0, exact)
            )
            drate = live * (
                jnp.sum(drhs * delta, axis=-1, keepdims=True)
                + jnp.sum(dlower * gram, axis=-1, keepdims=True)
            )
            dbeta_ref[rows, h : h + 1] = (drate * rate * (1.0 - rate)).astype(dbeta_ref.dtype)
            for part, da in enumerate((dq, dk, ddelta)):
                part_cols = slice(part * width + h * 128, part * width + (h + 1) * 128)
                pre = pre_s[rows, part_cols]
                sg = sigmoid(pre)
                if part < 2:
                    a = pre * sg
                    scale = 128 ** (-0.5) if part == 0 else 1.0
                    r = lax.rsqrt(jnp.sum(a * a, axis=-1, keepdims=True) + epsilon)
                    da = (scale * r) * (da - a * (r * r) * jnp.sum(da * a, axis=-1, keepdims=True))
                dpre_s[rows, part_cols] = da * (sg * (1.0 + pre * (1.0 - sg)))
        return tuple(new_dstates)

    lax.fori_loop(0, count, retreat, tuple(jnp.zeros((128, 128), f32) for _ in range(heads)))

    @pl.loop(0, count)
    def _(c):
        base = pl.multiple_of(c * chunk, chunk)
        rows = pl.ds(base, chunk)
        col = base + lax.broadcasted_iota(jnp.int32, (chunk, 1), 0)
        seg = segment_of(col)
        for part in range(3):
            cols = slice(part * width, (part + 1) * width)
            _, shifted = conv_part(proj_ref, tap_ref, segment_of, base, part, width, chunk)
            full = dpre_s[pl.ds(base, chunk + HALO), cols]
            main = full[:chunk]
            total = main * tap_ref[part * taps : part * taps + 1, :]
            for s in range(taps):
                at = slice(part * taps + s, part * taps + s + 1)
                dtap_ref[at, :] += jnp.sum(main * shifted[s], axis=0, keepdims=True)
                if s > 0:
                    valid = (segment_of(col + s) == seg) & (col + s < rows_all)
                    moved = pltpu.roll(full, chunk + HALO - s, 0)[:chunk]
                    total = total + jnp.where(valid, moved, 0.0) * tap_ref[at, :]
            dproj_ref[rows, cols] = total.astype(dproj_ref.dtype)


def vmem():
    return pl.BlockSpec(memory_space=pltpu.VMEM)


def mixer_forward(lengths_row, projected, beta_logits, taps, gain, exact=True, group=4):
    rows, wide = projected.shape
    width = wide // 4
    heads = width // 128
    places = rows // CHUNK * heads
    group = min(group, rows // CHUNK)
    return pl.pallas_call(
        partial(mixer_forward_kernel, exact, group),
        out_shape=(
            jax.ShapeDtypeStruct((rows, width), bf16),
            jax.ShapeDtypeStruct((rows, width), f32),
            jax.ShapeDtypeStruct((rows, width), f32),
            jax.ShapeDtypeStruct((rows, width), f32),
            jax.ShapeDtypeStruct((places, 128, 128), f32),
            jax.ShapeDtypeStruct((places, CHUNK, CHUNK), f32),
        ),
        in_specs=[pl.BlockSpec(memory_space=pltpu.SMEM)] + [vmem()] * 4,
        out_specs=(vmem(),) * 6,
        scratch_shapes=[pltpu.VMEM((rows, width), f32)] * 3
        + [pltpu.VMEM((places, CHUNK, CHUNK), f32 if exact else bf16)],
        compiler_params=pltpu.CompilerParams(vmem_limit_bytes=48 * 2**20),
        cost_estimate=pl.CostEstimate(flops=10**10, bytes_accessed=10**7, transcendentals=10**6),
        name="mixer_forward",
    )(lengths_row, projected, beta_logits, taps, gain)


def mixer_backward(lengths_row, projected, beta_logits, taps, gain, grad, saved, exact=True):
    rows, wide = projected.shape
    width = wide // 4
    heads = width // 128
    return pl.pallas_call(
        partial(mixer_backward_kernel, exact),
        out_shape=(
            jax.ShapeDtypeStruct((rows, wide), bf16),
            jax.ShapeDtypeStruct((rows, heads), bf16),
            jax.ShapeDtypeStruct(taps.shape, f32),
            jax.ShapeDtypeStruct(gain.shape, f32),
        ),
        in_specs=[pl.BlockSpec(memory_space=pltpu.SMEM)] + [vmem()] * 10,
        out_specs=(vmem(),) * 4,
        scratch_shapes=[pltpu.VMEM((rows, width), f32)] * 2
        + [pltpu.VMEM((rows, 3 * width), f32), pltpu.VMEM((rows, width), f32),
           pltpu.VMEM((rows + HALO, 3 * width), f32)],
        compiler_params=pltpu.CompilerParams(vmem_limit_bytes=56 * 2**20),
        cost_estimate=pl.CostEstimate(flops=10**10, bytes_accessed=10**7, transcendentals=10**6),
        name="mixer_backward",
    )(lengths_row, projected, beta_logits, taps, gain, grad, *saved)


def root_scale(row_values, gain_vector):
    row_scale = lax.rsqrt(jnp.mean(row_values * row_values, axis=-1, keepdims=True) + epsilon)
    return (row_values * row_scale * gain_vector, row_scale)


def norm_backward(row_values, row_scale, gain_vector, normed_grad):
    weighted = normed_grad * gain_vector
    rows_grad = row_scale * weighted - row_values * row_scale * row_scale * row_scale * jnp.mean(
        weighted * row_values, axis=-1, keepdims=True
    )
    gain_grad = jnp.sum(normed_grad * row_values * row_scale, axis=0)
    return (rows_grad, gain_grad)


def gather(x, axis_name, axis=0):
    return lax.all_gather(x, axis_name, axis=axis, tiled=True)


def scatter_sum(x, axis_name, axis=0):
    return lax.psum_scatter(
        x.astype(bf16), axis_name, scatter_dimension=axis, tiled=True
    ).astype(f32)


def dot(a, b):
    return jnp.dot(a, b, preferred_element_type=f32)


def dot_nt(a, b):
    return jnp.einsum("tk,nk->tn", a, b, preferred_element_type=f32)


def dot_tn(a, b):
    return jnp.einsum("tm,tn->mn", a, b, preferred_element_type=f32)


def per_device(
    inputs,
    lengths,
    norm_gain,
    ffn_gain,
    w_query,
    w_key,
    w_value,
    w_gate_out,
    w_beta,
    conv_weight,
    head_gain,
    w_out,
    w_gate,
    w_up,
    w_down,
    cotangent,
):
    batches = range(inputs.shape[0])
    local_width = w_query.shape[1]
    w_inner = jnp.concatenate([w_query, w_key, w_value, w_gate_out], axis=1)
    taps = conv_weight.astype(f32).reshape(-1, local_width)
    gain_heads = head_gain.astype(f32)
    gain_one = gather(norm_gain, "dp").astype(f32)
    gain_two = gather(ffn_gain, "dp").astype(f32)
    rows_in = [inputs[m].astype(f32) for m in batches]
    one = [root_scale(rows, gain_one) for rows in rows_in]
    gathered_one = [gather(one[m][0].astype(bf16), "tensor") for m in batches]
    projected = [dot(rows, w_inner) for rows in gathered_one]
    beta_logits = [dot(rows, w_beta) for rows in gathered_one]
    gate_full = gather(w_gate, "dp")
    up_full = gather(w_up, "dp")
    down_full = gather(w_down, "dp", 1)
    out_full = gather(w_out, "tensor")
    grad_rows = [gather(cotangent[m], "tensor") for m in batches]
    mixed, saved = [], []
    for m in batches:
        low, *kept = mixer_forward(lengths[m, 0], projected[m], beta_logits[m], taps, gain_heads)
        mixed.append(low)
        saved.append(kept)
    token_heads = [
        lax.all_to_all(low, "tensor", split_axis=0, concat_axis=1, tiled=True) for low in mixed
    ]
    hidden = [rows_in[m] + dot(token_heads[m], out_full) for m in batches]
    two = [root_scale(rows, gain_two) for rows in hidden]
    gathered_two = [gather(two[m][0].astype(bf16), "tensor") for m in batches]
    result_rows, inner_rows, gate_grads, up_grads, hidden_grads = [], [], [], [], []
    attended_low, mixed_grads = [], []
    gain_two_sum = 0.0
    for m in batches:
        gate_values = dot(gathered_two[m], gate_full)
        up_values = dot(gathered_two[m], up_full)
        sigmoid_gate = jax.nn.sigmoid(gate_values)
        silu_gate = gate_values * sigmoid_gate
        inner = (silu_gate * up_values).astype(bf16)
        inner_grad = dot_nt(grad_rows[m], down_full)
        gate_grad = (
            inner_grad * up_values * sigmoid_gate * (1.0 + gate_values * (1.0 - sigmoid_gate))
        ).astype(bf16)
        up_grad = (inner_grad * silu_gate).astype(bf16)
        normed_grad = scatter_sum(dot_nt(gate_grad, gate_full) + dot_nt(up_grad, up_full), "tensor")
        result_rows.append(hidden[m] + scatter_sum(dot(inner, down_full), "tensor"))
        norm_grad, gain_part = norm_backward(hidden[m], two[m][1], gain_two, normed_grad)
        gain_two_sum = gain_two_sum + gain_part
        hidden_grad = cotangent[m].astype(f32) + norm_grad
        low = hidden_grad.astype(bf16)
        token_grad = dot_nt(low, out_full).astype(bf16)
        mixed_grads.append(
            lax.all_to_all(token_grad, "tensor", split_axis=1, concat_axis=0, tiled=True)
        )
        inner_rows.append(inner)
        gate_grads.append(gate_grad)
        up_grads.append(up_grad)
        hidden_grads.append(hidden_grad)
        attended_low.append(low)
    grad_all = jnp.concatenate(grad_rows)
    two_all = jnp.concatenate(gathered_two)
    gate_share = scatter_sum(dot_tn(two_all, jnp.concatenate(gate_grads)), "dp")
    up_share = scatter_sum(dot_tn(two_all, jnp.concatenate(up_grads)), "dp")
    down_share = scatter_sum(dot_tn(jnp.concatenate(inner_rows), grad_all), "dp", 1)
    out_grad = lax.psum_scatter(
        dot_tn(jnp.concatenate(token_heads), jnp.concatenate(attended_low)).astype(bf16),
        "tensor",
        scatter_dimension=0,
        tiled=True,
    )
    input_grads, projected_low, beta_low = [], [], []
    taps_sum, heads_sum, gain_one_sum = 0.0, 0.0, 0.0
    for m in batches:
        projected_grad, beta_grad, taps_part, heads_part = mixer_backward(
            lengths[m, 0], projected[m], beta_logits[m], taps, gain_heads, mixed_grads[m], saved[m]
        )
        normed_grad = scatter_sum(dot_nt(projected_grad, w_inner) + dot_nt(beta_grad, w_beta), "tensor")
        norm_grad, gain_part = norm_backward(rows_in[m], one[m][1], gain_one, normed_grad)
        input_grads.append(hidden_grads[m] + norm_grad)
        gain_one_sum = gain_one_sum + gain_part
        taps_sum = taps_sum + taps_part
        heads_sum = heads_sum + heads_part
        projected_low.append(projected_grad)
        beta_low.append(beta_grad)
    one_all = jnp.concatenate(gathered_one)
    inner_sum = dot_tn(one_all, jnp.concatenate(projected_low))
    beta_sum = dot_tn(one_all, jnp.concatenate(beta_low))
    gain_one_total = lax.psum_scatter(
        gain_one_sum, ("dp", "tensor"), scatter_dimension=0, tiled=True)
    gain_two_total = lax.psum_scatter(
        gain_two_sum, ("dp", "tensor"), scatter_dimension=0, tiled=True)
    inner_total, beta_total, conv_total, heads_total, out_total = (
        lax.psum(part.astype(bf16), "dp").astype(f32)
        for part in (inner_sum, beta_sum, taps_sum, heads_sum, out_grad)
    )
    return (
        jnp.stack(result_rows),
        jnp.stack(input_grads),
        gain_one_total,
        gain_two_total,
        inner_total[:, :local_width],
        inner_total[:, local_width : 2 * local_width],
        inner_total[:, 2 * local_width : 3 * local_width],
        inner_total[:, 3 * local_width :],
        beta_total,
        conv_total.reshape(conv_weight.shape),
        heads_total,
        out_total,
        gate_share,
        up_share,
        down_share,
    )


def solution(mesh):
    in_specs = (
        P(None, ("dp", "tensor"), None),
        P(None, "dp", None),
        P("dp"),
        P("dp"),
        P(None, "tensor"),
        P(None, "tensor"),
        P(None, "tensor"),
        P(None, "tensor"),
        P(None, "tensor"),
        P(None, None, "tensor"),
        P("tensor", None),
        P("tensor", None),
        P("dp", "tensor"),
        P("dp", "tensor"),
        P("tensor", "dp"),
        P(None, ("dp", "tensor"), None),
    )
    out_specs = (
        P(None, ("dp", "tensor"), None),
        P(None, ("dp", "tensor"), None),
        P(("dp", "tensor")),
        P(("dp", "tensor")),
        P(None, "tensor"),
        P(None, "tensor"),
        P(None, "tensor"),
        P(None, "tensor"),
        P(None, "tensor"),
        P(None, None, "tensor"),
        P("tensor", None),
        P("tensor", None),
        P("dp", "tensor"),
        P("dp", "tensor"),
        P("tensor", "dp"),
    )
    return jax.shard_map(
        per_device, mesh=mesh, in_specs=in_specs, out_specs=out_specs, check_vma=False
    )
```

```python
from functools import partial

import jax
import jax.numpy as jnp
from jax import lax
from jax.experimental import pallas as pl
from jax.experimental.pallas import tpu as pltpu
from jax.sharding import PartitionSpec as P


CHUNK = 128
HALO = 8
epsilon = 1e-06
highest = lax.Precision.HIGHEST
f32 = jnp.float32
bf16 = jnp.bfloat16


def product(left, right, left_dim, right_dim, exact=False):
    dims = (((left_dim,), (right_dim,)), ((), ()))
    if exact:
        return lax.dot_general(left, right, dims, precision=highest, preferred_element_type=f32)
    return lax.dot_general(
        left.astype(bf16), right.astype(bf16), dims, preferred_element_type=f32
    )


def sigmoid(x):
    return 1.0 / (1.0 + jnp.exp(-x))


def segment_tools(lengths_ref):
    ends = []
    total = 0
    for i in range(lengths_ref.shape[0] - 1):
        total = total + lengths_ref[i]
        ends.append(total)

    def segment_of(pos):
        result = 0
        for end in ends:
            result = result + (pos >= end).astype(jnp.int32)
        return result

    return segment_of, len(ends)


def chunk_masks(segment_of, base, chunk):
    col = base + lax.broadcasted_iota(jnp.int32, (chunk, 1), 0)
    row = base + lax.broadcasted_iota(jnp.int32, (1, chunk), 1)
    seg_col = segment_of(col)
    seg_row = segment_of(row)
    first = segment_of(base - 1)
    last = segment_of(base + chunk - 1)
    same = seg_col == seg_row
    strict = (same & (col > row)).astype(f32)
    within = (same & (col >= row)).astype(f32)
    has_past = base > 0
    carry = ((seg_col == first) & has_past).astype(f32)
    close = (seg_col == last).astype(f32)
    keep = ((first == last) & has_past).astype(f32)
    return strict, within, carry, close, keep


def level_masks(chunk):
    row = lax.broadcasted_iota(jnp.int32, (chunk, chunk), 0)
    col = lax.broadcasted_iota(jnp.int32, (chunk, chunk), 1)
    masks = []
    width = 1
    while width < chunk:
        mask = (
            (row // (2 * width) == col // (2 * width))
            & ((row // width) % 2 == 1)
            & ((col // width) % 2 == 0)
        )
        masks.append(mask)
        width *= 2
    return masks, (row == col).astype(f32)


def conv_part(proj_ref, tap_ref, segment_of, base, part, width, chunk):
    taps = tap_ref.shape[0] // 3
    cols = pl.ds(part * width, width)
    main = proj_ref[pl.ds(base, chunk), cols]
    prev = proj_ref[pl.ds(pl.multiple_of(jnp.maximum(base - HALO, 0), HALO), HALO), cols]
    full = jnp.concatenate([prev, main], axis=0)
    col = base + lax.broadcasted_iota(jnp.int32, (chunk, 1), 0)
    seg = segment_of(col)
    total = main * tap_ref[part * taps : part * taps + 1, :]
    shifted = [main]
    for s in range(1, taps):
        valid = (segment_of(col - s) == seg) & (col >= s)
        moved = jnp.where(valid, pltpu.roll(full, s, 0)[HALO:], 0.0)
        shifted.append(moved)
        total = total + moved * tap_ref[part * taps + s : part * taps + s + 1, :]
    return total, shifted


def heads_of(x, heads):
    return [x[:, h * 128 : (h + 1) * 128] for h in range(heads)]


def unit_rows(a, scale):
    r = lax.rsqrt(jnp.sum(a * a, axis=-1, keepdims=True) + epsilon)
    return a * (r * scale)


def mixer_forward_kernel(exact, group, lengths_ref, proj_ref, beta_ref, tap_ref, gain_ref,
                         mixed_ref, heads_ref, fixed_ref, delta_ref, state_ref, inverse_ref,
                         query_s, key_s, value_s, score_s):
    rows_all = proj_ref.shape[0]
    width = proj_ref.shape[1] // 4
    heads = width // 128
    chunk = CHUNK
    count = rows_all // chunk
    segment_of, segments = segment_tools(lengths_ref)

    @pl.loop(0, count)
    def _(c):
        base = pl.multiple_of(c * chunk, chunk)
        rows = pl.ds(base, chunk)
        for part, target in enumerate((query_s, key_s, value_s)):
            pre, _ = conv_part(proj_ref, tap_ref, segment_of, base, part, width, chunk)
            act = pre * sigmoid(pre)
            if part == 2:
                target[rows, :] = act
            else:
                scale = 128 ** (-0.5) if part == 0 else 1.0
                for h, a in enumerate(heads_of(act, heads)):
                    target[rows, h * 128 : (h + 1) * 128] = unit_rows(a, scale)

    def beta_of(base, h):
        pos = base + lax.broadcasted_iota(jnp.int32, (chunk, 1), 0)
        live = (segment_of(pos) < segments).astype(f32)
        return sigmoid(beta_ref[pl.ds(base, chunk), h : h + 1]) * live

    masks, eye = level_masks(chunk)

    @pl.loop(0, count // group)
    def _(g):
        lowers, places = [], []
        for i in range(group):
            c = g * group + i
            base = pl.multiple_of(c * chunk, chunk)
            strict, within, _, _, _ = chunk_masks(segment_of, base, chunk)
            for h in range(heads):
                cols = slice(h * 128, (h + 1) * 128)
                k = key_s[pl.ds(base, chunk), cols]
                q = query_s[pl.ds(base, chunk), cols]
                lowers.append(product(k, k, 1, 1, exact) * strict * beta_of(base, h))
                score_s[c * heads + h] = (product(q, k, 1, 1, exact) * within).astype(score_s.dtype)
                places.append(c * heads + h)
        inverses = [eye - jnp.where(masks[0], lower, 0.0) for lower in lowers]
        for mask in masks[1:]:
            steps = [product(jnp.where(mask, lower, 0.0), x, 1, 0, True) for lower, x in zip(lowers, inverses)]
            inverses = [x - product(x, step, 1, 0, True) for x, step in zip(inverses, steps)]
        for place, x in zip(places, inverses):
            inverse_ref[place] = x

    def advance(c, states):
        base = pl.multiple_of(c * chunk, chunk)
        rows = pl.ds(base, chunk)
        _, _, carry, close, keep = chunk_masks(segment_of, base, chunk)
        new_states = []
        for h in range(heads):
            cols = slice(h * 128, (h + 1) * 128)
            state = states[h]
            k = key_s[rows, cols]
            q = query_s[rows, cols]
            delta = value_s[rows, cols] - carry * product(k, state, 1, 0, exact)
            fixed = product(inverse_ref[c * heads + h], beta_of(base, h) * delta, 1, 0, exact)
            out = carry * product(q, state, 1, 0, exact) + product(
                score_s[c * heads + h], fixed, 1, 0, exact)
            state_ref[c * heads + h] = state
            new_states.append(keep * state + product(k, close * fixed, 0, 0, exact))
            delta_ref[rows, cols] = delta
            fixed_ref[rows, cols] = fixed
            heads_ref[rows, cols] = out
            gate = proj_ref[rows, 3 * width + h * 128 : 3 * width + (h + 1) * 128]
            r = lax.rsqrt(jnp.mean(out * out, axis=-1, keepdims=True) + epsilon)
            mixed_ref[rows, cols] = (
                out * r * gain_ref[h : h + 1, :] * (gate * sigmoid(gate))
            ).astype(mixed_ref.dtype)
        return tuple(new_states)

    lax.fori_loop(0, count, advance, tuple(jnp.zeros((128, 128), f32) for _ in range(heads)))


def mixer_backward_kernel(exact, lengths_ref, proj_ref, beta_ref, tap_ref, gain_ref, grad_ref,
                          heads_ref, fixed_ref, delta_ref, state_ref, inverse_ref,
                          dproj_ref, dbeta_ref, dtap_ref, dgain_ref,
                          query_s, key_s, pre_s, dout_s, dpre_s):
    rows_all = proj_ref.shape[0]
    width = proj_ref.shape[1] // 4
    heads = width // 128
    chunk = CHUNK
    count = rows_all // chunk
    taps = tap_ref.shape[0] // 3
    segment_of, segments = segment_tools(lengths_ref)
    dgain_ref[...] = jnp.zeros_like(dgain_ref)
    dtap_ref[...] = jnp.zeros_like(dtap_ref)

    @pl.loop(0, count)
    def _(c):
        base = pl.multiple_of(c * chunk, chunk)
        rows = pl.ds(base, chunk)
        for part in range(3):
            pre, _ = conv_part(proj_ref, tap_ref, segment_of, base, part, width, chunk)
            pre_s[rows, part * width : (part + 1) * width] = pre
            if part < 2:
                act = pre * sigmoid(pre)
                target = (query_s, key_s)[part]
                scale = 128 ** (-0.5) if part == 0 else 1.0
                for h, a in enumerate(heads_of(act, heads)):
                    target[rows, h * 128 : (h + 1) * 128] = unit_rows(a, scale)
        for h in range(heads):
            cols = slice(h * 128, (h + 1) * 128)
            gate_cols = slice(3 * width + h * 128, 3 * width + (h + 1) * 128)
            out = heads_ref[rows, cols]
            gate = proj_ref[rows, gate_cols]
            grad = grad_ref[rows, cols].astype(f32)
            gain = gain_ref[h : h + 1, :]
            sg = sigmoid(gate)
            silu = gate * sg
            r = lax.rsqrt(jnp.mean(out * out, axis=-1, keepdims=True) + epsilon)
            normed = out * r
            dgain_ref[h : h + 1, :] += jnp.sum(grad * normed * silu, axis=0, keepdims=True)
            dproj_ref[rows, gate_cols] = (
                grad * normed * gain * (sg * (1.0 + gate * (1.0 - sg)))
            ).astype(dproj_ref.dtype)
            weighted = grad * gain * silu
            dout_s[rows, cols] = r * weighted - out * (r * r * r) * jnp.mean(
                weighted * out, axis=-1, keepdims=True)

    dpre_s[rows_all : rows_all + HALO, :] = jnp.zeros((HALO, 3 * width), f32)

    def retreat(step, dstates):
        c = count - 1 - step
        base = pl.multiple_of(c * chunk, chunk)
        rows = pl.ds(base, chunk)
        strict, within, carry, close, keep = chunk_masks(segment_of, base, chunk)
        pos = base + lax.broadcasted_iota(jnp.int32, (chunk, 1), 0)
        live = (segment_of(pos) < segments).astype(f32)
        new_dstates = []
        for h in range(heads):
            cols = slice(h * 128, (h + 1) * 128)
            place = c * heads + h
            k = key_s[rows, cols]
            q = query_s[rows, cols]
            dout = dout_s[rows, cols]
            state = state_ref[place]
            inverse = inverse_ref[place]
            fixed = fixed_ref[rows, cols]
            delta = delta_ref[rows, cols]
            dstate = dstates[h]
            rate = sigmoid(beta_ref[rows, h : h + 1])
            beta = rate * live
            scores = product(q, k, 1, 1, exact) * within
            gram = product(k, k, 1, 1, exact) * strict
            dfixed = product(scores, dout, 0, 0, exact) + close * product(k, dstate, 1, 0, exact)
            drhs = product(inverse, dfixed, 0, 0, exact)
            ddelta = beta * drhs
            carried_dout = carry * dout
            carried_ddelta = carry * ddelta
            new_dstates.append(
                keep * dstate
                + product(q, carried_dout, 0, 0, exact)
                - product(k, carried_ddelta, 0, 0, exact)
            )
            dscores = product(dout, fixed, 1, 1, exact) * within
            dlower = -product(drhs, fixed, 1, 1, exact) * strict
            dgram = beta * dlower
            dq = product(carried_dout, state, 1, 1, exact) + product(dscores, k, 1, 0, exact)
            dk = (
                product(dscores, q, 0, 0, exact)
                + close * product(fixed, dstate, 1, 1, exact)
                - product(carried_ddelta, state, 1, 1, exact)
                + product(dgram, k, 1, 0, exact)
                + product(dgram, k, 0, 0, exact)
            )
            drate = live * (
                jnp.sum(drhs * delta, axis=-1, keepdims=True)
                + jnp.sum(dlower * gram, axis=-1, keepdims=True)
            )
            dbeta_ref[rows, h : h + 1] = (drate * rate * (1.0 - rate)).astype(dbeta_ref.dtype)
            for part, da in enumerate((dq, dk, ddelta)):
                part_cols = slice(part * width + h * 128, part * width + (h + 1) * 128)
                pre = pre_s[rows, part_cols]
                sg = sigmoid(pre)
                if part < 2:
                    a = pre * sg
                    scale = 128 ** (-0.5) if part == 0 else 1.0
                    r = lax.rsqrt(jnp.sum(a * a, axis=-1, keepdims=True) + epsilon)
                    da = (scale * r) * (da - a * (r * r) * jnp.sum(da * a, axis=-1, keepdims=True))
                dpre_s[rows, part_cols] = da * (sg * (1.0 + pre * (1.0 - sg)))
        return tuple(new_dstates)

    lax.fori_loop(0, count, retreat, tuple(jnp.zeros((128, 128), f32) for _ in range(heads)))

    @pl.loop(0, count)
    def _(c):
        base = pl.multiple_of(c * chunk, chunk)
        rows = pl.ds(base, chunk)
        col = base + lax.broadcasted_iota(jnp.int32, (chunk, 1), 0)
        seg = segment_of(col)
        for part in range(3):
            cols = slice(part * width, (part + 1) * width)
            _, shifted = conv_part(proj_ref, tap_ref, segment_of, base, part, width, chunk)
            full = dpre_s[pl.ds(base, chunk + HALO), cols]
            main = full[:chunk]
            total = main * tap_ref[part * taps : part * taps + 1, :]
            for s in range(taps):
                at = slice(part * taps + s, part * taps + s + 1)
                dtap_ref[at, :] += jnp.sum(main * shifted[s], axis=0, keepdims=True)
                if s > 0:
                    valid = (segment_of(col + s) == seg) & (col + s < rows_all)
                    moved = pltpu.roll(full, chunk + HALO - s, 0)[:chunk]
                    total = total + jnp.where(valid, moved, 0.0) * tap_ref[at, :]
            dproj_ref[rows, cols] = total.astype(dproj_ref.dtype)


def vmem():
    return pl.BlockSpec(memory_space=pltpu.VMEM)


def mixer_forward(lengths_row, projected, beta_logits, taps, gain, exact=True, group=4):
    rows, wide = projected.shape
    width = wide // 4
    heads = width // 128
    places = rows // CHUNK * heads
    group = min(group, rows // CHUNK)
    return pl.pallas_call(
        partial(mixer_forward_kernel, exact, group),
        out_shape=(
            jax.ShapeDtypeStruct((rows, width), bf16),
            jax.ShapeDtypeStruct((rows, width), f32),
            jax.ShapeDtypeStruct((rows, width), f32),
            jax.ShapeDtypeStruct((rows, width), f32),
            jax.ShapeDtypeStruct((places, 128, 128), f32),
            jax.ShapeDtypeStruct((places, CHUNK, CHUNK), f32),
        ),
        in_specs=[pl.BlockSpec(memory_space=pltpu.SMEM)] + [vmem()] * 4,
        out_specs=(vmem(),) * 6,
        scratch_shapes=[pltpu.VMEM((rows, width), f32)] * 3
        + [pltpu.VMEM((places, CHUNK, CHUNK), f32 if exact else bf16)],
        compiler_params=pltpu.CompilerParams(vmem_limit_bytes=48 * 2**20),
        cost_estimate=pl.CostEstimate(flops=10**10, bytes_accessed=10**7, transcendentals=10**6),
        name="mixer_forward",
    )(lengths_row, projected, beta_logits, taps, gain)


def mixer_backward(lengths_row, projected, beta_logits, taps, gain, grad, saved, exact=True):
    rows, wide = projected.shape
    width = wide // 4
    heads = width // 128
    return pl.pallas_call(
        partial(mixer_backward_kernel, exact),
        out_shape=(
            jax.ShapeDtypeStruct((rows, wide), bf16),
            jax.ShapeDtypeStruct((rows, heads), bf16),
            jax.ShapeDtypeStruct(taps.shape, f32),
            jax.ShapeDtypeStruct(gain.shape, f32),
        ),
        in_specs=[pl.BlockSpec(memory_space=pltpu.SMEM)] + [vmem()] * 10,
        out_specs=(vmem(),) * 4,
        scratch_shapes=[pltpu.VMEM((rows, width), f32)] * 2
        + [pltpu.VMEM((rows, 3 * width), f32), pltpu.VMEM((rows, width), f32),
           pltpu.VMEM((rows + HALO, 3 * width), f32)],
        compiler_params=pltpu.CompilerParams(vmem_limit_bytes=56 * 2**20),
        cost_estimate=pl.CostEstimate(flops=10**10, bytes_accessed=10**7, transcendentals=10**6),
        name="mixer_backward",
    )(lengths_row, projected, beta_logits, taps, gain, grad, *saved)


NT = (((1,), (1,)), ((), ()))


def other(axis_name):
    return {axis_name: 1 - lax.axis_index(axis_name)}


def ffn_kernel(x_ref, c_ref, w_ref, out_ref, ngrad_ref, wgrad_ref,
               xs, cs, ws, inner_s, gate_s, up_s, acts_t, part, crecv, drecv, nrecv, stage, ctile,
               ag_send, ag_recv, pair_send, pair_recv, rs_send, rs_recv, c_sem, w_sem, g_sem, t_sem):
    half = xs.shape[1] // 2
    rows = 2 * half
    model = xs.shape[2]
    hidden = ws.shape[1]
    lines = w_ref.shape[0]
    quarter = w_ref.shape[2]
    tile_f = 256
    tile_d = min(512, model)
    tile_w = min(256, model)

    def remote(src, dst, send, recv, axis_name):
        return pltpu.make_async_remote_copy(
            src_ref=src, dst_ref=dst, send_sem=send, recv_sem=recv,
            device_id=other(axis_name), device_id_type=pl.DeviceIdType.MESH)

    def halves(ref, index, h):
        return ref.at[index, pl.ds(h * half, half)]

    barrier = pltpu.get_barrier_semaphore()
    for axis_name in ("core", "x", "y"):
        pl.semaphore_signal(
            barrier, inc=1, device_id=other(axis_name), device_id_type=pl.DeviceIdType.MESH)

    weight_copies = [
        pltpu.make_async_copy(
            w_ref.at[line, kind], ws.at[kind, pl.ds(line * quarter, quarter)], w_sem.at[line, kind])
        for line in range(lines) for kind in range(3)
    ]
    for copy in weight_copies:
        copy.start()

    def slot_of(step):
        return (1 - lax.rem(step, 2)) * 4 + step // 2

    def c_copy(step, slot):
        return pltpu.make_async_copy(
            c_ref.at[slot], cs.at[lax.rem(step, 2)], c_sem.at[lax.rem(step, 2)])

    c_copy(0, 4).start()
    pl.semaphore_wait(barrier, 3)

    own_pair = remote(x_ref, xs.at[4], ag_send.at[0], ag_recv.at[0], "core")
    own_x = [remote(x_ref.at[pl.ds(h * half, half)], halves(xs, 1, h), ag_send.at[1 + h], ag_recv.at[1 + h], "x") for h in range(2)]
    own_y = [remote(x_ref.at[pl.ds(h * half, half)], halves(xs, 2, h), ag_send.at[3 + h], ag_recv.at[3 + h], "y") for h in range(2)]
    relay_y = remote(halves(xs, 1, 0), halves(xs, 3, 0), ag_send.at[5], ag_recv.at[5], "y")
    relay_x = remote(halves(xs, 2, 1), halves(xs, 3, 1), ag_send.at[6], ag_recv.at[6], "x")
    pair_of = [None] + [remote(xs.at[j], xs.at[4 + j], ag_send.at[6 + j], ag_recv.at[6 + j], "core") for j in (1, 2, 3)]
    own_pair.start()
    own_x[0].start()
    own_y[1].start()
    own_x[1].start()
    own_y[0].start()
    own_copy = pltpu.make_async_copy(x_ref, xs.at[0], t_sem.at[0])
    own_copy.start()
    own_copy.wait()
    for copy in weight_copies:
        copy.wait()

    def part_send(j):
        return remote(part.at[lax.rem(j, 2)], crecv.at[j], pair_send.at[j], pair_recv.at[j], "core")

    x_sends = [[remote(crecv.at[1, a, pl.ds(h * half, half)], nrecv.at[0, a, pl.ds(h * half, half)],
                       rs_send.at[a * 2 + h], rs_recv.at[a * 2 + h], "x") for a in range(2)] for h in range(2)]
    y_sends = [[remote(crecv.at[2, a, pl.ds(h * half, half)], nrecv.at[1, a, pl.ds(h * half, half)],
                       rs_send.at[4 + a * 2 + h], rs_recv.at[4 + a * 2 + h], "y") for a in range(2)] for h in range(2)]
    d_sends = [[remote(crecv.at[3, a, pl.ds(h * half, half)], drecv.at[a, pl.ds(h * half, half)],
                       rs_send.at[8 + a * 2 + h], rs_recv.at[8 + a * 2 + h], ("x", "y")[h]) for a in range(2)] for h in range(2)]

    @pl.loop(0, 8)
    def _(step):
        j = step // 2
        slot = slot_of(step)
        pairing = lax.rem(step, 2) == 0

        @pl.when(step < 7)
        def _():
            c_copy(step + 1, slot_of(step + 1)).start()

        @pl.when(step == 0)
        def _():
            own_pair.wait_recv()

        @pl.when(step == 2)
        def _():
            own_x[0].wait_recv()
            relay_y.start()
            own_y[1].wait_recv()
            relay_x.start()
            own_x[1].wait_recv()
            pair_of[1].start()
            own_y[0].wait_recv()
            pair_of[2].start()
            pair_of[1].wait_recv()

        @pl.when(step == 4)
        def _():
            relay_y.wait_recv()
            relay_x.wait_recv()
            pair_of[3].start()
            pair_of[2].wait_recv()

        @pl.when(step == 6)
        def _():
            pair_of[3].wait_recv()

        c_copy(step, slot).wait()

        for start in range(0, hidden, tile_f):
            size = min(tile_f, hidden - start)
            cols = slice(start, start + size)
            x = xs[slot]
            gate = lax.dot_general(x, ws[0, cols, :], NT, preferred_element_type=f32)
            up = lax.dot_general(x, ws[1, cols, :], NT, preferred_element_type=f32)
            grad = lax.dot_general(cs[lax.rem(step, 2)], ws[2, cols, :], NT, preferred_element_type=f32)
            sg = sigmoid(gate)
            silu = gate * sg
            inner = (silu * up).astype(bf16)
            gate_grad = (grad * up * sg * (1.0 + gate * (1.0 - sg))).astype(bf16)
            up_grad = (grad * silu).astype(bf16)
            places = pl.ds(pl.multiple_of(slot * rows, rows), rows)
            for kind, (value, target) in enumerate(((gate_grad, gate_s), (up_grad, up_s), (inner, inner_s))):
                target[:, cols] = value
                acts_t[kind, cols, places] = value.T

        @pl.when(pairing & (step >= 4))
        def _():
            part_send(j - 2).wait_send()

        place = jnp.where(pairing, lax.rem(j, 2), 2)
        for start in range(0, model, tile_d):
            cols = slice(start, start + tile_d)
            part[place, 0, :, cols] = jnp.dot(
                inner_s[...], ws[2, :, cols], preferred_element_type=f32).astype(bf16)
            part[place, 1, :, cols] = (
                jnp.dot(gate_s[...], ws[0, :, cols], preferred_element_type=f32)
                + jnp.dot(up_s[...], ws[1, :, cols], preferred_element_type=f32)
            ).astype(bf16)

        @pl.when(pairing)
        def _():
            part_send(j).start()

        @pl.when(jnp.logical_not(pairing))
        def _():
            part_send(j).wait_recv()
            for a in range(2):
                for start in range(0, model, tile_d):
                    cols = slice(start, start + tile_d)
                    crecv[j, a, :, cols] = (
                        crecv[j, a, :, cols].astype(f32) + part[2, a, :, cols].astype(f32)
                    ).astype(bf16)

        @pl.when(step == 3)
        def _():
            for copy in x_sends[0]:
                copy.start()

        @pl.when(step == 5)
        def _():
            for copy in y_sends[1]:
                copy.start()

        @pl.when(step == 7)
        def _():
            for h in range(2):
                for copy in d_sends[h]:
                    copy.start()

    tiles = model // tile_w

    def c_tile(t):
        return pltpu.make_async_copy(
            c_ref.at[:, :, pl.ds(pl.multiple_of(t * tile_w, tile_w), tile_w)], ctile.at[lax.rem(t, 2)], t_sem.at[lax.rem(t, 2)])

    def grad_copy(kind, t, line):
        return pltpu.make_async_copy(
            stage.at[lax.rem(t, 2), pl.ds(line * quarter, quarter)],
            wgrad_ref.at[line, kind, :, pl.ds(pl.multiple_of(t * tile_w, tile_w), tile_w)],
            g_sem.at[lax.rem(t, 2), line])

    def weight_grads(kind):
        if kind == 2:
            c_tile(0).start()

        @pl.loop(0, tiles)
        def _(t):
            if kind == 2:
                @pl.when(t + 1 < tiles)
                def _():
                    c_tile(t + 1).start()
                c_tile(t).wait()
                right = ctile[lax.rem(t, 2)].reshape(8 * rows, tile_w)
            else:
                right = xs[:, :, pl.ds(pl.multiple_of(t * tile_w, tile_w), tile_w)].reshape(8 * rows, tile_w)

            @pl.when(t >= 2)
            def _():
                for line in range(lines):
                    grad_copy(kind, t - 2, line).wait()

            stage[lax.rem(t, 2)] = jnp.dot(
                acts_t[kind], right, preferred_element_type=f32).astype(bf16)
            for line in range(lines):
                grad_copy(kind, t, line).start()

        for t in range(max(tiles - 2, 0), tiles):
            for line in range(lines):
                grad_copy(kind, t, line).wait()

    weight_grads(0)
    for h in range(2):
        j = 2 - h
        for a in range(2):
            d_sends[h][a].wait_recv()
            at = pl.ds(h * half, half)
            crecv[j, a, at, :] = (
                crecv[j, a, at, :].astype(f32) + drecv[a, at, :].astype(f32)).astype(bf16)
        for copy in (y_sends, x_sends)[h][h]:
            copy.start()
    weight_grads(1)
    weight_grads(2)
    for a, target in enumerate((out_ref, ngrad_ref)):
        for h in range(2):
            x_sends[h][a].wait_recv()
            y_sends[h][a].wait_recv()
            at = pl.ds(h * half, half)
            target[at, :] = (
                crecv[0, a, at, :].astype(f32)
                + nrecv[0, a, at, :].astype(f32)
                + nrecv[1, a, at, :].astype(f32)
            )
    own_pair.wait_send()
    for h in range(2):
        own_x[h].wait_send()
        own_y[h].wait_send()
        for a in range(2):
            x_sends[h][a].wait_send()
            y_sends[h][a].wait_send()
            d_sends[h][a].wait_send()
    relay_x.wait_send()
    relay_y.wait_send()
    for j in (1, 2, 3):
        pair_of[j].wait_send()
    part_send(2).wait_send()
    part_send(3).wait_send()


def ffn_plane(x_own, c_all, weights):
    rows, model = x_own.shape
    lines, _, quarter, _ = weights.shape
    hidden = lines * quarter
    tile_w = min(256, model)
    sems = pltpu.SemaphoreType.DMA
    anywhere = pl.BlockSpec(memory_space=pl.ANY)
    return pl.pallas_call(
        ffn_kernel,
        out_shape=(
            jax.ShapeDtypeStruct((rows, model), f32),
            jax.ShapeDtypeStruct((rows, model), f32),
            jax.ShapeDtypeStruct(weights.shape, bf16),
        ),
        in_specs=[anywhere] * 3,
        out_specs=(vmem(), vmem(), anywhere),
        scratch_shapes=[
            pltpu.VMEM((8, rows, model), bf16),
            pltpu.VMEM((2, rows, model), bf16),
            pltpu.VMEM((3, hidden, model), bf16),
            pltpu.VMEM((rows, hidden), bf16),
            pltpu.VMEM((rows, hidden), bf16),
            pltpu.VMEM((rows, hidden), bf16),
            pltpu.VMEM((3, hidden, 8 * rows), bf16),
            pltpu.VMEM((3, 2, rows, model), bf16),
            pltpu.VMEM((4, 2, rows, model), bf16),
            pltpu.VMEM((2, rows, model), bf16),
            pltpu.VMEM((2, 2, rows, model), bf16),
            pltpu.VMEM((2, hidden, tile_w), bf16),
            pltpu.VMEM((2, 8, rows, tile_w), bf16),
            sems((10,)), sems((10,)), sems((4,)), sems((4,)), sems((12,)), sems((12,)),
            sems((2,)), sems((lines, 3)), sems((2, lines)), sems((2,)),
        ],
        compiler_params=pltpu.CompilerParams(
            collective_id=2, has_side_effects=True, vmem_limit_bytes=62 * 2**20),
        cost_estimate=pl.CostEstimate(flops=8 * 10**10, bytes_accessed=4 * 10**7, transcendentals=10**6),
        name="ffn_plane",
    )(x_own, c_all, weights)


def root_scale(row_values, gain_vector):
    row_scale = lax.rsqrt(jnp.mean(row_values * row_values, axis=-1, keepdims=True) + epsilon)
    return (row_values * row_scale * gain_vector, row_scale)


def norm_backward(row_values, row_scale, gain_vector, normed_grad):
    weighted = normed_grad * gain_vector
    rows_grad = row_scale * weighted - row_values * row_scale * row_scale * row_scale * jnp.mean(
        weighted * row_values, axis=-1, keepdims=True
    )
    gain_grad = jnp.sum(normed_grad * row_values * row_scale, axis=0)
    return (rows_grad, gain_grad)


DP = ("x", "core")
TP = ("z", "y")


def gather(x, axis_name, axis=0):
    return lax.all_gather(x, axis_name, axis=axis, tiled=True)


def scatter_sum(x, axis_name, axis=0):
    return lax.psum_scatter(
        x.astype(bf16), axis_name, scatter_dimension=axis, tiled=True
    ).astype(f32)


def dot(a, b):
    return jnp.dot(a, b, preferred_element_type=f32)


def dot_nt(a, b):
    return jnp.einsum("tk,nk->tn", a, b, preferred_element_type=f32)


def dot_tn(a, b):
    return jnp.einsum("tm,tn->mn", a, b, preferred_element_type=f32)


def exchange(x, axis_name, distance=1):
    size = lax.axis_size(axis_name)
    return lax.ppermute(x, axis_name, [(i, i ^ distance) for i in range(size)])


def swap_blocks(blocks):
    size = lax.axis_size(DP)
    me = lax.axis_index(DP)
    pieces = []
    for r in range(size):
        block = lax.dynamic_index_in_dim(blocks, me ^ r, keepdims=False)
        pieces.append(exchange(block, DP, r) if r else block)
    pieces = jnp.stack(pieces)
    return [lax.dynamic_index_in_dim(pieces, me ^ q, keepdims=False) for q in range(size)]


def plane_weights(w_gate, w_up, w_down):
    size = lax.axis_size(DP)
    local = jnp.stack([w_gate.T, w_up.T, w_down])
    kinds, hidden, part = local.shape
    quarter = hidden // size
    blocks = local.reshape(kinds, size, quarter, part).swapaxes(0, 1)
    own = jnp.concatenate(swap_blocks(blocks), axis=2)
    own = own.reshape(kinds * quarter, size * part)
    return gather(own, "z").reshape(-1, kinds, quarter, size * part)


def plane_weight_grads(grads):
    size = lax.axis_size(DP)
    lines, kinds, quarter, model = grads.shape
    own = lax.psum_scatter(
        grads.reshape(lines * kinds * quarter, model), "z", scatter_dimension=0, tiled=True)
    blocks = own.reshape(kinds * quarter, size, model // size).swapaxes(0, 1)
    pieces = [piece.reshape(kinds, quarter, -1) for piece in swap_blocks(blocks)]
    whole = jnp.concatenate(pieces, axis=1).astype(f32)
    return whole[0].T, whole[1].T, whole[2]


def plane_rows(x):
    for axis_name in ("x", "y", "core"):
        x = jnp.concatenate([x, exchange(x, axis_name)])
    return x


def feed_forward_plane(normed, cotangents, w_gate, w_up, w_down):
    weights = plane_weights(w_gate, w_up, w_down)
    rows = jnp.concatenate(normed)
    count, model = rows.shape
    c_all = plane_rows(cotangents.reshape(1, count, model))
    out, normed_grad, grads = ffn_plane(rows, c_all, weights)
    per_batch = (len(normed), count // len(normed), model)
    return out.reshape(per_batch), normed_grad.reshape(per_batch), plane_weight_grads(grads)


def feed_forward_groups(normed, cotangents, w_gate, w_up, w_down):
    gate_full = gather(w_gate, DP)
    up_full = gather(w_up, DP)
    down_full = gather(w_down, DP, 1)
    outs, normed_grads, inner_rows, gate_grads, up_grads, rows, grad_rows = [], [], [], [], [], [], []
    for m in range(len(normed)):
        rows.append(gather(normed[m], TP))
        grad_rows.append(gather(cotangents[m], TP))
        gate_values = dot(rows[m], gate_full)
        up_values = dot(rows[m], up_full)
        sigmoid_gate = jax.nn.sigmoid(gate_values)
        silu_gate = gate_values * sigmoid_gate
        inner = (silu_gate * up_values).astype(bf16)
        inner_grad = dot_nt(grad_rows[m], down_full)
        gate_grad = (
            inner_grad * up_values * sigmoid_gate * (1.0 + gate_values * (1.0 - sigmoid_gate))
        ).astype(bf16)
        up_grad = (inner_grad * silu_gate).astype(bf16)
        normed_grads.append(scatter_sum(dot_nt(gate_grad, gate_full) + dot_nt(up_grad, up_full), TP))
        outs.append(scatter_sum(dot(inner, down_full), TP))
        inner_rows.append(inner)
        gate_grads.append(gate_grad)
        up_grads.append(up_grad)
    grad_all = jnp.concatenate(grad_rows)
    rows_all = jnp.concatenate(rows)
    gate_share = scatter_sum(dot_tn(rows_all, jnp.concatenate(gate_grads)), DP)
    up_share = scatter_sum(dot_tn(rows_all, jnp.concatenate(up_grads)), DP)
    down_share = scatter_sum(dot_tn(jnp.concatenate(inner_rows), grad_all), DP, 1)
    return outs, normed_grads, (gate_share, up_share, down_share)


def per_device(
    inputs,
    lengths,
    norm_gain,
    ffn_gain,
    w_query,
    w_key,
    w_value,
    w_gate_out,
    w_beta,
    conv_weight,
    head_gain,
    w_out,
    w_gate,
    w_up,
    w_down,
    cotangent,
):
    batches = range(inputs.shape[0])
    local_width = w_query.shape[1]
    planar = all(lax.axis_size(name) == 2 for name in ("x", "core", "y"))
    w_inner = jnp.concatenate([w_query, w_key, w_value, w_gate_out], axis=1)
    taps = conv_weight.astype(f32).reshape(-1, local_width)
    gain_heads = head_gain.astype(f32)
    gain_one = gather(norm_gain, DP).astype(f32)
    gain_two = gather(ffn_gain, DP).astype(f32)
    rows_in = [inputs[m].astype(f32) for m in batches]
    one = [root_scale(rows, gain_one) for rows in rows_in]
    gathered_one = [gather(one[m][0].astype(bf16), TP) for m in batches]
    projected = [dot(rows, w_inner) for rows in gathered_one]
    beta_logits = [dot(rows, w_beta) for rows in gathered_one]
    out_full = gather(w_out, TP)
    mixed, saved = [], []
    for m in batches:
        low, *kept = mixer_forward(lengths[m, 0], projected[m], beta_logits[m], taps, gain_heads)
        mixed.append(low)
        saved.append(kept)
    token_heads = [
        lax.all_to_all(low, TP, split_axis=0, concat_axis=1, tiled=True) for low in mixed
    ]
    hidden = [rows_in[m] + dot(token_heads[m], out_full) for m in batches]
    two = [root_scale(rows, gain_two) for rows in hidden]
    feed_forward = feed_forward_plane if planar else feed_forward_groups
    ffn_out, normed_grads, (gate_share, up_share, down_share) = feed_forward(
        [two[m][0].astype(bf16) for m in batches], cotangent, w_gate, w_up, w_down)
    result_rows, hidden_grads, attended_low, mixed_grads = [], [], [], []
    gain_two_sum = 0.0
    for m in batches:
        result_rows.append(hidden[m] + ffn_out[m])
        norm_grad, gain_part = norm_backward(hidden[m], two[m][1], gain_two, normed_grads[m])
        gain_two_sum = gain_two_sum + gain_part
        hidden_grad = cotangent[m].astype(f32) + norm_grad
        low = hidden_grad.astype(bf16)
        token_grad = dot_nt(low, out_full).astype(bf16)
        mixed_grads.append(
            lax.all_to_all(token_grad, TP, split_axis=1, concat_axis=0, tiled=True)
        )
        hidden_grads.append(hidden_grad)
        attended_low.append(low)
    out_grad = lax.psum_scatter(
        dot_tn(jnp.concatenate(token_heads), jnp.concatenate(attended_low)).astype(bf16),
        TP,
        scatter_dimension=0,
        tiled=True,
    )
    input_grads, projected_low, beta_low = [], [], []
    taps_sum, heads_sum, gain_one_sum = 0.0, 0.0, 0.0
    for m in batches:
        projected_grad, beta_grad, taps_part, heads_part = mixer_backward(
            lengths[m, 0], projected[m], beta_logits[m], taps, gain_heads, mixed_grads[m], saved[m]
        )
        normed_grad = scatter_sum(dot_nt(projected_grad, w_inner) + dot_nt(beta_grad, w_beta), TP)
        norm_grad, gain_part = norm_backward(rows_in[m], one[m][1], gain_one, normed_grad)
        input_grads.append(hidden_grads[m] + norm_grad)
        gain_one_sum = gain_one_sum + gain_part
        taps_sum = taps_sum + taps_part
        heads_sum = heads_sum + heads_part
        projected_low.append(projected_grad)
        beta_low.append(beta_grad)
    one_all = jnp.concatenate(gathered_one)
    inner_sum = dot_tn(one_all, jnp.concatenate(projected_low))
    beta_sum = dot_tn(one_all, jnp.concatenate(beta_low))
    gain_totals = lax.psum_scatter(
        jnp.stack([gain_one_sum, gain_two_sum]), DP + TP, scatter_dimension=1, tiled=True)
    inner_total, beta_total, conv_total, heads_total, out_total = (
        lax.psum(part.astype(bf16), DP).astype(f32)
        for part in (inner_sum, beta_sum, taps_sum, heads_sum, out_grad)
    )
    return (
        jnp.stack(result_rows),
        jnp.stack(input_grads),
        gain_totals[0],
        gain_totals[1],
        inner_total[:, :local_width],
        inner_total[:, local_width : 2 * local_width],
        inner_total[:, 2 * local_width : 3 * local_width],
        inner_total[:, 3 * local_width :],
        beta_total,
        conv_total.reshape(conv_weight.shape),
        heads_total,
        out_total,
        gate_share,
        up_share,
        down_share,
    )


def solution(mesh):
    dp, tensor = mesh.shape["dp"], mesh.shape["tensor"]
    inner = 2 if tensor == 8 else 4
    axes = ("x", "core", "z", "y")
    fine = jax.sharding.Mesh(
        mesh.devices.reshape(dp // 2, 2, tensor // inner, inner), axes)
    tokens = P(None, DP + TP, None)
    in_specs = (
        tokens,
        P(None, DP, None),
        P(DP),
        P(DP),
        P(None, TP),
        P(None, TP),
        P(None, TP),
        P(None, TP),
        P(None, TP),
        P(None, None, TP),
        P(TP, None),
        P(TP, None),
        P(DP, TP),
        P(DP, TP),
        P(TP, DP),
        tokens,
    )
    out_specs = (
        tokens,
        tokens,
        P(DP + TP),
        P(DP + TP),
        P(None, TP),
        P(None, TP),
        P(None, TP),
        P(None, TP),
        P(None, TP),
        P(None, None, TP),
        P(TP, None),
        P(TP, None),
        P(DP, TP),
        P(DP, TP),
        P(TP, DP),
    )
    return jax.shard_map(
        per_device, mesh=fine, in_specs=in_specs, out_specs=out_specs, check_vma=False
    )
```

```python
from functools import partial

import jax
import jax.numpy as jnp
from jax import lax
from jax.experimental import pallas as pl
from jax.experimental.pallas import tpu as pltpu
from jax.sharding import PartitionSpec as P


CHUNK = 128
HALO = 8
epsilon = 1e-06
highest = lax.Precision.HIGHEST
f32 = jnp.float32
bf16 = jnp.bfloat16


def product(left, right, left_dim, right_dim, exact=False):
    dims = (((left_dim,), (right_dim,)), ((), ()))
    if exact:
        return lax.dot_general(left, right, dims, precision=highest, preferred_element_type=f32)
    return lax.dot_general(
        left.astype(bf16), right.astype(bf16), dims, preferred_element_type=f32
    )


def sigmoid(x):
    return 1.0 / (1.0 + jnp.exp(-x))


def segment_tools(lengths_ref):
    ends = []
    total = 0
    for i in range(lengths_ref.shape[0] - 1):
        total = total + lengths_ref[i]
        ends.append(total)

    def segment_of(pos):
        result = 0
        for end in ends:
            result = result + (pos >= end).astype(jnp.int32)
        return result

    return segment_of, len(ends)


def chunk_masks(segment_of, base, chunk):
    col = base + lax.broadcasted_iota(jnp.int32, (chunk, 1), 0)
    row = base + lax.broadcasted_iota(jnp.int32, (1, chunk), 1)
    seg_col = segment_of(col)
    seg_row = segment_of(row)
    first = segment_of(base - 1)
    last = segment_of(base + chunk - 1)
    same = seg_col == seg_row
    strict = (same & (col > row)).astype(f32)
    within = (same & (col >= row)).astype(f32)
    has_past = base > 0
    carry = ((seg_col == first) & has_past).astype(f32)
    close = (seg_col == last).astype(f32)
    keep = ((first == last) & has_past).astype(f32)
    return strict, within, carry, close, keep


def level_masks(chunk):
    row = lax.broadcasted_iota(jnp.int32, (chunk, chunk), 0)
    col = lax.broadcasted_iota(jnp.int32, (chunk, chunk), 1)
    masks = []
    width = 1
    while width < chunk:
        mask = (
            (row // (2 * width) == col // (2 * width))
            & ((row // width) % 2 == 1)
            & ((col // width) % 2 == 0)
        )
        masks.append(mask)
        width *= 2
    return masks, (row == col).astype(f32)


def conv_part(proj_ref, tap_ref, segment_of, base, part, width, chunk):
    taps = tap_ref.shape[0] // 3
    cols = pl.ds(part * width, width)
    main = proj_ref[pl.ds(base, chunk), cols]
    prev = proj_ref[pl.ds(pl.multiple_of(jnp.maximum(base - HALO, 0), HALO), HALO), cols]
    full = jnp.concatenate([prev, main], axis=0)
    col = base + lax.broadcasted_iota(jnp.int32, (chunk, 1), 0)
    seg = segment_of(col)
    total = main * tap_ref[part * taps : part * taps + 1, :]
    shifted = [main]
    for s in range(1, taps):
        valid = (segment_of(col - s) == seg) & (col >= s)
        moved = jnp.where(valid, pltpu.roll(full, s, 0)[HALO:], 0.0)
        shifted.append(moved)
        total = total + moved * tap_ref[part * taps + s : part * taps + s + 1, :]
    return total, shifted


def heads_of(x, heads):
    return [x[:, h * 128 : (h + 1) * 128] for h in range(heads)]


def unit_rows(a, scale):
    r = lax.rsqrt(jnp.sum(a * a, axis=-1, keepdims=True) + epsilon)
    return a * (r * scale)


def mixer_forward_kernel(exact, group, lengths_ref, proj_ref, beta_ref, tap_ref, gain_ref,
                         mixed_ref, heads_ref, fixed_ref, delta_ref, state_ref, inverse_ref,
                         query_s, key_s, value_s, score_s):
    rows_all = proj_ref.shape[0]
    width = proj_ref.shape[1] // 4
    heads = width // 128
    chunk = CHUNK
    count = rows_all // chunk
    segment_of, segments = segment_tools(lengths_ref)

    @pl.loop(0, count)
    def _(c):
        base = pl.multiple_of(c * chunk, chunk)
        rows = pl.ds(base, chunk)
        for part, target in enumerate((query_s, key_s, value_s)):
            pre, _ = conv_part(proj_ref, tap_ref, segment_of, base, part, width, chunk)
            act = pre * sigmoid(pre)
            if part == 2:
                target[rows, :] = act
            else:
                scale = 128 ** (-0.5) if part == 0 else 1.0
                for h, a in enumerate(heads_of(act, heads)):
                    target[rows, h * 128 : (h + 1) * 128] = unit_rows(a, scale)

    def beta_of(base, h):
        pos = base + lax.broadcasted_iota(jnp.int32, (chunk, 1), 0)
        live = (segment_of(pos) < segments).astype(f32)
        return sigmoid(beta_ref[pl.ds(base, chunk), h : h + 1]) * live

    masks, eye = level_masks(chunk)

    @pl.loop(0, count // group)
    def _(g):
        lowers, places = [], []
        for i in range(group):
            c = g * group + i
            base = pl.multiple_of(c * chunk, chunk)
            strict, within, _, _, _ = chunk_masks(segment_of, base, chunk)
            for h in range(heads):
                cols = slice(h * 128, (h + 1) * 128)
                k = key_s[pl.ds(base, chunk), cols]
                q = query_s[pl.ds(base, chunk), cols]
                lowers.append(product(k, k, 1, 1, exact) * strict * beta_of(base, h))
                score_s[c * heads + h] = (product(q, k, 1, 1, exact) * within).astype(score_s.dtype)
                places.append(c * heads + h)
        inverses = [eye - jnp.where(masks[0], lower, 0.0) for lower in lowers]
        for mask in masks[1:]:
            steps = [product(jnp.where(mask, lower, 0.0), x, 1, 0, True) for lower, x in zip(lowers, inverses)]
            inverses = [x - product(x, step, 1, 0, True) for x, step in zip(inverses, steps)]
        for place, x in zip(places, inverses):
            inverse_ref[place] = x

    def advance(c, states):
        base = pl.multiple_of(c * chunk, chunk)
        rows = pl.ds(base, chunk)
        _, _, carry, close, keep = chunk_masks(segment_of, base, chunk)
        new_states = []
        for h in range(heads):
            cols = slice(h * 128, (h + 1) * 128)
            state = states[h]
            k = key_s[rows, cols]
            q = query_s[rows, cols]
            delta = value_s[rows, cols] - carry * product(k, state, 1, 0, exact)
            fixed = product(inverse_ref[c * heads + h], beta_of(base, h) * delta, 1, 0, exact)
            out = carry * product(q, state, 1, 0, exact) + product(
                score_s[c * heads + h], fixed, 1, 0, exact)
            state_ref[c * heads + h] = state
            new_states.append(keep * state + product(k, close * fixed, 0, 0, exact))
            delta_ref[rows, cols] = delta
            fixed_ref[rows, cols] = fixed
            heads_ref[rows, cols] = out
            gate = proj_ref[rows, 3 * width + h * 128 : 3 * width + (h + 1) * 128]
            r = lax.rsqrt(jnp.mean(out * out, axis=-1, keepdims=True) + epsilon)
            mixed_ref[rows, cols] = (
                out * r * gain_ref[h : h + 1, :] * (gate * sigmoid(gate))
            ).astype(mixed_ref.dtype)
        return tuple(new_states)

    lax.fori_loop(0, count, advance, tuple(jnp.zeros((128, 128), f32) for _ in range(heads)))


def mixer_backward_kernel(exact, lengths_ref, proj_ref, beta_ref, tap_ref, gain_ref, grad_ref,
                          heads_ref, fixed_ref, delta_ref, state_ref, inverse_ref,
                          dproj_ref, dbeta_ref, dtap_ref, dgain_ref,
                          query_s, key_s, pre_s, dout_s, dpre_s):
    rows_all = proj_ref.shape[0]
    width = proj_ref.shape[1] // 4
    heads = width // 128
    chunk = CHUNK
    count = rows_all // chunk
    taps = tap_ref.shape[0] // 3
    segment_of, segments = segment_tools(lengths_ref)
    dgain_ref[...] = jnp.zeros_like(dgain_ref)
    dbeta_ref[...] = jnp.zeros_like(dbeta_ref)
    dtap_ref[...] = jnp.zeros_like(dtap_ref)

    @pl.loop(0, count)
    def _(c):
        base = pl.multiple_of(c * chunk, chunk)
        rows = pl.ds(base, chunk)
        for part in range(3):
            pre, _ = conv_part(proj_ref, tap_ref, segment_of, base, part, width, chunk)
            pre_s[rows, part * width : (part + 1) * width] = pre
            if part < 2:
                act = pre * sigmoid(pre)
                target = (query_s, key_s)[part]
                scale = 128 ** (-0.5) if part == 0 else 1.0
                for h, a in enumerate(heads_of(act, heads)):
                    target[rows, h * 128 : (h + 1) * 128] = unit_rows(a, scale)
        for h in range(heads):
            cols = slice(h * 128, (h + 1) * 128)
            gate_cols = slice(3 * width + h * 128, 3 * width + (h + 1) * 128)
            out = heads_ref[rows, cols]
            gate = proj_ref[rows, gate_cols]
            grad = grad_ref[rows, cols].astype(f32)
            gain = gain_ref[h : h + 1, :]
            sg = sigmoid(gate)
            silu = gate * sg
            r = lax.rsqrt(jnp.mean(out * out, axis=-1, keepdims=True) + epsilon)
            normed = out * r
            dgain_ref[h : h + 1, :] += jnp.sum(grad * normed * silu, axis=0, keepdims=True)
            dproj_ref[rows, gate_cols] = (
                grad * normed * gain * (sg * (1.0 + gate * (1.0 - sg)))
            ).astype(dproj_ref.dtype)
            weighted = grad * gain * silu
            dout_s[rows, cols] = r * weighted - out * (r * r * r) * jnp.mean(
                weighted * out, axis=-1, keepdims=True)

    dpre_s[rows_all : rows_all + HALO, :] = jnp.zeros((HALO, 3 * width), f32)

    def retreat(step, dstates):
        c = count - 1 - step
        base = pl.multiple_of(c * chunk, chunk)
        rows = pl.ds(base, chunk)
        strict, within, carry, close, keep = chunk_masks(segment_of, base, chunk)
        pos = base + lax.broadcasted_iota(jnp.int32, (chunk, 1), 0)
        live = (segment_of(pos) < segments).astype(f32)
        new_dstates = []
        for h in range(heads):
            cols = slice(h * 128, (h + 1) * 128)
            place = c * heads + h
            k = key_s[rows, cols]
            q = query_s[rows, cols]
            dout = dout_s[rows, cols]
            state = state_ref[place]
            inverse = inverse_ref[place]
            fixed = fixed_ref[rows, cols]
            delta = delta_ref[rows, cols]
            dstate = dstates[h]
            rate = sigmoid(beta_ref[rows, h : h + 1])
            beta = rate * live
            scores = product(q, k, 1, 1, exact) * within
            gram = product(k, k, 1, 1, exact) * strict
            dfixed = product(scores, dout, 0, 0, exact) + close * product(k, dstate, 1, 0, exact)
            drhs = product(inverse, dfixed, 0, 0, exact)
            ddelta = beta * drhs
            carried_dout = carry * dout
            carried_ddelta = carry * ddelta
            new_dstates.append(
                keep * dstate
                + product(q, carried_dout, 0, 0, exact)
                - product(k, carried_ddelta, 0, 0, exact)
            )
            dscores = product(dout, fixed, 1, 1, exact) * within
            dlower = -product(drhs, fixed, 1, 1, exact) * strict
            dgram = beta * dlower
            dq = product(carried_dout, state, 1, 1, exact) + product(dscores, k, 1, 0, exact)
            dk = (
                product(dscores, q, 0, 0, exact)
                + close * product(fixed, dstate, 1, 1, exact)
                - product(carried_ddelta, state, 1, 1, exact)
                + product(dgram, k, 1, 0, exact)
                + product(dgram, k, 0, 0, exact)
            )
            drate = live * (
                jnp.sum(drhs * delta, axis=-1, keepdims=True)
                + jnp.sum(dlower * gram, axis=-1, keepdims=True)
            )
            dbeta_ref[rows, h : h + 1] = (drate * rate * (1.0 - rate)).astype(dbeta_ref.dtype)
            for part, da in enumerate((dq, dk, ddelta)):
                part_cols = slice(part * width + h * 128, part * width + (h + 1) * 128)
                pre = pre_s[rows, part_cols]
                sg = sigmoid(pre)
                if part < 2:
                    a = pre * sg
                    scale = 128 ** (-0.5) if part == 0 else 1.0
                    r = lax.rsqrt(jnp.sum(a * a, axis=-1, keepdims=True) + epsilon)
                    da = (scale * r) * (da - a * (r * r) * jnp.sum(da * a, axis=-1, keepdims=True))
                dpre_s[rows, part_cols] = da * (sg * (1.0 + pre * (1.0 - sg)))
        return tuple(new_dstates)

    lax.fori_loop(0, count, retreat, tuple(jnp.zeros((128, 128), f32) for _ in range(heads)))

    @pl.loop(0, count)
    def _(c):
        base = pl.multiple_of(c * chunk, chunk)
        rows = pl.ds(base, chunk)
        col = base + lax.broadcasted_iota(jnp.int32, (chunk, 1), 0)
        seg = segment_of(col)
        for part in range(3):
            cols = slice(part * width, (part + 1) * width)
            _, shifted = conv_part(proj_ref, tap_ref, segment_of, base, part, width, chunk)
            full = dpre_s[pl.ds(base, chunk + HALO), cols]
            main = full[:chunk]
            total = main * tap_ref[part * taps : part * taps + 1, :]
            for s in range(taps):
                at = slice(part * taps + s, part * taps + s + 1)
                dtap_ref[at, :] += jnp.sum(main * shifted[s], axis=0, keepdims=True)
                if s > 0:
                    valid = (segment_of(col + s) == seg) & (col + s < rows_all)
                    moved = pltpu.roll(full, chunk + HALO - s, 0)[:chunk]
                    total = total + jnp.where(valid, moved, 0.0) * tap_ref[at, :]
            dproj_ref[rows, cols] = total.astype(dproj_ref.dtype)


def vmem():
    return pl.BlockSpec(memory_space=pltpu.VMEM)


def mixer_forward(lengths_row, projected, beta_logits, taps, gain, exact=True, group=4):
    rows, wide = projected.shape
    width = wide // 4
    heads = width // 128
    places = rows // CHUNK * heads
    group = min(group, rows // CHUNK)
    return pl.pallas_call(
        partial(mixer_forward_kernel, exact, group),
        out_shape=(
            jax.ShapeDtypeStruct((rows, width), bf16),
            jax.ShapeDtypeStruct((rows, width), f32),
            jax.ShapeDtypeStruct((rows, width), f32),
            jax.ShapeDtypeStruct((rows, width), f32),
            jax.ShapeDtypeStruct((places, 128, 128), f32),
            jax.ShapeDtypeStruct((places, CHUNK, CHUNK), f32),
        ),
        in_specs=[pl.BlockSpec(memory_space=pltpu.SMEM)] + [vmem()] * 4,
        out_specs=(vmem(),) * 6,
        scratch_shapes=[pltpu.VMEM((rows, width), f32)] * 3
        + [pltpu.VMEM((places, CHUNK, CHUNK), f32 if exact else bf16)],
        compiler_params=pltpu.CompilerParams(vmem_limit_bytes=48 * 2**20),
        cost_estimate=pl.CostEstimate(flops=10**10, bytes_accessed=10**7, transcendentals=10**6),
        name="mixer_forward",
    )(lengths_row, projected, beta_logits, taps, gain)


def mixer_backward(lengths_row, projected, beta_logits, taps, gain, grad, saved, exact=True):
    rows, wide = projected.shape
    width = wide // 4
    return pl.pallas_call(
        partial(mixer_backward_kernel, exact),
        out_shape=(
            jax.ShapeDtypeStruct((rows, wide), bf16),
            jax.ShapeDtypeStruct((rows, 128), bf16),
            jax.ShapeDtypeStruct(taps.shape, f32),
            jax.ShapeDtypeStruct(gain.shape, f32),
        ),
        in_specs=[pl.BlockSpec(memory_space=pltpu.SMEM)] + [vmem()] * 10,
        out_specs=(vmem(),) * 4,
        scratch_shapes=[pltpu.VMEM((rows, width), f32)] * 2
        + [pltpu.VMEM((rows, 3 * width), f32), pltpu.VMEM((rows, width), f32),
           pltpu.VMEM((rows + HALO, 3 * width), f32)],
        compiler_params=pltpu.CompilerParams(vmem_limit_bytes=56 * 2**20),
        cost_estimate=pl.CostEstimate(flops=10**10, bytes_accessed=10**7, transcendentals=10**6),
        name="mixer_backward",
    )(lengths_row, projected, beta_logits, taps, gain, grad, *saved)


NT = (((1,), (1,)), ((), ()))


def other(axis_name):
    return {axis_name: 1 - lax.axis_index(axis_name)}


def ffn_kernel(x_ref, c_ref, w_ref, out_ref, ngrad_ref, wgrad_ref,
               xs, cs, ws, inner_s, gate_s, up_s, acts_t, part, crecv, drecv, nrecv, stage, ctile,
               ag_send, ag_recv, pair_send, pair_recv, rs_send, rs_recv, c_sem, w_sem, g_sem, t_sem):
    half = xs.shape[1] // 2
    rows = 2 * half
    model = xs.shape[2]
    hidden = ws.shape[1]
    lines = w_ref.shape[0]
    quarter = w_ref.shape[2]
    tile_f = 256
    tile_d = min(512, model)
    tile_w = min(256, model)

    def remote(src, dst, send, recv, axis_name):
        return pltpu.make_async_remote_copy(
            src_ref=src, dst_ref=dst, send_sem=send, recv_sem=recv,
            device_id=other(axis_name), device_id_type=pl.DeviceIdType.MESH)

    def halves(ref, index, h):
        return ref.at[index, pl.ds(h * half, half)]

    barrier = pltpu.get_barrier_semaphore()
    for axis_name in ("core", "x", "y"):
        pl.semaphore_signal(
            barrier, inc=1, device_id=other(axis_name), device_id_type=pl.DeviceIdType.MESH)

    weight_copies = [
        pltpu.make_async_copy(
            w_ref.at[line, kind], ws.at[kind, pl.ds(line * quarter, quarter)], w_sem.at[line, kind])
        for line in range(lines) for kind in range(3)
    ]
    for copy in weight_copies:
        copy.start()

    def slot_of(step):
        return (1 - lax.rem(step, 2)) * 4 + step // 2

    def c_copy(step, slot):
        return pltpu.make_async_copy(
            c_ref.at[slot], cs.at[lax.rem(step, 2)], c_sem.at[lax.rem(step, 2)])

    c_copy(0, 4).start()
    pl.semaphore_wait(barrier, 3)

    own_pair = remote(x_ref, xs.at[4], ag_send.at[0], ag_recv.at[0], "core")
    own_x = [remote(x_ref.at[pl.ds(h * half, half)], halves(xs, 1, h), ag_send.at[1 + h], ag_recv.at[1 + h], "x") for h in range(2)]
    own_y = [remote(x_ref.at[pl.ds(h * half, half)], halves(xs, 2, h), ag_send.at[3 + h], ag_recv.at[3 + h], "y") for h in range(2)]
    relay_y = remote(halves(xs, 1, 0), halves(xs, 3, 0), ag_send.at[5], ag_recv.at[5], "y")
    relay_x = remote(halves(xs, 2, 1), halves(xs, 3, 1), ag_send.at[6], ag_recv.at[6], "x")
    pair_of = [None] + [remote(xs.at[j], xs.at[4 + j], ag_send.at[6 + j], ag_recv.at[6 + j], "core") for j in (1, 2, 3)]
    own_pair.start()
    own_x[0].start()
    own_y[1].start()
    own_x[1].start()
    own_y[0].start()
    own_copy = pltpu.make_async_copy(x_ref, xs.at[0], t_sem.at[0])
    own_copy.start()
    own_copy.wait()
    for copy in weight_copies:
        copy.wait()

    def part_send(j):
        return remote(part.at[lax.rem(j, 2)], crecv.at[j], pair_send.at[j], pair_recv.at[j], "core")

    x_sends = [[remote(crecv.at[1, a, pl.ds(h * half, half)], nrecv.at[0, a, pl.ds(h * half, half)],
                       rs_send.at[a * 2 + h], rs_recv.at[a * 2 + h], "x") for a in range(2)] for h in range(2)]
    y_sends = [[remote(crecv.at[2, a, pl.ds(h * half, half)], nrecv.at[1, a, pl.ds(h * half, half)],
                       rs_send.at[4 + a * 2 + h], rs_recv.at[4 + a * 2 + h], "y") for a in range(2)] for h in range(2)]
    d_sends = [[remote(crecv.at[3, a, pl.ds(h * half, half)], drecv.at[a, pl.ds(h * half, half)],
                       rs_send.at[8 + a * 2 + h], rs_recv.at[8 + a * 2 + h], ("x", "y")[h]) for a in range(2)] for h in range(2)]

    @pl.loop(0, 8)
    def _(step):
        j = step // 2
        slot = slot_of(step)
        pairing = lax.rem(step, 2) == 0

        @pl.when(step < 7)
        def _():
            c_copy(step + 1, slot_of(step + 1)).start()

        @pl.when(step == 0)
        def _():
            own_pair.wait_recv()

        @pl.when(step == 2)
        def _():
            own_x[0].wait_recv()
            relay_y.start()
            own_y[1].wait_recv()
            relay_x.start()
            own_x[1].wait_recv()
            pair_of[1].start()
            own_y[0].wait_recv()
            pair_of[2].start()
            pair_of[1].wait_recv()

        @pl.when(step == 4)
        def _():
            relay_y.wait_recv()
            relay_x.wait_recv()
            pair_of[3].start()
            pair_of[2].wait_recv()

        @pl.when(step == 6)
        def _():
            pair_of[3].wait_recv()

        c_copy(step, slot).wait()

        for start in range(0, hidden, tile_f):
            size = min(tile_f, hidden - start)
            cols = slice(start, start + size)
            x = xs[slot]
            gate = lax.dot_general(x, ws[0, cols, :], NT, preferred_element_type=f32)
            up = lax.dot_general(x, ws[1, cols, :], NT, preferred_element_type=f32)
            grad = lax.dot_general(cs[lax.rem(step, 2)], ws[2, cols, :], NT, preferred_element_type=f32)
            sg = sigmoid(gate)
            silu = gate * sg
            inner = (silu * up).astype(bf16)
            gate_grad = (grad * up * sg * (1.0 + gate * (1.0 - sg))).astype(bf16)
            up_grad = (grad * silu).astype(bf16)
            places = pl.ds(pl.multiple_of(slot * rows, rows), rows)
            for kind, (value, target) in enumerate(((gate_grad, gate_s), (up_grad, up_s), (inner, inner_s))):
                target[:, cols] = value
                acts_t[kind, cols, places] = value.T

        @pl.when(pairing & (step >= 4))
        def _():
            part_send(j - 2).wait_send()

        place = jnp.where(pairing, lax.rem(j, 2), 2)
        for start in range(0, model, tile_d):
            cols = slice(start, start + tile_d)
            part[place, 0, :, cols] = jnp.dot(
                inner_s[...], ws[2, :, cols], preferred_element_type=f32).astype(bf16)
            part[place, 1, :, cols] = (
                jnp.dot(gate_s[...], ws[0, :, cols], preferred_element_type=f32)
                + jnp.dot(up_s[...], ws[1, :, cols], preferred_element_type=f32)
            ).astype(bf16)

        @pl.when(pairing)
        def _():
            part_send(j).start()

        @pl.when(jnp.logical_not(pairing))
        def _():
            part_send(j).wait_recv()
            for a in range(2):
                for start in range(0, model, tile_d):
                    cols = slice(start, start + tile_d)
                    crecv[j, a, :, cols] = (
                        crecv[j, a, :, cols].astype(f32) + part[2, a, :, cols].astype(f32)
                    ).astype(bf16)

        @pl.when(step == 3)
        def _():
            for copy in x_sends[0]:
                copy.start()

        @pl.when(step == 5)
        def _():
            for copy in y_sends[1]:
                copy.start()

        @pl.when(step == 7)
        def _():
            for h in range(2):
                for copy in d_sends[h]:
                    copy.start()

    tiles = model // tile_w

    def c_tile(t):
        return pltpu.make_async_copy(
            c_ref.at[:, :, pl.ds(pl.multiple_of(t * tile_w, tile_w), tile_w)], ctile.at[lax.rem(t, 2)], t_sem.at[lax.rem(t, 2)])

    def grad_copy(kind, t, line):
        return pltpu.make_async_copy(
            stage.at[lax.rem(t, 2), pl.ds(line * quarter, quarter)],
            wgrad_ref.at[line, kind, :, pl.ds(pl.multiple_of(t * tile_w, tile_w), tile_w)],
            g_sem.at[lax.rem(t, 2), line])

    def weight_grads(kind):
        if kind == 2:
            c_tile(0).start()

        @pl.loop(0, tiles)
        def _(t):
            if kind == 2:
                @pl.when(t + 1 < tiles)
                def _():
                    c_tile(t + 1).start()
                c_tile(t).wait()
                right = ctile[lax.rem(t, 2)].reshape(8 * rows, tile_w)
            else:
                right = xs[:, :, pl.ds(pl.multiple_of(t * tile_w, tile_w), tile_w)].reshape(8 * rows, tile_w)

            @pl.when(t >= 2)
            def _():
                for line in range(lines):
                    grad_copy(kind, t - 2, line).wait()

            stage[lax.rem(t, 2)] = jnp.dot(
                acts_t[kind], right, preferred_element_type=f32).astype(bf16)
            for line in range(lines):
                grad_copy(kind, t, line).start()

        for t in range(max(tiles - 2, 0), tiles):
            for line in range(lines):
                grad_copy(kind, t, line).wait()

    weight_grads(0)
    for h in range(2):
        j = 2 - h
        for a in range(2):
            d_sends[h][a].wait_recv()
            at = pl.ds(h * half, half)
            crecv[j, a, at, :] = (
                crecv[j, a, at, :].astype(f32) + drecv[a, at, :].astype(f32)).astype(bf16)
        for copy in (y_sends, x_sends)[h][h]:
            copy.start()
    weight_grads(1)
    weight_grads(2)
    for a, target in enumerate((out_ref, ngrad_ref)):
        for h in range(2):
            x_sends[h][a].wait_recv()
            y_sends[h][a].wait_recv()
            at = pl.ds(h * half, half)
            target[at, :] = (
                crecv[0, a, at, :].astype(f32)
                + nrecv[0, a, at, :].astype(f32)
                + nrecv[1, a, at, :].astype(f32)
            )
    own_pair.wait_send()
    for h in range(2):
        own_x[h].wait_send()
        own_y[h].wait_send()
        for a in range(2):
            x_sends[h][a].wait_send()
            y_sends[h][a].wait_send()
            d_sends[h][a].wait_send()
    relay_x.wait_send()
    relay_y.wait_send()
    for j in (1, 2, 3):
        pair_of[j].wait_send()
    part_send(2).wait_send()
    part_send(3).wait_send()


def ffn_plane(x_own, c_all, weights):
    rows, model = x_own.shape
    lines, _, quarter, _ = weights.shape
    hidden = lines * quarter
    tile_w = min(256, model)
    sems = pltpu.SemaphoreType.DMA
    anywhere = pl.BlockSpec(memory_space=pl.ANY)
    return pl.pallas_call(
        ffn_kernel,
        out_shape=(
            jax.ShapeDtypeStruct((rows, model), f32),
            jax.ShapeDtypeStruct((rows, model), f32),
            jax.ShapeDtypeStruct(weights.shape, bf16),
        ),
        in_specs=[anywhere] * 3,
        out_specs=(vmem(), vmem(), anywhere),
        scratch_shapes=[
            pltpu.VMEM((8, rows, model), bf16),
            pltpu.VMEM((2, rows, model), bf16),
            pltpu.VMEM((3, hidden, model), bf16),
            pltpu.VMEM((rows, hidden), bf16),
            pltpu.VMEM((rows, hidden), bf16),
            pltpu.VMEM((rows, hidden), bf16),
            pltpu.VMEM((3, hidden, 8 * rows), bf16),
            pltpu.VMEM((3, 2, rows, model), bf16),
            pltpu.VMEM((4, 2, rows, model), bf16),
            pltpu.VMEM((2, rows, model), bf16),
            pltpu.VMEM((2, 2, rows, model), bf16),
            pltpu.VMEM((2, hidden, tile_w), bf16),
            pltpu.VMEM((2, 8, rows, tile_w), bf16),
            sems((10,)), sems((10,)), sems((4,)), sems((4,)), sems((12,)), sems((12,)),
            sems((2,)), sems((lines, 3)), sems((2, lines)), sems((2,)),
        ],
        compiler_params=pltpu.CompilerParams(
            collective_id=2, has_side_effects=True, vmem_limit_bytes=62 * 2**20),
        cost_estimate=pl.CostEstimate(flops=8 * 10**10, bytes_accessed=4 * 10**7, transcendentals=10**6),
        name="ffn_plane",
    )(x_own, c_all, weights)


def line_positions(lines):
    o = lax.axis_index("z")
    i = lax.axis_index("y")

    def at(z, y):
        return {"z": z, "y": y}

    return o, i, at


def line_barrier(lines):
    o = lax.axis_index("z")
    barrier = pltpu.get_barrier_semaphore()
    mesh_id = pl.DeviceIdType.MESH

    @pl.when(o > 0)
    def _():
        pl.semaphore_signal(barrier, inc=1, device_id={"z": o - 1}, device_id_type=mesh_id)

    @pl.when(o < lines - 1)
    def _():
        pl.semaphore_signal(barrier, inc=1, device_id={"z": o + 1}, device_id_type=mesh_id)

    pl.semaphore_signal(barrier, inc=1, device_id=other("y"), device_id_type=mesh_id)

    peers = 1 + (o > 0).astype(jnp.int32) + (o < lines - 1).astype(jnp.int32)
    pl.semaphore_wait(barrier, peers)


def line_copy(src, dst, send, recv, target):
    return pltpu.make_async_remote_copy(
        src_ref=src, dst_ref=dst, send_sem=send, recv_sem=recv,
        device_id=target, device_id_type=pl.DeviceIdType.MESH)


def gather_kernel(x_ref, w_ref, wb_ref, rows_ref, proj_ref, beta_ref, xs, stage, beta_stage,
                  right_send, left_send, line_recv, pair_send, pair_recv, row_sem, out_sem, beta_sem):
    batches = xs.shape[1]
    lines = xs.shape[0] // 2
    rows = xs.shape[2]
    model = xs.shape[3]
    o = lax.axis_index("z")
    i = lax.axis_index("y")
    line_barrier(lines)

    def right(z, m):
        return line_copy(xs.at[z * 2 + i, m], xs.at[z * 2 + i, m], right_send.at[z, m],
                         line_recv.at[z, m], {"z": o + 1})

    def left(z, m):
        return line_copy(xs.at[z * 2 + i, m], xs.at[z * 2 + i, m], left_send.at[z, m],
                         line_recv.at[z, m], {"z": o - 1})

    def across(z, m):
        return line_copy(xs.at[z * 2 + i, m], xs.at[z * 2 + i, m], pair_send.at[z, m],
                         pair_recv.at[z, m], other("y"))

    own = pltpu.make_async_copy(x_ref, xs.at[o * 2 + i], row_sem.at[2 * lines, 0])
    own.start()
    own.wait()

    def outs(turn, slot, m):
        return (
            pltpu.make_async_copy(stage.at[lax.rem(turn, 2), m], proj_ref.at[m, slot], out_sem.at[lax.rem(turn, 2), m]),
            pltpu.make_async_copy(beta_stage.at[lax.rem(turn, 2), m], beta_ref.at[m, slot], beta_sem.at[lax.rem(turn, 2), m]),
        )

    def keep(slot, m):
        return pltpu.make_async_copy(xs.at[slot, m], rows_ref.at[m, slot], row_sem.at[slot, m])

    def project(turn, slot):
        @pl.when(turn >= 2)
        def _():
            for m in range(batches):
                for copy in outs(turn, slot, m):
                    copy.wait()
        for m in range(batches):
            keep(slot, m).start()
        x = xs[slot].reshape(batches * rows, model)
        width = w_ref.shape[1]
        tile = min(256, width)
        for start in range(0, width, tile):
            cols = slice(start, start + tile)
            stage[lax.rem(turn, 2), :, :, cols] = jnp.dot(
                x, w_ref[:, cols], preferred_element_type=f32).reshape(batches, rows, tile)
        beta_stage[lax.rem(turn, 2)] = jnp.dot(
            x, wb_ref[...], preferred_element_type=f32).reshape(batches, rows, 128)
        for m in range(batches):
            for copy in outs(turn, slot, m):
                copy.start()

    def in_line(index):
        far = (index + 1) // 2
        side = 1 - 2 * lax.rem(index, 2)
        z = o + side * far
        return far, side, z, (z >= 0) & (z < lines)

    def first(index, turn):
        far, side, z, valid = in_line(index)

        @pl.when(valid)
        def _():
            for m in range(batches):
                @pl.when(far > 0)
                def _():
                    left(z, m).wait_recv()

                @pl.when((o < lines - 1) & (z <= o))
                def _():
                    right(z, m).start()

                @pl.when((o > 0) & (z >= o))
                def _():
                    left(z, m).start()

                across(z, m).start()
            project(turn, z * 2 + i)

        return turn + valid.astype(jnp.int32)

    turn = lax.fori_loop(0, 2 * lines - 1, first, jnp.int32(0))

    def second(index, turn):
        far, side, z, valid = in_line(index)

        @pl.when(valid)
        def _():
            for m in range(batches):
                across(z, m).wait_recv()
            project(turn, z * 2 + 1 - i)

        return turn + valid.astype(jnp.int32)

    lax.fori_loop(0, 2 * lines - 1, second, turn)

    for turn in range(2 * lines - 2, 2 * lines):
        for m in range(batches):
            for copy in outs(turn, 0, m):
                copy.wait()

    @pl.loop(0, lines)
    def _(z):
        for m in range(batches):
            @pl.when((o < lines - 1) & (z <= o))
            def _():
                right(z, m).wait_send()

            @pl.when((o > 0) & (z >= o))
            def _():
                left(z, m).wait_send()

            across(z, m).wait_send()
            keep(z * 2, m).wait()
            keep(z * 2 + 1, m).wait()


def gather_project(x, w_inner, w_beta):
    batches, rows, model = x.shape
    lines = lax.axis_size("z")
    width = w_inner.shape[1]
    slots = 2 * lines
    heads = w_beta.shape[1]
    w_beta = jnp.pad(w_beta, ((0, 0), (0, 128 - heads)))
    sems = pltpu.SemaphoreType.DMA
    anywhere = pl.BlockSpec(memory_space=pl.ANY)
    gathered, projected, beta = pl.pallas_call(
        gather_kernel,
        out_shape=(
            jax.ShapeDtypeStruct((batches, slots, rows, model), bf16),
            jax.ShapeDtypeStruct((batches, slots, rows, width), f32),
            jax.ShapeDtypeStruct((batches, slots, rows, 128), f32),
        ),
        in_specs=[anywhere, vmem(), vmem()],
        out_specs=(anywhere,) * 3,
        scratch_shapes=[
            pltpu.VMEM((slots, batches, rows, model), bf16),
            pltpu.VMEM((2, batches, rows, width), f32),
            pltpu.VMEM((2, batches, rows, 128), f32),
            sems((lines, batches)), sems((lines, batches)), sems((lines, batches)),
            sems((lines, batches)), sems((lines, batches)),
            sems((slots + 1, batches)), sems((2, batches)), sems((2, batches)),
        ],
        compiler_params=pltpu.CompilerParams(
            collective_id=1, has_side_effects=True, vmem_limit_bytes=40 * 2**20),
        cost_estimate=pl.CostEstimate(flops=7 * 10**10, bytes_accessed=4 * 10**7, transcendentals=0),
        name="gather_project",
    )(x, w_inner, w_beta)
    total = slots * rows
    return (gathered.reshape(batches, total, model), projected.reshape(batches, total, width),
            beta.reshape(batches, total, 128))


def scatter_kernel(g_ref, gb_ref, w_ref, wb_ref, out_ref, gs, bs, ysend, yrecv, from_left, from_right,
                   pair_send, pair_recv, right_send, left_send, right_recv, left_recv, g_sem, b_sem):
    batches, rows, width = gs.shape[1:]
    lines = yrecv.shape[0]
    model = yrecv.shape[3]
    o = lax.axis_index("z")
    i = lax.axis_index("y")
    tile = min(512, model)

    def target(index):
        far = lines - 1 - index // 2
        side = 1 - 2 * lax.rem(index, 2)
        z = o + side * far
        return far, z, (z >= 0) & (z < lines) & ((far > 0) | (side > 0))

    def load(z, y, buffer):
        slot = z * 2 + y
        return (pltpu.make_async_copy(g_ref.at[:, slot], gs.at[buffer], g_sem.at[buffer]),
                pltpu.make_async_copy(gb_ref.at[:, slot], bs.at[buffer], b_sem.at[buffer]))

    def partial_rows(z, y, buffer, store):
        for copy in load(z, y, buffer):
            copy.start()
        for copy in load(z, y, buffer):
            copy.wait()
        for m in range(batches):
            g = gs[buffer, m]
            b = bs[buffer, m]
            for start in range(0, model, tile):
                cols = slice(start, start + tile)
                store(m, cols, lax.dot_general(g, w_ref[cols, :], NT, preferred_element_type=f32)
                      + lax.dot_general(b, wb_ref[cols, :], NT, preferred_element_type=f32))

    def across(z, m):
        return line_copy(ysend.at[z, m], yrecv.at[z, m], pair_send.at[z, m], pair_recv.at[z, m], other("y"))

    def right(z, m):
        return line_copy(yrecv.at[z, m], from_left.at[z, m], right_send.at[z, m], right_recv.at[z, m], {"z": o + 1})

    def left(z, m):
        return line_copy(yrecv.at[z, m], from_right.at[z, m], left_send.at[z, m], left_recv.at[z, m], {"z": o - 1})

    line_barrier(lines)

    @pl.loop(0, 2 * lines)
    def _(index):
        far, z, valid = target(index)

        @pl.when(valid)
        def _():
            def store(m, cols, value):
                ysend[z, m, :, cols] = value.astype(bf16)
            partial_rows(z, 1 - i, 0, store)
            for m in range(batches):
                across(z, m).start()

    @pl.loop(0, 2 * lines)
    def _(index):
        far, z, valid = target(index)

        @pl.when(valid)
        def _():
            for m in range(batches):
                across(z, m).wait_recv()

            def store(m, cols, value):
                yrecv[z, m, :, cols] = (yrecv[z, m, :, cols].astype(f32) + value).astype(bf16)
            partial_rows(z, i, 0, store)
            for m in range(batches):
                @pl.when((z > o) & (o > 0))
                def _():
                    right(z, m).wait_recv()
                    yrecv[z, m] = (yrecv[z, m].astype(f32) + from_left[z, m].astype(f32)).astype(bf16)

                @pl.when(z > o)
                def _():
                    right(z, m).start()

                @pl.when((z < o) & (o < lines - 1))
                def _():
                    left(z, m).wait_recv()
                    yrecv[z, m] = (yrecv[z, m].astype(f32) + from_right[z, m].astype(f32)).astype(bf16)

                @pl.when(z < o)
                def _():
                    left(z, m).start()

    for m in range(batches):
        out_ref[m] = yrecv[o, m].astype(f32)

        @pl.when(o > 0)
        def _():
            right(o, m).wait_recv()
            out_ref[m] += from_left[o, m].astype(f32)

        @pl.when(o < lines - 1)
        def _():
            left(o, m).wait_recv()
            out_ref[m] += from_right[o, m].astype(f32)

    @pl.loop(0, lines)
    def _(z):
        for m in range(batches):
            across(z, m).wait_send()

            @pl.when(z > o)
            def _():
                right(z, m).wait_send()

            @pl.when(z < o)
            def _():
                left(z, m).wait_send()


def scatter_rows(grads, beta_grads, w_inner, w_beta):
    batches, total, width = grads.shape
    model = w_inner.shape[0]
    lines = lax.axis_size("z")
    slots = 2 * lines
    rows = total // slots
    heads = w_beta.shape[1]
    w_beta = jnp.pad(w_beta, ((0, 0), (0, 128 - heads)))
    sems = pltpu.SemaphoreType.DMA
    anywhere = pl.BlockSpec(memory_space=pl.ANY)
    slab = pltpu.VMEM((lines, batches, rows, model), bf16)
    return pl.pallas_call(
        scatter_kernel,
        out_shape=jax.ShapeDtypeStruct((batches, rows, model), f32),
        in_specs=[anywhere, anywhere, vmem(), vmem()],
        out_specs=vmem(),
        scratch_shapes=[
            pltpu.VMEM((2, batches, rows, width), bf16),
            pltpu.VMEM((2, batches, rows, 128), bf16),
            slab, slab, slab, slab,
            sems((lines, batches)), sems((lines, batches)), sems((lines, batches)),
            sems((lines, batches)), sems((lines, batches)), sems((lines, batches)),
            sems((2,)), sems((2,)),
        ],
        compiler_params=pltpu.CompilerParams(
            collective_id=3, has_side_effects=True, vmem_limit_bytes=40 * 2**20),
        cost_estimate=pl.CostEstimate(flops=7 * 10**10, bytes_accessed=4 * 10**7, transcendentals=0),
        name="scatter_rows",
    )(grads.reshape(batches, slots, rows, width), beta_grads.reshape(batches, slots, rows, 128), w_inner, w_beta)


def root_scale(row_values, gain_vector):
    row_scale = lax.rsqrt(jnp.mean(row_values * row_values, axis=-1, keepdims=True) + epsilon)
    return (row_values * row_scale * gain_vector, row_scale)


def norm_backward(row_values, row_scale, gain_vector, normed_grad):
    weighted = normed_grad * gain_vector
    rows_grad = row_scale * weighted - row_values * row_scale * row_scale * row_scale * jnp.mean(
        weighted * row_values, axis=-1, keepdims=True
    )
    gain_grad = jnp.sum(normed_grad * row_values * row_scale, axis=tuple(range(row_values.ndim - 1)))
    return (rows_grad, gain_grad)


DP = ("x", "core")
TP = ("z", "y")


def gather(x, axis_name, axis=0):
    return lax.all_gather(x, axis_name, axis=axis, tiled=True)


def scatter_sum(x, axis_name, axis=0):
    return lax.psum_scatter(
        x.astype(bf16), axis_name, scatter_dimension=axis, tiled=True
    ).astype(f32)


def dot(a, b):
    return jnp.dot(a, b, preferred_element_type=f32)


def dot_nt(a, b):
    return jnp.einsum("tk,nk->tn", a, b, preferred_element_type=f32)


def dot_tn(a, b):
    return jnp.einsum("tm,tn->mn", a, b, preferred_element_type=f32)


def exchange(x, axis_name, distance=1):
    size = lax.axis_size(axis_name)
    return lax.ppermute(x, axis_name, [(i, i ^ distance) for i in range(size)])


def swap_blocks(blocks):
    size = lax.axis_size(DP)
    me = lax.axis_index(DP)
    pieces = []
    for r in range(size):
        block = lax.dynamic_index_in_dim(blocks, me ^ r, keepdims=False)
        pieces.append(exchange(block, DP, r) if r else block)
    return ordered_blocks(pieces)


def plane_weights(w_gate, w_up, w_down):
    size = lax.axis_size(DP)
    local = jnp.stack([w_gate.T, w_up.T, w_down])
    kinds, hidden, part = local.shape
    quarter = hidden // size
    blocks = local.reshape(kinds, size, quarter, part).swapaxes(0, 1)
    own = jnp.concatenate(swap_blocks(blocks), axis=2)
    own = own.reshape(kinds * quarter, size * part)
    return gather(own, "z").reshape(-1, kinds, quarter, size * part)


def plane_weight_grads(grads):
    size = lax.axis_size(DP)
    lines, kinds, quarter, model = grads.shape
    own = lax.psum_scatter(
        grads.reshape(lines * kinds * quarter, model), "z", scatter_dimension=0, tiled=True)
    blocks = own.reshape(kinds * quarter, size, model // size).swapaxes(0, 1)
    pieces = [piece.reshape(kinds, quarter, -1) for piece in swap_blocks(blocks)]
    whole = jnp.concatenate(pieces, axis=1).astype(f32)
    return whole[0].T, whole[1].T, whole[2]


def plane_rows(x):
    for axis_name in ("x", "y", "core"):
        x = jnp.concatenate([x, exchange(x, axis_name)])
    return x


def ordered_blocks(pieces):
    me = lax.axis_index(DP)
    pieces = jnp.stack(pieces)
    return [lax.dynamic_index_in_dim(pieces, me ^ q, keepdims=False) for q in range(len(pieces))]


def pick(x, index, axis):
    return lax.dynamic_index_in_dim(x, index, axis, keepdims=False)


def gather_pairs(x):
    across = exchange(x, "x")
    return ordered_blocks([x, exchange(x, "core"), across, exchange(across, "core")])


def sum_pairs(x):
    core = lax.axis_index("core")
    halves = x.reshape(2, x.shape[0] // 2, *x.shape[1:])
    mine = pick(halves, core, 0).astype(f32)
    mine = mine + exchange(pick(halves, 1 - core, 0).astype(bf16), "core").astype(f32)
    low = mine.astype(bf16)
    mine = (mine + exchange(low, "x").astype(f32)).astype(bf16)
    theirs = exchange(mine, "core")
    first = jnp.where(core == 0, mine, theirs)
    second = jnp.where(core == 0, theirs, mine)
    return first, second


def gather_out(w_out):
    me = lax.axis_index(DP)
    quarters = w_out.reshape(lax.axis_size(DP), -1, w_out.shape[1])
    column = gather(pick(quarters, me, 0)[None], TP)
    return jnp.stack(gather_pairs(column), axis=1).reshape(-1, w_out.shape[1])


def scatter_out(grad):
    devices = lax.axis_size(TP)
    grad = grad.reshape(devices, 2, 2, -1, grad.shape[1])
    for axis_name, axis in (("core", 2), ("x", 1)):
        me = lax.axis_index(axis_name)
        theirs = exchange(pick(grad, 1 - me, axis), axis_name)
        grad = (pick(grad, me, axis).astype(f32) + theirs.astype(f32)).astype(bf16)
    own = lax.psum_scatter(grad, TP, scatter_dimension=0, tiled=True)[0]
    return jnp.concatenate(gather_pairs(own)).astype(f32)


def feed_forward_plane(normed, cotangents, w_gate, w_up, w_down):
    weights = plane_weights(w_gate, w_up, w_down)
    batches, rows, model = normed.shape
    rows = normed.reshape(batches * rows, model)
    count = rows.shape[0]
    c_all = plane_rows(cotangents.reshape(1, count, model))
    out, normed_grad, grads = ffn_plane(rows, c_all, weights)
    return out.reshape(normed.shape), normed_grad.reshape(normed.shape), plane_weight_grads(grads)


def feed_forward_groups(normed, cotangents, w_gate, w_up, w_down):
    gate_full = gather(w_gate, DP)
    up_full = gather(w_up, DP)
    down_full = gather(w_down, DP, 1)
    outs, normed_grads, inner_rows, gate_grads, up_grads, rows, grad_rows = [], [], [], [], [], [], []
    for m in range(normed.shape[0]):
        rows.append(gather(normed[m], TP))
        grad_rows.append(gather(cotangents[m], TP))
        gate_values = dot(rows[m], gate_full)
        up_values = dot(rows[m], up_full)
        sigmoid_gate = jax.nn.sigmoid(gate_values)
        silu_gate = gate_values * sigmoid_gate
        inner = (silu_gate * up_values).astype(bf16)
        inner_grad = dot_nt(grad_rows[m], down_full)
        gate_grad = (
            inner_grad * up_values * sigmoid_gate * (1.0 + gate_values * (1.0 - sigmoid_gate))
        ).astype(bf16)
        up_grad = (inner_grad * silu_gate).astype(bf16)
        normed_grads.append(scatter_sum(dot_nt(gate_grad, gate_full) + dot_nt(up_grad, up_full), TP))
        outs.append(scatter_sum(dot(inner, down_full), TP))
        inner_rows.append(inner)
        gate_grads.append(gate_grad)
        up_grads.append(up_grad)
    grad_all = jnp.concatenate(grad_rows)
    rows_all = jnp.concatenate(rows)
    gate_share = scatter_sum(dot_tn(rows_all, jnp.concatenate(gate_grads)), DP)
    up_share = scatter_sum(dot_tn(rows_all, jnp.concatenate(up_grads)), DP)
    down_share = scatter_sum(dot_tn(jnp.concatenate(inner_rows), grad_all), DP, 1)
    return jnp.stack(outs), jnp.stack(normed_grads), (gate_share, up_share, down_share)


def per_device(
    inputs,
    lengths,
    norm_gain,
    ffn_gain,
    w_query,
    w_key,
    w_value,
    w_gate_out,
    w_beta,
    conv_weight,
    head_gain,
    w_out,
    w_gate,
    w_up,
    w_down,
    cotangent,
):
    batches = range(inputs.shape[0])
    local_width = w_query.shape[1]
    heads = w_beta.shape[1]
    devices = lax.axis_size(TP)
    planar = all(lax.axis_size(name) == 2 for name in ("x", "core", "y"))
    w_inner = jnp.concatenate([w_query, w_key, w_value, w_gate_out], axis=1)
    taps = conv_weight.astype(f32).reshape(-1, local_width)
    gain_heads = head_gain.astype(f32)
    gains = gather(jnp.stack([norm_gain, ffn_gain]), DP, 1).astype(f32)
    gain_one, gain_two = gains[0], gains[1]
    rows_in = inputs.astype(f32)
    normed_one, scale_one = root_scale(rows_in, gain_one)
    normed_one = normed_one.astype(bf16)
    if planar:
        gathered_one, projected, beta_logits = gather_project(normed_one, w_inner, w_beta)
        out_full = gather_out(w_out)
    else:
        gathered_one = jnp.stack([gather(normed_one[m], TP) for m in batches])
        projected = [dot(gathered_one[m], w_inner) for m in batches]
        beta_logits = [
            jnp.pad(dot(gathered_one[m], w_beta), ((0, 0), (0, 128 - heads))) for m in batches]
        out_full = gather(w_out, TP)
    token_heads, saved = [], []
    for m in batches:
        low, *kept = mixer_forward(lengths[m, 0], projected[m], beta_logits[m], taps, gain_heads)
        saved.append(kept)
        token_heads.append(lax.all_to_all(low, TP, split_axis=0, concat_axis=1, tiled=True))
    token_heads = jnp.concatenate(token_heads)
    hidden = rows_in + dot(token_heads, out_full).reshape(rows_in.shape)
    normed_two, scale_two = root_scale(hidden, gain_two)
    feed_forward = feed_forward_plane if planar else feed_forward_groups
    ffn_out, normed_grad, (gate_share, up_share, down_share) = feed_forward(
        normed_two.astype(bf16), cotangent, w_gate, w_up, w_down)
    result_rows = hidden + ffn_out
    norm_grad, gain_two_sum = norm_backward(hidden, scale_two, gain_two, normed_grad)
    hidden_grad = cotangent.astype(f32) + norm_grad
    attended_low = hidden_grad.astype(bf16)
    mixed_grads = []
    for m in batches:
        token_grad = dot_nt(attended_low[m], out_full).astype(bf16)
        token_grad = token_grad.reshape(-1, devices, local_width).swapaxes(0, 1)
        mixed_grads.append(
            lax.all_to_all(token_grad, TP, split_axis=0, concat_axis=0, tiled=True).reshape(
                -1, local_width))
    out_grad = dot_tn(token_heads, attended_low.reshape(token_heads.shape[0], -1)).astype(bf16)
    projected_low, beta_low = [], []
    taps_sum, heads_sum = 0.0, 0.0
    for m in batches:
        projected_grad, beta_grad, taps_part, heads_part = mixer_backward(
            lengths[m, 0], projected[m], beta_logits[m], taps, gain_heads, mixed_grads[m], saved[m]
        )
        taps_sum = taps_sum + taps_part
        heads_sum = heads_sum + heads_part
        projected_low.append(projected_grad)
        beta_low.append(beta_grad)
    projected_low = jnp.stack(projected_low)
    beta_low = jnp.stack(beta_low)
    tokens = gathered_one.reshape(-1, gathered_one.shape[2])
    inner_sum = dot_tn(tokens, projected_low.reshape(-1, 4 * local_width))
    beta_sum = dot_tn(tokens, beta_low.reshape(-1, 128)[:, :heads])
    gain_one_sum = (
        jnp.sum(inner_sum * w_inner.astype(f32), axis=1)
        + jnp.sum(beta_sum * w_beta.astype(f32), axis=1)
    ) / gain_one
    gain_totals = lax.psum_scatter(
        jnp.stack([gain_one_sum, gain_two_sum]), DP + TP, scatter_dimension=1, tiled=True)
    small = jnp.concatenate([part.reshape(-1) for part in (beta_sum, taps_sum, heads_sum)])
    if planar:
        inner_total = sum_pairs(inner_sum)
        small = small + exchange(small, "core")
        small = small + exchange(small, "x")
        out_total = scatter_out(out_grad)
        input_norm = scatter_rows(projected_low, beta_low, w_inner, w_beta)
    else:
        inner_total = [lax.psum(inner_sum.astype(bf16), DP)]
        small = lax.psum(small, DP)
        out_grad = lax.psum_scatter(out_grad, TP, scatter_dimension=0, tiled=True)
        out_total = lax.psum(out_grad, DP).astype(f32)
        input_norm = jnp.stack([
            scatter_sum(
                dot_nt(projected_low[m], w_inner) + dot_nt(beta_low[m, :, :heads], w_beta), TP)
            for m in batches])
    norm_grad, _ = norm_backward(rows_in, scale_one, gain_one, input_norm)
    beta_total, conv_total, heads_total = (
        piece.reshape(shape) for piece, shape in zip(
            jnp.split(small, (beta_sum.size, beta_sum.size + taps_sum.size)),
            (beta_sum.shape, conv_weight.shape, head_gain.shape)))
    columns = [
        jnp.concatenate([part[:, n * local_width : (n + 1) * local_width] for part in inner_total])
        .astype(f32) for n in range(4)]
    return (
        result_rows,
        hidden_grad + norm_grad,
        gain_totals[0],
        gain_totals[1],
        *columns,
        beta_total,
        conv_total,
        heads_total,
        out_total,
        gate_share,
        up_share,
        down_share,
    )


def solution(mesh):
    dp, tensor = mesh.shape["dp"], mesh.shape["tensor"]
    inner = 2 if tensor == 8 else 4
    axes = ("x", "core", "z", "y")
    fine = jax.sharding.Mesh(
        mesh.devices.reshape(dp // 2, 2, tensor // inner, inner), axes)
    tokens = P(None, DP + TP, None)
    in_specs = (
        tokens,
        P(None, DP, None),
        P(DP),
        P(DP),
        P(None, TP),
        P(None, TP),
        P(None, TP),
        P(None, TP),
        P(None, TP),
        P(None, None, TP),
        P(TP, None),
        P(TP, None),
        P(DP, TP),
        P(DP, TP),
        P(TP, DP),
        tokens,
    )
    out_specs = (
        tokens,
        tokens,
        P(DP + TP),
        P(DP + TP),
        P(None, TP),
        P(None, TP),
        P(None, TP),
        P(None, TP),
        P(None, TP),
        P(None, None, TP),
        P(TP, None),
        P(TP, None),
        P(DP, TP),
        P(DP, TP),
        P(TP, DP),
    )
    return jax.shard_map(
        per_device, mesh=fine, in_specs=in_specs, out_specs=out_specs, check_vma=False
    )
```

```python
from functools import partial

import jax
import jax.numpy as jnp
from jax import lax
from jax.experimental import pallas as pl
from jax.experimental.pallas import tpu as pltpu
from jax.sharding import PartitionSpec as P


CHUNK = 128
HALO = 8
epsilon = 1e-06
highest = lax.Precision.HIGHEST
f32 = jnp.float32
bf16 = jnp.bfloat16


def product(left, right, left_dim, right_dim, exact=False):
    dims = (((left_dim,), (right_dim,)), ((), ()))
    if exact:
        return lax.dot_general(left, right, dims, precision=highest, preferred_element_type=f32)
    return lax.dot_general(
        left.astype(bf16), right.astype(bf16), dims, preferred_element_type=f32
    )


def sigmoid(x):
    return 1.0 / (1.0 + jnp.exp(-x))


def segment_tools(lengths_ref):
    ends = []
    total = 0
    for i in range(lengths_ref.shape[0] - 1):
        total = total + lengths_ref[i]
        ends.append(total)

    def segment_of(pos):
        result = 0
        for end in ends:
            result = result + (pos >= end).astype(jnp.int32)
        return result

    return segment_of, len(ends)


def chunk_masks(segment_of, base, chunk):
    col = base + lax.broadcasted_iota(jnp.int32, (chunk, 1), 0)
    row = base + lax.broadcasted_iota(jnp.int32, (1, chunk), 1)
    seg_col = segment_of(col)
    seg_row = segment_of(row)
    first = segment_of(base - 1)
    last = segment_of(base + chunk - 1)
    same = seg_col == seg_row
    strict = (same & (col > row)).astype(f32)
    within = (same & (col >= row)).astype(f32)
    has_past = base > 0
    carry = ((seg_col == first) & has_past).astype(f32)
    close = (seg_col == last).astype(f32)
    keep = ((first == last) & has_past).astype(f32)
    return strict, within, carry, close, keep


def level_masks(chunk):
    row = lax.broadcasted_iota(jnp.int32, (chunk, chunk), 0)
    col = lax.broadcasted_iota(jnp.int32, (chunk, chunk), 1)
    masks = []
    width = 1
    while width < chunk:
        mask = (
            (row // (2 * width) == col // (2 * width))
            & ((row // width) % 2 == 1)
            & ((col // width) % 2 == 0)
        )
        masks.append(mask)
        width *= 2
    return masks, (row == col).astype(f32)


def conv_part(proj_ref, tap_ref, segment_of, base, part, width, chunk):
    taps = tap_ref.shape[0] // 3
    cols = pl.ds(part * width, width)
    main = proj_ref[pl.ds(base, chunk), cols]
    prev = proj_ref[pl.ds(pl.multiple_of(jnp.maximum(base - HALO, 0), HALO), HALO), cols]
    full = jnp.concatenate([prev, main], axis=0)
    col = base + lax.broadcasted_iota(jnp.int32, (chunk, 1), 0)
    seg = segment_of(col)
    total = main * tap_ref[part * taps : part * taps + 1, :]
    shifted = [main]
    for s in range(1, taps):
        valid = (segment_of(col - s) == seg) & (col >= s)
        moved = jnp.where(valid, pltpu.roll(full, s, 0)[HALO:], 0.0)
        shifted.append(moved)
        total = total + moved * tap_ref[part * taps + s : part * taps + s + 1, :]
    return total, shifted


def heads_of(x, heads):
    return [x[:, h * 128 : (h + 1) * 128] for h in range(heads)]


def unit_rows(a, scale):
    r = lax.rsqrt(jnp.sum(a * a, axis=-1, keepdims=True) + epsilon)
    return a * (r * scale)


def mixer_forward_kernel(exact, group, lengths_ref, proj_ref, beta_ref, tap_ref, gain_ref,
                         mixed_ref, heads_ref, fixed_ref, delta_ref, state_ref, inverse_ref,
                         query_s, key_s, value_s, score_s):
    rows_all = proj_ref.shape[0]
    width = proj_ref.shape[1] // 4
    heads = width // 128
    chunk = CHUNK
    count = rows_all // chunk
    segment_of, segments = segment_tools(lengths_ref)

    @pl.loop(0, count)
    def _(c):
        base = pl.multiple_of(c * chunk, chunk)
        rows = pl.ds(base, chunk)
        for part, target in enumerate((query_s, key_s, value_s)):
            pre, _ = conv_part(proj_ref, tap_ref, segment_of, base, part, width, chunk)
            act = pre * sigmoid(pre)
            if part == 2:
                target[rows, :] = act
            else:
                scale = 128 ** (-0.5) if part == 0 else 1.0
                for h, a in enumerate(heads_of(act, heads)):
                    target[rows, h * 128 : (h + 1) * 128] = unit_rows(a, scale)

    def beta_of(base, h):
        pos = base + lax.broadcasted_iota(jnp.int32, (chunk, 1), 0)
        live = (segment_of(pos) < segments).astype(f32)
        return sigmoid(beta_ref[pl.ds(base, chunk), h : h + 1]) * live

    masks, eye = level_masks(chunk)

    @pl.loop(0, count // group)
    def _(g):
        lowers, places = [], []
        for i in range(group):
            c = g * group + i
            base = pl.multiple_of(c * chunk, chunk)
            strict, within, _, _, _ = chunk_masks(segment_of, base, chunk)
            for h in range(heads):
                cols = slice(h * 128, (h + 1) * 128)
                k = key_s[pl.ds(base, chunk), cols]
                q = query_s[pl.ds(base, chunk), cols]
                lowers.append(product(k, k, 1, 1, exact) * strict * beta_of(base, h))
                score_s[c * heads + h] = (product(q, k, 1, 1, exact) * within).astype(score_s.dtype)
                places.append(c * heads + h)
        inverses = [eye - jnp.where(masks[0], lower, 0.0) for lower in lowers]
        for mask in masks[1:]:
            steps = [product(jnp.where(mask, lower, 0.0), x, 1, 0, True) for lower, x in zip(lowers, inverses)]
            inverses = [x - product(x, step, 1, 0, True) for x, step in zip(inverses, steps)]
        for place, x in zip(places, inverses):
            inverse_ref[place] = x

    def advance(c, states):
        base = pl.multiple_of(c * chunk, chunk)
        rows = pl.ds(base, chunk)
        _, _, carry, close, keep = chunk_masks(segment_of, base, chunk)
        new_states = []
        for h in range(heads):
            cols = slice(h * 128, (h + 1) * 128)
            state = states[h]
            k = key_s[rows, cols]
            q = query_s[rows, cols]
            delta = value_s[rows, cols] - carry * product(k, state, 1, 0, exact)
            fixed = product(inverse_ref[c * heads + h], beta_of(base, h) * delta, 1, 0, exact)
            out = carry * product(q, state, 1, 0, exact) + product(
                score_s[c * heads + h], fixed, 1, 0, exact)
            state_ref[c * heads + h] = state
            new_states.append(keep * state + product(k, close * fixed, 0, 0, exact))
            delta_ref[rows, cols] = delta
            fixed_ref[rows, cols] = fixed
            heads_ref[rows, cols] = out
            gate = proj_ref[rows, 3 * width + h * 128 : 3 * width + (h + 1) * 128]
            r = lax.rsqrt(jnp.mean(out * out, axis=-1, keepdims=True) + epsilon)
            mixed_ref[rows, cols] = (
                out * r * gain_ref[h : h + 1, :] * (gate * sigmoid(gate))
            ).astype(mixed_ref.dtype)
        return tuple(new_states)

    lax.fori_loop(0, count, advance, tuple(jnp.zeros((128, 128), f32) for _ in range(heads)))


def mixer_backward_kernel(exact, lengths_ref, proj_ref, beta_ref, tap_ref, gain_ref, grad_ref,
                          heads_ref, fixed_ref, delta_ref, state_ref, inverse_ref,
                          dproj_ref, dbeta_ref, dtap_ref, dgain_ref,
                          query_s, key_s, pre_s, dout_s, dpre_s):
    rows_all = proj_ref.shape[0]
    width = proj_ref.shape[1] // 4
    heads = width // 128
    chunk = CHUNK
    count = rows_all // chunk
    taps = tap_ref.shape[0] // 3
    segment_of, segments = segment_tools(lengths_ref)
    dgain_ref[...] = jnp.zeros_like(dgain_ref)
    dbeta_ref[...] = jnp.zeros_like(dbeta_ref)
    dtap_ref[...] = jnp.zeros_like(dtap_ref)

    @pl.loop(0, count)
    def _(c):
        base = pl.multiple_of(c * chunk, chunk)
        rows = pl.ds(base, chunk)
        for part in range(3):
            pre, _ = conv_part(proj_ref, tap_ref, segment_of, base, part, width, chunk)
            pre_s[rows, part * width : (part + 1) * width] = pre
            if part < 2:
                act = pre * sigmoid(pre)
                target = (query_s, key_s)[part]
                scale = 128 ** (-0.5) if part == 0 else 1.0
                for h, a in enumerate(heads_of(act, heads)):
                    target[rows, h * 128 : (h + 1) * 128] = unit_rows(a, scale)
        for h in range(heads):
            cols = slice(h * 128, (h + 1) * 128)
            gate_cols = slice(3 * width + h * 128, 3 * width + (h + 1) * 128)
            out = heads_ref[rows, cols]
            gate = proj_ref[rows, gate_cols]
            grad = grad_ref[rows, cols].astype(f32)
            gain = gain_ref[h : h + 1, :]
            sg = sigmoid(gate)
            silu = gate * sg
            r = lax.rsqrt(jnp.mean(out * out, axis=-1, keepdims=True) + epsilon)
            normed = out * r
            dgain_ref[h : h + 1, :] += jnp.sum(grad * normed * silu, axis=0, keepdims=True)
            dproj_ref[rows, gate_cols] = (
                grad * normed * gain * (sg * (1.0 + gate * (1.0 - sg)))
            ).astype(dproj_ref.dtype)
            weighted = grad * gain * silu
            dout_s[rows, cols] = r * weighted - out * (r * r * r) * jnp.mean(
                weighted * out, axis=-1, keepdims=True)

    dpre_s[rows_all : rows_all + HALO, :] = jnp.zeros((HALO, 3 * width), f32)

    def retreat(step, dstates):
        c = count - 1 - step
        base = pl.multiple_of(c * chunk, chunk)
        rows = pl.ds(base, chunk)
        strict, within, carry, close, keep = chunk_masks(segment_of, base, chunk)
        pos = base + lax.broadcasted_iota(jnp.int32, (chunk, 1), 0)
        live = (segment_of(pos) < segments).astype(f32)
        new_dstates = []
        for h in range(heads):
            cols = slice(h * 128, (h + 1) * 128)
            place = c * heads + h
            k = key_s[rows, cols]
            q = query_s[rows, cols]
            dout = dout_s[rows, cols]
            state = state_ref[place]
            inverse = inverse_ref[place]
            fixed = fixed_ref[rows, cols]
            delta = delta_ref[rows, cols]
            dstate = dstates[h]
            rate = sigmoid(beta_ref[rows, h : h + 1])
            beta = rate * live
            scores = product(q, k, 1, 1, exact) * within
            gram = product(k, k, 1, 1, exact) * strict
            dfixed = product(scores, dout, 0, 0, exact) + close * product(k, dstate, 1, 0, exact)
            drhs = product(inverse, dfixed, 0, 0, exact)
            ddelta = beta * drhs
            carried_dout = carry * dout
            carried_ddelta = carry * ddelta
            new_dstates.append(
                keep * dstate
                + product(q, carried_dout, 0, 0, exact)
                - product(k, carried_ddelta, 0, 0, exact)
            )
            dscores = product(dout, fixed, 1, 1, exact) * within
            dlower = -product(drhs, fixed, 1, 1, exact) * strict
            dgram = beta * dlower
            dq = product(carried_dout, state, 1, 1, exact) + product(dscores, k, 1, 0, exact)
            dk = (
                product(dscores, q, 0, 0, exact)
                + close * product(fixed, dstate, 1, 1, exact)
                - product(carried_ddelta, state, 1, 1, exact)
                + product(dgram, k, 1, 0, exact)
                + product(dgram, k, 0, 0, exact)
            )
            drate = live * (
                jnp.sum(drhs * delta, axis=-1, keepdims=True)
                + jnp.sum(dlower * gram, axis=-1, keepdims=True)
            )
            dbeta_ref[rows, h : h + 1] = (drate * rate * (1.0 - rate)).astype(dbeta_ref.dtype)
            for part, da in enumerate((dq, dk, ddelta)):
                part_cols = slice(part * width + h * 128, part * width + (h + 1) * 128)
                pre = pre_s[rows, part_cols]
                sg = sigmoid(pre)
                if part < 2:
                    a = pre * sg
                    scale = 128 ** (-0.5) if part == 0 else 1.0
                    r = lax.rsqrt(jnp.sum(a * a, axis=-1, keepdims=True) + epsilon)
                    da = (scale * r) * (da - a * (r * r) * jnp.sum(da * a, axis=-1, keepdims=True))
                dpre_s[rows, part_cols] = da * (sg * (1.0 + pre * (1.0 - sg)))
        return tuple(new_dstates)

    lax.fori_loop(0, count, retreat, tuple(jnp.zeros((128, 128), f32) for _ in range(heads)))

    @pl.loop(0, count)
    def _(c):
        base = pl.multiple_of(c * chunk, chunk)
        rows = pl.ds(base, chunk)
        col = base + lax.broadcasted_iota(jnp.int32, (chunk, 1), 0)
        seg = segment_of(col)
        for part in range(3):
            cols = slice(part * width, (part + 1) * width)
            _, shifted = conv_part(proj_ref, tap_ref, segment_of, base, part, width, chunk)
            full = dpre_s[pl.ds(base, chunk + HALO), cols]
            main = full[:chunk]
            total = main * tap_ref[part * taps : part * taps + 1, :]
            for s in range(taps):
                at = slice(part * taps + s, part * taps + s + 1)
                dtap_ref[at, :] += jnp.sum(main * shifted[s], axis=0, keepdims=True)
                if s > 0:
                    valid = (segment_of(col + s) == seg) & (col + s < rows_all)
                    moved = pltpu.roll(full, chunk + HALO - s, 0)[:chunk]
                    total = total + jnp.where(valid, moved, 0.0) * tap_ref[at, :]
            dproj_ref[rows, cols] = total.astype(dproj_ref.dtype)


def vmem():
    return pl.BlockSpec(memory_space=pltpu.VMEM)


def mixer_forward(lengths_row, projected, beta_logits, taps, gain, exact=True, group=4):
    rows, wide = projected.shape
    width = wide // 4
    heads = width // 128
    places = rows // CHUNK * heads
    group = min(group, rows // CHUNK)
    return pl.pallas_call(
        partial(mixer_forward_kernel, exact, group),
        out_shape=(
            jax.ShapeDtypeStruct((rows, width), bf16),
            jax.ShapeDtypeStruct((rows, width), f32),
            jax.ShapeDtypeStruct((rows, width), f32),
            jax.ShapeDtypeStruct((rows, width), f32),
            jax.ShapeDtypeStruct((places, 128, 128), f32),
            jax.ShapeDtypeStruct((places, CHUNK, CHUNK), f32),
        ),
        in_specs=[pl.BlockSpec(memory_space=pltpu.SMEM)] + [vmem()] * 4,
        out_specs=(vmem(),) * 6,
        scratch_shapes=[pltpu.VMEM((rows, width), f32)] * 3
        + [pltpu.VMEM((places, CHUNK, CHUNK), f32 if exact else bf16)],
        compiler_params=pltpu.CompilerParams(vmem_limit_bytes=48 * 2**20),
        cost_estimate=pl.CostEstimate(flops=10**10, bytes_accessed=10**7, transcendentals=10**6),
        name="mixer_forward",
    )(lengths_row, projected, beta_logits, taps, gain)


def mixer_backward(lengths_row, projected, beta_logits, taps, gain, grad, saved, exact=True):
    rows, wide = projected.shape
    width = wide // 4
    return pl.pallas_call(
        partial(mixer_backward_kernel, exact),
        out_shape=(
            jax.ShapeDtypeStruct((rows, wide), bf16),
            jax.ShapeDtypeStruct((rows, 128), bf16),
            jax.ShapeDtypeStruct(taps.shape, f32),
            jax.ShapeDtypeStruct(gain.shape, f32),
        ),
        in_specs=[pl.BlockSpec(memory_space=pltpu.SMEM)] + [vmem()] * 10,
        out_specs=(vmem(),) * 4,
        scratch_shapes=[pltpu.VMEM((rows, width), f32)] * 2
        + [pltpu.VMEM((rows, 3 * width), f32), pltpu.VMEM((rows, width), f32),
           pltpu.VMEM((rows + HALO, 3 * width), f32)],
        compiler_params=pltpu.CompilerParams(vmem_limit_bytes=56 * 2**20),
        cost_estimate=pl.CostEstimate(flops=10**10, bytes_accessed=10**7, transcendentals=10**6),
        name="mixer_backward",
    )(lengths_row, projected, beta_logits, taps, gain, grad, *saved)


NT = (((1,), (1,)), ((), ()))


def other(axis_name):
    return {axis_name: 1 - lax.axis_index(axis_name)}


def ffn_kernel(x_ref, w_ref, c_refs, out_ref, ngrad_ref, wgrad_ref,
               xs, cs, ws, inner_s, gate_s, up_s, acts_t, part, crecv, drecv, nrecv, stage, ctile,
               ag_send, ag_recv, pair_send, pair_recv, rs_send, rs_recv, c_sem, w_sem, g_sem, t_sem):
    half = xs.shape[1] // 2
    rows = 2 * half
    model = xs.shape[2]
    hidden = ws.shape[1]
    lines = w_ref.shape[0]
    quarter = w_ref.shape[2]
    tile_f = 256
    tile_d = min(512, model)
    tile_w = min(256, model)

    def remote(src, dst, send, recv, axis_name):
        return pltpu.make_async_remote_copy(
            src_ref=src, dst_ref=dst, send_sem=send, recv_sem=recv,
            device_id=other(axis_name), device_id_type=pl.DeviceIdType.MESH)

    def halves(ref, index, h):
        return ref.at[index, pl.ds(h * half, half)]

    barrier = pltpu.get_barrier_semaphore()
    for axis_name in ("core", "x", "y"):
        pl.semaphore_signal(
            barrier, inc=1, device_id=other(axis_name), device_id_type=pl.DeviceIdType.MESH)

    weight_copies = [
        pltpu.make_async_copy(
            w_ref.at[line, kind], ws.at[kind, pl.ds(line * quarter, quarter)], w_sem.at[line, kind])
        for line in range(lines) for kind in range(3)
    ]
    for copy in weight_copies:
        copy.start()

    def slot_of(step):
        return (1 - lax.rem(step, 2)) * 4 + step // 2

    def c_copy(step, n):
        buffer = lax.rem(step, 2)
        return pltpu.make_async_copy(c_refs[n], cs.at[buffer], c_sem.at[buffer])

    def c_start(step):
        for n in range(8):
            @pl.when(slot_of(step) == n)
            def _():
                c_copy(step, n).start()

    c_copy(0, 4).start()
    pl.semaphore_wait(barrier, 3)

    own_pair = remote(x_ref, xs.at[4], ag_send.at[0], ag_recv.at[0], "core")
    own_x = [remote(x_ref.at[pl.ds(h * half, half)], halves(xs, 1, h), ag_send.at[1 + h], ag_recv.at[1 + h], "x") for h in range(2)]
    own_y = [remote(x_ref.at[pl.ds(h * half, half)], halves(xs, 2, h), ag_send.at[3 + h], ag_recv.at[3 + h], "y") for h in range(2)]
    relay_y = remote(halves(xs, 1, 0), halves(xs, 3, 0), ag_send.at[5], ag_recv.at[5], "y")
    relay_x = remote(halves(xs, 2, 1), halves(xs, 3, 1), ag_send.at[6], ag_recv.at[6], "x")
    pair_of = [None] + [remote(xs.at[j], xs.at[4 + j], ag_send.at[6 + j], ag_recv.at[6 + j], "core") for j in (1, 2, 3)]
    own_pair.start()
    own_x[0].start()
    own_y[1].start()
    own_x[1].start()
    own_y[0].start()
    own_copy = pltpu.make_async_copy(x_ref, xs.at[0], t_sem.at[0, 0])
    own_copy.start()
    own_copy.wait()
    for copy in weight_copies:
        copy.wait()

    def part_send(j):
        return remote(part.at[lax.rem(j, 2)], crecv.at[j], pair_send.at[j], pair_recv.at[j], "core")

    x_sends = [[remote(crecv.at[1, a, pl.ds(h * half, half)], nrecv.at[0, a, pl.ds(h * half, half)],
                       rs_send.at[a * 2 + h], rs_recv.at[a * 2 + h], "x") for a in range(2)] for h in range(2)]
    y_sends = [[remote(crecv.at[2, a, pl.ds(h * half, half)], nrecv.at[1, a, pl.ds(h * half, half)],
                       rs_send.at[4 + a * 2 + h], rs_recv.at[4 + a * 2 + h], "y") for a in range(2)] for h in range(2)]
    d_sends = [[remote(crecv.at[3, a, pl.ds(h * half, half)], drecv.at[a, pl.ds(h * half, half)],
                       rs_send.at[8 + a * 2 + h], rs_recv.at[8 + a * 2 + h], ("x", "y")[h]) for a in range(2)] for h in range(2)]

    @pl.loop(0, 8)
    def _(step):
        j = step // 2
        slot = slot_of(step)
        pairing = lax.rem(step, 2) == 0

        @pl.when(step < 7)
        def _():
            c_start(step + 1)

        @pl.when(step == 0)
        def _():
            own_pair.wait_recv()

        @pl.when(step == 2)
        def _():
            own_x[0].wait_recv()
            relay_y.start()
            own_y[1].wait_recv()
            relay_x.start()
            own_x[1].wait_recv()
            pair_of[1].start()
            own_y[0].wait_recv()
            pair_of[2].start()
            pair_of[1].wait_recv()

        @pl.when(step == 4)
        def _():
            relay_y.wait_recv()
            relay_x.wait_recv()
            pair_of[3].start()
            pair_of[2].wait_recv()

        @pl.when(step == 6)
        def _():
            pair_of[3].wait_recv()

        c_copy(step, 0).wait()

        for start in range(0, hidden, tile_f):
            size = min(tile_f, hidden - start)
            cols = slice(start, start + size)
            x = xs[slot]
            gate = lax.dot_general(x, ws[0, cols, :], NT, preferred_element_type=f32)
            up = lax.dot_general(x, ws[1, cols, :], NT, preferred_element_type=f32)
            grad = lax.dot_general(cs[lax.rem(step, 2)], ws[2, cols, :], NT, preferred_element_type=f32)
            sg = sigmoid(gate)
            silu = gate * sg
            inner = (silu * up).astype(bf16)
            gate_grad = (grad * up * sg * (1.0 + gate * (1.0 - sg))).astype(bf16)
            up_grad = (grad * silu).astype(bf16)
            places = pl.ds(pl.multiple_of(slot * rows, rows), rows)
            for kind, (value, target) in enumerate(((gate_grad, gate_s), (up_grad, up_s), (inner, inner_s))):
                target[:, cols] = value
                acts_t[kind, cols, places] = value.T

        @pl.when(pairing & (step >= 4))
        def _():
            part_send(j - 2).wait_send()

        place = jnp.where(pairing, lax.rem(j, 2), 2)
        for start in range(0, model, tile_d):
            cols = slice(start, start + tile_d)
            part[place, 0, :, cols] = jnp.dot(
                inner_s[...], ws[2, :, cols], preferred_element_type=f32).astype(bf16)
            part[place, 1, :, cols] = (
                jnp.dot(gate_s[...], ws[0, :, cols], preferred_element_type=f32)
                + jnp.dot(up_s[...], ws[1, :, cols], preferred_element_type=f32)
            ).astype(bf16)

        @pl.when(pairing)
        def _():
            part_send(j).start()

        @pl.when(jnp.logical_not(pairing))
        def _():
            part_send(j).wait_recv()
            for a in range(2):
                for start in range(0, model, tile_d):
                    cols = slice(start, start + tile_d)
                    crecv[j, a, :, cols] = (
                        crecv[j, a, :, cols].astype(f32) + part[2, a, :, cols].astype(f32)
                    ).astype(bf16)

        @pl.when(step == 3)
        def _():
            for copy in x_sends[0]:
                copy.start()

        @pl.when(step == 5)
        def _():
            for copy in y_sends[1]:
                copy.start()

        @pl.when(step == 7)
        def _():
            for h in range(2):
                for copy in d_sends[h]:
                    copy.start()

    tiles = model // tile_w

    def c_tile(t):
        buffer = lax.rem(t, 2)
        cols = pl.ds(pl.multiple_of(t * tile_w, tile_w), tile_w)
        return [
            pltpu.make_async_copy(ref.at[:, cols], ctile.at[buffer, n], t_sem.at[buffer, n])
            for n, ref in enumerate(c_refs)]

    def grad_copy(kind, t, line):
        return pltpu.make_async_copy(
            stage.at[lax.rem(t, 2), pl.ds(line * quarter, quarter)],
            wgrad_ref.at[line, kind, :, pl.ds(pl.multiple_of(t * tile_w, tile_w), tile_w)],
            g_sem.at[lax.rem(t, 2), line])

    def weight_grads(kind):
        if kind == 2:
            for copy in c_tile(0):
                copy.start()

        @pl.loop(0, tiles)
        def _(t):
            if kind == 2:
                @pl.when(t + 1 < tiles)
                def _():
                    for copy in c_tile(t + 1):
                        copy.start()
                for copy in c_tile(t):
                    copy.wait()
                right = ctile[lax.rem(t, 2)].reshape(8 * rows, tile_w)
            else:
                right = xs[:, :, pl.ds(pl.multiple_of(t * tile_w, tile_w), tile_w)].reshape(8 * rows, tile_w)

            @pl.when(t >= 2)
            def _():
                for line in range(lines):
                    grad_copy(kind, t - 2, line).wait()

            stage[lax.rem(t, 2)] = jnp.dot(
                acts_t[kind], right, preferred_element_type=f32).astype(bf16)
            for line in range(lines):
                grad_copy(kind, t, line).start()

        for t in range(max(tiles - 2, 0), tiles):
            for line in range(lines):
                grad_copy(kind, t, line).wait()

    weight_grads(0)
    for h in range(2):
        j = 2 - h
        for a in range(2):
            d_sends[h][a].wait_recv()
            at = pl.ds(h * half, half)
            crecv[j, a, at, :] = (
                crecv[j, a, at, :].astype(f32) + drecv[a, at, :].astype(f32)).astype(bf16)
        for copy in (y_sends, x_sends)[h][h]:
            copy.start()
    weight_grads(1)
    weight_grads(2)
    for a, target in enumerate((out_ref, ngrad_ref)):
        for h in range(2):
            x_sends[h][a].wait_recv()
            y_sends[h][a].wait_recv()
            at = pl.ds(h * half, half)
            target[at, :] = (
                crecv[0, a, at, :].astype(f32)
                + nrecv[0, a, at, :].astype(f32)
                + nrecv[1, a, at, :].astype(f32)
            )
    own_pair.wait_send()
    for h in range(2):
        own_x[h].wait_send()
        own_y[h].wait_send()
        for a in range(2):
            x_sends[h][a].wait_send()
            y_sends[h][a].wait_send()
            d_sends[h][a].wait_send()
    relay_x.wait_send()
    relay_y.wait_send()
    for j in (1, 2, 3):
        pair_of[j].wait_send()
    part_send(2).wait_send()
    part_send(3).wait_send()


def ffn_call_kernel(x_ref, w_ref, *refs):
    ffn_kernel(x_ref, w_ref, refs[:8], *refs[8:])


def ffn_plane(x_own, weights, c_rows):
    rows, model = x_own.shape
    lines, _, quarter, _ = weights.shape
    hidden = lines * quarter
    tile_w = min(256, model)
    sems = pltpu.SemaphoreType.DMA
    anywhere = pl.BlockSpec(memory_space=pl.ANY)
    return pl.pallas_call(
        ffn_call_kernel,
        out_shape=(
            jax.ShapeDtypeStruct((rows, model), f32),
            jax.ShapeDtypeStruct((rows, model), f32),
            jax.ShapeDtypeStruct(weights.shape, bf16),
        ),
        in_specs=[anywhere] * 10,
        out_specs=(vmem(), vmem(), anywhere),
        scratch_shapes=[
            pltpu.VMEM((8, rows, model), bf16),
            pltpu.VMEM((2, rows, model), bf16),
            pltpu.VMEM((3, hidden, model), bf16),
            pltpu.VMEM((rows, hidden), bf16),
            pltpu.VMEM((rows, hidden), bf16),
            pltpu.VMEM((rows, hidden), bf16),
            pltpu.VMEM((3, hidden, 8 * rows), bf16),
            pltpu.VMEM((3, 2, rows, model), bf16),
            pltpu.VMEM((4, 2, rows, model), bf16),
            pltpu.VMEM((2, rows, model), bf16),
            pltpu.VMEM((2, 2, rows, model), bf16),
            pltpu.VMEM((2, hidden, tile_w), bf16),
            pltpu.VMEM((2, 8, rows, tile_w), bf16),
            sems((10,)), sems((10,)), sems((4,)), sems((4,)), sems((12,)), sems((12,)),
            sems((2,)), sems((lines, 3)), sems((2, lines)), sems((2, 8)),
        ],
        compiler_params=pltpu.CompilerParams(
            collective_id=2, has_side_effects=True, vmem_limit_bytes=62 * 2**20),
        cost_estimate=pl.CostEstimate(flops=8 * 10**10, bytes_accessed=4 * 10**7, transcendentals=10**6),
        name="ffn_plane",
    )(x_own, weights, *c_rows)


def line_barrier(lines, others):
    o = lax.axis_index("z")
    barrier = pltpu.get_barrier_semaphore()
    mesh_id = pl.DeviceIdType.MESH

    @pl.when(o > 0)
    def _():
        pl.semaphore_signal(barrier, inc=1, device_id={"z": o - 1}, device_id_type=mesh_id)

    @pl.when(o < lines - 1)
    def _():
        pl.semaphore_signal(barrier, inc=1, device_id={"z": o + 1}, device_id_type=mesh_id)

    for target in others:
        pl.semaphore_signal(barrier, inc=1, device_id=target, device_id_type=mesh_id)
    peers = len(others) + (o > 0).astype(jnp.int32) + (o < lines - 1).astype(jnp.int32)
    pl.semaphore_wait(barrier, peers)


def line_copy(src, dst, send, recv, target):
    return pltpu.make_async_remote_copy(
        src_ref=src, dst_ref=dst, send_sem=send, recv_sem=recv,
        device_id=target, device_id_type=pl.DeviceIdType.MESH)


def gather_kernel(x_ref, o_ref, w_ref, wb_ref, rows_ref, outs_ref, proj_ref, beta_ref,
                  xs, stage, beta_stage, right_send, left_send, line_recv, pair_send, pair_recv,
                  own_sem, row_sem, outs_sem, out_sem, beta_sem):
    lines = xs.shape[0] // 2
    batches, rows, model = x_ref.shape
    more = o_ref.shape[1]
    o = lax.axis_index("z")
    i = lax.axis_index("y")
    line_barrier(lines, [other("y")])

    def right(z, m):
        ref = xs.at[z * 2 + i, m]
        return line_copy(ref, ref, right_send.at[z, m], line_recv.at[z, m], {"z": o + 1})

    def left(z, m):
        ref = xs.at[z * 2 + i, m]
        return line_copy(ref, ref, left_send.at[z, m], line_recv.at[z, m], {"z": o - 1})

    def across(z, m):
        ref = xs.at[z * 2 + i, m, pl.ds(0, rows)]
        return line_copy(ref, ref, pair_send.at[z, m], pair_recv.at[z, m], other("y"))

    own = [
        pltpu.make_async_copy(x_ref, xs.at[o * 2 + i, :, pl.ds(0, rows)], own_sem.at[0]),
        pltpu.make_async_copy(o_ref, xs.at[o * 2 + i, :, pl.ds(rows, more)], own_sem.at[1]),
    ]
    for copy in own:
        copy.start()
    for copy in own:
        copy.wait()

    def outs(turn, slot):
        buffer = lax.rem(turn, 2)
        return [
            copy for m in range(batches) for copy in (
                pltpu.make_async_copy(stage.at[buffer, m], proj_ref.at[m, slot], out_sem.at[buffer, m]),
                pltpu.make_async_copy(beta_stage.at[buffer, m], beta_ref.at[m, slot], beta_sem.at[buffer, m]))
        ]

    def keep(slot, m):
        return pltpu.make_async_copy(xs.at[slot, m, pl.ds(0, rows)], rows_ref.at[m, slot], row_sem.at[slot, m])

    def keep_outs(z):
        return pltpu.make_async_copy(xs.at[z * 2 + i, :, pl.ds(rows, more)], outs_ref.at[z], outs_sem.at[z])

    def project(turn, slot):
        @pl.when(turn >= 2)
        def _():
            for copy in outs(turn, slot):
                copy.wait()
        for m in range(batches):
            keep(slot, m).start()
        x = xs[slot, :, :rows].reshape(batches * rows, model)
        buffer = lax.rem(turn, 2)
        width = w_ref.shape[1]
        tile = min(256, width)
        for start in range(0, width, tile):
            cols = slice(start, start + tile)
            stage[buffer, :, :, cols] = jnp.dot(
                x, w_ref[:, cols], preferred_element_type=f32).reshape(batches, rows, tile)
        beta_stage[buffer] = jnp.dot(
            x, wb_ref[...], preferred_element_type=f32).reshape(batches, rows, 128)
        for copy in outs(turn, slot):
            copy.start()

    def in_line(index):
        far = (index + 1) // 2
        side = 1 - 2 * lax.rem(index, 2)
        z = o + side * far
        return far, z, (z >= 0) & (z < lines)

    def first(index, turn):
        far, z, valid = in_line(index)

        @pl.when(valid)
        def _():
            for m in range(batches):
                @pl.when(far > 0)
                def _():
                    left(z, m).wait_recv()

                @pl.when((o < lines - 1) & (z <= o))
                def _():
                    right(z, m).start()

                @pl.when((o > 0) & (z >= o))
                def _():
                    left(z, m).start()

                across(z, m).start()
            keep_outs(z).start()
            project(turn, z * 2 + i)

        return turn + valid.astype(jnp.int32)

    turn = lax.fori_loop(0, 2 * lines - 1, first, jnp.int32(0))

    def second(index, turn):
        far, z, valid = in_line(index)

        @pl.when(valid)
        def _():
            for m in range(batches):
                across(z, m).wait_recv()
            project(turn, z * 2 + 1 - i)

        return turn + valid.astype(jnp.int32)

    lax.fori_loop(0, 2 * lines - 1, second, turn)
    for turn in range(2 * lines - 2, 2 * lines):
        for copy in outs(turn, 0):
            copy.wait()

    @pl.loop(0, lines)
    def _(z):
        keep_outs(z).wait()
        for m in range(batches):
            @pl.when((o < lines - 1) & (z <= o))
            def _():
                right(z, m).wait_send()

            @pl.when((o > 0) & (z >= o))
            def _():
                left(z, m).wait_send()

            across(z, m).wait_send()
            for y in range(2):
                keep(z * 2 + y, m).wait()


def gather_project(x, w_out_part, w_inner, w_beta):
    batches, rows, model = x.shape
    more = w_out_part.shape[1]
    lines = lax.axis_size("z")
    width = w_inner.shape[1]
    slots = 2 * lines
    sems = pltpu.SemaphoreType.DMA
    anywhere = pl.BlockSpec(memory_space=pl.ANY)
    pair = sems((lines, batches))
    gathered, outs, projected, beta = pl.pallas_call(
        gather_kernel,
        out_shape=(
            jax.ShapeDtypeStruct((batches, slots, rows, model), bf16),
            jax.ShapeDtypeStruct((lines, batches, more, model), bf16),
            jax.ShapeDtypeStruct((batches, slots, rows, width), f32),
            jax.ShapeDtypeStruct((batches, slots, rows, 128), f32),
        ),
        in_specs=[anywhere] * 2 + [vmem()] * 2,
        out_specs=(anywhere,) * 4,
        scratch_shapes=[
            pltpu.VMEM((slots, batches, rows + more, model), bf16),
            pltpu.VMEM((2, batches, rows, width), f32),
            pltpu.VMEM((2, batches, rows, 128), f32),
            pair, pair, pair, pair, pair,
            sems((2,)), sems((slots, batches)), sems((lines,)), sems((2, batches)), sems((2, batches)),
        ],
        compiler_params=pltpu.CompilerParams(
            collective_id=1, has_side_effects=True, vmem_limit_bytes=40 * 2**20),
        cost_estimate=pl.CostEstimate(flops=10**11, bytes_accessed=4 * 10**7, transcendentals=0),
        name="gather_project",
    )(x, w_out_part, w_inner, w_beta)
    total = slots * rows
    return (gathered.reshape(batches, total, model), outs, projected.reshape(batches, total, width),
            beta.reshape(batches, total, 128))


def scatter_kernel(g_ref, gb_ref, o_ref, inner_ref, w_ref, wb_ref, small_ref, gains_ref,
                   out_ref, small_out, outs_ref, inner_out,
                   gs, bs, ysend, yrecv, from_left, from_right, outs_s, inner_s, inner_r, small_s, small_r, gains_r,
                   pair_send, pair_recv, right_send, left_send, right_recv, left_recv, g_sem,
                   sum_send, sum_recv, outs_send, outs_recv, gain_send, gain_recv, sum_sem):
    batches, rows, width = gs.shape
    lines = yrecv.shape[0]
    model = yrecv.shape[3]
    more = yrecv.shape[2] - rows
    o = lax.axis_index("z")
    i = lax.axis_index("y")
    core = lax.axis_index("core")
    me = lax.axis_index("x") * 2 + core
    tile = min(512, model)
    diagonal = {"x": 1 - lax.axis_index("x"), "core": 1 - core}
    slots = 2 * lines
    mine = o * 2 + i
    peers = []
    for d in range(1, slots):
        place = lax.rem(mine + d, slots)
        peers.append((place, {"z": place // 2, "y": lax.rem(place, 2)}))
    barrier = pltpu.get_barrier_semaphore()
    greeted = [other("core"), other("x"), diagonal] + [device for _, device in peers]
    for device in greeted:
        pl.semaphore_signal(barrier, inc=1, device_id=device, device_id_type=pl.DeviceIdType.MESH)
    pl.semaphore_wait(barrier, len(greeted))
    gain_copies = [
        line_copy(gains_ref.at[place], gains_r.at[mine], gain_send.at[d], gain_recv.at[d], device)
        for d, (place, device) in enumerate(peers)
    ]
    for copy in gain_copies:
        copy.start()

    inner_pair = line_copy(inner_ref.at[1 - core], inner_r.at[0], sum_send.at[0], sum_recv.at[0], other("core"))
    inner_across = line_copy(inner_s, inner_r.at[1], sum_send.at[1], sum_recv.at[1], other("x"))
    inner_back = line_copy(inner_s, inner_out.at[core], sum_send.at[2], sum_recv.at[2], other("core"))
    small_pair = line_copy(small_s.at[0], small_r.at[0], sum_send.at[3], sum_recv.at[3], other("core"))
    small_across = line_copy(small_s.at[1], small_r.at[1], sum_send.at[4], sum_recv.at[4], other("x"))
    inner_own = pltpu.make_async_copy(inner_ref.at[core], inner_s, sum_sem.at[0])
    inner_keep = pltpu.make_async_copy(inner_s, inner_out.at[core], sum_sem.at[1])
    outs_keep = pltpu.make_async_copy(outs_s, outs_ref.at[me], sum_sem.at[2])
    outs_away = [
        line_copy(outs_s, outs_ref.at[me], outs_send.at[n], outs_recv.at[n], target)
        for n, target in enumerate((other("core"), other("x"), diagonal))
    ]
    inner_pair.start()
    inner_own.start()

    def add_into(target, other_ref):
        height = target.shape[0]
        step = next(size for size in range(min(128, height), 0, -16) if height % size == 0)

        @pl.loop(0, height // step)
        def _(n):
            at = pl.ds(pl.multiple_of(n * step, step), step)
            target[at, :] = (target[at, :].astype(f32) + other_ref[at, :].astype(f32)).astype(target.dtype)

    def target(index):
        far = lines - 1 - index // 2
        side = 1 - 2 * lax.rem(index, 2)
        z = o + side * far
        return far, z, (z >= 0) & (z < lines) & ((far > 0) | (side > 0))

    def load(z, y):
        slot = z * 2 + y
        return (pltpu.make_async_copy(g_ref.at[:, slot], gs, g_sem.at[0]),
                pltpu.make_async_copy(gb_ref.at[:, slot], bs, g_sem.at[1]))

    def partial_rows(z, y, store):
        for copy in load(z, y):
            copy.start()
        for copy in load(z, y):
            copy.wait()
        for m in range(batches):
            g = gs[m]
            b = bs[m]
            for start in range(0, model, tile):
                cols = slice(start, start + tile)
                store(m, slice(0, rows), cols, lax.dot_general(g, w_ref[cols, :], NT, preferred_element_type=f32)
                      + lax.dot_general(b, wb_ref[cols, :], NT, preferred_element_type=f32))

    def across(z, m):
        return line_copy(ysend.at[z, m], yrecv.at[z, m, pl.ds(0, rows)], pair_send.at[z, m], pair_recv.at[z, m], other("y"))

    def right(z, m):
        return line_copy(yrecv.at[z, m], from_left.at[z, m], right_send.at[z, m], right_recv.at[z, m], {"z": o + 1})

    def left(z, m):
        return line_copy(yrecv.at[z, m], from_right.at[z, m], left_send.at[z, m], left_recv.at[z, m], {"z": o - 1})

    @pl.loop(0, 2 * lines)
    def _(index):
        far, z, valid = target(index)

        @pl.when(valid)
        def _():
            def store(m, at, cols, value):
                ysend[z, m, at, cols] = value.astype(bf16)
            partial_rows(z, 1 - i, store)
            for m in range(batches):
                across(z, m).start()

    inner_own.wait()
    inner_pair.wait_recv()
    add_into(inner_s, inner_r.at[0])
    inner_across.start()
    gains_r[mine] = gains_ref[mine]
    for copy in gain_copies:
        copy.wait_recv()
    tail = small_ref.shape[0]
    small_s[0, :tail] = small_ref[...]
    small_s[0, tail:] = jnp.sum(gains_r[...], axis=0)
    small_pair.start()

    @pl.loop(0, 2 * lines)
    def _(index):
        far, z, valid = target(index)

        @pl.when(valid)
        def _():
            for m in range(batches):
                across(z, m).wait_recv()

            def store(m, at, cols, value):
                yrecv[z, m, at, cols] = (yrecv[z, m, at, cols].astype(f32) + value).astype(bf16)
            partial_rows(z, i, store)
            for m in range(batches):
                yrecv[z, m, rows:, :] = o_ref[z, m]
                @pl.when((z > o) & (o > 0))
                def _():
                    right(z, m).wait_recv()
                    add_into(yrecv.at[z, m], from_left.at[z, m])

                @pl.when(z > o)
                def _():
                    right(z, m).start()

                @pl.when((z < o) & (o < lines - 1))
                def _():
                    left(z, m).wait_recv()
                    add_into(yrecv.at[z, m], from_right.at[z, m])

                @pl.when(z < o)
                def _():
                    left(z, m).start()

    inner_across.wait_recv()
    inner_across.wait_send()
    add_into(inner_s, inner_r.at[1])
    inner_back.start()
    inner_keep.start()
    small_pair.wait_recv()
    small_s[1] = small_s[0] + small_r[0]
    small_across.start()

    for m in range(batches):
        @pl.when(o > 0)
        def _():
            right(o, m).wait_recv()

        @pl.when(o < lines - 1)
        def _():
            left(o, m).wait_recv()

        out_ref[m] = yrecv[o, m, :rows, :].astype(f32)
        outs_s[m * more : (m + 1) * more, :] = yrecv[o, m, rows : rows + more, :]

        for side_ref, exists in ((from_left, o > 0), (from_right, o < lines - 1)):
            @pl.when(exists)
            def _():
                out_ref[m] += side_ref[o, m, :rows, :].astype(f32)
                at = slice(m * more, (m + 1) * more)
                outs_s[at, :] = (
                    outs_s[at, :].astype(f32) + side_ref[o, m, rows : rows + more, :].astype(f32)
                ).astype(bf16)

    outs_keep.start()
    for copy in outs_away:
        copy.start()

    @pl.loop(0, lines)
    def _(z):
        for m in range(batches):
            across(z, m).wait_send()

            @pl.when(z > o)
            def _():
                right(z, m).wait_send()

            @pl.when(z < o)
            def _():
                left(z, m).wait_send()

    small_across.wait_recv()
    small_out[...] = small_s[1] + small_r[1]
    for copy in gain_copies:
        copy.wait_send()
    inner_pair.wait_send()
    small_pair.wait_send()
    small_across.wait_send()
    inner_back.wait_recv()
    inner_back.wait_send()
    inner_keep.wait()
    outs_keep.wait()
    for copy in outs_away:
        copy.wait_recv()
        copy.wait_send()


def scatter_rows(grads, beta_grads, out_grads, inner_grads, w_inner, w_beta, small, gains):
    batches, total, width = grads.shape
    model = w_inner.shape[0]
    lines = lax.axis_size("z")
    slots = 2 * lines
    rows = total // slots
    more = out_grads.shape[2]
    sems = pltpu.SemaphoreType.DMA
    anywhere = pl.BlockSpec(memory_space=pl.ANY)
    slab = pltpu.VMEM((lines, batches, rows + more, model), bf16)
    half = inner_grads.shape[1:]
    flat = (small.shape[0] + gains.shape[1], 128)
    return pl.pallas_call(
        scatter_kernel,
        out_shape=(
            jax.ShapeDtypeStruct((batches, rows, model), f32),
            jax.ShapeDtypeStruct(flat, f32),
            jax.ShapeDtypeStruct((4, batches * more, model), bf16),
            jax.ShapeDtypeStruct(inner_grads.shape, bf16),
        ),
        in_specs=[anywhere, anywhere, vmem(), anywhere, vmem(), vmem(), vmem(), vmem()],
        out_specs=(vmem(), vmem(), anywhere, anywhere),
        scratch_shapes=[
            pltpu.VMEM((batches, rows, width), bf16),
            pltpu.VMEM((batches, rows, 128), bf16),
            pltpu.VMEM((lines, batches, rows, model), bf16), slab, slab, slab,
            pltpu.VMEM((batches * more, model), bf16),
            pltpu.VMEM(half, bf16),
            pltpu.VMEM((2, *half), bf16),
            pltpu.VMEM((2, *flat), f32),
            pltpu.VMEM((2, *flat), f32),
            pltpu.VMEM(gains.shape, f32),
            sems((lines, batches)), sems((lines, batches)), sems((lines, batches)),
            sems((lines, batches)), sems((lines, batches)), sems((lines, batches)),
            sems((2,)), sems((5,)), sems((5,)), sems((3,)), sems((3,)), sems((slots,)), sems((slots,)), sems((3,)),
        ],
        compiler_params=pltpu.CompilerParams(
            collective_id=3, has_side_effects=True, vmem_limit_bytes=58 * 2**20),
        cost_estimate=pl.CostEstimate(flops=7 * 10**10, bytes_accessed=4 * 10**7, transcendentals=0),
        name="scatter_rows",
    )(grads.reshape(batches, slots, rows, width), beta_grads.reshape(batches, slots, rows, 128),
      out_grads, inner_grads, w_inner, w_beta, small, gains)


def attend_kernel(x_ref, first_ref, second_ref, gain_ref, *refs):
    pieces, (hidden_ref, normed_ref, w_ref, ws, sem, w_sem) = refs[:8], refs[8:]
    x = lax.axis_index("x")
    core = lax.axis_index("core")
    y = lax.axis_index("y")
    copies = []
    for n, piece in enumerate(pieces):
        far_y, far_x, far_core = n // 4, n // 2 % 2, n % 2
        column = 1 - y if far_y else y
        quarter = (1 - x if far_x else x) * 2 + (1 - core if far_core else core)
        copies.append(pltpu.make_async_copy(piece, ws.at[:, column, quarter], sem.at[n]))
    for copy in copies:
        copy.start()
    for copy in copies:
        copy.wait()
    keep = pltpu.make_async_copy(ws, w_ref, w_sem.at[0])
    keep.start()
    model = x_ref.shape[1]
    tile = min(512, model)
    devices = first_ref.shape[0]
    width = first_ref.shape[2]
    squares = 0.0
    for start in range(0, model, tile):
        cols = slice(start, start + tile)
        total = x_ref[:, cols].astype(f32)
        for t in range(devices):
            left = jnp.concatenate([first_ref[t], second_ref[t]], axis=0)
            total = total + jnp.dot(
                left, ws[t // 2, t % 2, :, :, cols].reshape(width, tile), preferred_element_type=f32)
        hidden_ref[:, cols] = total
        squares = squares + jnp.sum(total * total, axis=-1, keepdims=True)
    scale = lax.rsqrt(squares / model + epsilon)
    for start in range(0, model, tile):
        cols = slice(start, start + tile)
        normed_ref[:, cols] = (hidden_ref[:, cols] * scale * gain_ref[:, cols]).astype(bf16)
    keep.wait()


def attend(x, first, second, gain, pieces):
    rows, model = x.shape
    lines, part, _ = pieces[0].shape
    full = (lines, 2, 4, part, model)
    anywhere = pl.BlockSpec(memory_space=pl.ANY)
    return pl.pallas_call(
        attend_kernel,
        out_shape=(
            jax.ShapeDtypeStruct((rows, model), f32),
            jax.ShapeDtypeStruct((rows, model), bf16),
            jax.ShapeDtypeStruct(full, bf16),
        ),
        in_specs=[vmem()] * 4 + [anywhere] * 8,
        out_specs=(vmem(), vmem(), anywhere),
        scratch_shapes=[
            pltpu.VMEM(full, bf16), pltpu.SemaphoreType.DMA((8,)), pltpu.SemaphoreType.DMA((1,))],
        compiler_params=pltpu.CompilerParams(vmem_limit_bytes=32 * 2**20),
        cost_estimate=pl.CostEstimate(flops=10**10, bytes_accessed=2 * 10**7, transcendentals=0),
        name="attend",
    )(x, first, second, gain, *pieces)


def attend_back_kernel(hidden_ref, ffn_ref, grad_ref, c_ref, gain_ref, w_ref, first_ref, second_ref,
                       result_ref, hgrad_ref, back_first, back_second, wgrad_ref, gain_out, low):
    rows, model = hidden_ref.shape
    half = rows // 2
    tile = min(512, model)
    squares, dots = 0.0, 0.0
    for start in range(0, model, tile):
        cols = slice(start, start + tile)
        hidden = hidden_ref[:, cols]
        squares = squares + jnp.sum(hidden * hidden, axis=-1, keepdims=True)
        dots = dots + jnp.sum(hidden * grad_ref[:, cols] * gain_ref[:, cols], axis=-1, keepdims=True)
    scale = lax.rsqrt(squares / model + epsilon)
    pull = scale * scale * scale * (dots / model)
    for start in range(0, model, tile):
        cols = slice(start, start + tile)
        hidden = hidden_ref[:, cols]
        grad = grad_ref[:, cols]
        result_ref[:, cols] = hidden + ffn_ref[:, cols]
        gain_out[:, cols] = jnp.sum(grad * hidden * scale, axis=0, keepdims=True)
        hgrad = c_ref[:, cols].astype(f32) + scale * (grad * gain_ref[:, cols]) - hidden * pull
        hgrad_ref[:, cols] = hgrad
        low[:, cols] = hgrad.astype(bf16)
    devices, _, width = first_ref.shape

    for t in range(devices):
        back = lax.dot_general(
            low[...], w_ref[t // 2, t % 2].reshape(width, model), NT, preferred_element_type=f32)
        back_first[t] = back[:half].astype(bf16)
        back_second[t] = back[half:].astype(bf16)
        left = jnp.concatenate([first_ref[t], second_ref[t]], axis=0)
        for start in range(0, model, tile):
            cols = slice(start, start + tile)
            wgrad_ref[t // 2, t % 2, :, :, cols] = lax.dot_general(
                left, low[:, cols], (((0,), (0,)), ((), ())), preferred_element_type=f32
            ).reshape(4, width // 4, tile).astype(bf16)


def attend_back(hidden, ffn_out, normed_grad, c_rows, gain, w_full, first, second):
    rows, model = hidden.shape
    wide = jax.ShapeDtypeStruct((rows, model), f32)
    return pl.pallas_call(
        attend_back_kernel,
        out_shape=(
            wide, wide,
            jax.ShapeDtypeStruct(first.shape, bf16),
            jax.ShapeDtypeStruct(second.shape, bf16),
            jax.ShapeDtypeStruct(w_full.shape, bf16),
            jax.ShapeDtypeStruct((1, model), f32),
        ),
        in_specs=[vmem()] * 8,
        out_specs=(vmem(),) * 6,
        scratch_shapes=[pltpu.VMEM((rows, model), bf16)],
        compiler_params=pltpu.CompilerParams(vmem_limit_bytes=56 * 2**20),
        cost_estimate=pl.CostEstimate(flops=10**10, bytes_accessed=4 * 10**7, transcendentals=0),
        name="attend_back",
    )(hidden, ffn_out, normed_grad, c_rows, gain, w_full, first, second)


def root_scale(row_values, gain_vector):
    row_scale = lax.rsqrt(jnp.mean(row_values * row_values, axis=-1, keepdims=True) + epsilon)
    return (row_values * row_scale * gain_vector, row_scale)


def norm_backward(row_values, row_scale, gain_vector, normed_grad):
    weighted = normed_grad * gain_vector
    rows_grad = row_scale * weighted - row_values * row_scale * row_scale * row_scale * jnp.mean(
        weighted * row_values, axis=-1, keepdims=True
    )
    gain_grad = jnp.sum(normed_grad * row_values * row_scale, axis=tuple(range(row_values.ndim - 1)))
    return (rows_grad, gain_grad)


DP = ("x", "core")
TP = ("z", "y")


def gather(x, axis_name, axis=0):
    return lax.all_gather(x, axis_name, axis=axis, tiled=True)


def scatter_sum(x, axis_name, axis=0):
    return lax.psum_scatter(
        x.astype(bf16), axis_name, scatter_dimension=axis, tiled=True
    ).astype(f32)


def dot(a, b):
    return jnp.dot(a, b, preferred_element_type=f32)


def dot_nt(a, b):
    return jnp.einsum("tk,nk->tn", a, b, preferred_element_type=f32)


def dot_tn(a, b):
    return jnp.einsum("tm,tn->mn", a, b, preferred_element_type=f32)


def exchange(x, axis_name, distance=1):
    size = lax.axis_size(axis_name)
    return lax.ppermute(x, axis_name, [(i, i ^ distance) for i in range(size)])


def swap_blocks(blocks):
    size = lax.axis_size(DP)
    me = lax.axis_index(DP)
    pieces = []
    for r in range(size):
        block = lax.dynamic_index_in_dim(blocks, me ^ r, keepdims=False)
        pieces.append(exchange(block, DP, r) if r else block)
    return ordered_blocks(pieces)


def plane_weights(w_gate, w_up, w_down):
    size = lax.axis_size(DP)
    local = jnp.stack([w_gate.T, w_up.T, w_down])
    kinds, hidden, part = local.shape
    quarter = hidden // size
    blocks = local.reshape(kinds, size, quarter, part).swapaxes(0, 1)
    own = jnp.concatenate(swap_blocks(blocks), axis=2)
    return own.reshape(kinds * quarter, size * part)


def plane_weight_grads(own, kinds):
    size = lax.axis_size(DP)
    quarter, model = own.shape[0] // kinds, own.shape[1]
    blocks = own.reshape(kinds * quarter, size, model // size).swapaxes(0, 1)
    pieces = [piece.reshape(kinds, quarter, -1) for piece in swap_blocks(blocks)]
    whole = jnp.concatenate(pieces, axis=1).astype(f32)
    return whole[0].T, whole[1].T, whole[2]


def ordered_blocks(pieces):
    me = lax.axis_index(DP)
    pieces = jnp.stack(pieces)
    return [lax.dynamic_index_in_dim(pieces, me ^ q, keepdims=False) for q in range(len(pieces))]


def pick(x, index, axis):
    return lax.dynamic_index_in_dim(x, index, axis, keepdims=False)


def after(x, *others):
    return lax.optimization_barrier((x, *others))[0]


def halve_sum(grad, axis_name, axis):
    me = lax.axis_index(axis_name)
    theirs = exchange(pick(grad, 1 - me, axis), axis_name)
    return (pick(grad, me, axis).astype(f32) + theirs.astype(f32)).astype(bf16)


def feed_forward_groups(normed, cotangents, w_gate, w_up, w_down):
    gate_full = gather(w_gate, DP)
    up_full = gather(w_up, DP)
    down_full = gather(w_down, DP, 1)
    outs, normed_grads, inner_rows, gate_grads, up_grads, rows, grad_rows = [], [], [], [], [], [], []
    for m in range(normed.shape[0]):
        rows.append(gather(normed[m], TP))
        grad_rows.append(gather(cotangents[m], TP))
        gate_values = dot(rows[m], gate_full)
        up_values = dot(rows[m], up_full)
        sigmoid_gate = jax.nn.sigmoid(gate_values)
        silu_gate = gate_values * sigmoid_gate
        inner = (silu_gate * up_values).astype(bf16)
        inner_grad = dot_nt(grad_rows[m], down_full)
        gate_grad = (
            inner_grad * up_values * sigmoid_gate * (1.0 + gate_values * (1.0 - sigmoid_gate))
        ).astype(bf16)
        up_grad = (inner_grad * silu_gate).astype(bf16)
        normed_grads.append(scatter_sum(dot_nt(gate_grad, gate_full) + dot_nt(up_grad, up_full), TP))
        outs.append(scatter_sum(dot(inner, down_full), TP))
        inner_rows.append(inner)
        gate_grads.append(gate_grad)
        up_grads.append(up_grad)
    grad_all = jnp.concatenate(grad_rows)
    rows_all = jnp.concatenate(rows)
    gate_share = scatter_sum(dot_tn(rows_all, jnp.concatenate(gate_grads)), DP)
    up_share = scatter_sum(dot_tn(rows_all, jnp.concatenate(up_grads)), DP)
    down_share = scatter_sum(dot_tn(jnp.concatenate(inner_rows), grad_all), DP, 1)
    return jnp.stack(outs), jnp.stack(normed_grads), (gate_share, up_share, down_share)


def per_device(
    inputs,
    lengths,
    norm_gain,
    ffn_gain,
    w_query,
    w_key,
    w_value,
    w_gate_out,
    w_beta,
    conv_weight,
    head_gain,
    w_out,
    w_gate,
    w_up,
    w_down,
    cotangent,
):
    batches = range(inputs.shape[0])
    local_width = w_query.shape[1]
    heads = w_beta.shape[1]
    devices = lax.axis_size(TP)
    planar = all(lax.axis_size(name) == 2 for name in ("x", "core", "y"))
    w_inner = jnp.concatenate([w_query, w_key, w_value, w_gate_out], axis=1)
    w_beta_wide = jnp.pad(w_beta, ((0, 0), (0, 128 - heads)))
    taps = conv_weight.astype(f32).reshape(-1, local_width)
    gain_heads = head_gain.astype(f32)
    gains = gather(jnp.stack([norm_gain, ffn_gain]), DP, 1)
    gain_one, gain_two = gains[0].astype(f32), gains[1].astype(f32)
    rows_in = inputs.astype(f32)
    normed_one, scale_one = root_scale(rows_in, gain_one)
    normed_one = normed_one.astype(bf16)

    def run_mixer(m, wide, logits):
        low, *kept = mixer_forward(lengths[m, 0], wide, logits, taps, gain_heads, exact=False)
        return low, kept

    def back_mixer(m, wide, logits, grad, kept):
        return mixer_backward(
            lengths[m, 0], wide, logits, taps, gain_heads, grad, kept, exact=False)

    if planar:
        count = rows_in.shape[0] * rows_in.shape[1]
        model = rows_in.shape[2]
        own_weights = plane_weights(*after((w_gate, w_up, w_down), gains))
        c_rows = [None] * 8
        c_rows[0] = after(cotangent.reshape(count, model), gains)
        c_rows[1] = exchange(c_rows[0], "x")
        c_rows[4] = exchange(c_rows[0], "core")
        out_shares = pick(
            w_out.reshape(lax.axis_size(DP), len(batches), -1, model), lax.axis_index(DP), 0)
        gathered_one, out_own, projected, beta_logits = gather_project(
            normed_one, out_shares, w_inner, w_beta_wide)
        own_weights, early, early_x, out_own = after(
            (own_weights, c_rows[0], c_rows[1], out_own), gathered_one)
        weights = gather(own_weights, "z").reshape(lax.axis_size("z"), 3, -1, model)
        c_rows[2], c_rows[3] = exchange(early, "y"), exchange(early_x, "y")
        c_rows[5], c_rows[6], c_rows[7] = (exchange(c_rows[n], "core") for n in (1, 2, 3))
        out_own = out_own.reshape(out_own.shape[0], -1, model)
        out_pieces = []
        for piece in (out_own, exchange(out_own, "y")):
            across = exchange(piece, "x")
            out_pieces += [piece, exchange(piece, "core"), across, exchange(across, "core")]
    else:
        gathered_one = jnp.stack([gather(normed_one[m], TP) for m in batches])
        projected = [dot(gathered_one[m], w_inner) for m in batches]
        beta_logits = [dot(gathered_one[m], w_beta_wide) for m in batches]
        out_full = gather(w_out, TP)
    token_heads, saved = [], []
    for m in batches:
        low, kept = run_mixer(m, projected[m], beta_logits[m])
        saved.append(kept)
        token_heads.append(lax.all_to_all(
            low.reshape(devices, -1, local_width), TP, split_axis=0, concat_axis=0, tiled=True))
    if planar:
        hidden, normed_two, out_full = attend(
            inputs.reshape(count, model), *token_heads, gain_two[None], out_pieces)
        ffn_out, normed_grad, weight_grads = ffn_plane(normed_two, weights, c_rows)
        own_grads = lax.psum_scatter(
            weight_grads.reshape(-1, model), "z", scatter_dimension=0, tiled=True)
        gate_share, up_share, down_share = plane_weight_grads(own_grads, 3)
        result_rows, hidden_grad, *mixed_grads, out_grad, gain_two_sum = attend_back(
            hidden, ffn_out, normed_grad, c_rows[0], gain_two[None], out_full, *token_heads)
        gain_two_sum = gain_two_sum[0]
        result_rows = result_rows.reshape(rows_in.shape)
        hidden_grad = hidden_grad.reshape(rows_in.shape)
        out_grad = halve_sum(
            out_grad.reshape(out_grad.shape[0], 2, 2, 2, *out_grad.shape[3:]), "core", 3)
    else:
        heads_rows = [
            block.swapaxes(0, 1).reshape(-1, devices * local_width) for block in token_heads]
        hidden = rows_in + jnp.stack([dot(rows, out_full) for rows in heads_rows])
        normed_two, scale_two = root_scale(hidden, gain_two)
        ffn_out, normed_grad, (gate_share, up_share, down_share) = feed_forward_groups(
            normed_two.astype(bf16), cotangent, w_gate, w_up, w_down)
        result_rows = hidden + ffn_out
        norm_grad, gain_two_sum = norm_backward(hidden, scale_two, gain_two, normed_grad)
        hidden_grad = cotangent.astype(f32) + norm_grad
        attended_low = hidden_grad.astype(bf16)
        mixed_grads = [
            dot_nt(attended_low[m], out_full).astype(bf16)
            .reshape(-1, devices, local_width).swapaxes(0, 1) for m in batches]
        out_grad = dot_tn(
            jnp.concatenate(heads_rows), jnp.concatenate(list(attended_low))).astype(bf16)
    mixed_grads = [
        lax.all_to_all(grad, TP, split_axis=0, concat_axis=0, tiled=True).reshape(-1, local_width)
        for grad in mixed_grads]
    if planar:
        mixed_grads[0] = after(mixed_grads[0], out_grad)
        out_grad = halve_sum(halve_sum(out_grad, "x", 2), "y", 1)
        out_grad = out_grad.reshape(out_grad.shape[0], len(batches), -1, model)
    projected_low, beta_low = [], []
    taps_sum, heads_sum = 0.0, 0.0
    for m in batches:
        projected_grad, beta_grad, taps_part, heads_part = back_mixer(
            m, projected[m], beta_logits[m], mixed_grads[m], saved[m])
        taps_sum = taps_sum + taps_part
        heads_sum = heads_sum + heads_part
        projected_low.append(projected_grad)
        beta_low.append(beta_grad)
    projected_low = jnp.stack(projected_low)
    beta_low = jnp.stack(beta_low)
    tokens = gathered_one.reshape(-1, gathered_one.shape[2])
    inner_sum = dot_tn(tokens, projected_low.reshape(-1, 4 * local_width))
    beta_sum = dot_tn(tokens, beta_low.reshape(-1, 128)[:, :heads])
    gain_one_sum = (
        jnp.sum(inner_sum * w_inner.astype(f32), axis=1)
        + jnp.sum(beta_sum * w_beta.astype(f32), axis=1)
    ) / gain_one
    gain_parts = jnp.stack([gain_one_sum, gain_two_sum])
    small = jnp.concatenate([part.reshape(-1) for part in (beta_sum, taps_sum, heads_sum)])
    low_sum = inner_sum.astype(bf16)
    if planar:
        ranks = lax.axis_size(DP)
        gain_parts = gain_parts.reshape(2, ranks, devices, -1).transpose(2, 0, 1, 3)
        chunk = gain_parts.shape[3]
        gain_parts = gain_parts.reshape(devices, -1, 128)
        gain_rows = gain_parts.shape[1]
        gain_parts = jnp.pad(gain_parts, ((0, 0), (0, -gain_rows % 8), (0, 0)))
        small = jnp.pad(small, (0, -small.size % 1024)).reshape(-1, 128)
        input_norm, flat, out_total, inner_total = scatter_rows(
            after(projected_low, own_grads), beta_low, out_grad,
            low_sum.reshape(2, -1, low_sum.shape[1]), w_inner, w_beta_wide, small, gain_parts)
        gain_totals = pick(
            flat[small.shape[0] :][:gain_rows].reshape(2, ranks, chunk), lax.axis_index(DP), 1)
        small = flat[: small.shape[0]].reshape(-1)
        out_total = out_total.reshape(w_out.shape).astype(f32)
        inner_total = inner_total.reshape(low_sum.shape)
    else:
        gain_totals = lax.psum_scatter(gain_parts, DP + TP, scatter_dimension=1, tiled=True)
        inner_total = lax.psum(low_sum, DP)
        small = lax.psum(small, DP)
        out_grad = lax.psum_scatter(out_grad, TP, scatter_dimension=0, tiled=True)
        out_total = lax.psum(out_grad, DP).astype(f32)
        input_norm = jnp.stack([
            scatter_sum(
                dot_nt(projected_low[m], w_inner) + dot_nt(beta_low[m], w_beta_wide), TP)
            for m in batches])
    norm_grad, _ = norm_backward(rows_in, scale_one, gain_one, input_norm)
    beta_total, conv_total, heads_total = (
        piece.reshape(shape) for piece, shape in zip(
            jnp.split(
                small[: beta_sum.size + taps_sum.size + heads_sum.size],
                (beta_sum.size, beta_sum.size + taps_sum.size)),
            (beta_sum.shape, conv_weight.shape, head_gain.shape)))
    columns = [
        inner_total[:, n * local_width : (n + 1) * local_width].astype(f32) for n in range(4)]
    return (
        result_rows,
        hidden_grad + norm_grad,
        gain_totals[0],
        gain_totals[1],
        *columns,
        beta_total,
        conv_total,
        heads_total,
        out_total,
        gate_share,
        up_share,
        down_share,
    )


def solution(mesh):
    dp, tensor = mesh.shape["dp"], mesh.shape["tensor"]
    inner = 2 if tensor == 8 else 4
    axes = ("x", "core", "z", "y")
    fine = jax.sharding.Mesh(
        mesh.devices.reshape(dp // 2, 2, tensor // inner, inner), axes)
    tokens = P(None, DP + TP, None)
    in_specs = (
        tokens,
        P(None, DP, None),
        P(DP),
        P(DP),
        P(None, TP),
        P(None, TP),
        P(None, TP),
        P(None, TP),
        P(None, TP),
        P(None, None, TP),
        P(TP, None),
        P(TP, None),
        P(DP, TP),
        P(DP, TP),
        P(TP, DP),
        tokens,
    )
    out_specs = (
        tokens,
        tokens,
        P(DP + TP),
        P(DP + TP),
        P(None, TP),
        P(None, TP),
        P(None, TP),
        P(None, TP),
        P(None, TP),
        P(None, None, TP),
        P(TP, None),
        P(TP, None),
        P(DP, TP),
        P(DP, TP),
        P(TP, DP),
    )
    return jax.shard_map(
        per_device, mesh=fine, in_specs=in_specs, out_specs=out_specs, check_vma=False
    )
```

```python
from functools import partial

import jax
import jax.numpy as jnp
from jax import lax
from jax.experimental import pallas as pl
from jax.experimental.pallas import tpu as pltpu
from jax.sharding import PartitionSpec as P


CHUNK = 128
HALO = 8
epsilon = 1e-06
highest = lax.Precision.HIGHEST
f32 = jnp.float32
bf16 = jnp.bfloat16


def product(left, right, left_dim, right_dim, exact=False):
    dims = (((left_dim,), (right_dim,)), ((), ()))
    if exact:
        return lax.dot_general(left, right, dims, precision=highest, preferred_element_type=f32)
    return lax.dot_general(
        left.astype(bf16), right.astype(bf16), dims, preferred_element_type=f32
    )


def sigmoid(x):
    return 1.0 / (1.0 + jnp.exp(-x))


def segment_tools(lengths_ref):
    ends = []
    total = 0
    for i in range(lengths_ref.shape[0] - 1):
        total = total + lengths_ref[i]
        ends.append(total)

    def segment_of(pos):
        result = 0
        for end in ends:
            result = result + (pos >= end).astype(jnp.int32)
        return result

    return segment_of, len(ends)


def chunk_masks(segment_of, base, chunk):
    col = base + lax.broadcasted_iota(jnp.int32, (chunk, 1), 0)
    row = base + lax.broadcasted_iota(jnp.int32, (1, chunk), 1)
    seg_col = segment_of(col)
    seg_row = segment_of(row)
    first = segment_of(base - 1)
    last = segment_of(base + chunk - 1)
    same = seg_col == seg_row
    strict = (same & (col > row)).astype(f32)
    within = (same & (col >= row)).astype(f32)
    has_past = base > 0
    carry = ((seg_col == first) & has_past).astype(f32)
    close = (seg_col == last).astype(f32)
    keep = ((first == last) & has_past).astype(f32)
    return strict, within, carry, close, keep


def level_masks(chunk):
    row = lax.broadcasted_iota(jnp.int32, (chunk, chunk), 0)
    col = lax.broadcasted_iota(jnp.int32, (chunk, chunk), 1)
    masks = []
    width = 1
    while width < chunk:
        mask = (
            (row // (2 * width) == col // (2 * width))
            & ((row // width) % 2 == 1)
            & ((col // width) % 2 == 0)
        )
        masks.append(mask)
        width *= 2
    return masks, (row == col).astype(f32)


def conv_part(proj_ref, tap_ref, segment_of, base, part, width, chunk):
    taps = tap_ref.shape[0] // 3
    cols = pl.ds(part * width, width)
    main = proj_ref[pl.ds(base, chunk), cols]
    prev = proj_ref[pl.ds(pl.multiple_of(jnp.maximum(base - HALO, 0), HALO), HALO), cols]
    full = jnp.concatenate([prev, main], axis=0)
    col = base + lax.broadcasted_iota(jnp.int32, (chunk, 1), 0)
    seg = segment_of(col)
    total = main * tap_ref[part * taps : part * taps + 1, :]
    shifted = [main]
    for s in range(1, taps):
        valid = (segment_of(col - s) == seg) & (col >= s)
        moved = jnp.where(valid, pltpu.roll(full, s, 0)[HALO:], 0.0)
        shifted.append(moved)
        total = total + moved * tap_ref[part * taps + s : part * taps + s + 1, :]
    return total, shifted


def heads_of(x, heads):
    return [x[:, h * 128 : (h + 1) * 128] for h in range(heads)]


def unit_rows(a, scale):
    r = lax.rsqrt(jnp.sum(a * a, axis=-1, keepdims=True) + epsilon)
    return a * (r * scale)


def mixer_forward_kernel(exact, group, lengths_ref, proj_ref, beta_ref, tap_ref, gain_ref,
                         mixed_ref, heads_ref, fixed_ref, delta_ref, state_ref, inverse_ref,
                         query_s, key_s, value_s, score_s):
    rows_all = proj_ref.shape[0]
    width = proj_ref.shape[1] // 4
    heads = width // 128
    chunk = CHUNK
    count = rows_all // chunk
    segment_of, segments = segment_tools(lengths_ref)

    @pl.loop(0, count)
    def _(c):
        base = pl.multiple_of(c * chunk, chunk)
        rows = pl.ds(base, chunk)
        for part, target in enumerate((query_s, key_s, value_s)):
            pre, _ = conv_part(proj_ref, tap_ref, segment_of, base, part, width, chunk)
            act = pre * sigmoid(pre)
            if part == 2:
                target[rows, :] = act
            else:
                scale = 128 ** (-0.5) if part == 0 else 1.0
                for h, a in enumerate(heads_of(act, heads)):
                    target[rows, h * 128 : (h + 1) * 128] = unit_rows(a, scale)

    def beta_of(base, h):
        pos = base + lax.broadcasted_iota(jnp.int32, (chunk, 1), 0)
        live = (segment_of(pos) < segments).astype(f32)
        return sigmoid(beta_ref[pl.ds(base, chunk), h : h + 1]) * live

    masks, eye = level_masks(chunk)

    @pl.loop(0, count // group)
    def _(g):
        lowers, places = [], []
        for i in range(group):
            c = g * group + i
            base = pl.multiple_of(c * chunk, chunk)
            strict, within, _, _, _ = chunk_masks(segment_of, base, chunk)
            for h in range(heads):
                cols = slice(h * 128, (h + 1) * 128)
                k = key_s[pl.ds(base, chunk), cols]
                q = query_s[pl.ds(base, chunk), cols]
                lowers.append(product(k, k, 1, 1, exact) * strict * beta_of(base, h))
                score_s[c * heads + h] = (product(q, k, 1, 1, exact) * within).astype(score_s.dtype)
                places.append(c * heads + h)
        inverses = [eye - jnp.where(masks[0], lower, 0.0) for lower in lowers]
        for mask in masks[1:]:
            steps = [product(jnp.where(mask, lower, 0.0), x, 1, 0, True) for lower, x in zip(lowers, inverses)]
            inverses = [x - product(x, step, 1, 0, True) for x, step in zip(inverses, steps)]
        for place, x in zip(places, inverses):
            inverse_ref[place] = x

    def advance(c, states):
        base = pl.multiple_of(c * chunk, chunk)
        rows = pl.ds(base, chunk)
        _, _, carry, close, keep = chunk_masks(segment_of, base, chunk)
        new_states = []
        for h in range(heads):
            cols = slice(h * 128, (h + 1) * 128)
            state = states[h]
            k = key_s[rows, cols]
            q = query_s[rows, cols]
            delta = value_s[rows, cols] - carry * product(k, state, 1, 0, exact)
            fixed = product(inverse_ref[c * heads + h], beta_of(base, h) * delta, 1, 0, exact)
            out = carry * product(q, state, 1, 0, exact) + product(
                score_s[c * heads + h], fixed, 1, 0, exact)
            state_ref[c * heads + h] = state
            new_states.append(keep * state + product(k, close * fixed, 0, 0, exact))
            delta_ref[rows, cols] = delta
            fixed_ref[rows, cols] = fixed
            heads_ref[rows, cols] = out
            gate = proj_ref[rows, 3 * width + h * 128 : 3 * width + (h + 1) * 128]
            r = lax.rsqrt(jnp.mean(out * out, axis=-1, keepdims=True) + epsilon)
            mixed_ref[rows, cols] = (
                out * r * gain_ref[h : h + 1, :] * (gate * sigmoid(gate))
            ).astype(mixed_ref.dtype)
        return tuple(new_states)

    lax.fori_loop(0, count, advance, tuple(jnp.zeros((128, 128), f32) for _ in range(heads)))


def mixer_backward_kernel(exact, lengths_ref, proj_ref, beta_ref, tap_ref, gain_ref, grad_ref,
                          heads_ref, fixed_ref, delta_ref, state_ref, inverse_ref,
                          dproj_ref, dbeta_ref, dtap_ref, dgain_ref,
                          query_s, key_s, pre_s, dout_s, dpre_s):
    rows_all = proj_ref.shape[0]
    width = proj_ref.shape[1] // 4
    heads = width // 128
    chunk = CHUNK
    count = rows_all // chunk
    taps = tap_ref.shape[0] // 3
    segment_of, segments = segment_tools(lengths_ref)
    dgain_ref[...] = jnp.zeros_like(dgain_ref)
    dbeta_ref[...] = jnp.zeros_like(dbeta_ref)
    dtap_ref[...] = jnp.zeros_like(dtap_ref)

    @pl.loop(0, count)
    def _(c):
        base = pl.multiple_of(c * chunk, chunk)
        rows = pl.ds(base, chunk)
        for part in range(3):
            pre, _ = conv_part(proj_ref, tap_ref, segment_of, base, part, width, chunk)
            pre_s[rows, part * width : (part + 1) * width] = pre
            if part < 2:
                act = pre * sigmoid(pre)
                target = (query_s, key_s)[part]
                scale = 128 ** (-0.5) if part == 0 else 1.0
                for h, a in enumerate(heads_of(act, heads)):
                    target[rows, h * 128 : (h + 1) * 128] = unit_rows(a, scale)
        for h in range(heads):
            cols = slice(h * 128, (h + 1) * 128)
            gate_cols = slice(3 * width + h * 128, 3 * width + (h + 1) * 128)
            out = heads_ref[rows, cols]
            gate = proj_ref[rows, gate_cols]
            grad = grad_ref[rows, cols].astype(f32)
            gain = gain_ref[h : h + 1, :]
            sg = sigmoid(gate)
            silu = gate * sg
            r = lax.rsqrt(jnp.mean(out * out, axis=-1, keepdims=True) + epsilon)
            normed = out * r
            dgain_ref[h : h + 1, :] += jnp.sum(grad * normed * silu, axis=0, keepdims=True)
            dproj_ref[rows, gate_cols] = (
                grad * normed * gain * (sg * (1.0 + gate * (1.0 - sg)))
            ).astype(dproj_ref.dtype)
            weighted = grad * gain * silu
            dout_s[rows, cols] = r * weighted - out * (r * r * r) * jnp.mean(
                weighted * out, axis=-1, keepdims=True)

    dpre_s[rows_all : rows_all + HALO, :] = jnp.zeros((HALO, 3 * width), f32)

    def retreat(step, dstates):
        c = count - 1 - step
        base = pl.multiple_of(c * chunk, chunk)
        rows = pl.ds(base, chunk)
        strict, within, carry, close, keep = chunk_masks(segment_of, base, chunk)
        pos = base + lax.broadcasted_iota(jnp.int32, (chunk, 1), 0)
        live = (segment_of(pos) < segments).astype(f32)
        new_dstates = []
        for h in range(heads):
            cols = slice(h * 128, (h + 1) * 128)
            place = c * heads + h
            k = key_s[rows, cols]
            q = query_s[rows, cols]
            dout = dout_s[rows, cols]
            state = state_ref[place]
            inverse = inverse_ref[place]
            fixed = fixed_ref[rows, cols]
            delta = delta_ref[rows, cols]
            dstate = dstates[h]
            rate = sigmoid(beta_ref[rows, h : h + 1])
            beta = rate * live
            scores = product(q, k, 1, 1, exact) * within
            gram = product(k, k, 1, 1, exact) * strict
            dfixed = product(scores, dout, 0, 0, exact) + close * product(k, dstate, 1, 0, exact)
            drhs = product(inverse, dfixed, 0, 0, exact)
            ddelta = beta * drhs
            carried_dout = carry * dout
            carried_ddelta = carry * ddelta
            new_dstates.append(
                keep * dstate
                + product(q, carried_dout, 0, 0, exact)
                - product(k, carried_ddelta, 0, 0, exact)
            )
            dscores = product(dout, fixed, 1, 1, exact) * within
            dlower = -product(drhs, fixed, 1, 1, exact) * strict
            dgram = beta * dlower
            dq = product(carried_dout, state, 1, 1, exact) + product(dscores, k, 1, 0, exact)
            dk = (
                product(dscores, q, 0, 0, exact)
                + close * product(fixed, dstate, 1, 1, exact)
                - product(carried_ddelta, state, 1, 1, exact)
                + product(dgram, k, 1, 0, exact)
                + product(dgram, k, 0, 0, exact)
            )
            drate = live * (
                jnp.sum(drhs * delta, axis=-1, keepdims=True)
                + jnp.sum(dlower * gram, axis=-1, keepdims=True)
            )
            dbeta_ref[rows, h : h + 1] = (drate * rate * (1.0 - rate)).astype(dbeta_ref.dtype)
            for part, da in enumerate((dq, dk, ddelta)):
                part_cols = slice(part * width + h * 128, part * width + (h + 1) * 128)
                pre = pre_s[rows, part_cols]
                sg = sigmoid(pre)
                if part < 2:
                    a = pre * sg
                    scale = 128 ** (-0.5) if part == 0 else 1.0
                    r = lax.rsqrt(jnp.sum(a * a, axis=-1, keepdims=True) + epsilon)
                    da = (scale * r) * (da - a * (r * r) * jnp.sum(da * a, axis=-1, keepdims=True))
                dpre_s[rows, part_cols] = da * (sg * (1.0 + pre * (1.0 - sg)))
        return tuple(new_dstates)

    lax.fori_loop(0, count, retreat, tuple(jnp.zeros((128, 128), f32) for _ in range(heads)))

    @pl.loop(0, count)
    def _(c):
        base = pl.multiple_of(c * chunk, chunk)
        rows = pl.ds(base, chunk)
        col = base + lax.broadcasted_iota(jnp.int32, (chunk, 1), 0)
        seg = segment_of(col)
        for part in range(3):
            cols = slice(part * width, (part + 1) * width)
            _, shifted = conv_part(proj_ref, tap_ref, segment_of, base, part, width, chunk)
            full = dpre_s[pl.ds(base, chunk + HALO), cols]
            main = full[:chunk]
            total = main * tap_ref[part * taps : part * taps + 1, :]
            for s in range(taps):
                at = slice(part * taps + s, part * taps + s + 1)
                dtap_ref[at, :] += jnp.sum(main * shifted[s], axis=0, keepdims=True)
                if s > 0:
                    valid = (segment_of(col + s) == seg) & (col + s < rows_all)
                    moved = pltpu.roll(full, chunk + HALO - s, 0)[:chunk]
                    total = total + jnp.where(valid, moved, 0.0) * tap_ref[at, :]
            dproj_ref[rows, cols] = total.astype(dproj_ref.dtype)


def vmem():
    return pl.BlockSpec(memory_space=pltpu.VMEM)


def mixer_forward(lengths_row, projected, beta_logits, taps, gain, exact=True, group=4):
    rows, wide = projected.shape
    width = wide // 4
    heads = width // 128
    places = rows // CHUNK * heads
    group = min(group, rows // CHUNK)
    return pl.pallas_call(
        partial(mixer_forward_kernel, exact, group),
        out_shape=(
            jax.ShapeDtypeStruct((rows, width), bf16),
            jax.ShapeDtypeStruct((rows, width), f32),
            jax.ShapeDtypeStruct((rows, width), f32),
            jax.ShapeDtypeStruct((rows, width), f32),
            jax.ShapeDtypeStruct((places, 128, 128), f32),
            jax.ShapeDtypeStruct((places, CHUNK, CHUNK), f32),
        ),
        in_specs=[pl.BlockSpec(memory_space=pltpu.SMEM)] + [vmem()] * 4,
        out_specs=(vmem(),) * 6,
        scratch_shapes=[pltpu.VMEM((rows, width), f32)] * 3
        + [pltpu.VMEM((places, CHUNK, CHUNK), f32 if exact else bf16)],
        compiler_params=pltpu.CompilerParams(vmem_limit_bytes=48 * 2**20),
        cost_estimate=pl.CostEstimate(flops=10**10, bytes_accessed=10**7, transcendentals=10**6),
        name="mixer_forward",
    )(lengths_row, projected, beta_logits, taps, gain)


def mixer_backward(lengths_row, projected, beta_logits, taps, gain, grad, saved, exact=True):
    rows, wide = projected.shape
    width = wide // 4
    return pl.pallas_call(
        partial(mixer_backward_kernel, exact),
        out_shape=(
            jax.ShapeDtypeStruct((rows, wide), bf16),
            jax.ShapeDtypeStruct((rows, 128), bf16),
            jax.ShapeDtypeStruct(taps.shape, f32),
            jax.ShapeDtypeStruct(gain.shape, f32),
        ),
        in_specs=[pl.BlockSpec(memory_space=pltpu.SMEM)] + [vmem()] * 10,
        out_specs=(vmem(),) * 4,
        scratch_shapes=[pltpu.VMEM((rows, width), f32)] * 2
        + [pltpu.VMEM((rows, 3 * width), f32), pltpu.VMEM((rows, width), f32),
           pltpu.VMEM((rows + HALO, 3 * width), f32)],
        compiler_params=pltpu.CompilerParams(vmem_limit_bytes=56 * 2**20),
        cost_estimate=pl.CostEstimate(flops=10**10, bytes_accessed=10**7, transcendentals=10**6),
        name="mixer_backward",
    )(lengths_row, projected, beta_logits, taps, gain, grad, *saved)


NT = (((1,), (1,)), ((), ()))


def other(axis_name):
    return {axis_name: 1 - lax.axis_index(axis_name)}


def ffn_kernel(x_ref, w_ref, down_ref, c_refs, out_ref, ngrad_ref, wgrad_ref, down_out,
               xs, cs, ws, gu, inner_s, gate_s, up_s, acts_t, part, crecv, drecv, nrecv, stage,
               ag_send, ag_recv, pair_send, pair_recv, rs_send, rs_recv, c_sem, w_sem, g_sem, t_sem,
               down_right, down_left, down_recv, down_sem, sum_sems, keep_sem, out_sem, ready):
    half = xs.shape[1] // 2
    rows = 2 * half
    model = xs.shape[2]
    hidden = ws.shape[1]
    lines = w_ref.shape[0]
    parts, _, quarter, width = w_ref.shape[1:]
    tile_f = 256
    tile_d = min(512, model)
    tile_w = min(256, width)

    def remote(src, dst, send, recv, axis_name):
        return pltpu.make_async_remote_copy(
            src_ref=src, dst_ref=dst, send_sem=send, recv_sem=recv,
            device_id=other(axis_name), device_id_type=pl.DeviceIdType.MESH)

    def halves(ref, index, h):
        return ref.at[index, pl.ds(h * half, half)]

    o = lax.axis_index("z")

    def down_rows(z):
        return ws.at[2, pl.ds(pl.multiple_of(z * quarter, 16), quarter)]

    def down_pass(z, right):
        send = down_right if right else down_left
        return pltpu.make_async_remote_copy(
            src_ref=down_rows(z), dst_ref=down_rows(z), send_sem=send.at[z], recv_sem=down_recv.at[z],
            device_id={"z": o + 1 if right else o - 1}, device_id_type=pl.DeviceIdType.MESH)

    def down_forward(z, right):
        @pl.when(o < lines - 1 if right else o > 0)
        def _():
            down_pass(z, right).start()

    def down_step(far):
        for side in (-1, 1):
            z = o + side * far

            @pl.when((z >= 0) & (z < lines))
            def _():
                down_pass(z, side < 0).wait_recv()
                down_forward(z, side < 0)

    weight_copies, down_copies = [], []
    for r in range(parts):
        cols = pl.ds(r * width, width)
        for line in range(lines):
            weight_copies.append(pltpu.make_async_copy(
                w_ref.at[line, r], ws.at[pl.ds(0, 2), pl.ds(line * quarter, quarter), cols],
                w_sem.at[line, r]))
        down_copies.append(pltpu.make_async_copy(
            down_ref.at[r], down_rows(o).at[:, cols], down_sem.at[r]))
    for copy in down_copies:
        copy.start()
    for copy in weight_copies:
        copy.start()

    def pair_at(turn):
        return jnp.where(turn < 2, 3 - 2 * turn, 6 - 2 * turn)

    def slot_of(step):
        return (1 - lax.rem(step, 2)) * 4 + pair_at(step // 2)

    def c_copy(step, n):
        buffer = lax.rem(step, 2)
        return pltpu.make_async_copy(c_refs[n], cs.at[buffer], c_sem.at[buffer])

    def c_start(step):
        for n in range(8):
            @pl.when(slot_of(step) == n)
            def _():
                c_copy(step, n).start()

    c_copy(0, 7).start()
    line_barrier(lines, [other(name) for name in ("core", "x", "y")])

    own_pair = remote(x_ref, xs.at[4], ag_send.at[0], ag_recv.at[0], "core")
    own_x = [remote(x_ref.at[pl.ds(h * half, half)], halves(xs, 1, h), ag_send.at[1 + h], ag_recv.at[1 + h], "x") for h in range(2)]
    own_y = [remote(x_ref.at[pl.ds(h * half, half)], halves(xs, 2, h), ag_send.at[3 + h], ag_recv.at[3 + h], "y") for h in range(2)]
    relay_y = remote(halves(xs, 1, 0), halves(xs, 3, 0), ag_send.at[5], ag_recv.at[5], "y")
    relay_x = remote(halves(xs, 2, 1), halves(xs, 3, 1), ag_send.at[6], ag_recv.at[6], "x")
    pair_of = [None] + [remote(xs.at[j], xs.at[4 + j], ag_send.at[6 + j], ag_recv.at[6 + j], "core") for j in (1, 2, 3)]
    own_pair.start()
    own_x[0].start()
    own_y[1].start()
    own_x[1].start()
    own_y[0].start()
    for copy in down_copies:
        copy.wait()
    down_forward(o, True)
    down_forward(o, False)
    own_copy = pltpu.make_async_copy(x_ref, xs.at[0], t_sem.at[0, 0])
    own_copy.start()
    own_copy.wait()
    for copy in weight_copies:
        copy.wait()

    def part_send(turn):
        j = pair_at(turn)
        return remote(part.at[lax.rem(turn, 2)], crecv.at[j], pair_send.at[j], pair_recv.at[j], "core")

    x_sends = [[remote(crecv.at[1, a, pl.ds(h * half, half)], nrecv.at[0, a, pl.ds(h * half, half)],
                       rs_send.at[a * 2 + h], rs_recv.at[a * 2 + h], "x") for a in range(2)] for h in range(2)]
    y_sends = [[remote(crecv.at[2, a, pl.ds(h * half, half)], nrecv.at[1, a, pl.ds(h * half, half)],
                       rs_send.at[4 + a * 2 + h], rs_recv.at[4 + a * 2 + h], "y") for a in range(2)] for h in range(2)]
    d_sends = [[remote(crecv.at[3, a, pl.ds(h * half, half)], drecv.at[a, pl.ds(h * half, half)],
                       rs_send.at[8 + a * 2 + h], rs_recv.at[8 + a * 2 + h], ("x", "y")[h]) for a in range(2)] for h in range(2)]

    def place_of(step):
        return jnp.where(step >= 6, step - 4, lax.rem(step, 2))

    def gates(step):
        slot = slot_of(step)
        for start in range(0, hidden, tile_f):
            cols = slice(start, min(start + tile_f, hidden))
            for kind in range(2):
                gu[place_of(step), kind, :, cols] = lax.dot_general(
                    xs[slot], ws[kind, cols, :], NT, preferred_element_type=f32)

    @pl.loop(0, 4)
    def _(early):
        step = jnp.where(early < 2, 6 + early, 3 - early)

        @pl.when(early == 0)
        def _():
            own_pair.wait_recv()

        @pl.when(early == 2)
        def _():
            down_step(1)
            own_x[0].wait_recv()
            relay_y.start()
            own_y[1].wait_recv()
            relay_x.start()
            own_x[1].wait_recv()
            pair_of[1].start()
            own_y[0].wait_recv()
            pair_of[2].start()
            if lines > 2:
                down_step(2)
            relay_y.wait_recv()
            relay_x.wait_recv()
            pair_of[3].start()

        @pl.when(early == 3)
        def _():
            pair_of[3].wait_recv()
        gates(step)

    pair_of[1].wait_recv()
    pair_of[2].wait_recv()
    for far in range(3, lines):
        down_step(far)

    tiles = model // tile_w

    def c_tile(t):
        buffer = lax.rem(t, 2)
        cols = pl.ds(pl.multiple_of(t * tile_w, tile_w), tile_w)
        return [
            pltpu.make_async_copy(
                ref.at[:, cols], part.at[0, buffer, :, pl.ds(n * tile_w, tile_w)], t_sem.at[buffer, n])
            for n, ref in enumerate(c_refs)]

    @pl.loop(0, 8)
    def _(step):
        turn = step // 2
        j = pair_at(turn)
        slot = slot_of(step)
        pairing = lax.rem(step, 2) == 0

        @pl.when(step < 7)
        def _():
            c_start(step + 1)

        @pl.when((step >= 2) & (step < 6))
        def _():
            gates(step)

        c_copy(step, 0).wait()

        for start in range(0, hidden, tile_f):
            size = min(tile_f, hidden - start)
            cols = slice(start, start + size)
            gate = gu[place_of(step), 0, :, cols]
            up = gu[place_of(step), 1, :, cols]
            grad = lax.dot_general(cs[lax.rem(step, 2)], ws[2, cols, :], NT, preferred_element_type=f32)
            sg = sigmoid(gate)
            silu = gate * sg
            inner = (silu * up).astype(bf16)
            gate_grad = (grad * up * sg * (1.0 + gate * (1.0 - sg))).astype(bf16)
            up_grad = (grad * silu).astype(bf16)
            places = pl.ds(pl.multiple_of(slot * rows, rows), rows)
            for kind, (value, target) in enumerate(((gate_grad, gate_s), (up_grad, up_s), (inner, inner_s))):
                target[:, cols] = value
                acts_t[kind, cols, places] = value.T

        @pl.when(pairing & (step >= 4))
        def _():
            part_send(turn - 2).wait_send()

        place = jnp.where(pairing, lax.rem(turn, 2), 2)
        for start in range(0, model, tile_d):
            cols = slice(start, start + tile_d)
            part[place, 0, :, cols] = jnp.dot(
                inner_s[...], ws[2, :, cols], preferred_element_type=f32).astype(bf16)
            part[place, 1, :, cols] = (
                jnp.dot(gate_s[...], ws[0, :, cols], preferred_element_type=f32)
                + jnp.dot(up_s[...], ws[1, :, cols], preferred_element_type=f32)
            ).astype(bf16)

        @pl.when(pairing)
        def _():
            part_send(turn).start()

        @pl.when(jnp.logical_not(pairing))
        def _():
            part_send(turn).wait_recv()
            for a in range(2):
                for start in range(0, model, tile_d):
                    cols = slice(start, start + tile_d)
                    crecv[j, a, :, cols] = (
                        crecv[j, a, :, cols].astype(f32) + part[2, a, :, cols].astype(f32)
                    ).astype(bf16)

        @pl.when(step == 1)
        def _():
            for h in range(2):
                for copy in d_sends[h]:
                    copy.start()

        @pl.when(step == 3)
        def _():
            for copy in x_sends[0]:
                copy.start()

        @pl.when(step == 5)
        def _():
            for copy in y_sends[1]:
                copy.start()

        @pl.when(step == 6)
        def _():
            part_send(2).wait_send()
            for t in range(2):
                for copy in c_tile(t):
                    copy.start()

    def grad_copy(kind, t, line):
        return pltpu.make_async_copy(
            stage.at[lax.rem(t, 2), pl.ds(line * quarter, quarter)],
            wgrad_ref.at[line, t * tile_w // width, kind, :,
                         pl.ds(pl.multiple_of(lax.rem(t * tile_w, width), tile_w), tile_w)],
            g_sem.at[lax.rem(t, 2), line])

    def weight_grads(kind):
        @pl.loop(0, tiles)
        def _(t):
            if kind == 2:
                for copy in c_tile(t):
                    copy.wait()
                right = jnp.concatenate(
                    [part[0, lax.rem(t, 2), :, n * tile_w : (n + 1) * tile_w] for n in range(8)])
            else:
                right = xs[:, :, pl.ds(pl.multiple_of(t * tile_w, tile_w), tile_w)].reshape(8 * rows, tile_w)

            if kind < 2:
                @pl.when(t >= 2)
                def _():
                    for line in range(lines):
                        grad_copy(kind, t - 2, line).wait()

            value = jnp.dot(acts_t[kind], right, preferred_element_type=f32).astype(bf16)
            if kind == 2:
                @pl.when(t + 2 < tiles)
                def _():
                    for copy in c_tile(t + 2):
                        copy.start()
            if kind < 2:
                stage[lax.rem(t, 2)] = value
                for line in range(lines):
                    grad_copy(kind, t, line).start()
            else:
                ws[0, :, pl.ds(pl.multiple_of(t * tile_w, tile_w), tile_w)] = value

        if kind == 2:
            return
        for t in range(max(tiles - 2, 0), tiles):
            for line in range(lines):
                grad_copy(kind, t, line).wait()

    @pl.loop(0, lines)
    def _(z):
        @pl.when((o < lines - 1) & (z <= o))
        def _():
            down_pass(z, True).wait_send()

        @pl.when((o > 0) & (z >= o))
        def _():
            down_pass(z, False).wait_send()

    mesh_id = pl.DeviceIdType.MESH

    @pl.when(o > 0)
    def _():
        pl.semaphore_signal(ready, inc=1, device_id={"z": o - 1}, device_id_type=mesh_id)

    @pl.when(o < lines - 1)
    def _():
        pl.semaphore_signal(ready, inc=1, device_id={"z": o + 1}, device_id_type=mesh_id)

    def rows_of(n, z):
        return ws.at[n, pl.ds(pl.multiple_of(z * quarter, 16), quarter)]

    def sum_pass(z, right):
        side = 0 if right else 2
        return pltpu.make_async_remote_copy(
            src_ref=rows_of(0, z), dst_ref=rows_of(1 if right else 2, z),
            send_sem=sum_sems.at[side, z], recv_sem=sum_sems.at[side + 1, z],
            device_id={"z": o + 1 if right else o - 1}, device_id_type=mesh_id)

    def sum_add(z, n):
        at = pl.ds(pl.multiple_of(z * quarter, 16), quarter)
        for start in range(0, model, tile_d):
            cols = slice(start, start + tile_d)
            ws[0, at, cols] = (ws[0, at, cols].astype(f32) + ws[n, at, cols].astype(f32)).astype(bf16)

    def sum_tick(k):
        z_right = lines - 1 - k + o

        @pl.when(o <= k)
        def _():
            @pl.when(o > 0)
            def _():
                sum_pass(z_right, True).wait_recv()
                sum_add(z_right, 1)

            @pl.when(o < k)
            def _():
                sum_pass(z_right + 1, True).wait_send()
            sum_pass(z_right, True).start()

        back = lines - 1 - o
        z_left = k - back

        @pl.when(back <= k)
        def _():
            @pl.when(back > 0)
            def _():
                sum_pass(z_left, False).wait_recv()
                sum_add(z_left, 2)

            @pl.when(back < k)
            def _():
                sum_pass(z_left - 1, False).wait_send()
            sum_pass(z_left, False).start()

    weight_grads(2)
    pl.semaphore_wait(ready, (o > 0).astype(jnp.int32) + (o < lines - 1).astype(jnp.int32))
    sum_tick(0)
    for h in range(2):
        j = 2 - h
        for a in range(2):
            d_sends[h][a].wait_recv()
            at = pl.ds(h * half, half)
            crecv[j, a, at, :] = (
                crecv[j, a, at, :].astype(f32) + drecv[a, at, :].astype(f32)).astype(bf16)
        for copy in (y_sends, x_sends)[h][h]:
            copy.start()
    weight_grads(0)
    if lines > 2:
        sum_tick(1)
    weight_grads(1)
    for k in range(2, lines - 1):
        sum_tick(k)
    out_copies = []
    for a, target in enumerate((out_ref, ngrad_ref)):
        for h in range(2):
            x_sends[h][a].wait_recv()
            y_sends[h][a].wait_recv()
        for n in range(model // tile_d):
            cols = slice(n * tile_d, (n + 1) * tile_d)
            gu[n, a, :, :tile_d] = (
                crecv[0, a, :, cols].astype(f32)
                + nrecv[0, a, :, cols].astype(f32)
                + nrecv[1, a, :, cols].astype(f32)
            )
            copy = pltpu.make_async_copy(
                gu.at[n, a, :, pl.ds(0, tile_d)], target.at[:, pl.ds(n * tile_d, tile_d)],
                out_sem.at[n, a])
            copy.start()
            out_copies.append(copy)
    for copy in out_copies:
        copy.wait()
    own_pair.wait_send()
    for h in range(2):
        own_x[h].wait_send()
        own_y[h].wait_send()
        for a in range(2):
            x_sends[h][a].wait_send()
            y_sends[h][a].wait_send()
            d_sends[h][a].wait_send()
    relay_x.wait_send()
    relay_y.wait_send()
    for j in (1, 2, 3):
        pair_of[j].wait_send()
    part_send(3).wait_send()

    @pl.when(o > 0)
    def _():
        sum_pass(o, True).wait_recv()
        sum_add(o, 1)

    @pl.when(o < lines - 1)
    def _():
        sum_pass(o, False).wait_recv()
        sum_add(o, 2)

    keeps = [
        pltpu.make_async_copy(
            rows_of(0, o).at[:, pl.ds(q * width, width)], down_out.at[q], keep_sem.at[q])
        for q in range(parts)
    ]
    for copy in keeps:
        copy.start()

    @pl.when(o < lines - 1)
    def _():
        sum_pass(o + 1, True).wait_send()

    @pl.when(o > 0)
    def _():
        sum_pass(o - 1, False).wait_send()
    for copy in keeps:
        copy.wait()


def ffn_call_kernel(x_ref, w_ref, down_ref, *refs):
    ffn_kernel(x_ref, w_ref, down_ref, refs[:8], *refs[8:])


def ffn_plane(x_own, weights, down_own, c_rows):
    rows, model = x_own.shape
    lines, parts, _, quarter, width = weights.shape
    hidden = lines * quarter
    tile_w = min(256, width)
    sems = pltpu.SemaphoreType.DMA
    anywhere = pl.BlockSpec(memory_space=pl.ANY)
    return pl.pallas_call(
        ffn_call_kernel,
        out_shape=(
            jax.ShapeDtypeStruct((rows, model), f32),
            jax.ShapeDtypeStruct((rows, model), f32),
            jax.ShapeDtypeStruct(weights.shape, bf16),
            jax.ShapeDtypeStruct((parts, quarter, width), bf16),
        ),
        in_specs=[anywhere] * 11,
        out_specs=(anywhere,) * 4,
        scratch_shapes=[
            pltpu.VMEM((8, rows, model), bf16),
            pltpu.VMEM((2, rows, model), bf16),
            pltpu.VMEM((3, hidden, model), bf16),
            pltpu.VMEM((4, 2, rows, max(hidden, min(512, model))), f32),
            pltpu.VMEM((rows, hidden), bf16),
            pltpu.VMEM((rows, hidden), bf16),
            pltpu.VMEM((rows, hidden), bf16),
            pltpu.VMEM((3, hidden, 8 * rows), bf16),
            pltpu.VMEM((3, 2, rows, model), bf16),
            pltpu.VMEM((4, 2, rows, model), bf16),
            pltpu.VMEM((2, rows, model), bf16),
            pltpu.VMEM((2, 2, rows, model), bf16),
            pltpu.VMEM((2, hidden, tile_w), bf16),
            sems((10,)), sems((10,)), sems((4,)), sems((4,)), sems((12,)), sems((12,)),
            sems((2,)), sems((lines, parts)), sems((2, lines)), sems((2, 8)),
            sems((lines,)), sems((lines,)), sems((lines,)), sems((parts,)),
            sems((4, lines)), sems((parts,)), sems((4, 2)), pltpu.SemaphoreType.REGULAR,
        ],
        compiler_params=pltpu.CompilerParams(
            collective_id=2, has_side_effects=True, vmem_limit_bytes=60 * 2**20),
        cost_estimate=pl.CostEstimate(flops=8 * 10**10, bytes_accessed=4 * 10**7, transcendentals=10**6),
        name="ffn_plane",
    )(x_own, weights, down_own, *c_rows)


def line_barrier(lines, others):
    o = lax.axis_index("z")
    barrier = pltpu.get_barrier_semaphore()
    mesh_id = pl.DeviceIdType.MESH

    @pl.when(o > 0)
    def _():
        pl.semaphore_signal(barrier, inc=1, device_id={"z": o - 1}, device_id_type=mesh_id)

    @pl.when(o < lines - 1)
    def _():
        pl.semaphore_signal(barrier, inc=1, device_id={"z": o + 1}, device_id_type=mesh_id)

    for target in others:
        pl.semaphore_signal(barrier, inc=1, device_id=target, device_id_type=mesh_id)
    peers = len(others) + (o > 0).astype(jnp.int32) + (o < lines - 1).astype(jnp.int32)
    pl.semaphore_wait(barrier, peers)


def line_copy(src, dst, send, recv, target):
    return pltpu.make_async_remote_copy(
        src_ref=src, dst_ref=dst, send_sem=send, recv_sem=recv,
        device_id=target, device_id_type=pl.DeviceIdType.MESH)


def pair_peers():
    x, core = lax.axis_index("x"), lax.axis_index("core")
    peers = [
        (x * 2 + 1 - core, {"core": 1 - core}),
        ((1 - x) * 2 + core, {"x": 1 - x}),
        ((1 - x) * 2 + 1 - core, {"x": 1 - x, "core": 1 - core}),
    ]
    return x * 2 + core, peers


class Swap:
    def __init__(self, pairs, send, recv, own):
        me, peers = pair_peers()
        self.own = [
            pltpu.make_async_copy(source.at[me], target(me), own.at[n])
            for n, (source, target) in enumerate(pairs)]
        self.away = [
            line_copy(source.at[place], target(me), send.at[n, d], recv.at[n, d], device)
            for n, (source, target) in enumerate(pairs) for d, (place, device) in enumerate(peers)]

    def start(self):
        for copy in self.away + self.own:
            copy.start()

    def wait(self):
        for copy in self.own:
            copy.wait()
        for copy in self.away:
            copy.wait_recv()
            copy.wait_send()


def gather_kernel(x_ref, o_ref, f_refs, w_refs, wb_ref, rows_ref, outs_ref, proj_refs, beta_ref,
                  pair_ref, down_ref,
                  xs, parts, stage, beta_stage, right_send, left_send, line_recv, pair_send, pair_recv,
                  part_right, part_left, part_recv, own_sem, row_sem, outs_sem, out_sem, beta_sem,
                  swap_send, swap_recv, swap_own):
    lines = xs.shape[0] // 2
    batches, rows, model = x_ref.shape
    o = lax.axis_index("z")
    i = lax.axis_index("y")
    line_barrier(lines, [other("y")] + [device for _, device in pair_peers()[1]])
    swap = Swap(
        [(f_refs[0], lambda place: pair_ref.at[place, 0]),
         (f_refs[1], lambda place: pair_ref.at[place, 1]),
         (f_refs[2], lambda place: down_ref.at[place])],
        swap_send, swap_recv, swap_own)

    def right(z, m):
        ref = xs.at[z * 2 + i, m]
        return line_copy(ref, ref, right_send.at[z, m], line_recv.at[z, m], {"z": o + 1})

    def left(z, m):
        ref = xs.at[z * 2 + i, m]
        return line_copy(ref, ref, left_send.at[z, m], line_recv.at[z, m], {"z": o - 1})

    def across(z, m):
        ref = xs.at[z * 2 + i, m]
        return line_copy(ref, ref, pair_send.at[z, m], pair_recv.at[z, m], other("y"))

    own = [
        pltpu.make_async_copy(x_ref, xs.at[o * 2 + i], own_sem.at[0]),
        pltpu.make_async_copy(o_ref, parts.at[o], own_sem.at[1]),
    ]

    def pass_part(z):
        ref = parts.at[z]
        return (line_copy(ref, ref, part_right.at[z], part_recv.at[z], {"z": o + 1}),
                line_copy(ref, ref, part_left.at[z], part_recv.at[z], {"z": o - 1}))

    for copy in own:
        copy.start()
    for copy in own:
        copy.wait()

    def outs(turn, slot):
        buffer = lax.rem(turn, 2)
        return [
            copy for m in range(batches) for copy in (
                pltpu.make_async_copy(stage.at[buffer, m], proj_refs[m].at[slot], out_sem.at[buffer, m]),
                pltpu.make_async_copy(beta_stage.at[buffer, m], beta_ref.at[m, slot], beta_sem.at[buffer, m]))
        ]

    def keep(slot, m):
        return pltpu.make_async_copy(xs.at[slot, m], rows_ref.at[m, slot], row_sem.at[slot, m])

    def keep_outs(z):
        return pltpu.make_async_copy(parts.at[z], outs_ref.at[z], outs_sem.at[z])

    def project(turn, slot):
        @pl.when(turn >= 2)
        def _():
            for copy in outs(turn, slot):
                copy.wait()
        for m in range(batches):
            keep(slot, m).start()
        x = xs[slot].reshape(batches * rows, model)
        buffer = lax.rem(turn, 2)
        width = w_refs[0].shape[1]
        for n, w_ref in enumerate(w_refs):
            stage[buffer, :, :, n * width : (n + 1) * width] = jnp.dot(
                x, w_ref[...], preferred_element_type=f32).reshape(batches, rows, width)
        beta_stage[buffer] = jnp.dot(
            x, wb_ref[...], preferred_element_type=f32).reshape(batches, rows, 128)
        for copy in outs(turn, slot):
            copy.start()

    def in_line(index):
        far = (index + 1) // 2
        side = 1 - 2 * lax.rem(index, 2)
        z = o + side * far
        return far, z, (z >= 0) & (z < lines)

    def first(index, turn):
        far, z, valid = in_line(index)

        @pl.when(valid)
        def _():
            for m in range(batches):
                @pl.when(far > 0)
                def _():
                    left(z, m).wait_recv()

                @pl.when((o < lines - 1) & (z <= o))
                def _():
                    right(z, m).start()

                @pl.when((o > 0) & (z >= o))
                def _():
                    left(z, m).start()

                across(z, m).start()
            project(turn, z * 2 + i)

        return turn + valid.astype(jnp.int32)

    swap.start()
    turn = lax.fori_loop(0, 2 * lines - 1, first, jnp.int32(0))

    def second(index, turn):
        far, z, valid = in_line(index)

        @pl.when(valid)
        def _():
            to_right, to_left = pass_part(z)

            @pl.when(far > 0)
            def _():
                to_left.wait_recv()

            @pl.when((o < lines - 1) & (z <= o))
            def _():
                to_right.start()

            @pl.when((o > 0) & (z >= o))
            def _():
                to_left.start()

            keep_outs(z).start()
            for m in range(batches):
                across(z, m).wait_recv()
            project(turn, z * 2 + 1 - i)

        return turn + valid.astype(jnp.int32)

    lax.fori_loop(0, 2 * lines - 1, second, turn)
    for turn in range(2 * lines - 2, 2 * lines):
        for copy in outs(turn, 0):
            copy.wait()

    @pl.loop(0, lines)
    def _(z):
        keep_outs(z).wait()

        @pl.when((o < lines - 1) & (z <= o))
        def _():
            pass_part(z)[0].wait_send()
            for m in range(batches):
                right(z, m).wait_send()

        @pl.when((o > 0) & (z >= o))
        def _():
            pass_part(z)[1].wait_send()
            for m in range(batches):
                left(z, m).wait_send()

        for m in range(batches):

            across(z, m).wait_send()
            for y in range(2):
                keep(z * 2 + y, m).wait()

    swap.wait()


def gather_call_kernel(x_ref, o_ref, *refs):
    gather_kernel(x_ref, o_ref, refs[:3], refs[3:7], refs[7], refs[8], refs[9], refs[10:12], *refs[12:])


def gather_project(x, w_out_part, ffn_parts, w_inner, w_beta):
    batches, rows, model = x.shape
    more = w_out_part.shape[1]
    lines = lax.axis_size("z")
    width = sum(w.shape[1] for w in w_inner)
    slots = 2 * lines
    sems = pltpu.SemaphoreType.DMA
    anywhere = pl.BlockSpec(memory_space=pl.ANY)
    pair = sems((lines, batches))
    ranks, quarter, share = ffn_parts[0].shape
    gathered, outs, *projected, beta, pair_parts, down_part = pl.pallas_call(
        gather_call_kernel,
        out_shape=(
            jax.ShapeDtypeStruct((batches, slots, rows, model), bf16),
            jax.ShapeDtypeStruct((lines, batches, more, model), bf16),
            *[jax.ShapeDtypeStruct((slots, rows, width), f32)] * batches,
            jax.ShapeDtypeStruct((batches, slots, rows, 128), f32),
            jax.ShapeDtypeStruct((ranks, 2, quarter, share), bf16),
            jax.ShapeDtypeStruct((ranks, quarter, share), bf16),
        ),
        in_specs=[anywhere] * 5 + [vmem()] * 5,
        out_specs=(anywhere,) * (5 + batches),
        scratch_shapes=[
            pltpu.VMEM((slots, batches, rows, model), bf16),
            pltpu.VMEM((lines, batches, more, model), bf16),
            pltpu.VMEM((2, batches, rows, width), f32),
            pltpu.VMEM((2, batches, rows, 128), f32),
            pair, pair, pair, pair, pair, sems((lines,)), sems((lines,)), sems((lines,)),
            sems((2,)), sems((slots, batches)), sems((lines,)), sems((2, batches)), sems((2, batches)),
            sems((3, 3)), sems((3, 3)), sems((3,)),
        ],
        compiler_params=pltpu.CompilerParams(
            collective_id=1, has_side_effects=True, vmem_limit_bytes=40 * 2**20),
        cost_estimate=pl.CostEstimate(flops=10**11, bytes_accessed=4 * 10**7, transcendentals=0),
        name="gather_project",
    )(x, w_out_part, *ffn_parts, *w_inner, w_beta)
    total = slots * rows
    return (gathered.reshape(batches, total, model), outs,
            [wide.reshape(total, width) for wide in projected],
            beta.reshape(batches, total, 128), pair_parts, down_part)


def scatter_kernel(w_refs, g_ref, gb_ref, o_ref, inner_ref, wb_ref, small_ref, gains_ref, pair_ref, down_ref,
                   out_ref, small_out, outs_ref, inner_out, pair_out, down_out,
                   gs, bs, ysend, yrecv, from_left, from_right, part_sum, part_left, part_right, outs_s, inner_s, inner_r, small_s, small_r, gains_r,
                   pair_send, pair_recv, right_send, left_send, right_recv, left_recv, g_sem,
                   sum_send, sum_recv, outs_send, outs_recv, gain_send, gain_recv, part_sems, swap_send, swap_recv, swap_own, sum_sem):
    batches, rows, width = gs.shape
    lines = yrecv.shape[0]
    model = yrecv.shape[3]
    o = lax.axis_index("z")
    i = lax.axis_index("y")
    core = lax.axis_index("core")
    me = lax.axis_index("x") * 2 + core
    tile = min(512, model)
    diagonal = {"x": 1 - lax.axis_index("x"), "core": 1 - core}
    slots = 2 * lines
    mine = o * 2 + i
    peers = []
    for d in range(1, slots):
        place = lax.rem(mine + d, slots)
        peers.append((place, {"z": place // 2, "y": lax.rem(place, 2)}))
    barrier = pltpu.get_barrier_semaphore()
    greeted = [other("core"), other("x"), diagonal] + [device for _, device in peers]
    for device in greeted:
        pl.semaphore_signal(barrier, inc=1, device_id=device, device_id_type=pl.DeviceIdType.MESH)
    pl.semaphore_wait(barrier, len(greeted))
    gain_copies = [
        line_copy(gains_ref.at[place], gains_r.at[mine], gain_send.at[d], gain_recv.at[d], device)
        for d, (place, device) in enumerate(peers)
    ]
    for copy in gain_copies:
        copy.start()

    inner_pair = line_copy(inner_ref.at[1 - core], inner_r.at[0], sum_send.at[0], sum_recv.at[0], other("core"))
    inner_across = line_copy(inner_s, inner_r.at[1], sum_send.at[1], sum_recv.at[1], other("x"))
    inner_back = line_copy(inner_s, inner_out.at[core], sum_send.at[2], sum_recv.at[2], other("core"))
    small_pair = line_copy(small_s.at[0], small_r.at[0], sum_send.at[3], sum_recv.at[3], other("core"))
    small_across = line_copy(small_s.at[1], small_r.at[1], sum_send.at[4], sum_recv.at[4], other("x"))
    inner_own = pltpu.make_async_copy(inner_ref.at[core], inner_s, sum_sem.at[0])
    inner_keep = pltpu.make_async_copy(inner_s, inner_out.at[core], sum_sem.at[1])
    outs_keep = pltpu.make_async_copy(outs_s, outs_ref.at[me], sum_sem.at[2])
    outs_away = [
        line_copy(outs_s, outs_ref.at[me], outs_send.at[n], outs_recv.at[n], target)
        for n, target in enumerate((other("core"), other("x"), diagonal))
    ]
    swap = Swap(
        [(pair_ref, lambda place: pair_out.at[place]), (down_ref, lambda place: down_out.at[place])],
        swap_send, swap_recv, swap_own)
    swap.start()
    inner_pair.start()
    inner_own.start()

    def add_into(target, other_ref):
        height = target.shape[0]
        step = next(size for size in range(min(128, height), 0, -16) if height % size == 0)

        @pl.loop(0, height // step)
        def _(n):
            at = pl.ds(pl.multiple_of(n * step, step), step)
            target[at, :] = (target[at, :].astype(f32) + other_ref[at, :].astype(f32)).astype(target.dtype)

    def target(index):
        far = lines - 1 - index // 2
        side = 1 - 2 * lax.rem(index, 2)
        z = o + side * far
        return far, z, (z >= 0) & (z < lines) & ((far > 0) | (side > 0))

    def load(z, y):
        slot = z * 2 + y
        return (pltpu.make_async_copy(g_ref.at[:, slot], gs, g_sem.at[0]),
                pltpu.make_async_copy(gb_ref.at[:, slot], bs, g_sem.at[1]))

    def partial_rows(z, y, store):
        for copy in load(z, y):
            copy.start()
        for copy in load(z, y):
            copy.wait()
        for m in range(batches):
            g = gs[m]
            b = bs[m]
            for start in range(0, model, tile):
                cols = slice(start, start + tile)
                value = lax.dot_general(b, wb_ref[cols, :], NT, preferred_element_type=f32)
                for n, w_ref in enumerate(w_refs):
                    part = g[:, n * w_ref.shape[1] : (n + 1) * w_ref.shape[1]]
                    value = value + lax.dot_general(part, w_ref[cols, :], NT, preferred_element_type=f32)
                store(m, cols, value)

    def across(z, m):
        return line_copy(ysend.at[z, m], yrecv.at[z, m], pair_send.at[z, m], pair_recv.at[z, m], other("y"))

    def right(z, m):
        return line_copy(yrecv.at[z, m], from_left.at[z, m], right_send.at[z, m], right_recv.at[z, m], {"z": o + 1})

    def left(z, m):
        return line_copy(yrecv.at[z, m], from_right.at[z, m], left_send.at[z, m], left_recv.at[z, m], {"z": o - 1})

    def across_partial(z):
        def store(m, cols, value):
            ysend[z, m, :, cols] = value.astype(bf16)
        partial_rows(z, 1 - i, store)

    def pass_part(z):
        return (line_copy(part_sum.at[z], part_left.at[z], part_sems.at[0, z], part_sems.at[1, z], {"z": o + 1}),
                line_copy(part_sum.at[z], part_right.at[z], part_sems.at[2, z], part_sems.at[3, z], {"z": o - 1}))

    def part_round():
        @pl.loop(0, 2 * lines)
        def _(index):
            far, z, valid = target(index)

            @pl.when(valid & (far > 0))
            def _():
                to_right, to_left = pass_part(z)

                @pl.when((z > o) & (o > 0))
                def _():
                    to_right.wait_recv()
                    add_into(part_sum.at[z], part_left.at[z])

                @pl.when((z < o) & (o < lines - 1))
                def _():
                    to_left.wait_recv()
                    add_into(part_sum.at[z], part_right.at[z])

                @pl.when(z > o)
                def _():
                    to_right.start()

                @pl.when(z < o)
                def _():
                    to_left.start()

        to_right, to_left = pass_part(o)
        outs_s[...] = part_sum[o]

        @pl.when(o > 0)
        def _():
            to_right.wait_recv()
            add_into(outs_s, part_left.at[o])

        @pl.when(o < lines - 1)
        def _():
            to_left.wait_recv()
            add_into(outs_s, part_right.at[o])
        outs_keep.start()
        for copy in outs_away:
            copy.start()

    def side_work():
        for z in range(lines):
            part_sum[z] = o_ref[z]
        part_round()
        inner_own.wait()
        inner_pair.wait_recv()
        add_into(inner_s, inner_r.at[0])
        inner_across.start()
        gains_r[mine] = gains_ref[mine]
        for copy in gain_copies:
            copy.wait_recv()
        tail = small_ref.shape[0]
        small_s[0, :tail] = small_ref[...]
        small_s[0, tail:] = jnp.sum(gains_r[...], axis=0)
        small_pair.start()

    def turn(index, before):
        far, z, valid = target(index)
        last = index == 2 * lines
        valid = valid & (index < 2 * lines)
        ready = (valid | last) & (before >= 0)

        @pl.when(valid)
        def _():
            across_partial(z)

        @pl.when(ready)
        def _():
            for m in range(batches):
                across(before, m).wait_recv()

        @pl.when(valid)
        def _():
            for m in range(batches):
                across(z, m).start()

        @pl.when(valid & (before < 0))
        def _():
            side_work()

        @pl.when(ready)
        def _():
            z = before

            def store(m, cols, value):
                yrecv[z, m, :, cols] = (yrecv[z, m, :, cols].astype(f32) + value).astype(bf16)
            partial_rows(z, i, store)
            for m in range(batches):
                @pl.when((z > o) & (o > 0))
                def _():
                    right(z, m).wait_recv()
                    add_into(yrecv.at[z, m], from_left.at[z, m])

                @pl.when(z > o)
                def _():
                    right(z, m).start()

                @pl.when((z < o) & (o < lines - 1))
                def _():
                    left(z, m).wait_recv()
                    add_into(yrecv.at[z, m], from_right.at[z, m])

                @pl.when(z < o)
                def _():
                    left(z, m).start()

        return jnp.where(valid, z, before)

    lax.fori_loop(0, 2 * lines + 1, turn, jnp.int32(-1))

    inner_across.wait_recv()
    inner_across.wait_send()
    add_into(inner_s, inner_r.at[1])
    inner_back.start()
    inner_keep.start()
    small_pair.wait_recv()
    small_s[1] = small_s[0] + small_r[0]
    small_across.start()

    for m in range(batches):
        out_ref[m] = yrecv[o, m].astype(f32)

        @pl.when(o > 0)
        def _():
            right(o, m).wait_recv()
            out_ref[m] += from_left[o, m].astype(f32)

        @pl.when(o < lines - 1)
        def _():
            left(o, m).wait_recv()
            out_ref[m] += from_right[o, m].astype(f32)

    @pl.loop(0, lines)
    def _(z):
        for m in range(batches):
            across(z, m).wait_send()

            @pl.when(z > o)
            def _():
                right(z, m).wait_send()

            @pl.when(z < o)
            def _():
                left(z, m).wait_send()

        @pl.when(z > o)
        def _():
            pass_part(z)[0].wait_send()

        @pl.when(z < o)
        def _():
            pass_part(z)[1].wait_send()

    small_across.wait_recv()
    small_out[...] = small_s[1] + small_r[1]
    for copy in gain_copies:
        copy.wait_send()
    inner_pair.wait_send()
    small_pair.wait_send()
    small_across.wait_send()
    inner_back.wait_recv()
    inner_back.wait_send()
    inner_keep.wait()
    outs_keep.wait()
    swap.wait()
    for copy in outs_away:
        copy.wait_recv()
        copy.wait_send()


def scatter_call_kernel(*refs):
    scatter_kernel(refs[:4], *refs[4:])


def scatter_rows(grads, beta_grads, out_grads, inner_grads, w_inner, w_beta, small, gains,
                 pair_grads, down_grads):
    batches, total, width = grads.shape
    model = w_inner[0].shape[0]
    lines = lax.axis_size("z")
    slots = 2 * lines
    rows = total // slots
    more = out_grads.shape[1]
    sems = pltpu.SemaphoreType.DMA
    anywhere = pl.BlockSpec(memory_space=pl.ANY)
    slab = pltpu.VMEM((lines, batches, rows, model), bf16)
    part = pltpu.VMEM((lines, more, model), bf16)
    half = inner_grads.shape[1:]
    flat = (small.shape[0] + gains.shape[1], 128)
    return pl.pallas_call(
        scatter_call_kernel,
        out_shape=(
            jax.ShapeDtypeStruct((batches, rows, model), f32),
            jax.ShapeDtypeStruct(flat, f32),
            jax.ShapeDtypeStruct((4, more, model), bf16),
            jax.ShapeDtypeStruct(inner_grads.shape, bf16),
            jax.ShapeDtypeStruct(pair_grads.shape, bf16),
            jax.ShapeDtypeStruct(down_grads.shape, bf16),
        ),
        in_specs=[vmem()] * 4 + [anywhere, anywhere, vmem(), anywhere, vmem(), vmem(), vmem(), anywhere, anywhere],
        out_specs=(vmem(), vmem()) + (anywhere,) * 4,
        scratch_shapes=[
            pltpu.VMEM((batches, rows, width), bf16),
            pltpu.VMEM((batches, rows, 128), bf16),
            slab, slab, slab, slab, part, part, part,
            pltpu.VMEM((more, model), bf16),
            pltpu.VMEM(half, bf16),
            pltpu.VMEM((2, *half), bf16),
            pltpu.VMEM((2, *flat), f32),
            pltpu.VMEM((2, *flat), f32),
            pltpu.VMEM(gains.shape, f32),
            sems((lines, batches)), sems((lines, batches)), sems((lines, batches)),
            sems((lines, batches)), sems((lines, batches)), sems((lines, batches)),
            sems((2,)), sems((5,)), sems((5,)), sems((3,)), sems((3,)), sems((slots,)), sems((slots,)), sems((4, lines)),
            sems((2, 3)), sems((2, 3)), sems((2,)), sems((3,)),
        ],
        compiler_params=pltpu.CompilerParams(
            collective_id=3, has_side_effects=True, vmem_limit_bytes=58 * 2**20),
        cost_estimate=pl.CostEstimate(flops=7 * 10**10, bytes_accessed=4 * 10**7, transcendentals=0),
        name="scatter_rows",
    )(*w_inner, grads.reshape(batches, slots, rows, width),
      beta_grads.reshape(batches, slots, rows, 128), out_grads, inner_grads, w_beta, small, gains,
      pair_grads, down_grads)


def tensor_peers(slots):
    mine = lax.axis_index("z") * 2 + lax.axis_index("y")
    places = [lax.rem(mine + d, slots) for d in range(1, slots)]
    return mine, [(place, {"z": place // 2, "y": lax.rem(place, 2)}) for place in places]


def greet(devices):
    barrier = pltpu.get_barrier_semaphore()
    for device in devices:
        pl.semaphore_signal(barrier, inc=1, device_id=device, device_id_type=pl.DeviceIdType.MESH)
    pl.semaphore_wait(barrier, len(devices))


def attend_kernel(x_ref, low_first, low_second, gain_ref, *refs):
    pieces, refs = refs[:8], refs[8:]
    hidden_ref, normed_ref, w_ref, heads_ref, ws, heads, send, recv, sem, own_sem = refs
    slots = heads.shape[1]
    mine, peers = tensor_peers(slots)
    greet([device for _, device in peers])
    lows = (low_first, low_second)
    away = [
        line_copy(low.at[place], heads.at[m, mine], send.at[m, d], recv.at[m, d], device)
        for d, (place, device) in enumerate(peers) for m, low in enumerate(lows)
    ]
    for copy in away:
        copy.start()
    own = [pltpu.make_async_copy(low.at[mine], heads.at[m, mine], own_sem.at[m]) for m, low in enumerate(lows)]
    for copy in own:
        copy.start()
    x = lax.axis_index("x")
    core = lax.axis_index("core")
    y = lax.axis_index("y")
    copies = []
    for n, piece in enumerate(pieces):
        far_y, far_x, far_core = n // 4, n // 2 % 2, n % 2
        column = 1 - y if far_y else y
        quarter = (1 - x if far_x else x) * 2 + (1 - core if far_core else core)
        copies.append(pltpu.make_async_copy(piece, ws.at[:, column, quarter], sem.at[n]))
    for copy in copies:
        copy.start()
    for copy in copies + own:
        copy.wait()
    keep = pltpu.make_async_copy(ws, w_ref, own_sem.at[2])
    keep.start()
    for copy in away:
        copy.wait_recv()
    keep_heads = pltpu.make_async_copy(heads, heads_ref, own_sem.at[3])
    keep_heads.start()
    model = x_ref.shape[1]
    tile = min(512, model)
    width = heads.shape[3]
    squares = 0.0
    for start in range(0, model, tile):
        cols = slice(start, start + tile)
        total = x_ref[:, cols].astype(f32)
        for t in range(slots):
            left = jnp.concatenate([heads[0, t], heads[1, t]], axis=0)
            total = total + jnp.dot(
                left, ws[t // 2, t % 2, :, :, cols].reshape(width, tile), preferred_element_type=f32)
        hidden_ref[:, cols] = total
        squares = squares + jnp.sum(total * total, axis=-1, keepdims=True)
    scale = lax.rsqrt(squares / model + epsilon)
    for start in range(0, model, tile):
        cols = slice(start, start + tile)
        normed_ref[:, cols] = (hidden_ref[:, cols] * scale * gain_ref[:, cols]).astype(bf16)
    keep.wait()
    keep_heads.wait()
    for copy in away:
        copy.wait_send()


def attend(x, lows, gain, pieces):
    rows, model = x.shape
    lines, part, _ = pieces[0].shape
    full = (lines, 2, 4, part, model)
    heads = (2, *lows[0].shape)
    slots = 2 * lines
    anywhere = pl.BlockSpec(memory_space=pl.ANY)
    sems = pltpu.SemaphoreType.DMA
    return pl.pallas_call(
        attend_kernel,
        out_shape=(
            jax.ShapeDtypeStruct((rows, model), f32),
            jax.ShapeDtypeStruct((rows, model), bf16),
            jax.ShapeDtypeStruct(full, bf16),
            jax.ShapeDtypeStruct(heads, bf16),
        ),
        in_specs=[vmem(), anywhere, anywhere, vmem()] + [anywhere] * 8,
        out_specs=(vmem(), vmem(), anywhere, anywhere),
        scratch_shapes=[
            pltpu.VMEM(full, bf16), pltpu.VMEM(heads, bf16),
            sems((2, slots)), sems((2, slots)), sems((8,)), sems((4,))],
        compiler_params=pltpu.CompilerParams(
            collective_id=4, has_side_effects=True, vmem_limit_bytes=32 * 2**20),
        cost_estimate=pl.CostEstimate(flops=3 * 10**10, bytes_accessed=2 * 10**7, transcendentals=0),
        name="attend",
    )(x, *lows, gain, *pieces)


def attend_back_kernel(hidden_ref, ffn_ref, grad_ref, c_ref, gain_ref, w_ref, heads,
                       result_ref, hgrad_ref, back_first, back_second, left_mine, left_theirs,
                       right_mine, right_theirs, gain_out, low, wgrad, wrecv, backs, send, recv, sem, core_sem):
    rows, model = hidden_ref.shape
    half = rows // 2
    tile = min(512, model)
    slots = heads.shape[1]
    width = heads.shape[3]
    mine, peers = tensor_peers(slots)
    greet([device for _, device in peers] + [other("core")])
    squares, dots = 0.0, 0.0
    for start in range(0, model, tile):
        cols = slice(start, start + tile)
        hidden = hidden_ref[:, cols]
        squares = squares + jnp.sum(hidden * hidden, axis=-1, keepdims=True)
        dots = dots + jnp.sum(hidden * grad_ref[:, cols] * gain_ref[:, cols], axis=-1, keepdims=True)
    scale = lax.rsqrt(squares / model + epsilon)
    pull = scale * scale * scale * (dots / model)
    for start in range(0, model, tile):
        cols = slice(start, start + tile)
        hidden = hidden_ref[:, cols]
        grad = grad_ref[:, cols]
        result_ref[:, cols] = hidden + ffn_ref[:, cols]
        gain_out[:, cols] = jnp.sum(grad * hidden * scale, axis=0, keepdims=True)
        hgrad = c_ref[:, cols].astype(f32) + scale * (grad * gain_ref[:, cols]) - hidden * pull
        hgrad_ref[:, cols] = hgrad
        low[:, cols] = hgrad.astype(bf16)

    outs = (back_first, back_second)

    def away(m, d):
        place = lax.rem(mine + d, slots)
        return line_copy(backs.at[m, d], outs[m].at[mine], send.at[m, d], recv.at[m, d],
                         {"z": place // 2, "y": lax.rem(place, 2)})

    @pl.loop(0, slots)
    def _(step):
        d = slots - 1 - step
        place = lax.rem(mine + d, slots)
        back = lax.dot_general(
            low[...], w_ref[place // 2, lax.rem(place, 2)].reshape(width, model), NT,
            preferred_element_type=f32)
        for m in range(2):
            backs[m, d] = back[m * half : (m + 1) * half].astype(bf16)

            @pl.when(d > 0)
            def _():
                away(m, d).start()

            @pl.when(d == 0)
            def _():
                pltpu.make_async_copy(backs.at[m, 0], outs[m].at[mine], sem.at[2 + m]).start()

    for t in range(slots):
        left = jnp.concatenate([heads[0, t], heads[1, t]], axis=0)
        for start in range(0, model, tile):
            cols = slice(start, start + tile)
            value = lax.dot_general(
                left, low[:, cols], (((0,), (0,)), ((), ())), preferred_element_type=f32
            ).astype(bf16).reshape(2, 2, width // 4, tile)
            for c in range(2):
                wgrad[c, :, t % 2, t // 2, :, cols] = value[:, c]
    core = lax.axis_index("core")
    to_pair = line_copy(wgrad.at[1 - core], wrecv, core_sem.at[0], core_sem.at[1], other("core"))
    to_pair.start()
    to_pair.wait_recv()
    lines = wgrad.shape[3]
    for far_x in range(2):
        for far_y in range(2):
            @pl.loop(0, lines)
            def _(z):
                wrecv[far_x, far_y, z] = (
                    wrecv[far_x, far_y, z].astype(f32) + wgrad[core, far_x, far_y, z].astype(f32)
                ).astype(bf16)
    x, y = lax.axis_index("x"), lax.axis_index("y")
    wide = model // 2
    keeps = [
        pltpu.make_async_copy(source.at[..., pl.ds(start, wide)], target, sem.at[4 + n])
        for n, (source, start, target) in enumerate((
            (wrecv.at[x], 0, left_mine), (wrecv.at[1 - x], 0, left_theirs),
            (wrecv.at[:, y], wide, right_mine), (wrecv.at[:, 1 - y], wide, right_theirs)))
    ]
    for copy in keeps:
        copy.start()
    for copy in keeps:
        copy.wait()
    to_pair.wait_send()
    for m in range(2):
        pltpu.make_async_copy(backs.at[m, 0], outs[m].at[mine], sem.at[2 + m]).wait()
        for d in range(1, slots):
            away(m, d).wait_recv()
            away(m, d).wait_send()


def attend_back(hidden, ffn_out, normed_grad, c_rows, gain, w_full, heads):
    rows, model = hidden.shape
    wide = jax.ShapeDtypeStruct((rows, model), f32)
    lines, _, _, part, _ = w_full.shape
    share = (2, 2, lines, part, model)
    slots = 2 * lines
    back = jax.ShapeDtypeStruct(heads.shape[1:], bf16)
    anywhere = pl.BlockSpec(memory_space=pl.ANY)
    sems = pltpu.SemaphoreType.DMA
    return pl.pallas_call(
        attend_back_kernel,
        out_shape=(
            wide, wide, back, back,
            *[jax.ShapeDtypeStruct((2, lines, part, model // 2), bf16)] * 4,
            jax.ShapeDtypeStruct((1, model), f32),
        ),
        in_specs=[vmem()] * 7,
        out_specs=(vmem(),) * 2 + (anywhere,) * 6 + (vmem(),),
        scratch_shapes=[
            pltpu.VMEM((rows, model), bf16), pltpu.VMEM((2, *share), bf16), pltpu.VMEM(share, bf16),
            pltpu.VMEM(heads.shape, bf16), sems((2, slots)), sems((2, slots)), sems((8,)), sems((2,))],
        compiler_params=pltpu.CompilerParams(
            collective_id=5, has_side_effects=True, vmem_limit_bytes=48 * 2**20),
        cost_estimate=pl.CostEstimate(flops=3 * 10**10, bytes_accessed=4 * 10**7, transcendentals=0),
        name="attend_back",
    )(hidden, ffn_out, normed_grad, c_rows, gain, w_full, heads)


def root_scale(row_values, gain_vector):
    row_scale = lax.rsqrt(jnp.mean(row_values * row_values, axis=-1, keepdims=True) + epsilon)
    return (row_values * row_scale * gain_vector, row_scale)


def norm_backward(row_values, row_scale, gain_vector, normed_grad):
    weighted = normed_grad * gain_vector
    rows_grad = row_scale * weighted - row_values * row_scale * row_scale * row_scale * jnp.mean(
        weighted * row_values, axis=-1, keepdims=True
    )
    gain_grad = jnp.sum(normed_grad * row_values * row_scale, axis=tuple(range(row_values.ndim - 1)))
    return (rows_grad, gain_grad)


DP = ("x", "core")
TP = ("z", "y")


def gather(x, axis_name, axis=0):
    return lax.all_gather(x, axis_name, axis=axis, tiled=True)


def scatter_sum(x, axis_name, axis=0):
    return lax.psum_scatter(
        x.astype(bf16), axis_name, scatter_dimension=axis, tiled=True
    ).astype(f32)


def dot(a, b):
    return jnp.dot(a, b, preferred_element_type=f32)


def dot_nt(a, b):
    return jnp.einsum("tk,nk->tn", a, b, preferred_element_type=f32)


def dot_tn(a, b):
    return jnp.einsum("tm,tn->mn", a, b, preferred_element_type=f32)


def exchange(x, axis_name, distance=1):
    size = lax.axis_size(axis_name)
    return lax.ppermute(x, axis_name, [(i, i ^ distance) for i in range(size)])


def pick(x, index, axis):
    return lax.dynamic_index_in_dim(x, index, axis, keepdims=False)


def after(x, *others):
    return lax.optimization_barrier((x, *others))[0]


def add_low(x, y):
    return (x.astype(f32) + y.astype(f32)).astype(bf16)


def halve_sum(grad, axis_name):
    me = lax.axis_index(axis_name)
    return add_low(pick(grad, me, 0), exchange(pick(grad, 1 - me, 0), axis_name))


def feed_forward_groups(normed, cotangents, w_gate, w_up, w_down):
    gate_full = gather(w_gate, DP)
    up_full = gather(w_up, DP)
    down_full = gather(w_down, DP, 1)
    outs, normed_grads, inner_rows, gate_grads, up_grads, rows, grad_rows = [], [], [], [], [], [], []
    for m in range(normed.shape[0]):
        rows.append(gather(normed[m], TP))
        grad_rows.append(gather(cotangents[m], TP))
        gate_values = dot(rows[m], gate_full)
        up_values = dot(rows[m], up_full)
        sigmoid_gate = jax.nn.sigmoid(gate_values)
        silu_gate = gate_values * sigmoid_gate
        inner = (silu_gate * up_values).astype(bf16)
        inner_grad = dot_nt(grad_rows[m], down_full)
        gate_grad = (
            inner_grad * up_values * sigmoid_gate * (1.0 + gate_values * (1.0 - sigmoid_gate))
        ).astype(bf16)
        up_grad = (inner_grad * silu_gate).astype(bf16)
        normed_grads.append(scatter_sum(dot_nt(gate_grad, gate_full) + dot_nt(up_grad, up_full), TP))
        outs.append(scatter_sum(dot(inner, down_full), TP))
        inner_rows.append(inner)
        gate_grads.append(gate_grad)
        up_grads.append(up_grad)
    grad_all = jnp.concatenate(grad_rows)
    rows_all = jnp.concatenate(rows)
    gate_share = scatter_sum(dot_tn(rows_all, jnp.concatenate(gate_grads)), DP)
    up_share = scatter_sum(dot_tn(rows_all, jnp.concatenate(up_grads)), DP)
    down_share = scatter_sum(dot_tn(jnp.concatenate(inner_rows), grad_all), DP, 1)
    return jnp.stack(outs), jnp.stack(normed_grads), (gate_share, up_share, down_share)


def per_device(
    inputs,
    lengths,
    norm_gain,
    ffn_gain,
    w_query,
    w_key,
    w_value,
    w_gate_out,
    w_beta,
    conv_weight,
    head_gain,
    w_out,
    w_gate,
    w_up,
    w_down,
    cotangent,
):
    batches = range(inputs.shape[0])
    local_width = w_query.shape[1]
    heads = w_beta.shape[1]
    devices = lax.axis_size(TP)
    planar = all(lax.axis_size(name) == 2 for name in ("x", "core", "y"))
    w_parts = (w_query, w_key, w_value, w_gate_out)
    w_inner = jnp.concatenate(w_parts, axis=1)
    w_beta_wide = jnp.pad(w_beta, ((0, 0), (0, 128 - heads)))
    taps = conv_weight.astype(f32).reshape(-1, local_width)
    gain_heads = head_gain.astype(f32)
    gains = gather(jnp.stack([norm_gain, ffn_gain]), DP, 1)
    gain_one, gain_two = gains[0].astype(f32), gains[1].astype(f32)
    rows_in = inputs.astype(f32)
    normed_one, scale_one = root_scale(rows_in, gain_one)
    normed_one = normed_one.astype(bf16)

    def run_mixer(m, wide, logits):
        low, *kept = mixer_forward(lengths[m, 0], wide, logits, taps, gain_heads, exact=False)
        return low, kept

    def back_mixer(m, wide, logits, grad, kept):
        return mixer_backward(
            lengths[m, 0], wide, logits, taps, gain_heads, grad, kept, exact=False)

    if planar:
        count = rows_in.shape[0] * rows_in.shape[1]
        model = rows_in.shape[2]
        ranks = lax.axis_size(DP)
        ffn_parts = [
            w.reshape(ranks, -1, w.shape[1]) for w in after((w_gate.T, w_up.T, w_down), gains)]
        c_rows = [None] * 8
        c_rows[0] = after(cotangent.reshape(count, model), gains)
        c_rows[4] = exchange(c_rows[0], "core")
        out_shares = pick(
            w_out.reshape(lax.axis_size(DP), len(batches), -1, model), lax.axis_index(DP), 0)
        gathered_one, out_own, projected, beta_logits, own_weights, own_down = gather_project(
            normed_one, out_shares, ffn_parts, w_parts, w_beta_wide)
        early = after(c_rows[0], gathered_one)
        c_rows[1] = exchange(early, "x")
        weights = gather(own_weights[None], "z")
        c_rows[2] = exchange(early, "y")
        out_own = out_own.reshape(out_own.shape[0], -1, model)
        out_y = exchange(out_own, "y")
        out_x = exchange(out_own, "x")
    else:
        gathered_one = jnp.stack([gather(normed_one[m], TP) for m in batches])
        projected = [dot(gathered_one[m], w_inner) for m in batches]
        beta_logits = [dot(gathered_one[m], w_beta_wide) for m in batches]
        out_full = gather(w_out, TP)
    token_heads, saved = [], []
    for m in batches:
        low, kept = run_mixer(m, projected[m], beta_logits[m])
        saved.append(kept)
        if planar and m == 0:
            out_y, c_rows[1], c_rows[2] = after((out_y, c_rows[1], c_rows[2]), low)
            out_xy = exchange(out_y, "x")
            c_rows[3] = exchange(c_rows[1], "y")
            c_rows[5] = exchange(c_rows[1], "core")
            c_rows[6] = exchange(c_rows[2], "core")
            projected[1] = after(projected[1], out_y, c_rows[2])
        low = low.reshape(devices, -1, local_width)
        if not planar:
            low = lax.all_to_all(low, TP, split_axis=0, concat_axis=0, tiled=True)
        token_heads.append(low)
    if planar:
        out_x, out_xy, c_rows[3] = after((out_x, out_xy, c_rows[3]), low)
        out_pieces = []
        for piece in (out_own, out_x, out_y, out_xy):
            out_pieces += [piece, exchange(piece, "core")]
        c_rows[7] = exchange(c_rows[3], "core")
        hidden, normed_two, out_full, token_heads = attend(
            inputs.reshape(count, model), token_heads, gain_two[None], out_pieces)
        ffn_out, normed_grad, weight_grads, down_grad = ffn_plane(normed_two, weights, own_down, c_rows)
        result_rows, hidden_grad, *mixed_grads, left, left_away, right, right_away, gain_two_sum = attend_back(
            hidden, ffn_out, normed_grad, c_rows[0], gain_two[None], out_full, token_heads)
        weight_grads = after(weight_grads, left)
        own_grads = lax.psum_scatter(weight_grads, "z", scatter_dimension=0, tiled=True)
        gain_two_sum = gain_two_sum[0]
        result_rows = result_rows.reshape(rows_in.shape)
        hidden_grad = hidden_grad.reshape(rows_in.shape)
    else:
        heads_rows = [
            block.swapaxes(0, 1).reshape(-1, devices * local_width) for block in token_heads]
        hidden = rows_in + jnp.stack([dot(rows, out_full) for rows in heads_rows])
        normed_two, scale_two = root_scale(hidden, gain_two)
        ffn_out, normed_grad, (gate_share, up_share, down_share) = feed_forward_groups(
            normed_two.astype(bf16), cotangent, w_gate, w_up, w_down)
        result_rows = hidden + ffn_out
        norm_grad, gain_two_sum = norm_backward(hidden, scale_two, gain_two, normed_grad)
        hidden_grad = cotangent.astype(f32) + norm_grad
        attended_low = hidden_grad.astype(bf16)
        mixed_grads = [
            dot_nt(attended_low[m], out_full).astype(bf16)
            .reshape(-1, devices, local_width).swapaxes(0, 1) for m in batches]
        out_grad = dot_tn(
            jnp.concatenate(heads_rows), jnp.concatenate(list(attended_low))).astype(bf16)
    if not planar:
        mixed_grads = [
            lax.all_to_all(grad, TP, split_axis=0, concat_axis=0, tiled=True)
            for grad in mixed_grads]
    mixed_grads = [grad.reshape(-1, local_width) for grad in mixed_grads]
    if planar:
        left = add_low(left, exchange(left_away, "x"))
        right = add_low(right, exchange(right_away, "y"))
    projected_low, beta_low = [], []
    taps_sum, heads_sum = 0.0, 0.0
    for m in batches:
        if planar and m > 0:
            mixed_grads[m] = after(mixed_grads[m], left, right)
        projected_grad, beta_grad, taps_part, heads_part = back_mixer(
            m, projected[m], beta_logits[m], mixed_grads[m], saved[m])
        taps_sum = taps_sum + taps_part
        heads_sum = heads_sum + heads_part
        projected_low.append(projected_grad)
        beta_low.append(beta_grad)
    projected_low = jnp.stack(projected_low)
    beta_low = jnp.stack(beta_low)
    if planar:
        left, right = halve_sum(left, "y"), halve_sum(right, "x")
        projected_low = after(projected_low, left, right)
        out_grad = jnp.concatenate([left, right], axis=2)
    tokens = gathered_one.reshape(-1, gathered_one.shape[2])
    inner_sum = dot_tn(tokens, projected_low.reshape(-1, 4 * local_width))
    beta_sum = dot_tn(tokens, beta_low.reshape(-1, 128)[:, :heads])
    gain_one_sum = (
        sum(
            jnp.sum(inner_sum[:, n * local_width : (n + 1) * local_width] * w.astype(f32), axis=1)
            for n, w in enumerate(w_parts))
        + jnp.sum(beta_sum * w_beta.astype(f32), axis=1)
    ) / gain_one
    gain_parts = jnp.stack([gain_one_sum, gain_two_sum])
    small = jnp.concatenate([part.reshape(-1) for part in (beta_sum, taps_sum, heads_sum)])
    low_sum = inner_sum.astype(bf16)
    if planar:
        ranks = lax.axis_size(DP)
        gain_parts = gain_parts.reshape(2, ranks, devices, -1).transpose(2, 0, 1, 3)
        chunk = gain_parts.shape[3]
        gain_parts = gain_parts.reshape(devices, -1, 128)
        gain_rows = gain_parts.shape[1]
        gain_parts = jnp.pad(gain_parts, ((0, 0), (0, -gain_rows % 8), (0, 0)))
        small = jnp.pad(small, (0, -small.size % 1024)).reshape(-1, 128)
        input_norm, flat, out_total, inner_total, pair_grads, down_grads = scatter_rows(
            projected_low, beta_low, out_grad,
            low_sum.reshape(2, -1, low_sum.shape[1]), w_parts, w_beta_wide, small, gain_parts,
            own_grads[0], down_grad)
        gate_share, up_share = (
            pair_grads[:, kind].reshape(-1, pair_grads.shape[3]).astype(f32).T for kind in range(2))
        down_share = down_grads.reshape(w_down.shape).astype(f32)
        gain_totals = pick(
            flat[small.shape[0] :][:gain_rows].reshape(2, ranks, chunk), lax.axis_index(DP), 1)
        small = flat[: small.shape[0]].reshape(-1)
        out_total = out_total.reshape(w_out.shape).astype(f32)
        inner_total = inner_total.reshape(low_sum.shape)
    else:
        gain_totals = lax.psum_scatter(gain_parts, DP + TP, scatter_dimension=1, tiled=True)
        inner_total = lax.psum(low_sum, DP)
        small = lax.psum(small, DP)
        out_grad = lax.psum_scatter(out_grad, TP, scatter_dimension=0, tiled=True)
        out_total = lax.psum(out_grad, DP).astype(f32)
        input_norm = jnp.stack([
            scatter_sum(
                dot_nt(projected_low[m], w_inner) + dot_nt(beta_low[m], w_beta_wide), TP)
            for m in batches])
    norm_grad, _ = norm_backward(rows_in, scale_one, gain_one, input_norm)
    beta_total, conv_total, heads_total = (
        piece.reshape(shape) for piece, shape in zip(
            jnp.split(
                small[: beta_sum.size + taps_sum.size + heads_sum.size],
                (beta_sum.size, beta_sum.size + taps_sum.size)),
            (beta_sum.shape, conv_weight.shape, head_gain.shape)))
    columns = [
        inner_total[:, n * local_width : (n + 1) * local_width].astype(f32) for n in range(4)]
    return (
        result_rows,
        hidden_grad + norm_grad,
        gain_totals[0],
        gain_totals[1],
        *columns,
        beta_total,
        conv_total,
        heads_total,
        out_total,
        gate_share,
        up_share,
        down_share,
    )


def solution(mesh):
    dp, tensor = mesh.shape["dp"], mesh.shape["tensor"]
    inner = 2 if tensor == 8 else 4
    axes = ("x", "core", "z", "y")
    fine = jax.sharding.Mesh(
        mesh.devices.reshape(dp // 2, 2, tensor // inner, inner), axes)
    tokens = P(None, DP + TP, None)
    in_specs = (
        tokens,
        P(None, DP, None),
        P(DP),
        P(DP),
        P(None, TP),
        P(None, TP),
        P(None, TP),
        P(None, TP),
        P(None, TP),
        P(None, None, TP),
        P(TP, None),
        P(TP, None),
        P(DP, TP),
        P(DP, TP),
        P(TP, DP),
        tokens,
    )
    out_specs = (
        tokens,
        tokens,
        P(DP + TP),
        P(DP + TP),
        P(None, TP),
        P(None, TP),
        P(None, TP),
        P(None, TP),
        P(None, TP),
        P(None, None, TP),
        P(TP, None),
        P(TP, None),
        P(DP, TP),
        P(DP, TP),
        P(TP, DP),
    )
    return jax.shard_map(
        per_device, mesh=fine, in_specs=in_specs, out_specs=out_specs, check_vma=False
    )
```

```python
from functools import partial

import jax
import jax.numpy as jnp
from jax import lax
from jax.experimental import pallas as pl
from jax.experimental.pallas import tpu as pltpu
from jax.sharding import PartitionSpec as P


CHUNK = 128
HALO = 8
epsilon = 1e-06
highest = lax.Precision.HIGHEST
f32 = jnp.float32
bf16 = jnp.bfloat16


def product(left, right, left_dim, right_dim, exact=False):
    dims = (((left_dim,), (right_dim,)), ((), ()))
    if exact:
        return lax.dot_general(left, right, dims, precision=highest, preferred_element_type=f32)
    return lax.dot_general(
        left.astype(bf16), right.astype(bf16), dims, preferred_element_type=f32
    )


def sigmoid(x):
    return 1.0 / (1.0 + jnp.exp(-x))


def segment_tools(lengths_ref):
    ends = []
    total = 0
    for i in range(lengths_ref.shape[0] - 1):
        total = total + lengths_ref[i]
        ends.append(total)

    def segment_of(pos):
        result = 0
        for end in ends:
            result = result + (pos >= end).astype(jnp.int32)
        return result

    return segment_of, len(ends)


def chunk_masks(segment_of, base, chunk):
    col = base + lax.broadcasted_iota(jnp.int32, (chunk, 1), 0)
    row = base + lax.broadcasted_iota(jnp.int32, (1, chunk), 1)
    seg_col = segment_of(col)
    seg_row = segment_of(row)
    first = segment_of(base - 1)
    last = segment_of(base + chunk - 1)
    same = seg_col == seg_row
    strict = (same & (col > row)).astype(f32)
    within = (same & (col >= row)).astype(f32)
    has_past = base > 0
    carry = ((seg_col == first) & has_past).astype(f32)
    close = (seg_col == last).astype(f32)
    keep = ((first == last) & has_past).astype(f32)
    return strict, within, carry, close, keep


def level_masks(chunk):
    row = lax.broadcasted_iota(jnp.int32, (chunk, chunk), 0)
    col = lax.broadcasted_iota(jnp.int32, (chunk, chunk), 1)
    masks = []
    width = 1
    while width < chunk:
        mask = (
            (row // (2 * width) == col // (2 * width))
            & ((row // width) % 2 == 1)
            & ((col // width) % 2 == 0)
        )
        masks.append(mask)
        width *= 2
    return masks, (row == col).astype(f32)


def conv_part(proj_ref, tap_ref, segment_of, base, part, width, chunk):
    taps = tap_ref.shape[0] // 3
    cols = pl.ds(part * width, width)
    main = proj_ref[pl.ds(base, chunk), cols]
    prev = proj_ref[pl.ds(pl.multiple_of(jnp.maximum(base - HALO, 0), HALO), HALO), cols]
    full = jnp.concatenate([prev, main], axis=0)
    col = base + lax.broadcasted_iota(jnp.int32, (chunk, 1), 0)
    seg = segment_of(col)
    total = main * tap_ref[part * taps : part * taps + 1, :]
    shifted = [main]
    for s in range(1, taps):
        valid = (segment_of(col - s) == seg) & (col >= s)
        moved = jnp.where(valid, pltpu.roll(full, s, 0)[HALO:], 0.0)
        shifted.append(moved)
        total = total + moved * tap_ref[part * taps + s : part * taps + s + 1, :]
    return total, shifted


def heads_of(x, heads):
    return [x[:, h * 128 : (h + 1) * 128] for h in range(heads)]


def unit_rows(a, scale):
    r = lax.rsqrt(jnp.sum(a * a, axis=-1, keepdims=True) + epsilon)
    return a * (r * scale)


def mixer_forward_kernel(exact, group, lengths_ref, proj_ref, beta_ref, tap_ref, gain_ref,
                         mixed_ref, heads_ref, fixed_ref, delta_ref, state_ref, inverse_ref,
                         query_s, key_s, value_s, score_s):
    rows_all = proj_ref.shape[0]
    width = proj_ref.shape[1] // 4
    heads = width // 128
    chunk = CHUNK
    count = rows_all // chunk
    segment_of, segments = segment_tools(lengths_ref)

    @pl.loop(0, count)
    def _(c):
        base = pl.multiple_of(c * chunk, chunk)
        rows = pl.ds(base, chunk)
        for part, target in enumerate((query_s, key_s, value_s)):
            pre, _ = conv_part(proj_ref, tap_ref, segment_of, base, part, width, chunk)
            act = pre * sigmoid(pre)
            if part == 2:
                target[rows, :] = act
            else:
                scale = 128 ** (-0.5) if part == 0 else 1.0
                for h, a in enumerate(heads_of(act, heads)):
                    target[rows, h * 128 : (h + 1) * 128] = unit_rows(a, scale)

    def beta_of(base, h):
        pos = base + lax.broadcasted_iota(jnp.int32, (chunk, 1), 0)
        live = (segment_of(pos) < segments).astype(f32)
        return sigmoid(beta_ref[pl.ds(base, chunk), h : h + 1]) * live

    masks, eye = level_masks(chunk)

    @pl.loop(0, count // group)
    def _(g):
        lowers, places = [], []
        for i in range(group):
            c = g * group + i
            base = pl.multiple_of(c * chunk, chunk)
            strict, within, _, _, _ = chunk_masks(segment_of, base, chunk)
            for h in range(heads):
                cols = slice(h * 128, (h + 1) * 128)
                k = key_s[pl.ds(base, chunk), cols]
                q = query_s[pl.ds(base, chunk), cols]
                lowers.append(product(k, k, 1, 1, exact) * strict * beta_of(base, h))
                score_s[c * heads + h] = (product(q, k, 1, 1, exact) * within).astype(score_s.dtype)
                places.append(c * heads + h)
        inverses = [eye - jnp.where(masks[0], lower, 0.0) for lower in lowers]
        for mask in masks[1:]:
            steps = [product(jnp.where(mask, lower, 0.0), x, 1, 0, True) for lower, x in zip(lowers, inverses)]
            inverses = [x - product(x, step, 1, 0, True) for x, step in zip(inverses, steps)]
        for place, x in zip(places, inverses):
            inverse_ref[place] = x

    def advance(c, states):
        base = pl.multiple_of(c * chunk, chunk)
        rows = pl.ds(base, chunk)
        _, _, carry, close, keep = chunk_masks(segment_of, base, chunk)
        new_states = []
        for h in range(heads):
            cols = slice(h * 128, (h + 1) * 128)
            state = states[h]
            k = key_s[rows, cols]
            q = query_s[rows, cols]
            delta = value_s[rows, cols] - carry * product(k, state, 1, 0, exact)
            fixed = product(inverse_ref[c * heads + h], beta_of(base, h) * delta, 1, 0, exact)
            out = carry * product(q, state, 1, 0, exact) + product(
                score_s[c * heads + h], fixed, 1, 0, exact)
            state_ref[c * heads + h] = state
            new_states.append(keep * state + product(k, close * fixed, 0, 0, exact))
            delta_ref[rows, cols] = delta
            fixed_ref[rows, cols] = fixed
            heads_ref[rows, cols] = out
            gate = proj_ref[rows, 3 * width + h * 128 : 3 * width + (h + 1) * 128]
            r = lax.rsqrt(jnp.mean(out * out, axis=-1, keepdims=True) + epsilon)
            mixed_ref[rows, cols] = (
                out * r * gain_ref[h : h + 1, :] * (gate * sigmoid(gate))
            ).astype(mixed_ref.dtype)
        return tuple(new_states)

    lax.fori_loop(0, count, advance, tuple(jnp.zeros((128, 128), f32) for _ in range(heads)))


def mixer_backward_kernel(exact, lengths_ref, proj_ref, beta_ref, tap_ref, gain_ref, grad_ref,
                          heads_ref, fixed_ref, delta_ref, state_ref, inverse_ref,
                          dproj_ref, dbeta_ref, dtap_ref, dgain_ref,
                          query_s, key_s, pre_s, dout_s, dpre_s):
    rows_all = proj_ref.shape[0]
    width = proj_ref.shape[1] // 4
    heads = width // 128
    chunk = CHUNK
    count = rows_all // chunk
    taps = tap_ref.shape[0] // 3
    segment_of, segments = segment_tools(lengths_ref)
    dgain_ref[...] = jnp.zeros_like(dgain_ref)
    dbeta_ref[...] = jnp.zeros_like(dbeta_ref)
    dtap_ref[...] = jnp.zeros_like(dtap_ref)

    @pl.loop(0, count)
    def _(c):
        base = pl.multiple_of(c * chunk, chunk)
        rows = pl.ds(base, chunk)
        for part in range(3):
            pre, _ = conv_part(proj_ref, tap_ref, segment_of, base, part, width, chunk)
            pre_s[rows, part * width : (part + 1) * width] = pre
            if part < 2:
                act = pre * sigmoid(pre)
                target = (query_s, key_s)[part]
                scale = 128 ** (-0.5) if part == 0 else 1.0
                for h, a in enumerate(heads_of(act, heads)):
                    target[rows, h * 128 : (h + 1) * 128] = unit_rows(a, scale)
        for h in range(heads):
            cols = slice(h * 128, (h + 1) * 128)
            gate_cols = slice(3 * width + h * 128, 3 * width + (h + 1) * 128)
            out = heads_ref[rows, cols]
            gate = proj_ref[rows, gate_cols]
            grad = grad_ref[rows, cols].astype(f32)
            gain = gain_ref[h : h + 1, :]
            sg = sigmoid(gate)
            silu = gate * sg
            r = lax.rsqrt(jnp.mean(out * out, axis=-1, keepdims=True) + epsilon)
            normed = out * r
            dgain_ref[h : h + 1, :] += jnp.sum(grad * normed * silu, axis=0, keepdims=True)
            dproj_ref[rows, gate_cols] = (
                grad * normed * gain * (sg * (1.0 + gate * (1.0 - sg)))
            ).astype(dproj_ref.dtype)
            weighted = grad * gain * silu
            dout_s[rows, cols] = r * weighted - out * (r * r * r) * jnp.mean(
                weighted * out, axis=-1, keepdims=True)

    dpre_s[rows_all : rows_all + HALO, :] = jnp.zeros((HALO, 3 * width), f32)

    def retreat(step, dstates):
        c = count - 1 - step
        base = pl.multiple_of(c * chunk, chunk)
        rows = pl.ds(base, chunk)
        strict, within, carry, close, keep = chunk_masks(segment_of, base, chunk)
        pos = base + lax.broadcasted_iota(jnp.int32, (chunk, 1), 0)
        live = (segment_of(pos) < segments).astype(f32)
        new_dstates = []
        for h in range(heads):
            cols = slice(h * 128, (h + 1) * 128)
            place = c * heads + h
            k = key_s[rows, cols]
            q = query_s[rows, cols]
            dout = dout_s[rows, cols]
            state = state_ref[place]
            inverse = inverse_ref[place]
            fixed = fixed_ref[rows, cols]
            delta = delta_ref[rows, cols]
            dstate = dstates[h]
            rate = sigmoid(beta_ref[rows, h : h + 1])
            beta = rate * live
            scores = product(q, k, 1, 1, exact) * within
            gram = product(k, k, 1, 1, exact) * strict
            dfixed = product(scores, dout, 0, 0, exact) + close * product(k, dstate, 1, 0, exact)
            drhs = product(inverse, dfixed, 0, 0, exact)
            ddelta = beta * drhs
            carried_dout = carry * dout
            carried_ddelta = carry * ddelta
            new_dstates.append(
                keep * dstate
                + product(q, carried_dout, 0, 0, exact)
                - product(k, carried_ddelta, 0, 0, exact)
            )
            dscores = product(dout, fixed, 1, 1, exact) * within
            dlower = -product(drhs, fixed, 1, 1, exact) * strict
            dgram = beta * dlower
            dq = product(carried_dout, state, 1, 1, exact) + product(dscores, k, 1, 0, exact)
            dk = (
                product(dscores, q, 0, 0, exact)
                + close * product(fixed, dstate, 1, 1, exact)
                - product(carried_ddelta, state, 1, 1, exact)
                + product(dgram, k, 1, 0, exact)
                + product(dgram, k, 0, 0, exact)
            )
            drate = live * (
                jnp.sum(drhs * delta, axis=-1, keepdims=True)
                + jnp.sum(dlower * gram, axis=-1, keepdims=True)
            )
            dbeta_ref[rows, h : h + 1] = (drate * rate * (1.0 - rate)).astype(dbeta_ref.dtype)
            for part, da in enumerate((dq, dk, ddelta)):
                part_cols = slice(part * width + h * 128, part * width + (h + 1) * 128)
                pre = pre_s[rows, part_cols]
                sg = sigmoid(pre)
                if part < 2:
                    a = pre * sg
                    scale = 128 ** (-0.5) if part == 0 else 1.0
                    r = lax.rsqrt(jnp.sum(a * a, axis=-1, keepdims=True) + epsilon)
                    da = (scale * r) * (da - a * (r * r) * jnp.sum(da * a, axis=-1, keepdims=True))
                dpre_s[rows, part_cols] = da * (sg * (1.0 + pre * (1.0 - sg)))
        return tuple(new_dstates)

    lax.fori_loop(0, count, retreat, tuple(jnp.zeros((128, 128), f32) for _ in range(heads)))

    @pl.loop(0, count)
    def _(c):
        base = pl.multiple_of(c * chunk, chunk)
        rows = pl.ds(base, chunk)
        col = base + lax.broadcasted_iota(jnp.int32, (chunk, 1), 0)
        seg = segment_of(col)
        for part in range(3):
            cols = slice(part * width, (part + 1) * width)
            _, shifted = conv_part(proj_ref, tap_ref, segment_of, base, part, width, chunk)
            full = dpre_s[pl.ds(base, chunk + HALO), cols]
            main = full[:chunk]
            total = main * tap_ref[part * taps : part * taps + 1, :]
            for s in range(taps):
                at = slice(part * taps + s, part * taps + s + 1)
                dtap_ref[at, :] += jnp.sum(main * shifted[s], axis=0, keepdims=True)
                if s > 0:
                    valid = (segment_of(col + s) == seg) & (col + s < rows_all)
                    moved = pltpu.roll(full, chunk + HALO - s, 0)[:chunk]
                    total = total + jnp.where(valid, moved, 0.0) * tap_ref[at, :]
            dproj_ref[rows, cols] = total.astype(dproj_ref.dtype)


def vmem():
    return pl.BlockSpec(memory_space=pltpu.VMEM)


def mixer_forward(lengths_row, projected, beta_logits, taps, gain, exact=True, group=4):
    rows, wide = projected.shape
    width = wide // 4
    heads = width // 128
    places = rows // CHUNK * heads
    group = min(group, rows // CHUNK)
    return pl.pallas_call(
        partial(mixer_forward_kernel, exact, group),
        out_shape=(
            jax.ShapeDtypeStruct((rows, width), bf16),
            jax.ShapeDtypeStruct((rows, width), f32),
            jax.ShapeDtypeStruct((rows, width), f32),
            jax.ShapeDtypeStruct((rows, width), f32),
            jax.ShapeDtypeStruct((places, 128, 128), f32),
            jax.ShapeDtypeStruct((places, CHUNK, CHUNK), f32),
        ),
        in_specs=[pl.BlockSpec(memory_space=pltpu.SMEM)] + [vmem()] * 4,
        out_specs=(vmem(),) * 6,
        scratch_shapes=[pltpu.VMEM((rows, width), f32)] * 3
        + [pltpu.VMEM((places, CHUNK, CHUNK), f32 if exact else bf16)],
        compiler_params=pltpu.CompilerParams(vmem_limit_bytes=48 * 2**20),
        cost_estimate=pl.CostEstimate(flops=10**10, bytes_accessed=10**7, transcendentals=10**6),
        name="mixer_forward",
    )(lengths_row, projected, beta_logits, taps, gain)


def mixer_backward(lengths_row, projected, beta_logits, taps, gain, grad, saved, exact=True):
    rows, wide = projected.shape
    width = wide // 4
    return pl.pallas_call(
        partial(mixer_backward_kernel, exact),
        out_shape=(
            jax.ShapeDtypeStruct((rows, wide), bf16),
            jax.ShapeDtypeStruct((rows, 128), bf16),
            jax.ShapeDtypeStruct(taps.shape, f32),
            jax.ShapeDtypeStruct(gain.shape, f32),
        ),
        in_specs=[pl.BlockSpec(memory_space=pltpu.SMEM)] + [vmem()] * 10,
        out_specs=(vmem(),) * 4,
        scratch_shapes=[pltpu.VMEM((rows, width), f32)] * 2
        + [pltpu.VMEM((rows, 3 * width), f32), pltpu.VMEM((rows, width), f32),
           pltpu.VMEM((rows + HALO, 3 * width), f32)],
        compiler_params=pltpu.CompilerParams(vmem_limit_bytes=56 * 2**20),
        cost_estimate=pl.CostEstimate(flops=10**10, bytes_accessed=10**7, transcendentals=10**6),
        name="mixer_backward",
    )(lengths_row, projected, beta_logits, taps, gain, grad, *saved)


NT = (((1,), (1,)), ((), ()))


def other(axis_name):
    return {axis_name: 1 - lax.axis_index(axis_name)}


def ffn_kernel(x_ref, w_ref, down_ref, c_refs, out_ref, ngrad_ref, wgrad_ref, down_out,
               xs, cs, ws, dsum, landed, outs, inner_s, gate_s, up_s, acts_t, part, crecv, drecv, nrecv, stage,
               ag_send, ag_recv, pair_send, pair_recv, rs_send, rs_recv, c_sem, w_sem, g_sem, t_sem,
               down_right, down_left, down_recv, down_sem, sum_sems, keep_sem, out_sem):
    half = xs.shape[1] // 2
    rows = 2 * half
    model = xs.shape[2]
    hidden = ws.shape[1]
    lines = w_ref.shape[0]
    parts, _, quarter, width = w_ref.shape[1:]
    tile_f = 256
    tile_d = min(512, model)
    tile_w = min(256, width)

    def remote(src, dst, send, recv, axis_name):
        return pltpu.make_async_remote_copy(
            src_ref=src, dst_ref=dst, send_sem=send, recv_sem=recv,
            device_id=other(axis_name), device_id_type=pl.DeviceIdType.MESH)

    def halves(ref, index, h):
        return ref.at[index, pl.ds(h * half, half)]

    o = lax.axis_index("z")

    def down_rows(z):
        return ws.at[2, pl.ds(pl.multiple_of(z * quarter, 16), quarter)]

    def down_pass(z, right):
        send = down_right if right else down_left
        return pltpu.make_async_remote_copy(
            src_ref=down_rows(z), dst_ref=down_rows(z), send_sem=send.at[z], recv_sem=down_recv.at[z],
            device_id={"z": o + 1 if right else o - 1}, device_id_type=pl.DeviceIdType.MESH)

    def down_forward(z, right):
        @pl.when(o < lines - 1 if right else o > 0)
        def _():
            down_pass(z, right).start()

    def down_step(far):
        for side in (-1, 1):
            z = o + side * far

            @pl.when((z >= 0) & (z < lines))
            def _():
                down_pass(z, side < 0).wait_recv()
                down_forward(z, side < 0)

    weight_copies, down_copies = [], []
    for r in range(parts):
        cols = pl.ds(r * width, width)
        for line in range(lines):
            weight_copies.append(pltpu.make_async_copy(
                w_ref.at[line, r], ws.at[pl.ds(0, 2), pl.ds(line * quarter, quarter), cols],
                w_sem.at[line, r]))
        down_copies.append(pltpu.make_async_copy(
            down_ref.at[r], down_rows(o).at[:, cols], down_sem.at[r]))
    for copy in down_copies:
        copy.start()
    for copy in weight_copies:
        copy.start()

    def pair_at(turn):
        return jnp.where(turn < 2, 3 - 2 * turn, 6 - 2 * turn)

    def slot_of(step):
        return (1 - lax.rem(step, 2)) * 4 + pair_at(step // 2)

    def c_copy(step, n):
        buffer = lax.rem(step, 2)
        return pltpu.make_async_copy(c_refs[n], cs.at[buffer], c_sem.at[buffer])

    def c_start(step):
        for n in range(8):
            @pl.when(slot_of(step) == n)
            def _():
                c_copy(step, n).start()

    c_copy(0, 7).start()
    line_barrier(lines, [other(name) for name in ("core", "x", "y")])

    own_pair = remote(x_ref, xs.at[4], ag_send.at[0], ag_recv.at[0], "core")
    own_x = [remote(x_ref.at[pl.ds(h * half, half)], halves(xs, 1, h), ag_send.at[1 + h], ag_recv.at[1 + h], "x") for h in range(2)]
    own_y = [remote(x_ref.at[pl.ds(h * half, half)], halves(xs, 2, h), ag_send.at[3 + h], ag_recv.at[3 + h], "y") for h in range(2)]
    relay_y = remote(halves(xs, 1, 0), halves(xs, 3, 0), ag_send.at[5], ag_recv.at[5], "y")
    relay_x = remote(halves(xs, 2, 1), halves(xs, 3, 1), ag_send.at[6], ag_recv.at[6], "x")
    pair_of = [None] + [remote(xs.at[j], xs.at[4 + j], ag_send.at[6 + j], ag_recv.at[6 + j], "core") for j in (1, 2, 3)]
    own_pair.start()
    own_x[0].start()
    own_y[1].start()
    own_x[1].start()
    own_y[0].start()
    for copy in down_copies:
        copy.wait()
    down_forward(o, True)
    down_forward(o, False)
    own_copy = pltpu.make_async_copy(x_ref, xs.at[0], t_sem.at[0, 0])
    own_copy.start()
    own_copy.wait()
    for copy in weight_copies:
        copy.wait()

    def part_send(turn):
        j = pair_at(turn)
        return remote(part.at[lax.rem(turn, 2)], crecv.at[j], pair_send.at[j], pair_recv.at[j], "core")

    x_sends = [[remote(crecv.at[1, a, pl.ds(h * half, half)], nrecv.at[0, a, pl.ds(h * half, half)],
                       rs_send.at[a * 2 + h], rs_recv.at[a * 2 + h], "x") for a in range(2)] for h in range(2)]
    y_sends = [[remote(crecv.at[2, a, pl.ds(h * half, half)], nrecv.at[1, a, pl.ds(h * half, half)],
                       rs_send.at[4 + a * 2 + h], rs_recv.at[4 + a * 2 + h], "y") for a in range(2)] for h in range(2)]
    d_sends = [[remote(crecv.at[3, a, pl.ds(h * half, half)], drecv.at[a, pl.ds(h * half, half)],
                       rs_send.at[8 + a * 2 + h], rs_recv.at[8 + a * 2 + h], ("x", "y")[h]) for a in range(2)] for h in range(2)]

    def gates(slot, cols):
        return [
            lax.dot_general(xs[slot], ws[kind, cols, :], NT, preferred_element_type=f32)
            for kind in range(2)]

    @pl.loop(0, 8)
    def _(early):
        slot = lax.rem(early + 1, 2) * 4 + early // 2

        @pl.when(early == 0)
        def _():
            own_pair.wait_recv()

        @pl.when(early == 2)
        def _():
            down_step(1)
            own_x[0].wait_recv()
            relay_y.start()
            own_y[1].wait_recv()
            relay_x.start()
            own_x[1].wait_recv()
            pair_of[1].start()
            own_y[0].wait_recv()
            pair_of[2].start()
            pair_of[1].wait_recv()

        @pl.when(early == 4)
        def _():
            pair_of[2].wait_recv()

        @pl.when(early == 6)
        def _():
            if lines > 2:
                down_step(2)
            relay_y.wait_recv()
            relay_x.wait_recv()
            pair_of[3].start()
            pair_of[3].wait_recv()

        places = pl.ds(pl.multiple_of(slot * rows, rows), rows)
        for start in range(0, hidden, tile_f):
            cols = slice(start, min(start + tile_f, hidden))
            gate, up = gates(slot, cols)
            acts_t[2, cols, places] = (gate * sigmoid(gate) * up).astype(bf16).T

    tiles = model // tile_w

    def c_tile(t):
        buffer = lax.rem(t, 2)
        cols = pl.ds(pl.multiple_of(t * tile_w, tile_w), tile_w)
        return [
            pltpu.make_async_copy(
                ref.at[:, cols], part.at[0, buffer, :, pl.ds(n * tile_w, tile_w)], t_sem.at[buffer, n])
            for n, ref in enumerate(c_refs)]

    def grad_copy(kind, t, line):
        return pltpu.make_async_copy(
            stage.at[lax.rem(t, 2), pl.ds(line * quarter, quarter)],
            wgrad_ref.at[line, t * tile_w // width, kind, :,
                         pl.ds(pl.multiple_of(lax.rem(t * tile_w, width), tile_w), tile_w)],
            g_sem.at[lax.rem(t, 2), line])

    def weight_grads(kind):
        @pl.loop(0, tiles)
        def _(t):
            if kind == 2:
                for copy in c_tile(t):
                    copy.wait()
                right = jnp.concatenate(
                    [part[0, lax.rem(t, 2), :, n * tile_w : (n + 1) * tile_w] for n in range(8)])
            else:
                right = xs[:, :, pl.ds(pl.multiple_of(t * tile_w, tile_w), tile_w)].reshape(8 * rows, tile_w)

            if kind < 2:
                @pl.when(t >= 2)
                def _():
                    for line in range(lines):
                        grad_copy(kind, t - 2, line).wait()

            value = jnp.dot(acts_t[kind], right, preferred_element_type=f32).astype(bf16)
            if kind == 2:
                @pl.when(t + 2 < tiles)
                def _():
                    for copy in c_tile(t + 2):
                        copy.start()
            if kind < 2:
                stage[lax.rem(t, 2)] = value
                for line in range(lines):
                    grad_copy(kind, t, line).start()
            else:
                dsum[:, pl.ds(pl.multiple_of(t * tile_w, tile_w), tile_w)] = value

        if kind == 2:
            return
        for t in range(max(tiles - 2, 0), tiles):
            for line in range(lines):
                grad_copy(kind, t, line).wait()

    mesh_id = pl.DeviceIdType.MESH

    def rows_of(z):
        return dsum.at[pl.ds(pl.multiple_of(z * quarter, 16), quarter)]

    def sum_pass(z, right):
        side = 0 if right else 2
        block = jnp.maximum(z - o - 1, 0) if right else jnp.minimum(lines - o + 1 + z, lines)
        return pltpu.make_async_remote_copy(
            src_ref=rows_of(z), dst_ref=landed.at[block],
            send_sem=sum_sems.at[side, z], recv_sem=sum_sems.at[side + 1, z],
            device_id={"z": o + 1 if right else o - 1}, device_id_type=mesh_id)

    def sum_add(z, block):
        at = pl.ds(pl.multiple_of(z * quarter, 16), quarter)
        for start in range(0, model, tile_d):
            cols = slice(start, start + tile_d)
            dsum[at, cols] = (
                dsum[at, cols].astype(f32) + landed[block, :, cols].astype(f32)).astype(bf16)

    def sum_tick(k):
        z_right = lines - 1 - k + o

        @pl.when(o <= k)
        def _():
            @pl.when(o > 0)
            def _():
                sum_pass(z_right, True).wait_recv()
                sum_add(z_right, z_right - o)

            @pl.when(o < k)
            def _():
                sum_pass(z_right + 1, True).wait_send()
            sum_pass(z_right, True).start()

        back = lines - 1 - o
        z_left = k - back

        @pl.when(back <= k)
        def _():
            @pl.when(back > 0)
            def _():
                sum_pass(z_left, False).wait_recv()
                sum_add(z_left, lines - o + z_left)

            @pl.when(back < k)
            def _():
                sum_pass(z_left - 1, False).wait_send()
            sum_pass(z_left, False).start()

    for t in range(2):
        for copy in c_tile(t):
            copy.start()
    weight_grads(2)
    sum_tick(0)
    for far in range(3, lines):
        down_step(far)

    @pl.loop(0, 8)
    def _(step):
        turn = step // 2
        j = pair_at(turn)
        slot = slot_of(step)
        pairing = lax.rem(step, 2) == 0

        @pl.when(step < 7)
        def _():
            c_start(step + 1)

        for k in range(1, lines - 1):
            @pl.when(step == min(1 + 3 * k, 7))
            def _():
                sum_tick(k)

        c_copy(step, 0).wait()

        for start in range(0, hidden, tile_f):
            size = min(tile_f, hidden - start)
            cols = slice(start, start + size)
            gate, up = gates(slot, cols)
            grad = lax.dot_general(cs[lax.rem(step, 2)], ws[2, cols, :], NT, preferred_element_type=f32)
            sg = sigmoid(gate)
            silu = gate * sg
            inner = (silu * up).astype(bf16)
            gate_grad = (grad * up * sg * (1.0 + gate * (1.0 - sg))).astype(bf16)
            up_grad = (grad * silu).astype(bf16)
            places = pl.ds(pl.multiple_of(slot * rows, rows), rows)
            for kind, (value, target) in enumerate(((gate_grad, gate_s), (up_grad, up_s), (inner, inner_s))):
                target[:, cols] = value
                if kind < 2:
                    acts_t[kind, cols, places] = value.T

        @pl.when(pairing & (step >= 4))
        def _():
            part_send(turn - 2).wait_send()

        place = jnp.where(pairing, lax.rem(turn, 2), 2)
        for start in range(0, model, tile_d):
            cols = slice(start, start + tile_d)
            part[place, 0, :, cols] = jnp.dot(
                inner_s[...], ws[2, :, cols], preferred_element_type=f32).astype(bf16)
            part[place, 1, :, cols] = (
                jnp.dot(gate_s[...], ws[0, :, cols], preferred_element_type=f32)
                + jnp.dot(up_s[...], ws[1, :, cols], preferred_element_type=f32)
            ).astype(bf16)

        @pl.when(pairing)
        def _():
            part_send(turn).start()

        @pl.when(jnp.logical_not(pairing))
        def _():
            part_send(turn).wait_recv()
            for a in range(2):
                for start in range(0, model, tile_d):
                    cols = slice(start, start + tile_d)
                    crecv[j, a, :, cols] = (
                        crecv[j, a, :, cols].astype(f32) + part[2, a, :, cols].astype(f32)
                    ).astype(bf16)

        @pl.when(step == 1)
        def _():
            for h in range(2):
                for copy in d_sends[h]:
                    copy.start()

        @pl.when(step == 3)
        def _():
            for copy in x_sends[0]:
                copy.start()

        @pl.when(step == 5)
        def _():
            for copy in y_sends[1]:
                copy.start()


    for h in range(2):
        j = 2 - h
        for a in range(2):
            d_sends[h][a].wait_recv()
            at = pl.ds(h * half, half)
            crecv[j, a, at, :] = (
                crecv[j, a, at, :].astype(f32) + drecv[a, at, :].astype(f32)).astype(bf16)
        for copy in (y_sends, x_sends)[h][h]:
            copy.start()
    weight_grads(0)
    weight_grads(1)
    out_copies = []
    for a, target in enumerate((out_ref, ngrad_ref)):
        for h in range(2):
            x_sends[h][a].wait_recv()
            y_sends[h][a].wait_recv()
        for n in range(model // tile_d):
            cols = slice(n * tile_d, (n + 1) * tile_d)
            if n >= 2:
                out_copies[-2].wait()
            outs[a, n % 2] = (
                crecv[0, a, :, cols].astype(f32)
                + nrecv[0, a, :, cols].astype(f32)
                + nrecv[1, a, :, cols].astype(f32)
            )
            copy = pltpu.make_async_copy(
                outs.at[a, n % 2], target.at[:, pl.ds(n * tile_d, tile_d)],
                out_sem.at[n, a])
            copy.start()
            out_copies.append(copy)
    steps = model // tile_d
    for a in range(2):
        for copy in out_copies[a * steps : (a + 1) * steps][-2:]:
            copy.wait()
    @pl.loop(0, lines)
    def _(z):
        @pl.when((o < lines - 1) & (z <= o))
        def _():
            down_pass(z, True).wait_send()

        @pl.when((o > 0) & (z >= o))
        def _():
            down_pass(z, False).wait_send()

    own_pair.wait_send()
    for h in range(2):
        own_x[h].wait_send()
        own_y[h].wait_send()
        for a in range(2):
            x_sends[h][a].wait_send()
            y_sends[h][a].wait_send()
            d_sends[h][a].wait_send()
    relay_x.wait_send()
    relay_y.wait_send()
    for j in (1, 2, 3):
        pair_of[j].wait_send()
    part_send(2).wait_send()
    part_send(3).wait_send()

    @pl.when(o > 0)
    def _():
        sum_pass(o, True).wait_recv()
        sum_add(o, 0)

    @pl.when(o < lines - 1)
    def _():
        sum_pass(o, False).wait_recv()
        sum_add(o, lines)

    keeps = [
        pltpu.make_async_copy(
            rows_of(o).at[:, pl.ds(q * width, width)], down_out.at[q], keep_sem.at[q])
        for q in range(parts)
    ]
    for copy in keeps:
        copy.start()

    @pl.when(o < lines - 1)
    def _():
        sum_pass(o + 1, True).wait_send()

    @pl.when(o > 0)
    def _():
        sum_pass(o - 1, False).wait_send()
    for copy in keeps:
        copy.wait()


def ffn_call_kernel(x_ref, w_ref, down_ref, *refs):
    ffn_kernel(x_ref, w_ref, down_ref, refs[:8], *refs[8:])


def ffn_plane(x_own, weights, down_own, c_rows):
    rows, model = x_own.shape
    lines, parts, _, quarter, width = weights.shape
    hidden = lines * quarter
    tile_w = min(256, width)
    sems = pltpu.SemaphoreType.DMA
    anywhere = pl.BlockSpec(memory_space=pl.ANY)
    return pl.pallas_call(
        ffn_call_kernel,
        out_shape=(
            jax.ShapeDtypeStruct((rows, model), f32),
            jax.ShapeDtypeStruct((rows, model), f32),
            jax.ShapeDtypeStruct(weights.shape, bf16),
            jax.ShapeDtypeStruct((parts, quarter, width), bf16),
        ),
        in_specs=[anywhere] * 11,
        out_specs=(anywhere,) * 4,
        scratch_shapes=[
            pltpu.VMEM((8, rows, model), bf16),
            pltpu.VMEM((2, rows, model), bf16),
            pltpu.VMEM((3, hidden, model), bf16),
            pltpu.VMEM((hidden, model), bf16),
            pltpu.VMEM((lines + 1, quarter, model), bf16),
            pltpu.VMEM((2, 2, rows, min(512, model)), f32),
            pltpu.VMEM((rows, hidden), bf16),
            pltpu.VMEM((rows, hidden), bf16),
            pltpu.VMEM((rows, hidden), bf16),
            pltpu.VMEM((3, hidden, 8 * rows), bf16),
            pltpu.VMEM((3, 2, rows, model), bf16),
            pltpu.VMEM((4, 2, rows, model), bf16),
            pltpu.VMEM((2, rows, model), bf16),
            pltpu.VMEM((2, 2, rows, model), bf16),
            pltpu.VMEM((2, hidden, tile_w), bf16),
            sems((10,)), sems((10,)), sems((4,)), sems((4,)), sems((12,)), sems((12,)),
            sems((2,)), sems((lines, parts)), sems((2, lines)), sems((2, 8)),
            sems((lines,)), sems((lines,)), sems((lines,)), sems((parts,)),
            sems((4, lines)), sems((parts,)), sems((4, 2)),
        ],
        compiler_params=pltpu.CompilerParams(
            collective_id=2, has_side_effects=True, vmem_limit_bytes=60 * 2**20),
        cost_estimate=pl.CostEstimate(flops=8 * 10**10, bytes_accessed=4 * 10**7, transcendentals=10**6),
        name="ffn_plane",
    )(x_own, weights, down_own, *c_rows)


def line_barrier(lines, others):
    o = lax.axis_index("z")
    barrier = pltpu.get_barrier_semaphore()
    mesh_id = pl.DeviceIdType.MESH

    @pl.when(o > 0)
    def _():
        pl.semaphore_signal(barrier, inc=1, device_id={"z": o - 1}, device_id_type=mesh_id)

    @pl.when(o < lines - 1)
    def _():
        pl.semaphore_signal(barrier, inc=1, device_id={"z": o + 1}, device_id_type=mesh_id)

    for target in others:
        pl.semaphore_signal(barrier, inc=1, device_id=target, device_id_type=mesh_id)
    peers = len(others) + (o > 0).astype(jnp.int32) + (o < lines - 1).astype(jnp.int32)
    pl.semaphore_wait(barrier, peers)


def line_copy(src, dst, send, recv, target):
    return pltpu.make_async_remote_copy(
        src_ref=src, dst_ref=dst, send_sem=send, recv_sem=recv,
        device_id=target, device_id_type=pl.DeviceIdType.MESH)


def pair_peers():
    x, core = lax.axis_index("x"), lax.axis_index("core")
    peers = [
        (x * 2 + 1 - core, {"core": 1 - core}),
        ((1 - x) * 2 + core, {"x": 1 - x}),
        ((1 - x) * 2 + 1 - core, {"x": 1 - x, "core": 1 - core}),
    ]
    return x * 2 + core, peers


class Swap:
    def __init__(self, pairs, send, recv, own):
        me, peers = pair_peers()
        self.own = [
            pltpu.make_async_copy(source.at[me], target(me), own.at[n])
            for n, (source, target) in enumerate(pairs)]
        self.away = [
            line_copy(source.at[place], target(me), send.at[n, d], recv.at[n, d], device)
            for n, (source, target) in enumerate(pairs) for d, (place, device) in enumerate(peers)]

    def start(self):
        for copy in self.away + self.own:
            copy.start()

    def wait(self):
        for copy in self.own:
            copy.wait()
        for copy in self.away:
            copy.wait_recv()
            copy.wait_send()


def gather_kernel(x_ref, o_ref, f_refs, w_refs, wb_ref, rows_ref, outs_ref, proj_refs, beta_ref,
                  pair_ref, down_ref,
                  xs, parts, stage, beta_stage, right_send, left_send, line_recv, pair_send, pair_recv,
                  part_right, part_left, part_recv, own_sem, row_sem, outs_sem, out_sem, beta_sem,
                  swap_send, swap_recv, swap_own):
    lines = xs.shape[0] // 2
    batches, rows, model = x_ref.shape
    o = lax.axis_index("z")
    i = lax.axis_index("y")
    line_barrier(lines, [other("y")] + [device for _, device in pair_peers()[1]])
    swap = Swap(
        [(f_refs[0], lambda place: pair_ref.at[place, 0]),
         (f_refs[1], lambda place: pair_ref.at[place, 1]),
         (f_refs[2], lambda place: down_ref.at[place])],
        swap_send, swap_recv, swap_own)

    def right(z, m):
        ref = xs.at[z * 2 + i, m]
        return line_copy(ref, ref, right_send.at[z, m], line_recv.at[z, m], {"z": o + 1})

    def left(z, m):
        ref = xs.at[z * 2 + i, m]
        return line_copy(ref, ref, left_send.at[z, m], line_recv.at[z, m], {"z": o - 1})

    def across(z, m):
        ref = xs.at[z * 2 + i, m]
        return line_copy(ref, ref, pair_send.at[z, m], pair_recv.at[z, m], other("y"))

    own = [
        pltpu.make_async_copy(x_ref, xs.at[o * 2 + i], own_sem.at[0]),
        pltpu.make_async_copy(o_ref, parts.at[o], own_sem.at[1]),
    ]

    def pass_part(z):
        ref = parts.at[z]
        return (line_copy(ref, ref, part_right.at[z], part_recv.at[z], {"z": o + 1}),
                line_copy(ref, ref, part_left.at[z], part_recv.at[z], {"z": o - 1}))

    for copy in own:
        copy.start()
    for copy in own:
        copy.wait()

    def outs(turn, slot):
        buffer = lax.rem(turn, 2)
        return [
            copy for m in range(batches) for copy in (
                pltpu.make_async_copy(stage.at[buffer, m], proj_refs[m].at[slot], out_sem.at[buffer, m]),
                pltpu.make_async_copy(beta_stage.at[buffer, m], beta_ref.at[m, slot], beta_sem.at[buffer, m]))
        ]

    def keep(slot, m):
        return pltpu.make_async_copy(xs.at[slot, m], rows_ref.at[m, slot], row_sem.at[slot, m])

    def keep_outs(z):
        return pltpu.make_async_copy(parts.at[z], outs_ref.at[z], outs_sem.at[z])

    def project(turn, slot):
        @pl.when(turn >= 2)
        def _():
            for copy in outs(turn, slot):
                copy.wait()
        for m in range(batches):
            keep(slot, m).start()
        x = xs[slot].reshape(batches * rows, model)
        buffer = lax.rem(turn, 2)
        width = w_refs[0].shape[1]
        for n, w_ref in enumerate(w_refs):
            stage[buffer, :, :, n * width : (n + 1) * width] = jnp.dot(
                x, w_ref[...], preferred_element_type=f32).reshape(batches, rows, width)
        beta_stage[buffer] = jnp.dot(
            x, wb_ref[...], preferred_element_type=f32).reshape(batches, rows, 128)
        for copy in outs(turn, slot):
            copy.start()

    def in_line(index):
        far = (index + 1) // 2
        side = 1 - 2 * lax.rem(index, 2)
        z = o + side * far
        return far, z, (z >= 0) & (z < lines)

    def first(index, turn):
        far, z, valid = in_line(index)

        @pl.when(valid)
        def _():
            for m in range(batches):
                @pl.when(far > 0)
                def _():
                    left(z, m).wait_recv()

                @pl.when((o < lines - 1) & (z <= o))
                def _():
                    right(z, m).start()

                @pl.when((o > 0) & (z >= o))
                def _():
                    left(z, m).start()

                across(z, m).start()
            project(turn, z * 2 + i)

        return turn + valid.astype(jnp.int32)

    swap.start()
    turn = lax.fori_loop(0, 2 * lines - 1, first, jnp.int32(0))

    def second(index, turn):
        far, z, valid = in_line(index)

        @pl.when(valid)
        def _():
            to_right, to_left = pass_part(z)

            @pl.when(far > 0)
            def _():
                to_left.wait_recv()

            @pl.when((o < lines - 1) & (z <= o))
            def _():
                to_right.start()

            @pl.when((o > 0) & (z >= o))
            def _():
                to_left.start()

            keep_outs(z).start()
            for m in range(batches):
                across(z, m).wait_recv()
            project(turn, z * 2 + 1 - i)

        return turn + valid.astype(jnp.int32)

    lax.fori_loop(0, 2 * lines - 1, second, turn)
    for turn in range(2 * lines - 2, 2 * lines):
        for copy in outs(turn, 0):
            copy.wait()

    @pl.loop(0, lines)
    def _(z):
        keep_outs(z).wait()

        @pl.when((o < lines - 1) & (z <= o))
        def _():
            pass_part(z)[0].wait_send()
            for m in range(batches):
                right(z, m).wait_send()

        @pl.when((o > 0) & (z >= o))
        def _():
            pass_part(z)[1].wait_send()
            for m in range(batches):
                left(z, m).wait_send()

        for m in range(batches):

            across(z, m).wait_send()
            for y in range(2):
                keep(z * 2 + y, m).wait()

    swap.wait()


def gather_call_kernel(x_ref, o_ref, *refs):
    gather_kernel(x_ref, o_ref, refs[:3], refs[3:7], refs[7], refs[8], refs[9], refs[10:12], *refs[12:])


def gather_project(x, w_out_part, ffn_parts, w_inner, w_beta):
    batches, rows, model = x.shape
    more = w_out_part.shape[1]
    lines = lax.axis_size("z")
    width = sum(w.shape[1] for w in w_inner)
    slots = 2 * lines
    sems = pltpu.SemaphoreType.DMA
    anywhere = pl.BlockSpec(memory_space=pl.ANY)
    pair = sems((lines, batches))
    ranks, quarter, share = ffn_parts[0].shape
    gathered, outs, *projected, beta, pair_parts, down_part = pl.pallas_call(
        gather_call_kernel,
        out_shape=(
            jax.ShapeDtypeStruct((batches, slots, rows, model), bf16),
            jax.ShapeDtypeStruct((lines, batches, more, model), bf16),
            *[jax.ShapeDtypeStruct((slots, rows, width), f32)] * batches,
            jax.ShapeDtypeStruct((batches, slots, rows, 128), f32),
            jax.ShapeDtypeStruct((ranks, 2, quarter, share), bf16),
            jax.ShapeDtypeStruct((ranks, quarter, share), bf16),
        ),
        in_specs=[anywhere] * 5 + [vmem()] * 5,
        out_specs=(anywhere,) * (5 + batches),
        scratch_shapes=[
            pltpu.VMEM((slots, batches, rows, model), bf16),
            pltpu.VMEM((lines, batches, more, model), bf16),
            pltpu.VMEM((2, batches, rows, width), f32),
            pltpu.VMEM((2, batches, rows, 128), f32),
            pair, pair, pair, pair, pair, sems((lines,)), sems((lines,)), sems((lines,)),
            sems((2,)), sems((slots, batches)), sems((lines,)), sems((2, batches)), sems((2, batches)),
            sems((3, 3)), sems((3, 3)), sems((3,)),
        ],
        compiler_params=pltpu.CompilerParams(
            collective_id=1, has_side_effects=True, vmem_limit_bytes=40 * 2**20),
        cost_estimate=pl.CostEstimate(flops=10**11, bytes_accessed=4 * 10**7, transcendentals=0),
        name="gather_project",
    )(x, w_out_part, *ffn_parts, *w_inner, w_beta)
    total = slots * rows
    return (gathered.reshape(batches, total, model), outs,
            [wide.reshape(total, width) for wide in projected],
            beta.reshape(batches, total, 128), pair_parts, down_part)


def scatter_kernel(w_refs, g_ref, gb_ref, o_ref, inner_ref, wb_ref, small_ref, gains_ref, pair_ref, down_ref,
                   out_ref, small_out, outs_ref, inner_out, pair_out, down_out,
                   gs, bs, ysend, yrecv, from_left, from_right, part_sum, part_left, part_right, outs_s, inner_s, inner_r, small_s, small_r, gains_r,
                   pair_send, pair_recv, right_send, left_send, right_recv, left_recv, g_sem,
                   sum_send, sum_recv, outs_send, outs_recv, gain_send, gain_recv, part_sems, swap_send, swap_recv, swap_own, sum_sem):
    batches, rows, width = gs.shape
    lines = yrecv.shape[0]
    model = yrecv.shape[3]
    o = lax.axis_index("z")
    i = lax.axis_index("y")
    core = lax.axis_index("core")
    me = lax.axis_index("x") * 2 + core
    tile = min(512, model)
    diagonal = {"x": 1 - lax.axis_index("x"), "core": 1 - core}
    slots = 2 * lines
    mine = o * 2 + i
    peers = []
    for d in range(1, slots):
        place = lax.rem(mine + d, slots)
        peers.append((place, {"z": place // 2, "y": lax.rem(place, 2)}))
    barrier = pltpu.get_barrier_semaphore()
    greeted = [other("core"), other("x"), diagonal] + [device for _, device in peers]
    for device in greeted:
        pl.semaphore_signal(barrier, inc=1, device_id=device, device_id_type=pl.DeviceIdType.MESH)
    pl.semaphore_wait(barrier, len(greeted))
    gain_copies = [
        line_copy(gains_ref.at[place], gains_r.at[mine], gain_send.at[d], gain_recv.at[d], device)
        for d, (place, device) in enumerate(peers)
    ]
    for copy in gain_copies:
        copy.start()

    inner_pair = line_copy(inner_ref.at[1 - core], inner_r.at[0], sum_send.at[0], sum_recv.at[0], other("core"))
    inner_across = line_copy(inner_s, inner_r.at[1], sum_send.at[1], sum_recv.at[1], other("x"))
    inner_back = line_copy(inner_s, inner_out.at[core], sum_send.at[2], sum_recv.at[2], other("core"))
    small_pair = line_copy(small_s.at[0], small_r.at[0], sum_send.at[3], sum_recv.at[3], other("core"))
    small_across = line_copy(small_s.at[1], small_r.at[1], sum_send.at[4], sum_recv.at[4], other("x"))
    inner_own = pltpu.make_async_copy(inner_ref.at[core], inner_s, sum_sem.at[0])
    inner_keep = pltpu.make_async_copy(inner_s, inner_out.at[core], sum_sem.at[1])
    outs_keep = pltpu.make_async_copy(outs_s, outs_ref.at[me], sum_sem.at[2])
    outs_away = [
        line_copy(outs_s, outs_ref.at[me], outs_send.at[n], outs_recv.at[n], target)
        for n, target in enumerate((other("core"), other("x"), diagonal))
    ]
    swap = Swap(
        [(pair_ref, lambda place: pair_out.at[place]), (down_ref, lambda place: down_out.at[place])],
        swap_send, swap_recv, swap_own)
    swap.start()
    inner_pair.start()
    inner_own.start()

    def add_into(target, other_ref):
        height = target.shape[0]
        step = next(size for size in range(min(128, height), 0, -16) if height % size == 0)

        @pl.loop(0, height // step)
        def _(n):
            at = pl.ds(pl.multiple_of(n * step, step), step)
            target[at, :] = (target[at, :].astype(f32) + other_ref[at, :].astype(f32)).astype(target.dtype)

    def target(index):
        far = lines - 1 - index // 2
        side = 1 - 2 * lax.rem(index, 2)
        z = o + side * far
        return far, z, (z >= 0) & (z < lines) & ((far > 0) | (side > 0))

    def load(z, y):
        slot = z * 2 + y
        return (pltpu.make_async_copy(g_ref.at[:, slot], gs, g_sem.at[0]),
                pltpu.make_async_copy(gb_ref.at[:, slot], bs, g_sem.at[1]))

    def partial_rows(z, y, store):
        for copy in load(z, y):
            copy.start()
        for copy in load(z, y):
            copy.wait()
        for m in range(batches):
            g = gs[m]
            b = bs[m]
            for start in range(0, model, tile):
                cols = slice(start, start + tile)
                value = lax.dot_general(b, wb_ref[cols, :], NT, preferred_element_type=f32)
                for n, w_ref in enumerate(w_refs):
                    part = g[:, n * w_ref.shape[1] : (n + 1) * w_ref.shape[1]]
                    value = value + lax.dot_general(part, w_ref[cols, :], NT, preferred_element_type=f32)
                store(m, cols, value)

    def across(z, m):
        return line_copy(ysend.at[z, m], yrecv.at[z, m], pair_send.at[z, m], pair_recv.at[z, m], other("y"))

    def right(z, m):
        return line_copy(yrecv.at[z, m], from_left.at[z, m], right_send.at[z, m], right_recv.at[z, m], {"z": o + 1})

    def left(z, m):
        return line_copy(yrecv.at[z, m], from_right.at[z, m], left_send.at[z, m], left_recv.at[z, m], {"z": o - 1})

    def across_partial(z):
        def store(m, cols, value):
            ysend[z, m, :, cols] = value.astype(bf16)
        partial_rows(z, 1 - i, store)

    def pass_part(z):
        return (line_copy(part_sum.at[z], part_left.at[z], part_sems.at[0, z], part_sems.at[1, z], {"z": o + 1}),
                line_copy(part_sum.at[z], part_right.at[z], part_sems.at[2, z], part_sems.at[3, z], {"z": o - 1}))

    def part_round():
        @pl.loop(0, 2 * lines)
        def _(index):
            far, z, valid = target(index)

            @pl.when(valid & (far > 0))
            def _():
                to_right, to_left = pass_part(z)

                @pl.when((z > o) & (o > 0))
                def _():
                    to_right.wait_recv()
                    add_into(part_sum.at[z], part_left.at[z])

                @pl.when((z < o) & (o < lines - 1))
                def _():
                    to_left.wait_recv()
                    add_into(part_sum.at[z], part_right.at[z])

                @pl.when(z > o)
                def _():
                    to_right.start()

                @pl.when(z < o)
                def _():
                    to_left.start()

        to_right, to_left = pass_part(o)
        outs_s[...] = part_sum[o]

        @pl.when(o > 0)
        def _():
            to_right.wait_recv()
            add_into(outs_s, part_left.at[o])

        @pl.when(o < lines - 1)
        def _():
            to_left.wait_recv()
            add_into(outs_s, part_right.at[o])
        outs_keep.start()
        for copy in outs_away:
            copy.start()

    def side_work():
        for z in range(lines):
            part_sum[z] = o_ref[z]
        part_round()
        inner_own.wait()
        inner_pair.wait_recv()
        add_into(inner_s, inner_r.at[0])
        inner_across.start()
        gains_r[mine] = gains_ref[mine]
        for copy in gain_copies:
            copy.wait_recv()
        tail = small_ref.shape[0]
        small_s[0, :tail] = small_ref[...]
        small_s[0, tail:] = jnp.sum(gains_r[...], axis=0)
        small_pair.start()

    def turn(index, before):
        far, z, valid = target(index)
        last = index == 2 * lines
        valid = valid & (index < 2 * lines)
        ready = (valid | last) & (before >= 0)

        @pl.when(valid)
        def _():
            across_partial(z)

        @pl.when(ready)
        def _():
            for m in range(batches):
                across(before, m).wait_recv()

        @pl.when(valid)
        def _():
            for m in range(batches):
                across(z, m).start()

        @pl.when(valid & (before < 0))
        def _():
            side_work()

        @pl.when(ready)
        def _():
            z = before

            def store(m, cols, value):
                yrecv[z, m, :, cols] = (yrecv[z, m, :, cols].astype(f32) + value).astype(bf16)
            partial_rows(z, i, store)
            for m in range(batches):
                @pl.when((z > o) & (o > 0))
                def _():
                    right(z, m).wait_recv()
                    add_into(yrecv.at[z, m], from_left.at[z, m])

                @pl.when(z > o)
                def _():
                    right(z, m).start()

                @pl.when((z < o) & (o < lines - 1))
                def _():
                    left(z, m).wait_recv()
                    add_into(yrecv.at[z, m], from_right.at[z, m])

                @pl.when(z < o)
                def _():
                    left(z, m).start()

        return jnp.where(valid, z, before)

    lax.fori_loop(0, 2 * lines + 1, turn, jnp.int32(-1))

    inner_across.wait_recv()
    inner_across.wait_send()
    add_into(inner_s, inner_r.at[1])
    inner_back.start()
    inner_keep.start()
    small_pair.wait_recv()
    small_s[1] = small_s[0] + small_r[0]
    small_across.start()

    for m in range(batches):
        out_ref[m] = yrecv[o, m].astype(f32)

        @pl.when(o > 0)
        def _():
            right(o, m).wait_recv()
            out_ref[m] += from_left[o, m].astype(f32)

        @pl.when(o < lines - 1)
        def _():
            left(o, m).wait_recv()
            out_ref[m] += from_right[o, m].astype(f32)

    @pl.loop(0, lines)
    def _(z):
        for m in range(batches):
            across(z, m).wait_send()

            @pl.when(z > o)
            def _():
                right(z, m).wait_send()

            @pl.when(z < o)
            def _():
                left(z, m).wait_send()

        @pl.when(z > o)
        def _():
            pass_part(z)[0].wait_send()

        @pl.when(z < o)
        def _():
            pass_part(z)[1].wait_send()

    small_across.wait_recv()
    small_out[...] = small_s[1] + small_r[1]
    for copy in gain_copies:
        copy.wait_send()
    inner_pair.wait_send()
    small_pair.wait_send()
    small_across.wait_send()
    inner_back.wait_recv()
    inner_back.wait_send()
    inner_keep.wait()
    outs_keep.wait()
    swap.wait()
    for copy in outs_away:
        copy.wait_recv()
        copy.wait_send()


def scatter_call_kernel(*refs):
    scatter_kernel(refs[:4], *refs[4:])


def scatter_rows(grads, beta_grads, out_grads, inner_grads, w_inner, w_beta, small, gains,
                 pair_grads, down_grads):
    batches, total, width = grads.shape
    model = w_inner[0].shape[0]
    lines = lax.axis_size("z")
    slots = 2 * lines
    rows = total // slots
    more = out_grads.shape[1]
    sems = pltpu.SemaphoreType.DMA
    anywhere = pl.BlockSpec(memory_space=pl.ANY)
    slab = pltpu.VMEM((lines, batches, rows, model), bf16)
    part = pltpu.VMEM((lines, more, model), bf16)
    half = inner_grads.shape[1:]
    flat = (small.shape[0] + gains.shape[1], 128)
    return pl.pallas_call(
        scatter_call_kernel,
        out_shape=(
            jax.ShapeDtypeStruct((batches, rows, model), f32),
            jax.ShapeDtypeStruct(flat, f32),
            jax.ShapeDtypeStruct((4, more, model), bf16),
            jax.ShapeDtypeStruct(inner_grads.shape, bf16),
            jax.ShapeDtypeStruct(pair_grads.shape, bf16),
            jax.ShapeDtypeStruct(down_grads.shape, bf16),
        ),
        in_specs=[vmem()] * 4 + [anywhere, anywhere, vmem(), anywhere, vmem(), vmem(), vmem(), anywhere, anywhere],
        out_specs=(vmem(), vmem()) + (anywhere,) * 4,
        scratch_shapes=[
            pltpu.VMEM((batches, rows, width), bf16),
            pltpu.VMEM((batches, rows, 128), bf16),
            slab, slab, slab, slab, part, part, part,
            pltpu.VMEM((more, model), bf16),
            pltpu.VMEM(half, bf16),
            pltpu.VMEM((2, *half), bf16),
            pltpu.VMEM((2, *flat), f32),
            pltpu.VMEM((2, *flat), f32),
            pltpu.VMEM(gains.shape, f32),
            sems((lines, batches)), sems((lines, batches)), sems((lines, batches)),
            sems((lines, batches)), sems((lines, batches)), sems((lines, batches)),
            sems((2,)), sems((5,)), sems((5,)), sems((3,)), sems((3,)), sems((slots,)), sems((slots,)), sems((4, lines)),
            sems((2, 3)), sems((2, 3)), sems((2,)), sems((3,)),
        ],
        compiler_params=pltpu.CompilerParams(
            collective_id=3, has_side_effects=True, vmem_limit_bytes=58 * 2**20),
        cost_estimate=pl.CostEstimate(flops=7 * 10**10, bytes_accessed=4 * 10**7, transcendentals=0),
        name="scatter_rows",
    )(*w_inner, grads.reshape(batches, slots, rows, width),
      beta_grads.reshape(batches, slots, rows, 128), out_grads, inner_grads, w_beta, small, gains,
      pair_grads, down_grads)


def tensor_peers(slots):
    mine = lax.axis_index("z") * 2 + lax.axis_index("y")
    places = [lax.rem(mine + d, slots) for d in range(1, slots)]
    return mine, [(place, {"z": place // 2, "y": lax.rem(place, 2)}) for place in places]


def greet(devices):
    barrier = pltpu.get_barrier_semaphore()
    for device in devices:
        pl.semaphore_signal(barrier, inc=1, device_id=device, device_id_type=pl.DeviceIdType.MESH)
    pl.semaphore_wait(barrier, len(devices))


def attend_kernel(x_ref, low_first, low_second, gain_ref, *refs):
    pieces, refs = refs[:8], refs[8:]
    hidden_ref, normed_ref, w_ref, heads_ref, ws, heads, send, recv, sem, own_sem = refs
    slots = heads.shape[1]
    mine, peers = tensor_peers(slots)
    greet([device for _, device in peers])
    lows = (low_first, low_second)
    away = [
        line_copy(low.at[place], heads.at[m, mine], send.at[m, d], recv.at[m, d], device)
        for d, (place, device) in enumerate(peers) for m, low in enumerate(lows)
    ]
    for copy in away:
        copy.start()
    own = [pltpu.make_async_copy(low.at[mine], heads.at[m, mine], own_sem.at[m]) for m, low in enumerate(lows)]
    for copy in own:
        copy.start()
    x = lax.axis_index("x")
    core = lax.axis_index("core")
    y = lax.axis_index("y")
    copies = []
    for n, piece in enumerate(pieces):
        far_y, far_x, far_core = n // 4, n // 2 % 2, n % 2
        column = 1 - y if far_y else y
        quarter = (1 - x if far_x else x) * 2 + (1 - core if far_core else core)
        copies.append(pltpu.make_async_copy(piece, ws.at[:, column, quarter], sem.at[n]))
    for copy in copies:
        copy.start()
    for copy in copies + own:
        copy.wait()
    keep = pltpu.make_async_copy(ws, w_ref, own_sem.at[2])
    keep.start()
    for copy in away:
        copy.wait_recv()
    keep_heads = pltpu.make_async_copy(heads, heads_ref, own_sem.at[3])
    keep_heads.start()
    model = x_ref.shape[1]
    tile = min(512, model)
    width = heads.shape[3]
    squares = 0.0
    for start in range(0, model, tile):
        cols = slice(start, start + tile)
        total = x_ref[:, cols].astype(f32)
        for t in range(slots):
            left = jnp.concatenate([heads[0, t], heads[1, t]], axis=0)
            total = total + jnp.dot(
                left, ws[t // 2, t % 2, :, :, cols].reshape(width, tile), preferred_element_type=f32)
        hidden_ref[:, cols] = total
        squares = squares + jnp.sum(total * total, axis=-1, keepdims=True)
    scale = lax.rsqrt(squares / model + epsilon)
    for start in range(0, model, tile):
        cols = slice(start, start + tile)
        normed_ref[:, cols] = (hidden_ref[:, cols] * scale * gain_ref[:, cols]).astype(bf16)
    keep.wait()
    keep_heads.wait()
    for copy in away:
        copy.wait_send()


def attend(x, lows, gain, pieces):
    rows, model = x.shape
    lines, part, _ = pieces[0].shape
    full = (lines, 2, 4, part, model)
    heads = (2, *lows[0].shape)
    slots = 2 * lines
    anywhere = pl.BlockSpec(memory_space=pl.ANY)
    sems = pltpu.SemaphoreType.DMA
    return pl.pallas_call(
        attend_kernel,
        out_shape=(
            jax.ShapeDtypeStruct((rows, model), f32),
            jax.ShapeDtypeStruct((rows, model), bf16),
            jax.ShapeDtypeStruct(full, bf16),
            jax.ShapeDtypeStruct(heads, bf16),
        ),
        in_specs=[vmem(), anywhere, anywhere, vmem()] + [anywhere] * 8,
        out_specs=(vmem(), vmem(), anywhere, anywhere),
        scratch_shapes=[
            pltpu.VMEM(full, bf16), pltpu.VMEM(heads, bf16),
            sems((2, slots)), sems((2, slots)), sems((8,)), sems((4,))],
        compiler_params=pltpu.CompilerParams(
            collective_id=4, has_side_effects=True, vmem_limit_bytes=32 * 2**20),
        cost_estimate=pl.CostEstimate(flops=3 * 10**10, bytes_accessed=2 * 10**7, transcendentals=0),
        name="attend",
    )(x, *lows, gain, *pieces)


def attend_back_kernel(hidden_ref, ffn_ref, grad_ref, c_ref, gain_ref, w_ref, heads,
                       result_ref, hgrad_ref, back_first, back_second, left_mine, left_theirs,
                       right_mine, right_theirs, gain_out, low, wgrad, wrecv, backs, send, recv, sem, core_sem):
    rows, model = hidden_ref.shape
    half = rows // 2
    tile = min(512, model)
    slots = heads.shape[1]
    width = heads.shape[3]
    mine, peers = tensor_peers(slots)
    greet([device for _, device in peers] + [other("core")])
    squares, dots = 0.0, 0.0
    for start in range(0, model, tile):
        cols = slice(start, start + tile)
        hidden = hidden_ref[:, cols]
        squares = squares + jnp.sum(hidden * hidden, axis=-1, keepdims=True)
        dots = dots + jnp.sum(hidden * grad_ref[:, cols] * gain_ref[:, cols], axis=-1, keepdims=True)
    scale = lax.rsqrt(squares / model + epsilon)
    pull = scale * scale * scale * (dots / model)
    for start in range(0, model, tile):
        cols = slice(start, start + tile)
        hidden = hidden_ref[:, cols]
        grad = grad_ref[:, cols]
        result_ref[:, cols] = hidden + ffn_ref[:, cols]
        gain_out[:, cols] = jnp.sum(grad * hidden * scale, axis=0, keepdims=True)
        hgrad = c_ref[:, cols].astype(f32) + scale * (grad * gain_ref[:, cols]) - hidden * pull
        hgrad_ref[:, cols] = hgrad
        low[:, cols] = hgrad.astype(bf16)

    outs = (back_first, back_second)

    def away(m, d):
        place = lax.rem(mine + d, slots)
        return line_copy(backs.at[m, d], outs[m].at[mine], send.at[m, d], recv.at[m, d],
                         {"z": place // 2, "y": lax.rem(place, 2)})

    @pl.loop(0, slots)
    def _(step):
        d = slots - 1 - step
        place = lax.rem(mine + d, slots)
        back = lax.dot_general(
            low[...], w_ref[place // 2, lax.rem(place, 2)].reshape(width, model), NT,
            preferred_element_type=f32)
        for m in range(2):
            backs[m, d] = back[m * half : (m + 1) * half].astype(bf16)

            @pl.when(d > 0)
            def _():
                away(m, d).start()

            @pl.when(d == 0)
            def _():
                pltpu.make_async_copy(backs.at[m, 0], outs[m].at[mine], sem.at[2 + m]).start()

    for t in range(slots):
        left = jnp.concatenate([heads[0, t], heads[1, t]], axis=0)
        for start in range(0, model, tile):
            cols = slice(start, start + tile)
            value = lax.dot_general(
                left, low[:, cols], (((0,), (0,)), ((), ())), preferred_element_type=f32
            ).astype(bf16).reshape(2, 2, width // 4, tile)
            for c in range(2):
                wgrad[c, :, t % 2, t // 2, :, cols] = value[:, c]
    core = lax.axis_index("core")
    to_pair = line_copy(wgrad.at[1 - core], wrecv, core_sem.at[0], core_sem.at[1], other("core"))
    to_pair.start()
    to_pair.wait_recv()
    lines = wgrad.shape[3]
    for far_x in range(2):
        for far_y in range(2):
            @pl.loop(0, lines)
            def _(z):
                wrecv[far_x, far_y, z] = (
                    wrecv[far_x, far_y, z].astype(f32) + wgrad[core, far_x, far_y, z].astype(f32)
                ).astype(bf16)
    x, y = lax.axis_index("x"), lax.axis_index("y")
    wide = model // 2
    keeps = [
        pltpu.make_async_copy(source.at[..., pl.ds(start, wide)], target, sem.at[4 + n])
        for n, (source, start, target) in enumerate((
            (wrecv.at[x], 0, left_mine), (wrecv.at[1 - x], 0, left_theirs),
            (wrecv.at[:, y], wide, right_mine), (wrecv.at[:, 1 - y], wide, right_theirs)))
    ]
    for copy in keeps:
        copy.start()
    for copy in keeps:
        copy.wait()
    to_pair.wait_send()
    for m in range(2):
        pltpu.make_async_copy(backs.at[m, 0], outs[m].at[mine], sem.at[2 + m]).wait()
        for d in range(1, slots):
            away(m, d).wait_recv()
            away(m, d).wait_send()


def attend_back(hidden, ffn_out, normed_grad, c_rows, gain, w_full, heads):
    rows, model = hidden.shape
    wide = jax.ShapeDtypeStruct((rows, model), f32)
    lines, _, _, part, _ = w_full.shape
    share = (2, 2, lines, part, model)
    slots = 2 * lines
    back = jax.ShapeDtypeStruct(heads.shape[1:], bf16)
    anywhere = pl.BlockSpec(memory_space=pl.ANY)
    sems = pltpu.SemaphoreType.DMA
    return pl.pallas_call(
        attend_back_kernel,
        out_shape=(
            wide, wide, back, back,
            *[jax.ShapeDtypeStruct((2, lines, part, model // 2), bf16)] * 4,
            jax.ShapeDtypeStruct((1, model), f32),
        ),
        in_specs=[vmem()] * 7,
        out_specs=(vmem(),) * 2 + (anywhere,) * 6 + (vmem(),),
        scratch_shapes=[
            pltpu.VMEM((rows, model), bf16), pltpu.VMEM((2, *share), bf16), pltpu.VMEM(share, bf16),
            pltpu.VMEM(heads.shape, bf16), sems((2, slots)), sems((2, slots)), sems((8,)), sems((2,))],
        compiler_params=pltpu.CompilerParams(
            collective_id=5, has_side_effects=True, vmem_limit_bytes=48 * 2**20),
        cost_estimate=pl.CostEstimate(flops=3 * 10**10, bytes_accessed=4 * 10**7, transcendentals=0),
        name="attend_back",
    )(hidden, ffn_out, normed_grad, c_rows, gain, w_full, heads)


def root_scale(row_values, gain_vector):
    row_scale = lax.rsqrt(jnp.mean(row_values * row_values, axis=-1, keepdims=True) + epsilon)
    return (row_values * row_scale * gain_vector, row_scale)


def norm_backward(row_values, row_scale, gain_vector, normed_grad):
    weighted = normed_grad * gain_vector
    rows_grad = row_scale * weighted - row_values * row_scale * row_scale * row_scale * jnp.mean(
        weighted * row_values, axis=-1, keepdims=True
    )
    gain_grad = jnp.sum(normed_grad * row_values * row_scale, axis=tuple(range(row_values.ndim - 1)))
    return (rows_grad, gain_grad)


DP = ("x", "core")
TP = ("z", "y")


def gather(x, axis_name, axis=0):
    return lax.all_gather(x, axis_name, axis=axis, tiled=True)


def scatter_sum(x, axis_name, axis=0):
    return lax.psum_scatter(
        x.astype(bf16), axis_name, scatter_dimension=axis, tiled=True
    ).astype(f32)


def dot(a, b):
    return jnp.dot(a, b, preferred_element_type=f32)


def dot_nt(a, b):
    return jnp.einsum("tk,nk->tn", a, b, preferred_element_type=f32)


def dot_tn(a, b):
    return jnp.einsum("tm,tn->mn", a, b, preferred_element_type=f32)


def exchange(x, axis_name, distance=1):
    size = lax.axis_size(axis_name)
    return lax.ppermute(x, axis_name, [(i, i ^ distance) for i in range(size)])


def pick(x, index, axis):
    return lax.dynamic_index_in_dim(x, index, axis, keepdims=False)


def after(x, *others):
    return lax.optimization_barrier((x, *others))[0]


def add_low(x, y):
    return (x.astype(f32) + y.astype(f32)).astype(bf16)


def halve_sum(grad, axis_name):
    me = lax.axis_index(axis_name)
    return add_low(pick(grad, me, 0), exchange(pick(grad, 1 - me, 0), axis_name))


def feed_forward_groups(normed, cotangents, w_gate, w_up, w_down):
    gate_full = gather(w_gate, DP)
    up_full = gather(w_up, DP)
    down_full = gather(w_down, DP, 1)
    outs, normed_grads, inner_rows, gate_grads, up_grads, rows, grad_rows = [], [], [], [], [], [], []
    for m in range(normed.shape[0]):
        rows.append(gather(normed[m], TP))
        grad_rows.append(gather(cotangents[m], TP))
        gate_values = dot(rows[m], gate_full)
        up_values = dot(rows[m], up_full)
        sigmoid_gate = jax.nn.sigmoid(gate_values)
        silu_gate = gate_values * sigmoid_gate
        inner = (silu_gate * up_values).astype(bf16)
        inner_grad = dot_nt(grad_rows[m], down_full)
        gate_grad = (
            inner_grad * up_values * sigmoid_gate * (1.0 + gate_values * (1.0 - sigmoid_gate))
        ).astype(bf16)
        up_grad = (inner_grad * silu_gate).astype(bf16)
        normed_grads.append(scatter_sum(dot_nt(gate_grad, gate_full) + dot_nt(up_grad, up_full), TP))
        outs.append(scatter_sum(dot(inner, down_full), TP))
        inner_rows.append(inner)
        gate_grads.append(gate_grad)
        up_grads.append(up_grad)
    grad_all = jnp.concatenate(grad_rows)
    rows_all = jnp.concatenate(rows)
    gate_share = scatter_sum(dot_tn(rows_all, jnp.concatenate(gate_grads)), DP)
    up_share = scatter_sum(dot_tn(rows_all, jnp.concatenate(up_grads)), DP)
    down_share = scatter_sum(dot_tn(jnp.concatenate(inner_rows), grad_all), DP, 1)
    return jnp.stack(outs), jnp.stack(normed_grads), (gate_share, up_share, down_share)


def per_device(
    inputs,
    lengths,
    norm_gain,
    ffn_gain,
    w_query,
    w_key,
    w_value,
    w_gate_out,
    w_beta,
    conv_weight,
    head_gain,
    w_out,
    w_gate,
    w_up,
    w_down,
    cotangent,
):
    batches = range(inputs.shape[0])
    local_width = w_query.shape[1]
    heads = w_beta.shape[1]
    devices = lax.axis_size(TP)
    planar = all(lax.axis_size(name) == 2 for name in ("x", "core", "y"))
    w_parts = (w_query, w_key, w_value, w_gate_out)
    w_inner = jnp.concatenate(w_parts, axis=1)
    w_beta_wide = jnp.pad(w_beta, ((0, 0), (0, 128 - heads)))
    taps = conv_weight.astype(f32).reshape(-1, local_width)
    gain_heads = head_gain.astype(f32)
    gains = gather(jnp.stack([norm_gain, ffn_gain]), DP, 1)
    gain_one, gain_two = gains[0].astype(f32), gains[1].astype(f32)
    rows_in = inputs.astype(f32)
    normed_one, scale_one = root_scale(rows_in, gain_one)
    normed_one = normed_one.astype(bf16)

    def run_mixer(m, wide, logits):
        low, *kept = mixer_forward(lengths[m, 0], wide, logits, taps, gain_heads, exact=False)
        return low, kept

    def back_mixer(m, wide, logits, grad, kept):
        return mixer_backward(
            lengths[m, 0], wide, logits, taps, gain_heads, grad, kept, exact=False)

    if planar:
        count = rows_in.shape[0] * rows_in.shape[1]
        model = rows_in.shape[2]
        ranks = lax.axis_size(DP)
        ffn_parts = [
            w.reshape(ranks, -1, w.shape[1]) for w in after((w_gate.T, w_up.T, w_down), gains)]
        c_rows = [None] * 8
        c_rows[0] = after(cotangent.reshape(count, model), gains)
        c_rows[4] = exchange(c_rows[0], "core")
        out_shares = pick(
            w_out.reshape(lax.axis_size(DP), len(batches), -1, model), lax.axis_index(DP), 0)
        gathered_one, out_own, projected, beta_logits, own_weights, own_down = gather_project(
            normed_one, out_shares, ffn_parts, w_parts, w_beta_wide)
        early = after(c_rows[0], gathered_one)
        c_rows[1] = exchange(early, "x")
        weights = gather(own_weights[None], "z")
        c_rows[2] = exchange(early, "y")
        out_own = out_own.reshape(out_own.shape[0], -1, model)
        out_y = exchange(out_own, "y")
        out_x = exchange(out_own, "x")
    else:
        gathered_one = jnp.stack([gather(normed_one[m], TP) for m in batches])
        projected = [dot(gathered_one[m], w_inner) for m in batches]
        beta_logits = [dot(gathered_one[m], w_beta_wide) for m in batches]
        out_full = gather(w_out, TP)
    token_heads, saved = [], []
    for m in batches:
        low, kept = run_mixer(m, projected[m], beta_logits[m])
        saved.append(kept)
        if planar and m == 0:
            out_y, c_rows[1], c_rows[2] = after((out_y, c_rows[1], c_rows[2]), low)
            out_xy = exchange(out_y, "x")
            c_rows[3] = exchange(c_rows[1], "y")
            c_rows[5] = exchange(c_rows[1], "core")
            c_rows[6] = exchange(c_rows[2], "core")
            projected[1] = after(projected[1], out_y, c_rows[2])
        low = low.reshape(devices, -1, local_width)
        if not planar:
            low = lax.all_to_all(low, TP, split_axis=0, concat_axis=0, tiled=True)
        token_heads.append(low)
    if planar:
        out_x, out_xy, c_rows[3] = after((out_x, out_xy, c_rows[3]), low)
        out_pieces = []
        for piece in (out_own, out_x, out_y, out_xy):
            out_pieces += [piece, exchange(piece, "core")]
        c_rows[7] = exchange(c_rows[3], "core")
        hidden, normed_two, out_full, token_heads = attend(
            inputs.reshape(count, model), token_heads, gain_two[None], out_pieces)
        ffn_out, normed_grad, weight_grads, down_grad = ffn_plane(normed_two, weights, own_down, c_rows)
        result_rows, hidden_grad, *mixed_grads, left, left_away, right, right_away, gain_two_sum = attend_back(
            hidden, ffn_out, normed_grad, c_rows[0], gain_two[None], out_full, token_heads)
        weight_grads = after(weight_grads, left)
        own_grads = lax.psum_scatter(weight_grads, "z", scatter_dimension=0, tiled=True)
        gain_two_sum = gain_two_sum[0]
        result_rows = result_rows.reshape(rows_in.shape)
        hidden_grad = hidden_grad.reshape(rows_in.shape)
    else:
        heads_rows = [
            block.swapaxes(0, 1).reshape(-1, devices * local_width) for block in token_heads]
        hidden = rows_in + jnp.stack([dot(rows, out_full) for rows in heads_rows])
        normed_two, scale_two = root_scale(hidden, gain_two)
        ffn_out, normed_grad, (gate_share, up_share, down_share) = feed_forward_groups(
            normed_two.astype(bf16), cotangent, w_gate, w_up, w_down)
        result_rows = hidden + ffn_out
        norm_grad, gain_two_sum = norm_backward(hidden, scale_two, gain_two, normed_grad)
        hidden_grad = cotangent.astype(f32) + norm_grad
        attended_low = hidden_grad.astype(bf16)
        mixed_grads = [
            dot_nt(attended_low[m], out_full).astype(bf16)
            .reshape(-1, devices, local_width).swapaxes(0, 1) for m in batches]
        out_grad = dot_tn(
            jnp.concatenate(heads_rows), jnp.concatenate(list(attended_low))).astype(bf16)
    if not planar:
        mixed_grads = [
            lax.all_to_all(grad, TP, split_axis=0, concat_axis=0, tiled=True)
            for grad in mixed_grads]
    mixed_grads = [grad.reshape(-1, local_width) for grad in mixed_grads]
    if planar:
        left = add_low(left, exchange(left_away, "x"))
        right = add_low(right, exchange(right_away, "y"))
    projected_low, beta_low = [], []
    taps_sum, heads_sum = 0.0, 0.0
    for m in batches:
        if planar and m > 0:
            mixed_grads[m] = after(mixed_grads[m], left, right)
        projected_grad, beta_grad, taps_part, heads_part = back_mixer(
            m, projected[m], beta_logits[m], mixed_grads[m], saved[m])
        taps_sum = taps_sum + taps_part
        heads_sum = heads_sum + heads_part
        projected_low.append(projected_grad)
        beta_low.append(beta_grad)
    projected_low = jnp.stack(projected_low)
    beta_low = jnp.stack(beta_low)
    if planar:
        left, right = halve_sum(left, "y"), halve_sum(right, "x")
        projected_low = after(projected_low, left, right)
        out_grad = jnp.concatenate([left, right], axis=2)
    tokens = gathered_one.reshape(-1, gathered_one.shape[2])
    inner_sum = dot_tn(tokens, projected_low.reshape(-1, 4 * local_width))
    beta_sum = dot_tn(tokens, beta_low.reshape(-1, 128)[:, :heads])
    gain_one_sum = (
        sum(
            jnp.sum(inner_sum[:, n * local_width : (n + 1) * local_width] * w.astype(f32), axis=1)
            for n, w in enumerate(w_parts))
        + jnp.sum(beta_sum * w_beta.astype(f32), axis=1)
    ) / gain_one
    gain_parts = jnp.stack([gain_one_sum, gain_two_sum])
    small = jnp.concatenate([part.reshape(-1) for part in (beta_sum, taps_sum, heads_sum)])
    low_sum = inner_sum.astype(bf16)
    if planar:
        ranks = lax.axis_size(DP)
        gain_parts = gain_parts.reshape(2, ranks, devices, -1).transpose(2, 0, 1, 3)
        chunk = gain_parts.shape[3]
        gain_parts = gain_parts.reshape(devices, -1, 128)
        gain_rows = gain_parts.shape[1]
        gain_parts = jnp.pad(gain_parts, ((0, 0), (0, -gain_rows % 8), (0, 0)))
        small = jnp.pad(small, (0, -small.size % 1024)).reshape(-1, 128)
        input_norm, flat, out_total, inner_total, pair_grads, down_grads = scatter_rows(
            projected_low, beta_low, out_grad,
            low_sum.reshape(2, -1, low_sum.shape[1]), w_parts, w_beta_wide, small, gain_parts,
            own_grads[0], down_grad)
        gate_share, up_share = (
            pair_grads[:, kind].reshape(-1, pair_grads.shape[3]).astype(f32).T for kind in range(2))
        down_share = down_grads.reshape(w_down.shape).astype(f32)
        gain_totals = pick(
            flat[small.shape[0] :][:gain_rows].reshape(2, ranks, chunk), lax.axis_index(DP), 1)
        small = flat[: small.shape[0]].reshape(-1)
        out_total = out_total.reshape(w_out.shape).astype(f32)
        inner_total = inner_total.reshape(low_sum.shape)
    else:
        gain_totals = lax.psum_scatter(gain_parts, DP + TP, scatter_dimension=1, tiled=True)
        inner_total = lax.psum(low_sum, DP)
        small = lax.psum(small, DP)
        out_grad = lax.psum_scatter(out_grad, TP, scatter_dimension=0, tiled=True)
        out_total = lax.psum(out_grad, DP).astype(f32)
        input_norm = jnp.stack([
            scatter_sum(
                dot_nt(projected_low[m], w_inner) + dot_nt(beta_low[m], w_beta_wide), TP)
            for m in batches])
    norm_grad, _ = norm_backward(rows_in, scale_one, gain_one, input_norm)
    beta_total, conv_total, heads_total = (
        piece.reshape(shape) for piece, shape in zip(
            jnp.split(
                small[: beta_sum.size + taps_sum.size + heads_sum.size],
                (beta_sum.size, beta_sum.size + taps_sum.size)),
            (beta_sum.shape, conv_weight.shape, head_gain.shape)))
    columns = [
        inner_total[:, n * local_width : (n + 1) * local_width].astype(f32) for n in range(4)]
    return (
        result_rows,
        hidden_grad + norm_grad,
        gain_totals[0],
        gain_totals[1],
        *columns,
        beta_total,
        conv_total,
        heads_total,
        out_total,
        gate_share,
        up_share,
        down_share,
    )


def solution(mesh):
    dp, tensor = mesh.shape["dp"], mesh.shape["tensor"]
    inner = 2 if tensor == 8 else 4
    axes = ("x", "core", "z", "y")
    fine = jax.sharding.Mesh(
        mesh.devices.reshape(dp // 2, 2, tensor // inner, inner), axes)
    tokens = P(None, DP + TP, None)
    in_specs = (
        tokens,
        P(None, DP, None),
        P(DP),
        P(DP),
        P(None, TP),
        P(None, TP),
        P(None, TP),
        P(None, TP),
        P(None, TP),
        P(None, None, TP),
        P(TP, None),
        P(TP, None),
        P(DP, TP),
        P(DP, TP),
        P(TP, DP),
        tokens,
    )
    out_specs = (
        tokens,
        tokens,
        P(DP + TP),
        P(DP + TP),
        P(None, TP),
        P(None, TP),
        P(None, TP),
        P(None, TP),
        P(None, TP),
        P(None, None, TP),
        P(TP, None),
        P(TP, None),
        P(DP, TP),
        P(DP, TP),
        P(TP, DP),
    )
    return jax.shard_map(
        per_device, mesh=fine, in_specs=in_specs, out_specs=out_specs, check_vma=False
    )
```

```python
from functools import partial

import jax
import jax.numpy as jnp
from jax import lax
from jax.experimental import pallas as pl
from jax.experimental.pallas import tpu as pltpu
from jax.sharding import PartitionSpec as P


CHUNK = 128
HALO = 8
epsilon = 1e-06
highest = lax.Precision.HIGHEST
f32 = jnp.float32
bf16 = jnp.bfloat16


def product(left, right, left_dim, right_dim, exact=False):
    dims = (((left_dim,), (right_dim,)), ((), ()))
    if exact:
        return lax.dot_general(left, right, dims, precision=highest, preferred_element_type=f32)
    return lax.dot_general(
        left.astype(bf16), right.astype(bf16), dims, preferred_element_type=f32
    )


def sigmoid(x):
    return 1.0 / (1.0 + jnp.exp(-x))


def segment_tools(lengths_ref):
    ends = []
    total = 0
    for i in range(lengths_ref.shape[0] - 1):
        total = total + lengths_ref[i]
        ends.append(total)

    def segment_of(pos):
        result = 0
        for end in ends:
            result = result + (pos >= end).astype(jnp.int32)
        return result

    return segment_of, len(ends)


def chunk_masks(segment_of, base, chunk):
    col = base + lax.broadcasted_iota(jnp.int32, (chunk, 1), 0)
    row = base + lax.broadcasted_iota(jnp.int32, (1, chunk), 1)
    seg_col = segment_of(col)
    seg_row = segment_of(row)
    first = segment_of(base - 1)
    last = segment_of(base + chunk - 1)
    same = seg_col == seg_row
    strict = (same & (col > row)).astype(f32)
    within = (same & (col >= row)).astype(f32)
    has_past = base > 0
    carry = ((seg_col == first) & has_past).astype(f32)
    close = (seg_col == last).astype(f32)
    keep = ((first == last) & has_past).astype(f32)
    return strict, within, carry, close, keep


def level_masks(chunk):
    row = lax.broadcasted_iota(jnp.int32, (chunk, chunk), 0)
    col = lax.broadcasted_iota(jnp.int32, (chunk, chunk), 1)
    masks = []
    width = 1
    while width < chunk:
        mask = (
            (row // (2 * width) == col // (2 * width))
            & ((row // width) % 2 == 1)
            & ((col // width) % 2 == 0)
        )
        masks.append(mask)
        width *= 2
    return masks, (row == col).astype(f32)


def conv_part(proj_ref, tap_ref, segment_of, base, part, width, chunk):
    taps = tap_ref.shape[0] // 3
    cols = pl.ds(part * width, width)
    main = proj_ref[pl.ds(base, chunk), cols]
    prev = proj_ref[pl.ds(pl.multiple_of(jnp.maximum(base - HALO, 0), HALO), HALO), cols]
    full = jnp.concatenate([prev, main], axis=0)
    col = base + lax.broadcasted_iota(jnp.int32, (chunk, 1), 0)
    seg = segment_of(col)
    total = main * tap_ref[part * taps : part * taps + 1, :]
    shifted = [main]
    for s in range(1, taps):
        valid = (segment_of(col - s) == seg) & (col >= s)
        moved = jnp.where(valid, pltpu.roll(full, s, 0)[HALO:], 0.0)
        shifted.append(moved)
        total = total + moved * tap_ref[part * taps + s : part * taps + s + 1, :]
    return total, shifted


def heads_of(x, heads):
    return [x[:, h * 128 : (h + 1) * 128] for h in range(heads)]


def unit_rows(a, scale):
    r = lax.rsqrt(jnp.sum(a * a, axis=-1, keepdims=True) + epsilon)
    return a * (r * scale)


def mixer_forward_kernel(exact, group, lengths_ref, proj_ref, beta_ref, tap_ref, gain_ref,
                         mixed_ref, heads_ref, fixed_ref, delta_ref, state_ref, inverse_ref,
                         query_s, key_s, value_s, score_s):
    rows_all = proj_ref.shape[0]
    width = proj_ref.shape[1] // 4
    heads = width // 128
    chunk = CHUNK
    count = rows_all // chunk
    segment_of, segments = segment_tools(lengths_ref)

    @pl.loop(0, count)
    def _(c):
        base = pl.multiple_of(c * chunk, chunk)
        rows = pl.ds(base, chunk)
        for part, target in enumerate((query_s, key_s, value_s)):
            pre, _ = conv_part(proj_ref, tap_ref, segment_of, base, part, width, chunk)
            act = pre * sigmoid(pre)
            if part == 2:
                target[rows, :] = act
            else:
                scale = 128 ** (-0.5) if part == 0 else 1.0
                for h, a in enumerate(heads_of(act, heads)):
                    target[rows, h * 128 : (h + 1) * 128] = unit_rows(a, scale)

    def beta_of(base, h):
        pos = base + lax.broadcasted_iota(jnp.int32, (chunk, 1), 0)
        live = (segment_of(pos) < segments).astype(f32)
        return sigmoid(beta_ref[pl.ds(base, chunk), h : h + 1]) * live

    masks, eye = level_masks(chunk)

    @pl.loop(0, count // group)
    def _(g):
        lowers, places = [], []
        for i in range(group):
            c = g * group + i
            base = pl.multiple_of(c * chunk, chunk)
            strict, within, _, _, _ = chunk_masks(segment_of, base, chunk)
            for h in range(heads):
                cols = slice(h * 128, (h + 1) * 128)
                k = key_s[pl.ds(base, chunk), cols]
                q = query_s[pl.ds(base, chunk), cols]
                lowers.append(product(k, k, 1, 1, exact) * strict * beta_of(base, h))
                score_s[c * heads + h] = (product(q, k, 1, 1, exact) * within).astype(score_s.dtype)
                places.append(c * heads + h)
        inverses = [eye - jnp.where(masks[0], lower, 0.0) for lower in lowers]
        for mask in masks[1:]:
            steps = [product(jnp.where(mask, lower, 0.0), x, 1, 0, True) for lower, x in zip(lowers, inverses)]
            inverses = [x - product(x, step, 1, 0, True) for x, step in zip(inverses, steps)]
        for place, x in zip(places, inverses):
            inverse_ref[place] = x

    def advance(c, states):
        base = pl.multiple_of(c * chunk, chunk)
        rows = pl.ds(base, chunk)
        _, _, carry, close, keep = chunk_masks(segment_of, base, chunk)
        new_states = []
        for h in range(heads):
            cols = slice(h * 128, (h + 1) * 128)
            state = states[h]
            k = key_s[rows, cols]
            q = query_s[rows, cols]
            delta = value_s[rows, cols] - carry * product(k, state, 1, 0, exact)
            fixed = product(inverse_ref[c * heads + h], beta_of(base, h) * delta, 1, 0, exact)
            out = carry * product(q, state, 1, 0, exact) + product(
                score_s[c * heads + h], fixed, 1, 0, exact)
            state_ref[c * heads + h] = state
            new_states.append(keep * state + product(k, close * fixed, 0, 0, exact))
            delta_ref[rows, cols] = delta
            fixed_ref[rows, cols] = fixed
            heads_ref[rows, cols] = out
            gate = proj_ref[rows, 3 * width + h * 128 : 3 * width + (h + 1) * 128]
            r = lax.rsqrt(jnp.mean(out * out, axis=-1, keepdims=True) + epsilon)
            mixed_ref[rows, cols] = (
                out * r * gain_ref[h : h + 1, :] * (gate * sigmoid(gate))
            ).astype(mixed_ref.dtype)
        return tuple(new_states)

    lax.fori_loop(0, count, advance, tuple(jnp.zeros((128, 128), f32) for _ in range(heads)))


def mixer_backward_kernel(exact, lengths_ref, proj_ref, beta_ref, tap_ref, gain_ref, grad_ref,
                          heads_ref, fixed_ref, delta_ref, state_ref, inverse_ref,
                          dproj_ref, dbeta_ref, dtap_ref, dgain_ref,
                          query_s, key_s, pre_s, dout_s, dpre_s):
    rows_all = proj_ref.shape[0]
    width = proj_ref.shape[1] // 4
    heads = width // 128
    chunk = CHUNK
    count = rows_all // chunk
    taps = tap_ref.shape[0] // 3
    segment_of, segments = segment_tools(lengths_ref)
    dgain_ref[...] = jnp.zeros_like(dgain_ref)
    dbeta_ref[...] = jnp.zeros_like(dbeta_ref)
    dtap_ref[...] = jnp.zeros_like(dtap_ref)

    @pl.loop(0, count)
    def _(c):
        base = pl.multiple_of(c * chunk, chunk)
        rows = pl.ds(base, chunk)
        for part in range(3):
            pre, _ = conv_part(proj_ref, tap_ref, segment_of, base, part, width, chunk)
            pre_s[rows, part * width : (part + 1) * width] = pre
            if part < 2:
                act = pre * sigmoid(pre)
                target = (query_s, key_s)[part]
                scale = 128 ** (-0.5) if part == 0 else 1.0
                for h, a in enumerate(heads_of(act, heads)):
                    target[rows, h * 128 : (h + 1) * 128] = unit_rows(a, scale)
        for h in range(heads):
            cols = slice(h * 128, (h + 1) * 128)
            gate_cols = slice(3 * width + h * 128, 3 * width + (h + 1) * 128)
            out = heads_ref[rows, cols]
            gate = proj_ref[rows, gate_cols]
            grad = grad_ref[rows, cols].astype(f32)
            gain = gain_ref[h : h + 1, :]
            sg = sigmoid(gate)
            silu = gate * sg
            r = lax.rsqrt(jnp.mean(out * out, axis=-1, keepdims=True) + epsilon)
            normed = out * r
            dgain_ref[h : h + 1, :] += jnp.sum(grad * normed * silu, axis=0, keepdims=True)
            dproj_ref[rows, gate_cols] = (
                grad * normed * gain * (sg * (1.0 + gate * (1.0 - sg)))
            ).astype(dproj_ref.dtype)
            weighted = grad * gain * silu
            dout_s[rows, cols] = r * weighted - out * (r * r * r) * jnp.mean(
                weighted * out, axis=-1, keepdims=True)

    dpre_s[rows_all : rows_all + HALO, :] = jnp.zeros((HALO, 3 * width), f32)

    def retreat(step, dstates):
        c = count - 1 - step
        base = pl.multiple_of(c * chunk, chunk)
        rows = pl.ds(base, chunk)
        strict, within, carry, close, keep = chunk_masks(segment_of, base, chunk)
        pos = base + lax.broadcasted_iota(jnp.int32, (chunk, 1), 0)
        live = (segment_of(pos) < segments).astype(f32)
        new_dstates = []
        for h in range(heads):
            cols = slice(h * 128, (h + 1) * 128)
            place = c * heads + h
            k = key_s[rows, cols]
            q = query_s[rows, cols]
            dout = dout_s[rows, cols]
            state = state_ref[place]
            inverse = inverse_ref[place]
            fixed = fixed_ref[rows, cols]
            delta = delta_ref[rows, cols]
            dstate = dstates[h]
            rate = sigmoid(beta_ref[rows, h : h + 1])
            beta = rate * live
            scores = product(q, k, 1, 1, exact) * within
            gram = product(k, k, 1, 1, exact) * strict
            dfixed = product(scores, dout, 0, 0, exact) + close * product(k, dstate, 1, 0, exact)
            drhs = product(inverse, dfixed, 0, 0, exact)
            ddelta = beta * drhs
            carried_dout = carry * dout
            carried_ddelta = carry * ddelta
            new_dstates.append(
                keep * dstate
                + product(q, carried_dout, 0, 0, exact)
                - product(k, carried_ddelta, 0, 0, exact)
            )
            dscores = product(dout, fixed, 1, 1, exact) * within
            dlower = -product(drhs, fixed, 1, 1, exact) * strict
            dgram = beta * dlower
            dq = product(carried_dout, state, 1, 1, exact) + product(dscores, k, 1, 0, exact)
            dk = (
                product(dscores, q, 0, 0, exact)
                + close * product(fixed, dstate, 1, 1, exact)
                - product(carried_ddelta, state, 1, 1, exact)
                + product(dgram, k, 1, 0, exact)
                + product(dgram, k, 0, 0, exact)
            )
            drate = live * (
                jnp.sum(drhs * delta, axis=-1, keepdims=True)
                + jnp.sum(dlower * gram, axis=-1, keepdims=True)
            )
            dbeta_ref[rows, h : h + 1] = (drate * rate * (1.0 - rate)).astype(dbeta_ref.dtype)
            for part, da in enumerate((dq, dk, ddelta)):
                part_cols = slice(part * width + h * 128, part * width + (h + 1) * 128)
                pre = pre_s[rows, part_cols]
                sg = sigmoid(pre)
                if part < 2:
                    a = pre * sg
                    scale = 128 ** (-0.5) if part == 0 else 1.0
                    r = lax.rsqrt(jnp.sum(a * a, axis=-1, keepdims=True) + epsilon)
                    da = (scale * r) * (da - a * (r * r) * jnp.sum(da * a, axis=-1, keepdims=True))
                dpre_s[rows, part_cols] = da * (sg * (1.0 + pre * (1.0 - sg)))
        return tuple(new_dstates)

    lax.fori_loop(0, count, retreat, tuple(jnp.zeros((128, 128), f32) for _ in range(heads)))

    @pl.loop(0, count)
    def _(c):
        base = pl.multiple_of(c * chunk, chunk)
        rows = pl.ds(base, chunk)
        col = base + lax.broadcasted_iota(jnp.int32, (chunk, 1), 0)
        seg = segment_of(col)
        for part in range(3):
            cols = slice(part * width, (part + 1) * width)
            _, shifted = conv_part(proj_ref, tap_ref, segment_of, base, part, width, chunk)
            full = dpre_s[pl.ds(base, chunk + HALO), cols]
            main = full[:chunk]
            total = main * tap_ref[part * taps : part * taps + 1, :]
            for s in range(taps):
                at = slice(part * taps + s, part * taps + s + 1)
                dtap_ref[at, :] += jnp.sum(main * shifted[s], axis=0, keepdims=True)
                if s > 0:
                    valid = (segment_of(col + s) == seg) & (col + s < rows_all)
                    moved = pltpu.roll(full, chunk + HALO - s, 0)[:chunk]
                    total = total + jnp.where(valid, moved, 0.0) * tap_ref[at, :]
            dproj_ref[rows, cols] = total.astype(dproj_ref.dtype)


def vmem():
    return pl.BlockSpec(memory_space=pltpu.VMEM)


def mixer_forward(lengths_row, projected, beta_logits, taps, gain, exact=True, group=4):
    rows, wide = projected.shape
    width = wide // 4
    heads = width // 128
    places = rows // CHUNK * heads
    group = min(group, rows // CHUNK)
    return pl.pallas_call(
        partial(mixer_forward_kernel, exact, group),
        out_shape=(
            jax.ShapeDtypeStruct((rows, width), bf16),
            jax.ShapeDtypeStruct((rows, width), f32),
            jax.ShapeDtypeStruct((rows, width), f32),
            jax.ShapeDtypeStruct((rows, width), f32),
            jax.ShapeDtypeStruct((places, 128, 128), f32),
            jax.ShapeDtypeStruct((places, CHUNK, CHUNK), f32),
        ),
        in_specs=[pl.BlockSpec(memory_space=pltpu.SMEM)] + [vmem()] * 4,
        out_specs=(vmem(),) * 6,
        scratch_shapes=[pltpu.VMEM((rows, width), f32)] * 3
        + [pltpu.VMEM((places, CHUNK, CHUNK), f32 if exact else bf16)],
        compiler_params=pltpu.CompilerParams(vmem_limit_bytes=48 * 2**20),
        cost_estimate=pl.CostEstimate(flops=10**10, bytes_accessed=10**7, transcendentals=10**6),
        name="mixer_forward",
    )(lengths_row, projected, beta_logits, taps, gain)


def mixer_backward(lengths_row, projected, beta_logits, taps, gain, grad, saved, exact=True):
    rows, wide = projected.shape
    width = wide // 4
    return pl.pallas_call(
        partial(mixer_backward_kernel, exact),
        out_shape=(
            jax.ShapeDtypeStruct((rows, wide), bf16),
            jax.ShapeDtypeStruct((rows, 128), bf16),
            jax.ShapeDtypeStruct(taps.shape, f32),
            jax.ShapeDtypeStruct(gain.shape, f32),
        ),
        in_specs=[pl.BlockSpec(memory_space=pltpu.SMEM)] + [vmem()] * 10,
        out_specs=(vmem(),) * 4,
        scratch_shapes=[pltpu.VMEM((rows, width), f32)] * 2
        + [pltpu.VMEM((rows, 3 * width), f32), pltpu.VMEM((rows, width), f32),
           pltpu.VMEM((rows + HALO, 3 * width), f32)],
        compiler_params=pltpu.CompilerParams(vmem_limit_bytes=56 * 2**20),
        cost_estimate=pl.CostEstimate(flops=10**10, bytes_accessed=10**7, transcendentals=10**6),
        name="mixer_backward",
    )(lengths_row, projected, beta_logits, taps, gain, grad, *saved)


NT = (((1,), (1,)), ((), ()))


def other(axis_name):
    return {axis_name: 1 - lax.axis_index(axis_name)}


def ffn_kernel(x_ref, w_ref, down_ref, c_refs, out_ref, ngrad_ref, wgrad_ref, down_out,
               xs, cs, ws, dsum, landed, outs, inner_s, gate_s, up_s, acts_t, part, crecv, drecv, nrecv, stage,
               ag_send, ag_recv, pair_send, pair_recv, rs_send, rs_recv, c_sem, w_sem, g_sem, t_sem,
               down_right, down_left, down_recv, down_sem, sum_sems, keep_sem, out_sem):
    half = xs.shape[1] // 2
    rows = 2 * half
    model = xs.shape[2]
    hidden = ws.shape[1]
    lines = w_ref.shape[0]
    parts, _, quarter, width = w_ref.shape[1:]
    tile_f = 256
    tile_d = min(512, model)
    tile_w = min(256, width)

    def remote(src, dst, send, recv, axis_name):
        return pltpu.make_async_remote_copy(
            src_ref=src, dst_ref=dst, send_sem=send, recv_sem=recv,
            device_id=other(axis_name), device_id_type=pl.DeviceIdType.MESH)

    def halves(ref, index, h):
        return ref.at[index, pl.ds(h * half, half)]

    o = lax.axis_index("z")

    def down_rows(z):
        return ws.at[2, pl.ds(pl.multiple_of(z * quarter, 16), quarter)]

    def down_pass(z, right):
        send = down_right if right else down_left
        return pltpu.make_async_remote_copy(
            src_ref=down_rows(z), dst_ref=down_rows(z), send_sem=send.at[z], recv_sem=down_recv.at[z],
            device_id={"z": o + 1 if right else o - 1}, device_id_type=pl.DeviceIdType.MESH)

    def down_forward(z, right):
        @pl.when(o < lines - 1 if right else o > 0)
        def _():
            down_pass(z, right).start()

    def down_step(far):
        for side in (-1, 1):
            z = o + side * far

            @pl.when((z >= 0) & (z < lines))
            def _():
                down_pass(z, side < 0).wait_recv()
                down_forward(z, side < 0)

    weight_copies, down_copies = [], []
    for r in range(parts):
        cols = pl.ds(r * width, width)
        for line in range(lines):
            weight_copies.append(pltpu.make_async_copy(
                w_ref.at[line, r], ws.at[pl.ds(0, 2), pl.ds(line * quarter, quarter), cols],
                w_sem.at[line, r]))
        down_copies.append(pltpu.make_async_copy(
            down_ref.at[r], down_rows(o).at[:, cols], down_sem.at[r]))
    for copy in down_copies:
        copy.start()
    for copy in weight_copies:
        copy.start()

    def pair_at(turn):
        return jnp.where(turn < 2, 3 - 2 * turn, 6 - 2 * turn)

    def slot_of(step):
        return (1 - lax.rem(step, 2)) * 4 + pair_at(step // 2)

    def c_copy(step, n):
        buffer = lax.rem(step, 2)
        return pltpu.make_async_copy(c_refs[n], cs.at[buffer], c_sem.at[buffer])

    def c_start(step):
        for n in range(8):
            @pl.when(slot_of(step) == n)
            def _():
                c_copy(step, n).start()

    c_copy(0, 7).start()
    line_barrier(lines, [other(name) for name in ("core", "x", "y")])

    own_pair = remote(x_ref, xs.at[4], ag_send.at[0], ag_recv.at[0], "core")
    own_x = [remote(x_ref.at[pl.ds(h * half, half)], halves(xs, 1, h), ag_send.at[1 + h], ag_recv.at[1 + h], "x") for h in range(2)]
    own_y = [remote(x_ref.at[pl.ds(h * half, half)], halves(xs, 2, h), ag_send.at[3 + h], ag_recv.at[3 + h], "y") for h in range(2)]
    relay_y = remote(halves(xs, 1, 0), halves(xs, 3, 0), ag_send.at[5], ag_recv.at[5], "y")
    relay_x = remote(halves(xs, 2, 1), halves(xs, 3, 1), ag_send.at[6], ag_recv.at[6], "x")
    pair_of = [None] + [remote(xs.at[j], xs.at[4 + j], ag_send.at[6 + j], ag_recv.at[6 + j], "core") for j in (1, 2, 3)]
    own_pair.start()
    own_x[0].start()
    own_y[1].start()
    own_x[1].start()
    own_y[0].start()
    for copy in down_copies:
        copy.wait()
    down_forward(o, True)
    down_forward(o, False)
    own_copy = pltpu.make_async_copy(x_ref, xs.at[0], t_sem.at[0, 0])
    own_copy.start()
    own_copy.wait()
    for copy in weight_copies:
        copy.wait()

    def part_send(turn):
        j = pair_at(turn)
        return remote(part.at[lax.rem(turn, 2)], crecv.at[j], pair_send.at[j], pair_recv.at[j], "core")

    x_sends = [[remote(crecv.at[1, a, pl.ds(h * half, half)], nrecv.at[0, a, pl.ds(h * half, half)],
                       rs_send.at[a * 2 + h], rs_recv.at[a * 2 + h], "x") for a in range(2)] for h in range(2)]
    y_sends = [[remote(crecv.at[2, a, pl.ds(h * half, half)], nrecv.at[1, a, pl.ds(h * half, half)],
                       rs_send.at[4 + a * 2 + h], rs_recv.at[4 + a * 2 + h], "y") for a in range(2)] for h in range(2)]
    d_sends = [[remote(crecv.at[3, a, pl.ds(h * half, half)], drecv.at[a, pl.ds(h * half, half)],
                       rs_send.at[8 + a * 2 + h], rs_recv.at[8 + a * 2 + h], ("x", "y")[h]) for a in range(2)] for h in range(2)]

    def gates(slot, cols):
        return [
            lax.dot_general(xs[slot], ws[kind, cols, :], NT, preferred_element_type=f32)
            for kind in range(2)]

    @pl.loop(0, 8)
    def _(early):
        slot = lax.rem(early + 1, 2) * 4 + early // 2

        @pl.when(early == 0)
        def _():
            own_pair.wait_recv()

        @pl.when(early == 2)
        def _():
            down_step(1)
            own_x[0].wait_recv()
            relay_y.start()
            own_y[1].wait_recv()
            relay_x.start()
            own_x[1].wait_recv()
            pair_of[1].start()
            own_y[0].wait_recv()
            pair_of[2].start()
            pair_of[1].wait_recv()

        @pl.when(early == 4)
        def _():
            pair_of[2].wait_recv()

        @pl.when(early == 6)
        def _():
            if lines > 2:
                down_step(2)
            relay_y.wait_recv()
            relay_x.wait_recv()
            pair_of[3].start()
            pair_of[3].wait_recv()

        places = pl.ds(pl.multiple_of(slot * rows, rows), rows)
        for start in range(0, hidden, tile_f):
            cols = slice(start, min(start + tile_f, hidden))
            gate, up = gates(slot, cols)
            acts_t[2, cols, places] = (gate * sigmoid(gate) * up).astype(bf16).T

    tiles = model // tile_w

    def c_tile(t):
        buffer = lax.rem(t, 2)
        cols = pl.ds(pl.multiple_of(t * tile_w, tile_w), tile_w)
        return [
            pltpu.make_async_copy(
                ref.at[:, cols], part.at[0, buffer, :, pl.ds(n * tile_w, tile_w)], t_sem.at[buffer, n])
            for n, ref in enumerate(c_refs)]

    def grad_copy(kind, t, line):
        return pltpu.make_async_copy(
            stage.at[lax.rem(t, 2), pl.ds(line * quarter, quarter)],
            wgrad_ref.at[line, t * tile_w // width, kind, :,
                         pl.ds(pl.multiple_of(lax.rem(t * tile_w, width), tile_w), tile_w)],
            g_sem.at[lax.rem(t, 2), line])

    def weight_grads(kind):
        @pl.loop(0, tiles)
        def _(t):
            if kind == 2:
                for copy in c_tile(t):
                    copy.wait()
                right = jnp.concatenate(
                    [part[0, lax.rem(t, 2), :, n * tile_w : (n + 1) * tile_w] for n in range(8)])
            else:
                right = xs[:, :, pl.ds(pl.multiple_of(t * tile_w, tile_w), tile_w)].reshape(8 * rows, tile_w)

            if kind < 2:
                @pl.when(t >= 2)
                def _():
                    for line in range(lines):
                        grad_copy(kind, t - 2, line).wait()

            value = jnp.dot(acts_t[kind], right, preferred_element_type=f32).astype(bf16)
            if kind == 2:
                @pl.when(t + 2 < tiles)
                def _():
                    for copy in c_tile(t + 2):
                        copy.start()
            if kind < 2:
                stage[lax.rem(t, 2)] = value
                for line in range(lines):
                    grad_copy(kind, t, line).start()
            else:
                dsum[:, pl.ds(pl.multiple_of(t * tile_w, tile_w), tile_w)] = value

        if kind == 2:
            return
        for t in range(max(tiles - 2, 0), tiles):
            for line in range(lines):
                grad_copy(kind, t, line).wait()

    mesh_id = pl.DeviceIdType.MESH

    def rows_of(z):
        return dsum.at[pl.ds(pl.multiple_of(z * quarter, 16), quarter)]

    def sum_pass(z, right):
        side = 0 if right else 2
        block = jnp.maximum(z - o - 1, 0) if right else jnp.minimum(lines - o + 1 + z, lines)
        return pltpu.make_async_remote_copy(
            src_ref=rows_of(z), dst_ref=landed.at[block],
            send_sem=sum_sems.at[side, z], recv_sem=sum_sems.at[side + 1, z],
            device_id={"z": o + 1 if right else o - 1}, device_id_type=mesh_id)

    def sum_add(z, block):
        at = pl.ds(pl.multiple_of(z * quarter, 16), quarter)
        for start in range(0, model, tile_d):
            cols = slice(start, start + tile_d)
            dsum[at, cols] = (
                dsum[at, cols].astype(f32) + landed[block, :, cols].astype(f32)).astype(bf16)

    def sum_tick(k):
        z_right = lines - 1 - k + o

        @pl.when(o <= k)
        def _():
            @pl.when(o > 0)
            def _():
                sum_pass(z_right, True).wait_recv()
                sum_add(z_right, z_right - o)

            @pl.when(o < k)
            def _():
                sum_pass(z_right + 1, True).wait_send()
            sum_pass(z_right, True).start()

        back = lines - 1 - o
        z_left = k - back

        @pl.when(back <= k)
        def _():
            @pl.when(back > 0)
            def _():
                sum_pass(z_left, False).wait_recv()
                sum_add(z_left, lines - o + z_left)

            @pl.when(back < k)
            def _():
                sum_pass(z_left - 1, False).wait_send()
            sum_pass(z_left, False).start()

    for t in range(2):
        for copy in c_tile(t):
            copy.start()
    weight_grads(2)
    sum_tick(0)
    for far in range(3, lines):
        down_step(far)

    @pl.loop(0, 8)
    def _(step):
        turn = step // 2
        j = pair_at(turn)
        slot = slot_of(step)
        pairing = lax.rem(step, 2) == 0

        @pl.when(step < 7)
        def _():
            c_start(step + 1)

        for k in range(1, lines - 1):
            @pl.when(step == min(1 + 3 * k, 7))
            def _():
                sum_tick(k)

        c_copy(step, 0).wait()

        for start in range(0, hidden, tile_f):
            size = min(tile_f, hidden - start)
            cols = slice(start, start + size)
            gate, up = gates(slot, cols)
            grad = lax.dot_general(cs[lax.rem(step, 2)], ws[2, cols, :], NT, preferred_element_type=f32)
            sg = sigmoid(gate)
            silu = gate * sg
            inner = (silu * up).astype(bf16)
            gate_grad = (grad * up * sg * (1.0 + gate * (1.0 - sg))).astype(bf16)
            up_grad = (grad * silu).astype(bf16)
            places = pl.ds(pl.multiple_of(slot * rows, rows), rows)
            for kind, (value, target) in enumerate(((gate_grad, gate_s), (up_grad, up_s), (inner, inner_s))):
                target[:, cols] = value
                if kind < 2:
                    acts_t[kind, cols, places] = value.T

        @pl.when(pairing & (step >= 4))
        def _():
            part_send(turn - 2).wait_send()

        place = jnp.where(pairing, lax.rem(turn, 2), 2)
        for start in range(0, model, tile_d):
            cols = slice(start, start + tile_d)
            part[place, 0, :, cols] = jnp.dot(
                inner_s[...], ws[2, :, cols], preferred_element_type=f32).astype(bf16)
            part[place, 1, :, cols] = (
                jnp.dot(gate_s[...], ws[0, :, cols], preferred_element_type=f32)
                + jnp.dot(up_s[...], ws[1, :, cols], preferred_element_type=f32)
            ).astype(bf16)

        @pl.when(pairing)
        def _():
            part_send(turn).start()

        @pl.when(jnp.logical_not(pairing))
        def _():
            part_send(turn).wait_recv()
            for a in range(2):
                for start in range(0, model, tile_d):
                    cols = slice(start, start + tile_d)
                    crecv[j, a, :, cols] = (
                        crecv[j, a, :, cols].astype(f32) + part[2, a, :, cols].astype(f32)
                    ).astype(bf16)

        @pl.when(step == 1)
        def _():
            for h in range(2):
                for copy in d_sends[h]:
                    copy.start()

        @pl.when(step == 3)
        def _():
            for copy in x_sends[0]:
                copy.start()

        @pl.when(step == 5)
        def _():
            for copy in y_sends[1]:
                copy.start()


    for h in range(2):
        j = 2 - h
        for a in range(2):
            d_sends[h][a].wait_recv()
            at = pl.ds(h * half, half)
            crecv[j, a, at, :] = (
                crecv[j, a, at, :].astype(f32) + drecv[a, at, :].astype(f32)).astype(bf16)
        for copy in (y_sends, x_sends)[h][h]:
            copy.start()
    weight_grads(0)
    weight_grads(1)
    out_copies = []
    for a, target in enumerate((out_ref, ngrad_ref)):
        for h in range(2):
            x_sends[h][a].wait_recv()
            y_sends[h][a].wait_recv()
        for n in range(model // tile_d):
            cols = slice(n * tile_d, (n + 1) * tile_d)
            if n >= 2:
                out_copies[-2].wait()
            outs[a, n % 2] = (
                crecv[0, a, :, cols].astype(f32)
                + nrecv[0, a, :, cols].astype(f32)
                + nrecv[1, a, :, cols].astype(f32)
            )
            copy = pltpu.make_async_copy(
                outs.at[a, n % 2], target.at[:, pl.ds(n * tile_d, tile_d)],
                out_sem.at[n, a])
            copy.start()
            out_copies.append(copy)
    steps = model // tile_d
    for a in range(2):
        for copy in out_copies[a * steps : (a + 1) * steps][-2:]:
            copy.wait()
    @pl.loop(0, lines)
    def _(z):
        @pl.when((o < lines - 1) & (z <= o))
        def _():
            down_pass(z, True).wait_send()

        @pl.when((o > 0) & (z >= o))
        def _():
            down_pass(z, False).wait_send()

    own_pair.wait_send()
    for h in range(2):
        own_x[h].wait_send()
        own_y[h].wait_send()
        for a in range(2):
            x_sends[h][a].wait_send()
            y_sends[h][a].wait_send()
            d_sends[h][a].wait_send()
    relay_x.wait_send()
    relay_y.wait_send()
    for j in (1, 2, 3):
        pair_of[j].wait_send()
    part_send(2).wait_send()
    part_send(3).wait_send()

    @pl.when(o > 0)
    def _():
        sum_pass(o, True).wait_recv()
        sum_add(o, 0)

    @pl.when(o < lines - 1)
    def _():
        sum_pass(o, False).wait_recv()
        sum_add(o, lines)

    keeps = [
        pltpu.make_async_copy(
            rows_of(o).at[:, pl.ds(q * width, width)], down_out.at[q], keep_sem.at[q])
        for q in range(parts)
    ]
    for copy in keeps:
        copy.start()

    @pl.when(o < lines - 1)
    def _():
        sum_pass(o + 1, True).wait_send()

    @pl.when(o > 0)
    def _():
        sum_pass(o - 1, False).wait_send()
    for copy in keeps:
        copy.wait()


def ffn_call_kernel(x_ref, w_ref, down_ref, *refs):
    ffn_kernel(x_ref, w_ref, down_ref, refs[:8], *refs[8:])


def ffn_plane(x_own, weights, down_own, c_rows):
    rows, model = x_own.shape
    lines, parts, _, quarter, width = weights.shape
    hidden = lines * quarter
    tile_w = min(256, width)
    sems = pltpu.SemaphoreType.DMA
    anywhere = pl.BlockSpec(memory_space=pl.ANY)
    return pl.pallas_call(
        ffn_call_kernel,
        out_shape=(
            jax.ShapeDtypeStruct((rows, model), f32),
            jax.ShapeDtypeStruct((rows, model), f32),
            jax.ShapeDtypeStruct(weights.shape, bf16),
            jax.ShapeDtypeStruct((parts, quarter, width), bf16),
        ),
        in_specs=[anywhere] * 11,
        out_specs=(anywhere,) * 4,
        scratch_shapes=[
            pltpu.VMEM((8, rows, model), bf16),
            pltpu.VMEM((2, rows, model), bf16),
            pltpu.VMEM((3, hidden, model), bf16),
            pltpu.VMEM((hidden, model), bf16),
            pltpu.VMEM((lines + 1, quarter, model), bf16),
            pltpu.VMEM((2, 2, rows, min(512, model)), f32),
            pltpu.VMEM((rows, hidden), bf16),
            pltpu.VMEM((rows, hidden), bf16),
            pltpu.VMEM((rows, hidden), bf16),
            pltpu.VMEM((3, hidden, 8 * rows), bf16),
            pltpu.VMEM((3, 2, rows, model), bf16),
            pltpu.VMEM((4, 2, rows, model), bf16),
            pltpu.VMEM((2, rows, model), bf16),
            pltpu.VMEM((2, 2, rows, model), bf16),
            pltpu.VMEM((2, hidden, tile_w), bf16),
            sems((10,)), sems((10,)), sems((4,)), sems((4,)), sems((12,)), sems((12,)),
            sems((2,)), sems((lines, parts)), sems((2, lines)), sems((2, 8)),
            sems((lines,)), sems((lines,)), sems((lines,)), sems((parts,)),
            sems((4, lines)), sems((parts,)), sems((4, 2)),
        ],
        compiler_params=pltpu.CompilerParams(
            collective_id=2, has_side_effects=True, vmem_limit_bytes=60 * 2**20),
        cost_estimate=pl.CostEstimate(flops=8 * 10**10, bytes_accessed=4 * 10**7, transcendentals=10**6),
        name="ffn_plane",
    )(x_own, weights, down_own, *c_rows)


def line_barrier(lines, others):
    o = lax.axis_index("z")
    barrier = pltpu.get_barrier_semaphore()
    mesh_id = pl.DeviceIdType.MESH

    @pl.when(o > 0)
    def _():
        pl.semaphore_signal(barrier, inc=1, device_id={"z": o - 1}, device_id_type=mesh_id)

    @pl.when(o < lines - 1)
    def _():
        pl.semaphore_signal(barrier, inc=1, device_id={"z": o + 1}, device_id_type=mesh_id)

    for target in others:
        pl.semaphore_signal(barrier, inc=1, device_id=target, device_id_type=mesh_id)
    peers = len(others) + (o > 0).astype(jnp.int32) + (o < lines - 1).astype(jnp.int32)
    pl.semaphore_wait(barrier, peers)


def line_copy(src, dst, send, recv, target):
    return pltpu.make_async_remote_copy(
        src_ref=src, dst_ref=dst, send_sem=send, recv_sem=recv,
        device_id=target, device_id_type=pl.DeviceIdType.MESH)


def pair_peers():
    x, core = lax.axis_index("x"), lax.axis_index("core")
    peers = [
        (x * 2 + 1 - core, {"core": 1 - core}),
        ((1 - x) * 2 + core, {"x": 1 - x}),
        ((1 - x) * 2 + 1 - core, {"x": 1 - x, "core": 1 - core}),
    ]
    return x * 2 + core, peers


class Swap:
    def __init__(self, pairs, send, recv, own):
        me, peers = pair_peers()
        self.own = [
            pltpu.make_async_copy(source.at[me], target(me), own.at[n])
            for n, (source, target) in enumerate(pairs)]
        self.away = [
            line_copy(source.at[place], target(me), send.at[n, d], recv.at[n, d], device)
            for n, (source, target) in enumerate(pairs) for d, (place, device) in enumerate(peers)]

    def start(self):
        for copy in self.away + self.own:
            copy.start()

    def wait(self):
        for copy in self.own:
            copy.wait()
        for copy in self.away:
            copy.wait_recv()
            copy.wait_send()


def gather_kernel(x_ref, o_ref, f_refs, w_refs, wb_ref, rows_ref, outs_ref, proj_refs, beta_ref,
                  pair_ref, down_ref,
                  xs, parts, stage, beta_stage, right_send, left_send, line_recv, pair_send, pair_recv,
                  part_right, part_left, part_recv, own_sem, row_sem, outs_sem, out_sem, beta_sem,
                  swap_send, swap_recv, swap_own):
    lines = xs.shape[0] // 2
    batches, rows, model = x_ref.shape
    o = lax.axis_index("z")
    i = lax.axis_index("y")
    line_barrier(lines, [other("y")] + [device for _, device in pair_peers()[1]])
    swap = Swap(
        [(f_refs[0], lambda place: pair_ref.at[place, 0]),
         (f_refs[1], lambda place: pair_ref.at[place, 1]),
         (f_refs[2], lambda place: down_ref.at[place])],
        swap_send, swap_recv, swap_own)

    def right(z, m):
        ref = xs.at[z * 2 + i, m]
        return line_copy(ref, ref, right_send.at[z, m], line_recv.at[z, m], {"z": o + 1})

    def left(z, m):
        ref = xs.at[z * 2 + i, m]
        return line_copy(ref, ref, left_send.at[z, m], line_recv.at[z, m], {"z": o - 1})

    def across(z, m):
        ref = xs.at[z * 2 + i, m]
        return line_copy(ref, ref, pair_send.at[z, m], pair_recv.at[z, m], other("y"))

    own = [
        pltpu.make_async_copy(x_ref, xs.at[o * 2 + i], own_sem.at[0]),
        pltpu.make_async_copy(o_ref, parts.at[o], own_sem.at[1]),
    ]

    def pass_part(z):
        ref = parts.at[z]
        return (line_copy(ref, ref, part_right.at[z], part_recv.at[z], {"z": o + 1}),
                line_copy(ref, ref, part_left.at[z], part_recv.at[z], {"z": o - 1}))

    for copy in own:
        copy.start()
    for copy in own:
        copy.wait()

    def outs(turn, slot):
        buffer = lax.rem(turn, 2)
        return [
            copy for m in range(batches) for copy in (
                pltpu.make_async_copy(stage.at[buffer, m], proj_refs[m].at[slot], out_sem.at[buffer, m]),
                pltpu.make_async_copy(beta_stage.at[buffer, m], beta_ref.at[m, slot], beta_sem.at[buffer, m]))
        ]

    def keep(slot, m):
        return pltpu.make_async_copy(xs.at[slot, m], rows_ref.at[m, slot], row_sem.at[slot, m])

    def keep_outs(z):
        return pltpu.make_async_copy(parts.at[z], outs_ref.at[z], outs_sem.at[z])

    def project(turn, slot):
        @pl.when(turn >= 2)
        def _():
            for copy in outs(turn, slot):
                copy.wait()
        for m in range(batches):
            keep(slot, m).start()
        x = xs[slot].reshape(batches * rows, model)
        buffer = lax.rem(turn, 2)
        width = w_refs[0].shape[1]
        for n, w_ref in enumerate(w_refs):
            stage[buffer, :, :, n * width : (n + 1) * width] = jnp.dot(
                x, w_ref[...], preferred_element_type=f32).reshape(batches, rows, width)
        beta_stage[buffer] = jnp.dot(
            x, wb_ref[...], preferred_element_type=f32).reshape(batches, rows, 128)
        for copy in outs(turn, slot):
            copy.start()

    def in_line(index):
        far = (index + 1) // 2
        side = 1 - 2 * lax.rem(index, 2)
        z = o + side * far
        return far, z, (z >= 0) & (z < lines)

    def first(index, turn):
        far, z, valid = in_line(index)

        @pl.when(valid)
        def _():
            for m in range(batches):
                @pl.when(far > 0)
                def _():
                    left(z, m).wait_recv()

                @pl.when((o < lines - 1) & (z <= o))
                def _():
                    right(z, m).start()

                @pl.when((o > 0) & (z >= o))
                def _():
                    left(z, m).start()

                across(z, m).start()
            project(turn, z * 2 + i)

        return turn + valid.astype(jnp.int32)

    swap.start()
    turn = lax.fori_loop(0, 2 * lines - 1, first, jnp.int32(0))

    def second(index, turn):
        far, z, valid = in_line(index)

        @pl.when(valid)
        def _():
            to_right, to_left = pass_part(z)

            @pl.when(far > 0)
            def _():
                to_left.wait_recv()

            @pl.when((o < lines - 1) & (z <= o))
            def _():
                to_right.start()

            @pl.when((o > 0) & (z >= o))
            def _():
                to_left.start()

            keep_outs(z).start()
            for m in range(batches):
                across(z, m).wait_recv()
            project(turn, z * 2 + 1 - i)

        return turn + valid.astype(jnp.int32)

    lax.fori_loop(0, 2 * lines - 1, second, turn)
    for turn in range(2 * lines - 2, 2 * lines):
        for copy in outs(turn, 0):
            copy.wait()

    @pl.loop(0, lines)
    def _(z):
        keep_outs(z).wait()

        @pl.when((o < lines - 1) & (z <= o))
        def _():
            pass_part(z)[0].wait_send()
            for m in range(batches):
                right(z, m).wait_send()

        @pl.when((o > 0) & (z >= o))
        def _():
            pass_part(z)[1].wait_send()
            for m in range(batches):
                left(z, m).wait_send()

        for m in range(batches):

            across(z, m).wait_send()
            for y in range(2):
                keep(z * 2 + y, m).wait()

    swap.wait()


def gather_call_kernel(x_ref, o_ref, *refs):
    gather_kernel(x_ref, o_ref, refs[:3], refs[3:7], refs[7], refs[8], refs[9], refs[10:12], *refs[12:])


def gather_project(x, w_out_part, ffn_parts, w_inner, w_beta):
    batches, rows, model = x.shape
    more = w_out_part.shape[1]
    lines = lax.axis_size("z")
    width = sum(w.shape[1] for w in w_inner)
    slots = 2 * lines
    sems = pltpu.SemaphoreType.DMA
    anywhere = pl.BlockSpec(memory_space=pl.ANY)
    pair = sems((lines, batches))
    ranks, quarter, share = ffn_parts[0].shape
    gathered, outs, *projected, beta, pair_parts, down_part = pl.pallas_call(
        gather_call_kernel,
        out_shape=(
            jax.ShapeDtypeStruct((batches, slots, rows, model), bf16),
            jax.ShapeDtypeStruct((lines, batches, more, model), bf16),
            *[jax.ShapeDtypeStruct((slots, rows, width), f32)] * batches,
            jax.ShapeDtypeStruct((batches, slots, rows, 128), f32),
            jax.ShapeDtypeStruct((ranks, 2, quarter, share), bf16),
            jax.ShapeDtypeStruct((ranks, quarter, share), bf16),
        ),
        in_specs=[anywhere] * 5 + [vmem()] * 5,
        out_specs=(anywhere,) * (5 + batches),
        scratch_shapes=[
            pltpu.VMEM((slots, batches, rows, model), bf16),
            pltpu.VMEM((lines, batches, more, model), bf16),
            pltpu.VMEM((2, batches, rows, width), f32),
            pltpu.VMEM((2, batches, rows, 128), f32),
            pair, pair, pair, pair, pair, sems((lines,)), sems((lines,)), sems((lines,)),
            sems((2,)), sems((slots, batches)), sems((lines,)), sems((2, batches)), sems((2, batches)),
            sems((3, 3)), sems((3, 3)), sems((3,)),
        ],
        compiler_params=pltpu.CompilerParams(
            collective_id=1, has_side_effects=True, vmem_limit_bytes=40 * 2**20),
        cost_estimate=pl.CostEstimate(flops=10**11, bytes_accessed=4 * 10**7, transcendentals=0),
        name="gather_project",
    )(x, w_out_part, *ffn_parts, *w_inner, w_beta)
    total = slots * rows
    return (gathered.reshape(batches, total, model), outs,
            [wide.reshape(total, width) for wide in projected],
            beta.reshape(batches, total, 128), pair_parts, down_part)


def scatter_kernel(w_refs, g_refs, gb_refs, o_refs, inner_ref, wb_ref, small_ref, gains_ref, pair_ref, down_ref,
                   out_ref, small_out, outs_ref, inner_out, pair_out, down_out,
                   gs, bs, ysend, yrecv, from_left, from_right, part_sum, part_left, part_right, outs_s, inner_s, inner_r, small_s, small_r, gains_r,
                   pair_send, pair_recv, right_send, left_send, right_recv, left_recv, g_sem,
                   sum_send, sum_recv, outs_send, outs_recv, gain_send, gain_recv, part_sems, swap_send, swap_recv, swap_own, sum_sem):
    batches = len(g_refs)
    rows, width = gs.shape
    lines = yrecv.shape[0]
    model = yrecv.shape[3]
    o = lax.axis_index("z")
    i = lax.axis_index("y")
    core = lax.axis_index("core")
    me = lax.axis_index("x") * 2 + core
    tile = min(512, model)
    diagonal = {"x": 1 - lax.axis_index("x"), "core": 1 - core}
    slots = 2 * lines
    mine = o * 2 + i
    peers = []
    for d in range(1, slots):
        place = lax.rem(mine + d, slots)
        peers.append((place, {"z": place // 2, "y": lax.rem(place, 2)}))
    barrier = pltpu.get_barrier_semaphore()
    greeted = [other("core"), other("x"), diagonal] + [device for _, device in peers]
    for device in greeted:
        pl.semaphore_signal(barrier, inc=1, device_id=device, device_id_type=pl.DeviceIdType.MESH)
    pl.semaphore_wait(barrier, len(greeted))
    gain_copies = [
        line_copy(gains_ref.at[place], gains_r.at[mine], gain_send.at[d], gain_recv.at[d], device)
        for d, (place, device) in enumerate(peers)
    ]
    for copy in gain_copies:
        copy.start()

    inner_pair = line_copy(inner_ref.at[1 - core], inner_r.at[0], sum_send.at[0], sum_recv.at[0], other("core"))
    inner_across = line_copy(inner_s, inner_r.at[1], sum_send.at[1], sum_recv.at[1], other("x"))
    inner_back = line_copy(inner_s, inner_out.at[core], sum_send.at[2], sum_recv.at[2], other("core"))
    small_pair = line_copy(small_s.at[0], small_r.at[0], sum_send.at[3], sum_recv.at[3], other("core"))
    small_across = line_copy(small_s.at[1], small_r.at[1], sum_send.at[4], sum_recv.at[4], other("x"))
    inner_own = pltpu.make_async_copy(inner_ref.at[core], inner_s, sum_sem.at[0])
    inner_keep = pltpu.make_async_copy(inner_s, inner_out.at[core], sum_sem.at[1])
    outs_keep = pltpu.make_async_copy(outs_s, outs_ref.at[me], sum_sem.at[2])
    outs_away = [
        line_copy(outs_s, outs_ref.at[me], outs_send.at[n], outs_recv.at[n], target)
        for n, target in enumerate((other("core"), other("x"), diagonal))
    ]
    swap = Swap(
        [(pair_ref, lambda place: pair_out.at[place]), (down_ref, lambda place: down_out.at[place])],
        swap_send, swap_recv, swap_own)
    swap.start()
    inner_pair.start()
    inner_own.start()

    def add_into(target, other_ref):
        height = target.shape[0]
        step = next(size for size in range(min(128, height), 0, -16) if height % size == 0)

        @pl.loop(0, height // step)
        def _(n):
            at = pl.ds(pl.multiple_of(n * step, step), step)
            target[at, :] = (target[at, :].astype(f32) + other_ref[at, :].astype(f32)).astype(target.dtype)

    def target(index):
        far = lines - 1 - index // 2
        side = 1 - 2 * lax.rem(index, 2)
        z = o + side * far
        return far, z, (z >= 0) & (z < lines) & ((far > 0) | (side > 0))

    def load(z, y, m):
        slot = z * 2 + y
        return (pltpu.make_async_copy(g_refs[m].at[slot], gs, g_sem.at[0]),
                pltpu.make_async_copy(gb_refs[m].at[slot], bs, g_sem.at[1]))

    def partial_rows(z, y, m, store):
        for n in range(batches):
            @pl.when(m == n)
            def _():
                for copy in load(z, y, n):
                    copy.start()
        for copy in load(z, y, 0):
            copy.wait()
        g = gs[...]
        b = bs[...]
        for start in range(0, model, tile):
            cols = slice(start, start + tile)
            value = lax.dot_general(b, wb_ref[cols, :], NT, preferred_element_type=f32)
            for n, w_ref in enumerate(w_refs):
                part = g[:, n * w_ref.shape[1] : (n + 1) * w_ref.shape[1]]
                value = value + lax.dot_general(part, w_ref[cols, :], NT, preferred_element_type=f32)
            store(cols, value)

    def across(z, m):
        return line_copy(ysend.at[z, m], yrecv.at[z, m], pair_send.at[z, m], pair_recv.at[z, m], other("y"))

    def right(z, m):
        return line_copy(yrecv.at[z, m], from_left.at[z, m], right_send.at[z, m], right_recv.at[z, m], {"z": o + 1})

    def left(z, m):
        return line_copy(yrecv.at[z, m], from_right.at[z, m], left_send.at[z, m], left_recv.at[z, m], {"z": o - 1})

    def across_partial(z, m):
        def store(cols, value):
            ysend[z, m, :, cols] = value.astype(bf16)
        partial_rows(z, 1 - i, m, store)

    def pass_part(z):
        return (line_copy(part_sum.at[z], part_left.at[z], part_sems.at[0, z], part_sems.at[1, z], {"z": o + 1}),
                line_copy(part_sum.at[z], part_right.at[z], part_sems.at[2, z], part_sems.at[3, z], {"z": o - 1}))

    def part_round():
        @pl.loop(0, 2 * lines)
        def _(index):
            far, z, valid = target(index)

            @pl.when(valid & (far > 0))
            def _():
                to_right, to_left = pass_part(z)

                @pl.when((z > o) & (o > 0))
                def _():
                    to_right.wait_recv()
                    add_into(part_sum.at[z], part_left.at[z])

                @pl.when((z < o) & (o < lines - 1))
                def _():
                    to_left.wait_recv()
                    add_into(part_sum.at[z], part_right.at[z])

                @pl.when(z > o)
                def _():
                    to_right.start()

                @pl.when(z < o)
                def _():
                    to_left.start()

        to_right, to_left = pass_part(o)
        outs_s[...] = part_sum[o]

        @pl.when(o > 0)
        def _():
            to_right.wait_recv()
            add_into(outs_s, part_left.at[o])

        @pl.when(o < lines - 1)
        def _():
            to_left.wait_recv()
            add_into(outs_s, part_right.at[o])
        outs_keep.start()
        for copy in outs_away:
            copy.start()

    def side_work():
        left, left_in, right, right_in = o_refs
        column, row = lax.axis_index("y"), lax.axis_index("x")
        wide = model // 2
        for z in range(lines):
            part_sum[z, :, :wide] = (
                left[column, z].astype(f32) + left_in[z].astype(f32)).astype(bf16)
            part_sum[z, :, wide:] = (
                right[row, z].astype(f32) + right_in[z].astype(f32)).astype(bf16)
        part_round()
        inner_own.wait()
        inner_pair.wait_recv()
        add_into(inner_s, inner_r.at[0])
        inner_across.start()
        gains_r[mine] = gains_ref[mine]
        for copy in gain_copies:
            copy.wait_recv()
        tail = small_ref.shape[0]
        small_s[0, :tail] = small_ref[...]
        small_s[0, tail:] = jnp.sum(gains_r[...], axis=0)
        small_pair.start()

    total = 2 * lines * batches

    def turn(index, carry):
        before, earlier = carry
        far, z, valid = target(index // batches)
        m = lax.rem(index, batches)
        last = index >= total
        valid = valid & jnp.logical_not(last)
        moves = valid | last

        @pl.when(valid)
        def _():
            across_partial(z, m)

        @pl.when(valid)
        def _():
            across(z, m).start()

        @pl.when(moves & (before >= 0))
        def _():
            across(before // batches, lax.rem(before, batches)).wait_recv()

        @pl.when(valid & (before < 0))
        def _():
            side_work()

        @pl.when(moves & (before >= 0))
        def _():
            place, n = before // batches, lax.rem(before, batches)

            def store(cols, value):
                yrecv[place, n, :, cols] = (
                    yrecv[place, n, :, cols].astype(f32) + value).astype(bf16)
            partial_rows(place, i, n, store)

            @pl.when((place > o) & (o == 0))
            def _():
                right(place, n).start()

            @pl.when((place < o) & (o == lines - 1))
            def _():
                left(place, n).start()

        @pl.when(moves & (earlier >= 0))
        def _():
            place, n = earlier // batches, lax.rem(earlier, batches)

            @pl.when((place > o) & (o > 0))
            def _():
                right(place, n).wait_recv()
                add_into(yrecv.at[place, n], from_left.at[place, n])
                right(place, n).start()

            @pl.when((place < o) & (o < lines - 1))
            def _():
                left(place, n).wait_recv()
                add_into(yrecv.at[place, n], from_right.at[place, n])
                left(place, n).start()

        code = jnp.where(valid, z * batches + m, -1)
        return jnp.where(moves, code, before), jnp.where(moves, before, earlier)

    lax.fori_loop(0, total + 2, turn, (jnp.int32(-1), jnp.int32(-1)))

    inner_across.wait_recv()
    inner_across.wait_send()
    add_into(inner_s, inner_r.at[1])
    inner_back.start()
    inner_keep.start()
    small_pair.wait_recv()
    small_s[1] = small_s[0] + small_r[0]
    small_across.start()

    for m in range(batches):
        out_ref[m] = yrecv[o, m].astype(f32)

        @pl.when(o > 0)
        def _():
            right(o, m).wait_recv()
            out_ref[m] += from_left[o, m].astype(f32)

        @pl.when(o < lines - 1)
        def _():
            left(o, m).wait_recv()
            out_ref[m] += from_right[o, m].astype(f32)

    @pl.loop(0, lines)
    def _(z):
        for m in range(batches):
            across(z, m).wait_send()

            @pl.when(z > o)
            def _():
                right(z, m).wait_send()

            @pl.when(z < o)
            def _():
                left(z, m).wait_send()

        @pl.when(z > o)
        def _():
            pass_part(z)[0].wait_send()

        @pl.when(z < o)
        def _():
            pass_part(z)[1].wait_send()

    small_across.wait_recv()
    small_out[...] = small_s[1] + small_r[1]
    for copy in gain_copies:
        copy.wait_send()
    inner_pair.wait_send()
    small_pair.wait_send()
    small_across.wait_send()
    inner_back.wait_recv()
    inner_back.wait_send()
    inner_keep.wait()
    outs_keep.wait()
    swap.wait()
    for copy in outs_away:
        copy.wait_recv()
        copy.wait_send()


def scatter_call_kernel(*refs):
    scatter_kernel(refs[:4], refs[4:6], refs[6:8], refs[8:12], *refs[12:])


def scatter_rows(grads, beta_grads, out_grads, inner_grads, w_inner, w_beta, small, gains,
                 pair_grads, down_grads):
    batches = len(grads)
    total, width = grads[0].shape
    model = w_inner[0].shape[0]
    lines = lax.axis_size("z")
    slots = 2 * lines
    rows = total // slots
    more = out_grads[1].shape[1]
    sems = pltpu.SemaphoreType.DMA
    anywhere = pl.BlockSpec(memory_space=pl.ANY)
    slab = pltpu.VMEM((lines, batches, rows, model), bf16)
    part = pltpu.VMEM((lines, more, model), bf16)
    half = inner_grads.shape[1:]
    flat = (small.shape[0] + gains.shape[1], 128)
    return pl.pallas_call(
        scatter_call_kernel,
        out_shape=(
            jax.ShapeDtypeStruct((batches, rows, model), f32),
            jax.ShapeDtypeStruct(flat, f32),
            jax.ShapeDtypeStruct((4, more, model), bf16),
            jax.ShapeDtypeStruct(inner_grads.shape, bf16),
            jax.ShapeDtypeStruct(pair_grads.shape, bf16),
            jax.ShapeDtypeStruct(down_grads.shape, bf16),
        ),
        in_specs=[vmem()] * 4 + [anywhere] * 4 + [vmem()] * 4
        + [anywhere, vmem(), vmem(), vmem(), anywhere, anywhere],
        out_specs=(vmem(), vmem()) + (anywhere,) * 4,
        scratch_shapes=[
            pltpu.VMEM((rows, width), bf16),
            pltpu.VMEM((rows, 128), bf16),
            slab, slab, slab, slab, part, part, part,
            pltpu.VMEM((more, model), bf16),
            pltpu.VMEM(half, bf16),
            pltpu.VMEM((2, *half), bf16),
            pltpu.VMEM((2, *flat), f32),
            pltpu.VMEM((2, *flat), f32),
            pltpu.VMEM(gains.shape, f32),
            sems((lines, batches)), sems((lines, batches)), sems((lines, batches)),
            sems((lines, batches)), sems((lines, batches)), sems((lines, batches)),
            sems((2,)), sems((5,)), sems((5,)), sems((3,)), sems((3,)), sems((slots,)), sems((slots,)), sems((4, lines)),
            sems((2, 3)), sems((2, 3)), sems((2,)), sems((3,)),
        ],
        compiler_params=pltpu.CompilerParams(
            collective_id=3, has_side_effects=True, vmem_limit_bytes=58 * 2**20),
        cost_estimate=pl.CostEstimate(flops=7 * 10**10, bytes_accessed=4 * 10**7, transcendentals=0),
        name="scatter_rows",
    )(*w_inner, *[grad.reshape(slots, rows, width) for grad in grads],
      *[grad.reshape(slots, rows, 128) for grad in beta_grads], *out_grads,
      inner_grads, w_beta, small, gains,
      pair_grads, down_grads)


def tensor_peers(slots):
    mine = lax.axis_index("z") * 2 + lax.axis_index("y")
    places = [lax.rem(mine + d, slots) for d in range(1, slots)]
    return mine, [(place, {"z": place // 2, "y": lax.rem(place, 2)}) for place in places]


def greet(devices):
    barrier = pltpu.get_barrier_semaphore()
    for device in devices:
        pl.semaphore_signal(barrier, inc=1, device_id=device, device_id_type=pl.DeviceIdType.MESH)
    pl.semaphore_wait(barrier, len(devices))


def attend_kernel(x_ref, low_first, low_second, gain_ref, *refs):
    pieces, refs = refs[:8], refs[8:]
    hidden_ref, normed_ref, w_ref, heads_ref, ws, heads, send, recv, sem, own_sem = refs
    slots = heads.shape[1]
    mine, peers = tensor_peers(slots)
    greet([device for _, device in peers])
    lows = (low_first, low_second)
    away = [
        line_copy(low.at[place], heads.at[m, mine], send.at[m, d], recv.at[m, d], device)
        for d, (place, device) in enumerate(peers) for m, low in enumerate(lows)
    ]
    for copy in away:
        copy.start()
    own = [pltpu.make_async_copy(low.at[mine], heads.at[m, mine], own_sem.at[m]) for m, low in enumerate(lows)]
    for copy in own:
        copy.start()
    x = lax.axis_index("x")
    core = lax.axis_index("core")
    y = lax.axis_index("y")
    copies = []
    for n, piece in enumerate(pieces):
        far_y, far_x, far_core = n // 4, n // 2 % 2, n % 2
        column = 1 - y if far_y else y
        quarter = (1 - x if far_x else x) * 2 + (1 - core if far_core else core)
        copies.append(pltpu.make_async_copy(piece, ws.at[:, column, quarter], sem.at[n]))
    for copy in copies:
        copy.start()
    for copy in copies + own:
        copy.wait()
    keep = pltpu.make_async_copy(ws, w_ref, own_sem.at[2])
    keep.start()
    for copy in away:
        copy.wait_recv()
    keep_heads = pltpu.make_async_copy(heads, heads_ref, own_sem.at[3])
    keep_heads.start()
    model = x_ref.shape[1]
    tile = min(512, model)
    width = heads.shape[3]
    squares = 0.0
    for start in range(0, model, tile):
        cols = slice(start, start + tile)
        total = x_ref[:, cols].astype(f32)
        for t in range(slots):
            left = jnp.concatenate([heads[0, t], heads[1, t]], axis=0)
            total = total + jnp.dot(
                left, ws[t // 2, t % 2, :, :, cols].reshape(width, tile), preferred_element_type=f32)
        hidden_ref[:, cols] = total
        squares = squares + jnp.sum(total * total, axis=-1, keepdims=True)
    scale = lax.rsqrt(squares / model + epsilon)
    for start in range(0, model, tile):
        cols = slice(start, start + tile)
        normed_ref[:, cols] = (hidden_ref[:, cols] * scale * gain_ref[:, cols]).astype(bf16)
    keep.wait()
    keep_heads.wait()
    for copy in away:
        copy.wait_send()


def attend(x, lows, gain, pieces):
    rows, model = x.shape
    lines, part, _ = pieces[0].shape
    full = (lines, 2, 4, part, model)
    heads = (2, *lows[0].shape)
    slots = 2 * lines
    anywhere = pl.BlockSpec(memory_space=pl.ANY)
    sems = pltpu.SemaphoreType.DMA
    return pl.pallas_call(
        attend_kernel,
        out_shape=(
            jax.ShapeDtypeStruct((rows, model), f32),
            jax.ShapeDtypeStruct((rows, model), bf16),
            jax.ShapeDtypeStruct(full, bf16),
            jax.ShapeDtypeStruct(heads, bf16),
        ),
        in_specs=[vmem(), anywhere, anywhere, vmem()] + [anywhere] * 8,
        out_specs=(vmem(), vmem(), anywhere, anywhere),
        scratch_shapes=[
            pltpu.VMEM(full, bf16), pltpu.VMEM(heads, bf16),
            sems((2, slots)), sems((2, slots)), sems((8,)), sems((4,))],
        compiler_params=pltpu.CompilerParams(
            collective_id=4, has_side_effects=True, vmem_limit_bytes=32 * 2**20),
        cost_estimate=pl.CostEstimate(flops=3 * 10**10, bytes_accessed=2 * 10**7, transcendentals=0),
        name="attend",
    )(x, *lows, gain, *pieces)


def attend_back_kernel(hidden_ref, ffn_ref, grad_ref, c_ref, gain_ref, w_ref, heads,
                       result_ref, hgrad_ref, back_first, back_second, left_mine, left_theirs,
                       right_mine, right_theirs, gain_out, low, wgrad, wrecv, backs, send, recv, sem, core_sem):
    rows, model = hidden_ref.shape
    half = rows // 2
    tile = min(512, model)
    slots = heads.shape[1]
    width = heads.shape[3]
    mine, peers = tensor_peers(slots)
    greet([device for _, device in peers] + [other("core")])
    squares, dots = 0.0, 0.0
    for start in range(0, model, tile):
        cols = slice(start, start + tile)
        hidden = hidden_ref[:, cols]
        squares = squares + jnp.sum(hidden * hidden, axis=-1, keepdims=True)
        dots = dots + jnp.sum(hidden * grad_ref[:, cols] * gain_ref[:, cols], axis=-1, keepdims=True)
    scale = lax.rsqrt(squares / model + epsilon)
    pull = scale * scale * scale * (dots / model)
    for start in range(0, model, tile):
        cols = slice(start, start + tile)
        hidden = hidden_ref[:, cols]
        grad = grad_ref[:, cols]
        result_ref[:, cols] = hidden + ffn_ref[:, cols]
        gain_out[:, cols] = jnp.sum(grad * hidden * scale, axis=0, keepdims=True)
        hgrad = c_ref[:, cols].astype(f32) + scale * (grad * gain_ref[:, cols]) - hidden * pull
        hgrad_ref[:, cols] = hgrad
        low[:, cols] = hgrad.astype(bf16)

    outs = (back_first, back_second)

    def away(m, d):
        place = lax.rem(mine + d, slots)
        return line_copy(backs.at[m, d], outs[m].at[mine], send.at[m, d], recv.at[m, d],
                         {"z": place // 2, "y": lax.rem(place, 2)})

    @pl.loop(0, slots)
    def _(step):
        d = slots - 1 - step
        place = lax.rem(mine + d, slots)
        back = lax.dot_general(
            low[...], w_ref[place // 2, lax.rem(place, 2)].reshape(width, model), NT,
            preferred_element_type=f32)
        for m in range(2):
            backs[m, d] = back[m * half : (m + 1) * half].astype(bf16)

            @pl.when(d > 0)
            def _():
                away(m, d).start()

            @pl.when(d == 0)
            def _():
                pltpu.make_async_copy(backs.at[m, 0], outs[m].at[mine], sem.at[2 + m]).start()

    for t in range(slots):
        left = jnp.concatenate([heads[0, t], heads[1, t]], axis=0)
        for start in range(0, model, tile):
            cols = slice(start, start + tile)
            value = lax.dot_general(
                left, low[:, cols], (((0,), (0,)), ((), ())), preferred_element_type=f32
            ).astype(bf16).reshape(2, 2, width // 4, tile)
            for c in range(2):
                wgrad[c, :, t % 2, t // 2, :, cols] = value[:, c]
    core = lax.axis_index("core")
    to_pair = line_copy(wgrad.at[1 - core], wrecv, core_sem.at[0], core_sem.at[1], other("core"))
    to_pair.start()
    to_pair.wait_recv()
    lines = wgrad.shape[3]
    for far_x in range(2):
        for far_y in range(2):
            @pl.loop(0, lines)
            def _(z):
                wrecv[far_x, far_y, z] = (
                    wrecv[far_x, far_y, z].astype(f32) + wgrad[core, far_x, far_y, z].astype(f32)
                ).astype(bf16)
    x, y = lax.axis_index("x"), lax.axis_index("y")
    wide = model // 2
    keeps = [
        pltpu.make_async_copy(source.at[..., pl.ds(start, wide)], target, sem.at[4 + n])
        for n, (source, start, target) in enumerate((
            (wrecv.at[x], 0, left_mine), (wrecv.at[1 - x], 0, left_theirs),
            (wrecv.at[:, y], wide, right_mine), (wrecv.at[:, 1 - y], wide, right_theirs)))
    ]
    for copy in keeps:
        copy.start()
    for copy in keeps:
        copy.wait()
    to_pair.wait_send()
    for m in range(2):
        pltpu.make_async_copy(backs.at[m, 0], outs[m].at[mine], sem.at[2 + m]).wait()
        for d in range(1, slots):
            away(m, d).wait_recv()
            away(m, d).wait_send()


def attend_back(hidden, ffn_out, normed_grad, c_rows, gain, w_full, heads):
    rows, model = hidden.shape
    wide = jax.ShapeDtypeStruct((rows, model), f32)
    lines, _, _, part, _ = w_full.shape
    share = (2, 2, lines, part, model)
    slots = 2 * lines
    back = jax.ShapeDtypeStruct(heads.shape[1:], bf16)
    anywhere = pl.BlockSpec(memory_space=pl.ANY)
    sems = pltpu.SemaphoreType.DMA
    return pl.pallas_call(
        attend_back_kernel,
        out_shape=(
            wide, wide, back, back,
            *[jax.ShapeDtypeStruct((2, lines, part, model // 2), bf16)] * 4,
            jax.ShapeDtypeStruct((1, model), f32),
        ),
        in_specs=[vmem()] * 7,
        out_specs=(vmem(),) * 2 + (anywhere,) * 6 + (vmem(),),
        scratch_shapes=[
            pltpu.VMEM((rows, model), bf16), pltpu.VMEM((2, *share), bf16), pltpu.VMEM(share, bf16),
            pltpu.VMEM(heads.shape, bf16), sems((2, slots)), sems((2, slots)), sems((8,)), sems((2,))],
        compiler_params=pltpu.CompilerParams(
            collective_id=5, has_side_effects=True, vmem_limit_bytes=48 * 2**20),
        cost_estimate=pl.CostEstimate(flops=3 * 10**10, bytes_accessed=4 * 10**7, transcendentals=0),
        name="attend_back",
    )(hidden, ffn_out, normed_grad, c_rows, gain, w_full, heads)


def inner_grads_kernel(x_ref, g_first, g_second, b_first, b_second, w0, w1, w2, w3, wb_ref,
                       low_ref, beta_ref, gain_ref):
    dims = (((0,), (0,)), ((), ()))
    beta = 0.0
    for m, b_ref in enumerate((b_first, b_second)):
        beta = beta + lax.dot_general(x_ref[m], b_ref[...], dims, preferred_element_type=f32)
    beta_ref[...] = beta
    gain = jnp.sum(beta * wb_ref[...].astype(f32), axis=1, keepdims=True)
    for n, w_ref in enumerate((w0, w1, w2, w3)):
        width = w_ref.shape[1]
        cols = slice(n * width, (n + 1) * width)
        value = 0.0
        for m, g_ref in enumerate((g_first, g_second)):
            value = value + lax.dot_general(x_ref[m], g_ref[:, cols], dims, preferred_element_type=f32)
        low_ref[:, cols] = value.astype(bf16)
        gain = gain + jnp.sum(value * w_ref[...].astype(f32), axis=1, keepdims=True)
    gain_ref[...] = jnp.broadcast_to(gain, gain_ref.shape)


def inner_grads(tokens, grads, beta_grads, w_inner, w_beta):
    _, total, model = tokens.shape
    wide = grads[0].shape[1]
    width = w_inner[0].shape[1]
    tile = 256

    def whole(columns):
        return pl.BlockSpec((total, columns), lambda n: (0, 0))

    def rows(columns):
        return pl.BlockSpec((tile, columns), lambda n: (n, 0))

    return pl.pallas_call(
        inner_grads_kernel,
        out_shape=(
            jax.ShapeDtypeStruct((model, wide), bf16),
            jax.ShapeDtypeStruct((model, 128), f32),
            jax.ShapeDtypeStruct((model, 128), f32),
        ),
        grid=(model // tile,),
        in_specs=[pl.BlockSpec((2, total, tile), lambda n: (0, 0, n))]
        + [whole(wide)] * 2 + [whole(128)] * 2 + [rows(width)] * 4 + [rows(128)],
        out_specs=(rows(wide), rows(128), rows(128)),
        compiler_params=pltpu.CompilerParams(vmem_limit_bytes=40 * 2**20),
        cost_estimate=pl.CostEstimate(flops=10**10, bytes_accessed=2 * 10**7, transcendentals=0),
        name="inner_grads",
    )(tokens, *grads, *beta_grads, *w_inner, w_beta)


def root_scale(row_values, gain_vector):
    row_scale = lax.rsqrt(jnp.mean(row_values * row_values, axis=-1, keepdims=True) + epsilon)
    return (row_values * row_scale * gain_vector, row_scale)


def norm_backward(row_values, row_scale, gain_vector, normed_grad):
    weighted = normed_grad * gain_vector
    rows_grad = row_scale * weighted - row_values * row_scale * row_scale * row_scale * jnp.mean(
        weighted * row_values, axis=-1, keepdims=True
    )
    gain_grad = jnp.sum(normed_grad * row_values * row_scale, axis=tuple(range(row_values.ndim - 1)))
    return (rows_grad, gain_grad)


DP = ("x", "core")
TP = ("z", "y")


def gather(x, axis_name, axis=0):
    return lax.all_gather(x, axis_name, axis=axis, tiled=True)


def scatter_sum(x, axis_name, axis=0):
    return lax.psum_scatter(
        x.astype(bf16), axis_name, scatter_dimension=axis, tiled=True
    ).astype(f32)


def dot(a, b):
    return jnp.dot(a, b, preferred_element_type=f32)


def dot_nt(a, b):
    return jnp.einsum("tk,nk->tn", a, b, preferred_element_type=f32)


def dot_tn(a, b):
    return jnp.einsum("tm,tn->mn", a, b, preferred_element_type=f32)


def exchange(x, axis_name, distance=1):
    size = lax.axis_size(axis_name)
    return lax.ppermute(x, axis_name, [(i, i ^ distance) for i in range(size)])


def pick(x, index, axis):
    return lax.dynamic_index_in_dim(x, index, axis, keepdims=False)


def after(x, *others):
    return lax.optimization_barrier((x, *others))[0]


def add_low(x, y):
    return (x.astype(f32) + y.astype(f32)).astype(bf16)


def halve_sum(grad, axis_name):
    me = lax.axis_index(axis_name)
    return add_low(pick(grad, me, 0), exchange(pick(grad, 1 - me, 0), axis_name))


def feed_forward_groups(normed, cotangents, w_gate, w_up, w_down):
    gate_full = gather(w_gate, DP)
    up_full = gather(w_up, DP)
    down_full = gather(w_down, DP, 1)
    outs, normed_grads, inner_rows, gate_grads, up_grads, rows, grad_rows = [], [], [], [], [], [], []
    for m in range(normed.shape[0]):
        rows.append(gather(normed[m], TP))
        grad_rows.append(gather(cotangents[m], TP))
        gate_values = dot(rows[m], gate_full)
        up_values = dot(rows[m], up_full)
        sigmoid_gate = jax.nn.sigmoid(gate_values)
        silu_gate = gate_values * sigmoid_gate
        inner = (silu_gate * up_values).astype(bf16)
        inner_grad = dot_nt(grad_rows[m], down_full)
        gate_grad = (
            inner_grad * up_values * sigmoid_gate * (1.0 + gate_values * (1.0 - sigmoid_gate))
        ).astype(bf16)
        up_grad = (inner_grad * silu_gate).astype(bf16)
        normed_grads.append(scatter_sum(dot_nt(gate_grad, gate_full) + dot_nt(up_grad, up_full), TP))
        outs.append(scatter_sum(dot(inner, down_full), TP))
        inner_rows.append(inner)
        gate_grads.append(gate_grad)
        up_grads.append(up_grad)
    grad_all = jnp.concatenate(grad_rows)
    rows_all = jnp.concatenate(rows)
    gate_share = scatter_sum(dot_tn(rows_all, jnp.concatenate(gate_grads)), DP)
    up_share = scatter_sum(dot_tn(rows_all, jnp.concatenate(up_grads)), DP)
    down_share = scatter_sum(dot_tn(jnp.concatenate(inner_rows), grad_all), DP, 1)
    return jnp.stack(outs), jnp.stack(normed_grads), (gate_share, up_share, down_share)


def per_device(
    inputs,
    lengths,
    norm_gain,
    ffn_gain,
    w_query,
    w_key,
    w_value,
    w_gate_out,
    w_beta,
    conv_weight,
    head_gain,
    w_out,
    w_gate,
    w_up,
    w_down,
    cotangent,
):
    batches = range(inputs.shape[0])
    local_width = w_query.shape[1]
    heads = w_beta.shape[1]
    devices = lax.axis_size(TP)
    planar = all(lax.axis_size(name) == 2 for name in ("x", "core", "y"))
    w_parts = (w_query, w_key, w_value, w_gate_out)
    w_inner = jnp.concatenate(w_parts, axis=1)
    w_beta_wide = jnp.pad(w_beta, ((0, 0), (0, 128 - heads)))
    taps = conv_weight.astype(f32).reshape(-1, local_width)
    gain_heads = head_gain.astype(f32)
    gains = gather(jnp.stack([norm_gain, ffn_gain]), DP, 1)
    gain_one, gain_two = gains[0].astype(f32), gains[1].astype(f32)
    rows_in = inputs.astype(f32)
    normed_one, scale_one = root_scale(rows_in, gain_one)
    normed_one = normed_one.astype(bf16)

    def run_mixer(m, wide, logits):
        low, *kept = mixer_forward(lengths[m, 0], wide, logits, taps, gain_heads, exact=False)
        return low, kept

    def back_mixer(m, wide, logits, grad, kept):
        return mixer_backward(
            lengths[m, 0], wide, logits, taps, gain_heads, grad, kept, exact=False)

    if planar:
        count = rows_in.shape[0] * rows_in.shape[1]
        model = rows_in.shape[2]
        ranks = lax.axis_size(DP)
        ffn_parts = [
            w.reshape(ranks, -1, w.shape[1]) for w in after((w_gate.T, w_up.T, w_down), gains)]
        c_rows = [None] * 8
        c_rows[0] = after(cotangent.reshape(count, model), gains)
        c_rows[4] = exchange(c_rows[0], "core")
        out_shares = pick(
            w_out.reshape(lax.axis_size(DP), len(batches), -1, model), lax.axis_index(DP), 0)
        gathered_one, out_own, projected, beta_logits, own_weights, own_down = gather_project(
            normed_one, out_shares, ffn_parts, w_parts, w_beta_wide)
        early = after(c_rows[0], gathered_one)
        c_rows[1] = exchange(early, "x")
        weights = gather(own_weights[None], "z")
        c_rows[2] = exchange(early, "y")
        out_own = out_own.reshape(out_own.shape[0], -1, model)
        out_y = exchange(out_own, "y")
        out_x = exchange(out_own, "x")
    else:
        gathered_one = jnp.stack([gather(normed_one[m], TP) for m in batches])
        projected = [dot(gathered_one[m], w_inner) for m in batches]
        beta_logits = [dot(gathered_one[m], w_beta_wide) for m in batches]
        out_full = gather(w_out, TP)
    token_heads, saved = [], []
    for m in batches:
        low, kept = run_mixer(m, projected[m], beta_logits[m])
        saved.append(kept)
        if planar and m == 0:
            out_y, c_rows[1], c_rows[2] = after((out_y, c_rows[1], c_rows[2]), low)
            out_xy = exchange(out_y, "x")
            c_rows[3] = exchange(c_rows[1], "y")
            c_rows[5] = exchange(c_rows[1], "core")
            c_rows[6] = exchange(c_rows[2], "core")
            projected[1] = after(projected[1], out_y, c_rows[2])
        low = low.reshape(devices, -1, local_width)
        if not planar:
            low = lax.all_to_all(low, TP, split_axis=0, concat_axis=0, tiled=True)
        token_heads.append(low)
    if planar:
        out_x, out_xy, c_rows[3] = after((out_x, out_xy, c_rows[3]), low)
        out_pieces = []
        for piece in (out_own, out_x, out_y, out_xy):
            out_pieces += [piece, exchange(piece, "core")]
        c_rows[7] = exchange(c_rows[3], "core")
        hidden, normed_two, out_full, token_heads = attend(
            inputs.reshape(count, model), token_heads, gain_two[None], out_pieces)
        ffn_out, normed_grad, weight_grads, down_grad = ffn_plane(normed_two, weights, own_down, c_rows)
        result_rows, hidden_grad, *mixed_grads, left, left_away, right, right_away, gain_two_sum = attend_back(
            hidden, ffn_out, normed_grad, c_rows[0], gain_two[None], out_full, token_heads)
        weight_grads = after(weight_grads, left)
        own_grads = lax.psum_scatter(weight_grads, "z", scatter_dimension=0, tiled=True)
        gain_two_sum = gain_two_sum[0]
        result_rows = result_rows.reshape(rows_in.shape)
        hidden_grad = hidden_grad.reshape(rows_in.shape)
    else:
        heads_rows = [
            block.swapaxes(0, 1).reshape(-1, devices * local_width) for block in token_heads]
        hidden = rows_in + jnp.stack([dot(rows, out_full) for rows in heads_rows])
        normed_two, scale_two = root_scale(hidden, gain_two)
        ffn_out, normed_grad, (gate_share, up_share, down_share) = feed_forward_groups(
            normed_two.astype(bf16), cotangent, w_gate, w_up, w_down)
        result_rows = hidden + ffn_out
        norm_grad, gain_two_sum = norm_backward(hidden, scale_two, gain_two, normed_grad)
        hidden_grad = cotangent.astype(f32) + norm_grad
        attended_low = hidden_grad.astype(bf16)
        mixed_grads = [
            dot_nt(attended_low[m], out_full).astype(bf16)
            .reshape(-1, devices, local_width).swapaxes(0, 1) for m in batches]
        out_grad = dot_tn(
            jnp.concatenate(heads_rows), jnp.concatenate(list(attended_low))).astype(bf16)
    if not planar:
        mixed_grads = [
            lax.all_to_all(grad, TP, split_axis=0, concat_axis=0, tiled=True)
            for grad in mixed_grads]
    mixed_grads = [grad.reshape(-1, local_width) for grad in mixed_grads]
    if planar:
        left = add_low(left, exchange(left_away, "x"))
        right = add_low(right, exchange(right_away, "y"))
    projected_low, beta_low = [], []
    taps_sum, heads_sum = 0.0, 0.0
    for m in batches:
        if planar and m > 0:
            mixed_grads[m] = after(mixed_grads[m], left, right)
        projected_grad, beta_grad, taps_part, heads_part = back_mixer(
            m, projected[m], beta_logits[m], mixed_grads[m], saved[m])
        taps_sum = taps_sum + taps_part
        heads_sum = heads_sum + heads_part
        projected_low.append(projected_grad)
        beta_low.append(beta_grad)
    if planar:
        left_in = exchange(pick(left, 1 - lax.axis_index("y"), 0), "y")
        right_in = exchange(pick(right, 1 - lax.axis_index("x"), 0), "x")
        low_sum, beta_sum, gain_rows = inner_grads(
            gathered_one, projected_low, beta_low, w_parts, w_beta_wide)
        beta_sum = beta_sum[:, :heads]
        gain_one_sum = gain_rows[:, 0] / gain_one
    else:
        tokens = gathered_one.reshape(-1, gathered_one.shape[2])
        inner_sum = dot_tn(tokens, jnp.concatenate(projected_low))
        beta_sum = dot_tn(tokens, jnp.concatenate(beta_low)[:, :heads])
        gain_one_sum = (
            jnp.sum(inner_sum * w_inner.astype(f32), axis=1)
            + jnp.sum(beta_sum * w_beta.astype(f32), axis=1)
        ) / gain_one
        low_sum = inner_sum.astype(bf16)
    gain_parts = jnp.stack([gain_one_sum, gain_two_sum])
    sums = [part.reshape(-1, 128) for part in (beta_sum.T, taps_sum, heads_sum)]
    marks = [sums[0].shape[0], sums[0].shape[0] + sums[1].shape[0], sum(part.shape[0] for part in sums)]
    small = jnp.concatenate(sums)
    if planar:
        ranks = lax.axis_size(DP)
        gain_parts = gain_parts.reshape(2, ranks, devices, -1).transpose(2, 0, 1, 3)
        chunk = gain_parts.shape[3]
        gain_parts = gain_parts.reshape(devices, -1, 128)
        gain_rows = gain_parts.shape[1]
        gain_parts = jnp.pad(gain_parts, ((0, 0), (0, -gain_rows % 8), (0, 0)))
        small = jnp.pad(small, ((0, -small.shape[0] % 8), (0, 0)))
        input_norm, flat, out_total, inner_total, pair_grads, down_grads = scatter_rows(
            projected_low, beta_low, (left, left_in, right, right_in),
            low_sum.reshape(2, -1, low_sum.shape[1]), w_parts, w_beta_wide, small, gain_parts,
            own_grads[0], down_grad)
        gate_share, up_share = (
            pair_grads[:, kind].reshape(-1, pair_grads.shape[3]).astype(f32).T for kind in range(2))
        down_share = down_grads.reshape(w_down.shape).astype(f32)
        gain_totals = pick(
            flat[small.shape[0] :][:gain_rows].reshape(2, ranks, chunk), lax.axis_index(DP), 1)
        small = flat[: small.shape[0]]
        out_total = out_total.reshape(w_out.shape).astype(f32)
        inner_total = inner_total.reshape(low_sum.shape)
    else:
        gain_totals = lax.psum_scatter(gain_parts, DP + TP, scatter_dimension=1, tiled=True)
        inner_total = lax.psum(low_sum, DP)
        small = lax.psum(small, DP)
        out_grad = lax.psum_scatter(out_grad, TP, scatter_dimension=0, tiled=True)
        out_total = lax.psum(out_grad, DP).astype(f32)
        input_norm = jnp.stack([
            scatter_sum(
                dot_nt(projected_low[m], w_inner) + dot_nt(beta_low[m], w_beta_wide), TP)
            for m in batches])
    norm_grad, _ = norm_backward(rows_in, scale_one, gain_one, input_norm)
    beta_total = small[: marks[0]].reshape(heads, -1).T
    conv_total = small[marks[0] : marks[1]].reshape(conv_weight.shape)
    heads_total = small[marks[1] : marks[2]].reshape(head_gain.shape)
    columns = [
        inner_total[:, n * local_width : (n + 1) * local_width].astype(f32) for n in range(4)]
    return (
        result_rows,
        hidden_grad + norm_grad,
        gain_totals[0],
        gain_totals[1],
        *columns,
        beta_total,
        conv_total,
        heads_total,
        out_total,
        gate_share,
        up_share,
        down_share,
    )


def solution(mesh):
    dp, tensor = mesh.shape["dp"], mesh.shape["tensor"]
    inner = 2 if tensor == 8 else 4
    axes = ("x", "core", "z", "y")
    fine = jax.sharding.Mesh(
        mesh.devices.reshape(dp // 2, 2, tensor // inner, inner), axes)
    tokens = P(None, DP + TP, None)
    in_specs = (
        tokens,
        P(None, DP, None),
        P(DP),
        P(DP),
        P(None, TP),
        P(None, TP),
        P(None, TP),
        P(None, TP),
        P(None, TP),
        P(None, None, TP),
        P(TP, None),
        P(TP, None),
        P(DP, TP),
        P(DP, TP),
        P(TP, DP),
        tokens,
    )
    out_specs = (
        tokens,
        tokens,
        P(DP + TP),
        P(DP + TP),
        P(None, TP),
        P(None, TP),
        P(None, TP),
        P(None, TP),
        P(None, TP),
        P(None, None, TP),
        P(TP, None),
        P(TP, None),
        P(DP, TP),
        P(DP, TP),
        P(TP, DP),
    )
    return jax.shard_map(
        per_device, mesh=fine, in_specs=in_specs, out_specs=out_specs, check_vma=False
    )
```

```python
from functools import partial

import jax
import jax.numpy as jnp
from jax import lax
from jax.experimental import pallas as pl
from jax.experimental.pallas import tpu as pltpu
from jax.sharding import PartitionSpec as P


CHUNK = 128
HALO = 8
epsilon = 1e-06
highest = lax.Precision.HIGHEST
f32 = jnp.float32
bf16 = jnp.bfloat16


def product(left, right, left_dim, right_dim, exact=False):
    dims = (((left_dim,), (right_dim,)), ((), ()))
    if exact:
        return lax.dot_general(left, right, dims, precision=highest, preferred_element_type=f32)
    return lax.dot_general(
        left.astype(bf16), right.astype(bf16), dims, preferred_element_type=f32
    )


def sigmoid(x):
    return 1.0 / (1.0 + jnp.exp(-x))


def segment_tools(lengths_ref):
    ends = []
    total = 0
    for i in range(lengths_ref.shape[0] - 1):
        total = total + lengths_ref[i]
        ends.append(total)

    def segment_of(pos):
        result = 0
        for end in ends:
            result = result + (pos >= end).astype(jnp.int32)
        return result

    return segment_of, len(ends)


def chunk_masks(segment_of, base, chunk):
    col = base + lax.broadcasted_iota(jnp.int32, (chunk, 1), 0)
    row = base + lax.broadcasted_iota(jnp.int32, (1, chunk), 1)
    seg_col = segment_of(col)
    seg_row = segment_of(row)
    first = segment_of(base - 1)
    last = segment_of(base + chunk - 1)
    same = seg_col == seg_row
    strict = (same & (col > row)).astype(f32)
    within = (same & (col >= row)).astype(f32)
    has_past = base > 0
    carry = ((seg_col == first) & has_past).astype(f32)
    close = (seg_col == last).astype(f32)
    keep = ((first == last) & has_past).astype(f32)
    return strict, within, carry, close, keep


def level_masks(chunk):
    row = lax.broadcasted_iota(jnp.int32, (chunk, chunk), 0)
    col = lax.broadcasted_iota(jnp.int32, (chunk, chunk), 1)
    masks = []
    width = 1
    while width < chunk:
        mask = (
            (row // (2 * width) == col // (2 * width))
            & ((row // width) % 2 == 1)
            & ((col // width) % 2 == 0)
        )
        masks.append(mask)
        width *= 2
    return masks, (row == col).astype(f32)


def conv_part(proj_ref, tap_ref, segment_of, base, part, width, chunk):
    taps = tap_ref.shape[0] // 3
    cols = pl.ds(part * width, width)
    main = proj_ref[pl.ds(base, chunk), cols]
    prev = proj_ref[pl.ds(pl.multiple_of(jnp.maximum(base - HALO, 0), HALO), HALO), cols]
    full = jnp.concatenate([prev, main], axis=0)
    col = base + lax.broadcasted_iota(jnp.int32, (chunk, 1), 0)
    seg = segment_of(col)
    total = main * tap_ref[part * taps : part * taps + 1, :]
    shifted = [main]
    for s in range(1, taps):
        valid = (segment_of(col - s) == seg) & (col >= s)
        moved = jnp.where(valid, pltpu.roll(full, s, 0)[HALO:], 0.0)
        shifted.append(moved)
        total = total + moved * tap_ref[part * taps + s : part * taps + s + 1, :]
    return total, shifted


def heads_of(x, heads):
    return [x[:, h * 128 : (h + 1) * 128] for h in range(heads)]


def unit_rows(a, scale):
    r = lax.rsqrt(jnp.sum(a * a, axis=-1, keepdims=True) + epsilon)
    return a * (r * scale)


def mixer_forward_kernel(exact, group, lengths_ref, proj_ref, beta_ref, tap_ref, gain_ref,
                         mixed_ref, heads_ref, fixed_ref, delta_ref, state_ref, inverse_ref,
                         query_s, key_s, value_s, score_s):
    rows_all = proj_ref.shape[0]
    width = proj_ref.shape[1] // 4
    heads = width // 128
    chunk = CHUNK
    count = rows_all // chunk
    segment_of, segments = segment_tools(lengths_ref)

    @pl.loop(0, count)
    def _(c):
        base = pl.multiple_of(c * chunk, chunk)
        rows = pl.ds(base, chunk)
        for part, target in enumerate((query_s, key_s, value_s)):
            pre, _ = conv_part(proj_ref, tap_ref, segment_of, base, part, width, chunk)
            act = pre * sigmoid(pre)
            if part == 2:
                target[rows, :] = act
            else:
                scale = 128 ** (-0.5) if part == 0 else 1.0
                for h, a in enumerate(heads_of(act, heads)):
                    target[rows, h * 128 : (h + 1) * 128] = unit_rows(a, scale)

    def beta_of(base, h):
        pos = base + lax.broadcasted_iota(jnp.int32, (chunk, 1), 0)
        live = (segment_of(pos) < segments).astype(f32)
        return sigmoid(beta_ref[pl.ds(base, chunk), h : h + 1]) * live

    masks, eye = level_masks(chunk)

    @pl.loop(0, count // group)
    def _(g):
        lowers, places = [], []
        for i in range(group):
            c = g * group + i
            base = pl.multiple_of(c * chunk, chunk)
            strict, within, _, _, _ = chunk_masks(segment_of, base, chunk)
            for h in range(heads):
                cols = slice(h * 128, (h + 1) * 128)
                k = key_s[pl.ds(base, chunk), cols]
                q = query_s[pl.ds(base, chunk), cols]
                lowers.append(product(k, k, 1, 1, exact) * strict * beta_of(base, h))
                score_s[c * heads + h] = (product(q, k, 1, 1, exact) * within).astype(score_s.dtype)
                places.append(c * heads + h)
        inverses = [eye - jnp.where(masks[0], lower, 0.0) for lower in lowers]
        for mask in masks[1:]:
            steps = [product(jnp.where(mask, lower, 0.0), x, 1, 0, True) for lower, x in zip(lowers, inverses)]
            inverses = [x - product(x, step, 1, 0, True) for x, step in zip(inverses, steps)]
        for place, x in zip(places, inverses):
            inverse_ref[place] = x

    def advance(c, states):
        base = pl.multiple_of(c * chunk, chunk)
        rows = pl.ds(base, chunk)
        _, _, carry, close, keep = chunk_masks(segment_of, base, chunk)
        new_states = []
        for h in range(heads):
            cols = slice(h * 128, (h + 1) * 128)
            state = states[h]
            k = key_s[rows, cols]
            q = query_s[rows, cols]
            delta = value_s[rows, cols] - carry * product(k, state, 1, 0, exact)
            fixed = product(inverse_ref[c * heads + h], beta_of(base, h) * delta, 1, 0, exact)
            out = carry * product(q, state, 1, 0, exact) + product(
                score_s[c * heads + h], fixed, 1, 0, exact)
            state_ref[c * heads + h] = state
            new_states.append(keep * state + product(k, close * fixed, 0, 0, exact))
            delta_ref[rows, cols] = delta
            fixed_ref[rows, cols] = fixed
            heads_ref[rows, cols] = out
            gate = proj_ref[rows, 3 * width + h * 128 : 3 * width + (h + 1) * 128]
            r = lax.rsqrt(jnp.mean(out * out, axis=-1, keepdims=True) + epsilon)
            mixed_ref[rows, cols] = (
                out * r * gain_ref[h : h + 1, :] * (gate * sigmoid(gate))
            ).astype(mixed_ref.dtype)
        return tuple(new_states)

    lax.fori_loop(0, count, advance, tuple(jnp.zeros((128, 128), f32) for _ in range(heads)))


def mixer_backward_kernel(exact, lengths_ref, proj_ref, beta_ref, tap_ref, gain_ref, grad_ref,
                          heads_ref, fixed_ref, delta_ref, state_ref, inverse_ref,
                          dproj_ref, dbeta_ref, dtap_ref, dgain_ref,
                          query_s, key_s, pre_s, dout_s, dpre_s):
    rows_all = proj_ref.shape[0]
    width = proj_ref.shape[1] // 4
    heads = width // 128
    chunk = CHUNK
    count = rows_all // chunk
    taps = tap_ref.shape[0] // 3
    segment_of, segments = segment_tools(lengths_ref)
    dgain_ref[...] = jnp.zeros_like(dgain_ref)
    dbeta_ref[...] = jnp.zeros_like(dbeta_ref)
    dtap_ref[...] = jnp.zeros_like(dtap_ref)

    @pl.loop(0, count)
    def _(c):
        base = pl.multiple_of(c * chunk, chunk)
        rows = pl.ds(base, chunk)
        for part in range(3):
            pre, _ = conv_part(proj_ref, tap_ref, segment_of, base, part, width, chunk)
            pre_s[rows, part * width : (part + 1) * width] = pre
            if part < 2:
                act = pre * sigmoid(pre)
                target = (query_s, key_s)[part]
                scale = 128 ** (-0.5) if part == 0 else 1.0
                for h, a in enumerate(heads_of(act, heads)):
                    target[rows, h * 128 : (h + 1) * 128] = unit_rows(a, scale)
        for h in range(heads):
            cols = slice(h * 128, (h + 1) * 128)
            gate_cols = slice(3 * width + h * 128, 3 * width + (h + 1) * 128)
            out = heads_ref[rows, cols]
            gate = proj_ref[rows, gate_cols]
            grad = grad_ref[rows, cols].astype(f32)
            gain = gain_ref[h : h + 1, :]
            sg = sigmoid(gate)
            silu = gate * sg
            r = lax.rsqrt(jnp.mean(out * out, axis=-1, keepdims=True) + epsilon)
            normed = out * r
            dgain_ref[h : h + 1, :] += jnp.sum(grad * normed * silu, axis=0, keepdims=True)
            dproj_ref[rows, gate_cols] = (
                grad * normed * gain * (sg * (1.0 + gate * (1.0 - sg)))
            ).astype(dproj_ref.dtype)
            weighted = grad * gain * silu
            dout_s[rows, cols] = r * weighted - out * (r * r * r) * jnp.mean(
                weighted * out, axis=-1, keepdims=True)

    dpre_s[rows_all : rows_all + HALO, :] = jnp.zeros((HALO, 3 * width), f32)

    def retreat(step, dstates):
        c = count - 1 - step
        base = pl.multiple_of(c * chunk, chunk)
        rows = pl.ds(base, chunk)
        strict, within, carry, close, keep = chunk_masks(segment_of, base, chunk)
        pos = base + lax.broadcasted_iota(jnp.int32, (chunk, 1), 0)
        live = (segment_of(pos) < segments).astype(f32)
        new_dstates = []
        for h in range(heads):
            cols = slice(h * 128, (h + 1) * 128)
            place = c * heads + h
            k = key_s[rows, cols]
            q = query_s[rows, cols]
            dout = dout_s[rows, cols]
            state = state_ref[place]
            inverse = inverse_ref[place]
            fixed = fixed_ref[rows, cols]
            delta = delta_ref[rows, cols]
            dstate = dstates[h]
            rate = sigmoid(beta_ref[rows, h : h + 1])
            beta = rate * live
            scores = product(q, k, 1, 1, exact) * within
            gram = product(k, k, 1, 1, exact) * strict
            dfixed = product(scores, dout, 0, 0, exact) + close * product(k, dstate, 1, 0, exact)
            drhs = product(inverse, dfixed, 0, 0, exact)
            ddelta = beta * drhs
            carried_dout = carry * dout
            carried_ddelta = carry * ddelta
            new_dstates.append(
                keep * dstate
                + product(q, carried_dout, 0, 0, exact)
                - product(k, carried_ddelta, 0, 0, exact)
            )
            dscores = product(dout, fixed, 1, 1, exact) * within
            dlower = -product(drhs, fixed, 1, 1, exact) * strict
            dgram = beta * dlower
            dq = product(carried_dout, state, 1, 1, exact) + product(dscores, k, 1, 0, exact)
            dk = (
                product(dscores, q, 0, 0, exact)
                + close * product(fixed, dstate, 1, 1, exact)
                - product(carried_ddelta, state, 1, 1, exact)
                + product(dgram, k, 1, 0, exact)
                + product(dgram, k, 0, 0, exact)
            )
            drate = live * (
                jnp.sum(drhs * delta, axis=-1, keepdims=True)
                + jnp.sum(dlower * gram, axis=-1, keepdims=True)
            )
            dbeta_ref[rows, h : h + 1] = (drate * rate * (1.0 - rate)).astype(dbeta_ref.dtype)
            for part, da in enumerate((dq, dk, ddelta)):
                part_cols = slice(part * width + h * 128, part * width + (h + 1) * 128)
                pre = pre_s[rows, part_cols]
                sg = sigmoid(pre)
                if part < 2:
                    a = pre * sg
                    scale = 128 ** (-0.5) if part == 0 else 1.0
                    r = lax.rsqrt(jnp.sum(a * a, axis=-1, keepdims=True) + epsilon)
                    da = (scale * r) * (da - a * (r * r) * jnp.sum(da * a, axis=-1, keepdims=True))
                dpre_s[rows, part_cols] = da * (sg * (1.0 + pre * (1.0 - sg)))
        return tuple(new_dstates)

    lax.fori_loop(0, count, retreat, tuple(jnp.zeros((128, 128), f32) for _ in range(heads)))

    @pl.loop(0, count)
    def _(c):
        base = pl.multiple_of(c * chunk, chunk)
        rows = pl.ds(base, chunk)
        col = base + lax.broadcasted_iota(jnp.int32, (chunk, 1), 0)
        seg = segment_of(col)
        for part in range(3):
            cols = slice(part * width, (part + 1) * width)
            _, shifted = conv_part(proj_ref, tap_ref, segment_of, base, part, width, chunk)
            full = dpre_s[pl.ds(base, chunk + HALO), cols]
            main = full[:chunk]
            total = main * tap_ref[part * taps : part * taps + 1, :]
            for s in range(taps):
                at = slice(part * taps + s, part * taps + s + 1)
                dtap_ref[at, :] += jnp.sum(main * shifted[s], axis=0, keepdims=True)
                if s > 0:
                    valid = (segment_of(col + s) == seg) & (col + s < rows_all)
                    moved = pltpu.roll(full, chunk + HALO - s, 0)[:chunk]
                    total = total + jnp.where(valid, moved, 0.0) * tap_ref[at, :]
            dproj_ref[rows, cols] = total.astype(dproj_ref.dtype)


def vmem():
    return pl.BlockSpec(memory_space=pltpu.VMEM)


def mixer_forward(lengths_row, projected, beta_logits, taps, gain, exact=True, group=4):
    rows, wide = projected.shape
    width = wide // 4
    heads = width // 128
    places = rows // CHUNK * heads
    group = min(group, rows // CHUNK)
    return pl.pallas_call(
        partial(mixer_forward_kernel, exact, group),
        out_shape=(
            jax.ShapeDtypeStruct((rows, width), bf16),
            jax.ShapeDtypeStruct((rows, width), f32),
            jax.ShapeDtypeStruct((rows, width), f32),
            jax.ShapeDtypeStruct((rows, width), f32),
            jax.ShapeDtypeStruct((places, 128, 128), f32),
            jax.ShapeDtypeStruct((places, CHUNK, CHUNK), f32),
        ),
        in_specs=[pl.BlockSpec(memory_space=pltpu.SMEM)] + [vmem()] * 4,
        out_specs=(vmem(),) * 6,
        scratch_shapes=[pltpu.VMEM((rows, width), f32)] * 3
        + [pltpu.VMEM((places, CHUNK, CHUNK), f32 if exact else bf16)],
        compiler_params=pltpu.CompilerParams(vmem_limit_bytes=48 * 2**20),
        cost_estimate=pl.CostEstimate(flops=10**10, bytes_accessed=10**7, transcendentals=10**6),
        name="mixer_forward",
    )(lengths_row, projected, beta_logits, taps, gain)


def mixer_backward(lengths_row, projected, beta_logits, taps, gain, grad, saved, exact=True):
    rows, wide = projected.shape
    width = wide // 4
    return pl.pallas_call(
        partial(mixer_backward_kernel, exact),
        out_shape=(
            jax.ShapeDtypeStruct((rows, wide), bf16),
            jax.ShapeDtypeStruct((rows, 128), bf16),
            jax.ShapeDtypeStruct(taps.shape, f32),
            jax.ShapeDtypeStruct(gain.shape, f32),
        ),
        in_specs=[pl.BlockSpec(memory_space=pltpu.SMEM)] + [vmem()] * 10,
        out_specs=(vmem(),) * 4,
        scratch_shapes=[pltpu.VMEM((rows, width), f32)] * 2
        + [pltpu.VMEM((rows, 3 * width), f32), pltpu.VMEM((rows, width), f32),
           pltpu.VMEM((rows + HALO, 3 * width), f32)],
        compiler_params=pltpu.CompilerParams(vmem_limit_bytes=56 * 2**20),
        cost_estimate=pl.CostEstimate(flops=10**10, bytes_accessed=10**7, transcendentals=10**6),
        name="mixer_backward",
    )(lengths_row, projected, beta_logits, taps, gain, grad, *saved)


NT = (((1,), (1,)), ((), ()))


def other(axis_name):
    return {axis_name: 1 - lax.axis_index(axis_name)}


def ffn_kernel(x_ref, w_ref, down_ref, c_refs, out_ref, ngrad_ref, wgrad_ref, down_out,
               xs, cs, ws, dsum, landed, outs, inner_s, gate_s, up_s, acts_t, part, crecv, drecv, nrecv, stage,
               ag_send, ag_recv, pair_send, pair_recv, rs_send, rs_recv, c_sem, w_sem, g_sem, t_sem,
               down_right, down_left, down_recv, down_sem, sum_sems, keep_sem, out_sem):
    half = xs.shape[1] // 2
    rows = 2 * half
    model = xs.shape[2]
    hidden = ws.shape[1]
    lines = w_ref.shape[0]
    parts, _, quarter, width = w_ref.shape[1:]
    tile_f = 256
    tile_d = min(512, model)
    tile_w = min(256, width)

    def remote(src, dst, send, recv, axis_name):
        return pltpu.make_async_remote_copy(
            src_ref=src, dst_ref=dst, send_sem=send, recv_sem=recv,
            device_id=other(axis_name), device_id_type=pl.DeviceIdType.MESH)

    def halves(ref, index, h):
        return ref.at[index, pl.ds(h * half, half)]

    o = lax.axis_index("z")

    def down_rows(z):
        return ws.at[2, pl.ds(pl.multiple_of(z * quarter, 16), quarter)]

    def down_pass(z, right):
        send = down_right if right else down_left
        return pltpu.make_async_remote_copy(
            src_ref=down_rows(z), dst_ref=down_rows(z), send_sem=send.at[z], recv_sem=down_recv.at[z],
            device_id={"z": o + 1 if right else o - 1}, device_id_type=pl.DeviceIdType.MESH)

    def down_forward(z, right):
        @pl.when(o < lines - 1 if right else o > 0)
        def _():
            down_pass(z, right).start()

    def down_step(far):
        for side in (-1, 1):
            z = o + side * far

            @pl.when((z >= 0) & (z < lines))
            def _():
                down_pass(z, side < 0).wait_recv()
                down_forward(z, side < 0)

    weight_copies, down_copies = [], []
    for r in range(parts):
        cols = pl.ds(r * width, width)
        for line in range(lines):
            weight_copies.append(pltpu.make_async_copy(
                w_ref.at[line, r], ws.at[pl.ds(0, 2), pl.ds(line * quarter, quarter), cols],
                w_sem.at[line, r]))
        down_copies.append(pltpu.make_async_copy(
            down_ref.at[r], down_rows(o).at[:, cols], down_sem.at[r]))
    for copy in down_copies:
        copy.start()
    for copy in weight_copies:
        copy.start()

    def pair_at(turn):
        return jnp.where(turn < 2, 3 - 2 * turn, 6 - 2 * turn)

    def slot_of(step):
        return (1 - lax.rem(step, 2)) * 4 + pair_at(step // 2)

    def c_copy(step, n):
        buffer = lax.rem(step, 2)
        return pltpu.make_async_copy(c_refs[n], cs.at[buffer], c_sem.at[buffer])

    def c_start(step):
        for n in range(8):
            @pl.when(slot_of(step) == n)
            def _():
                c_copy(step, n).start()

    c_copy(0, 7).start()
    line_barrier(lines, [other(name) for name in ("core", "x", "y")])

    own_pair = remote(x_ref, xs.at[4], ag_send.at[0], ag_recv.at[0], "core")
    own_x = [remote(x_ref.at[pl.ds(h * half, half)], halves(xs, 1, h), ag_send.at[1 + h], ag_recv.at[1 + h], "x") for h in range(2)]
    own_y = [remote(x_ref.at[pl.ds(h * half, half)], halves(xs, 2, h), ag_send.at[3 + h], ag_recv.at[3 + h], "y") for h in range(2)]
    relay_y = remote(halves(xs, 1, 0), halves(xs, 3, 0), ag_send.at[5], ag_recv.at[5], "y")
    relay_x = remote(halves(xs, 2, 1), halves(xs, 3, 1), ag_send.at[6], ag_recv.at[6], "x")
    pair_of = [None] + [remote(xs.at[j], xs.at[4 + j], ag_send.at[6 + j], ag_recv.at[6 + j], "core") for j in (1, 2, 3)]
    own_pair.start()
    own_x[0].start()
    own_y[1].start()
    own_x[1].start()
    own_y[0].start()
    for copy in down_copies:
        copy.wait()
    down_forward(o, True)
    down_forward(o, False)
    own_copy = pltpu.make_async_copy(x_ref, xs.at[0], t_sem.at[0, 0])
    own_copy.start()
    own_copy.wait()
    for copy in weight_copies:
        copy.wait()

    def part_send(turn):
        j = pair_at(turn)
        return remote(part.at[lax.rem(turn, 2)], crecv.at[j], pair_send.at[j], pair_recv.at[j], "core")

    x_sends = [[remote(crecv.at[1, a, pl.ds(h * half, half)], nrecv.at[0, a, pl.ds(h * half, half)],
                       rs_send.at[a * 2 + h], rs_recv.at[a * 2 + h], "x") for a in range(2)] for h in range(2)]
    y_sends = [[remote(crecv.at[2, a, pl.ds(h * half, half)], nrecv.at[1, a, pl.ds(h * half, half)],
                       rs_send.at[4 + a * 2 + h], rs_recv.at[4 + a * 2 + h], "y") for a in range(2)] for h in range(2)]
    d_sends = [[remote(crecv.at[3, a, pl.ds(h * half, half)], drecv.at[a, pl.ds(h * half, half)],
                       rs_send.at[8 + a * 2 + h], rs_recv.at[8 + a * 2 + h], ("x", "y")[h]) for a in range(2)] for h in range(2)]

    def gates(slot, cols):
        return [
            lax.dot_general(xs[slot], ws[kind, cols, :], NT, preferred_element_type=f32)
            for kind in range(2)]

    @pl.loop(0, 8)
    def _(early):
        slot = lax.rem(early + 1, 2) * 4 + early // 2

        @pl.when(early == 0)
        def _():
            own_pair.wait_recv()

        @pl.when(early == 2)
        def _():
            down_step(1)
            own_x[0].wait_recv()
            relay_y.start()
            own_y[1].wait_recv()
            relay_x.start()
            own_x[1].wait_recv()
            pair_of[1].start()
            own_y[0].wait_recv()
            pair_of[2].start()
            pair_of[1].wait_recv()

        @pl.when(early == 4)
        def _():
            pair_of[2].wait_recv()

        @pl.when(early == 6)
        def _():
            if lines > 2:
                down_step(2)
            relay_y.wait_recv()
            relay_x.wait_recv()
            pair_of[3].start()
            pair_of[3].wait_recv()

        places = pl.ds(pl.multiple_of(slot * rows, rows), rows)
        for start in range(0, hidden, tile_f):
            cols = slice(start, min(start + tile_f, hidden))
            gate, up = gates(slot, cols)
            acts_t[2, cols, places] = (gate * sigmoid(gate) * up).astype(bf16).T

    tiles = model // tile_w

    def c_tile(t):
        buffer = lax.rem(t, 2)
        cols = pl.ds(pl.multiple_of(t * tile_w, tile_w), tile_w)
        return [
            pltpu.make_async_copy(
                ref.at[:, cols], part.at[0, buffer, :, pl.ds(n * tile_w, tile_w)], t_sem.at[buffer, n])
            for n, ref in enumerate(c_refs)]

    def grad_copy(kind, t, line):
        return pltpu.make_async_copy(
            stage.at[lax.rem(t, 2), pl.ds(line * quarter, quarter)],
            wgrad_ref.at[line, t * tile_w // width, kind, :,
                         pl.ds(pl.multiple_of(lax.rem(t * tile_w, width), tile_w), tile_w)],
            g_sem.at[lax.rem(t, 2), line])

    def weight_grads(kind):
        @pl.loop(0, tiles)
        def _(t):
            if kind == 2:
                for copy in c_tile(t):
                    copy.wait()
                right = jnp.concatenate(
                    [part[0, lax.rem(t, 2), :, n * tile_w : (n + 1) * tile_w] for n in range(8)])
            else:
                right = xs[:, :, pl.ds(pl.multiple_of(t * tile_w, tile_w), tile_w)].reshape(8 * rows, tile_w)

            if kind < 2:
                @pl.when(t >= 2)
                def _():
                    for line in range(lines):
                        grad_copy(kind, t - 2, line).wait()

            value = jnp.dot(acts_t[kind], right, preferred_element_type=f32).astype(bf16)
            if kind == 2:
                @pl.when(t + 2 < tiles)
                def _():
                    for copy in c_tile(t + 2):
                        copy.start()
            if kind < 2:
                stage[lax.rem(t, 2)] = value
                for line in range(lines):
                    grad_copy(kind, t, line).start()
            else:
                dsum[:, pl.ds(pl.multiple_of(t * tile_w, tile_w), tile_w)] = value

        if kind == 2:
            return
        for t in range(max(tiles - 2, 0), tiles):
            for line in range(lines):
                grad_copy(kind, t, line).wait()

    mesh_id = pl.DeviceIdType.MESH

    def rows_of(z):
        return dsum.at[pl.ds(pl.multiple_of(z * quarter, 16), quarter)]

    def sum_pass(z, right):
        side = 0 if right else 2
        block = jnp.maximum(z - o - 1, 0) if right else jnp.minimum(lines - o + 1 + z, lines)
        return pltpu.make_async_remote_copy(
            src_ref=rows_of(z), dst_ref=landed.at[block],
            send_sem=sum_sems.at[side, z], recv_sem=sum_sems.at[side + 1, z],
            device_id={"z": o + 1 if right else o - 1}, device_id_type=mesh_id)

    def sum_add(z, block):
        at = pl.ds(pl.multiple_of(z * quarter, 16), quarter)
        for start in range(0, model, tile_d):
            cols = slice(start, start + tile_d)
            dsum[at, cols] = (
                dsum[at, cols].astype(f32) + landed[block, :, cols].astype(f32)).astype(bf16)

    def sum_tick(k):
        z_right = lines - 1 - k + o

        @pl.when(o <= k)
        def _():
            @pl.when(o > 0)
            def _():
                sum_pass(z_right, True).wait_recv()
                sum_add(z_right, z_right - o)

            @pl.when(o < k)
            def _():
                sum_pass(z_right + 1, True).wait_send()
            sum_pass(z_right, True).start()

        back = lines - 1 - o
        z_left = k - back

        @pl.when(back <= k)
        def _():
            @pl.when(back > 0)
            def _():
                sum_pass(z_left, False).wait_recv()
                sum_add(z_left, lines - o + z_left)

            @pl.when(back < k)
            def _():
                sum_pass(z_left - 1, False).wait_send()
            sum_pass(z_left, False).start()

    for t in range(2):
        for copy in c_tile(t):
            copy.start()
    weight_grads(2)
    sum_tick(0)
    for far in range(3, lines):
        down_step(far)

    @pl.loop(0, 8)
    def _(step):
        turn = step // 2
        j = pair_at(turn)
        slot = slot_of(step)
        pairing = lax.rem(step, 2) == 0

        @pl.when(step < 7)
        def _():
            c_start(step + 1)

        for k in range(1, lines - 1):
            @pl.when(step == min(1 + 3 * k, 7))
            def _():
                sum_tick(k)

        c_copy(step, 0).wait()

        for start in range(0, hidden, tile_f):
            size = min(tile_f, hidden - start)
            cols = slice(start, start + size)
            gate, up = gates(slot, cols)
            grad = lax.dot_general(cs[lax.rem(step, 2)], ws[2, cols, :], NT, preferred_element_type=f32)
            sg = sigmoid(gate)
            silu = gate * sg
            inner = (silu * up).astype(bf16)
            gate_grad = (grad * up * sg * (1.0 + gate * (1.0 - sg))).astype(bf16)
            up_grad = (grad * silu).astype(bf16)
            places = pl.ds(pl.multiple_of(slot * rows, rows), rows)
            for kind, (value, target) in enumerate(((gate_grad, gate_s), (up_grad, up_s), (inner, inner_s))):
                target[:, cols] = value
                if kind < 2:
                    acts_t[kind, cols, places] = value.T

        @pl.when(pairing & (step >= 4))
        def _():
            part_send(turn - 2).wait_send()

        place = jnp.where(pairing, lax.rem(turn, 2), 2)
        for start in range(0, model, tile_d):
            cols = slice(start, start + tile_d)
            part[place, 0, :, cols] = jnp.dot(
                inner_s[...], ws[2, :, cols], preferred_element_type=f32).astype(bf16)
            part[place, 1, :, cols] = (
                jnp.dot(gate_s[...], ws[0, :, cols], preferred_element_type=f32)
                + jnp.dot(up_s[...], ws[1, :, cols], preferred_element_type=f32)
            ).astype(bf16)

        @pl.when(pairing)
        def _():
            part_send(turn).start()

        @pl.when(jnp.logical_not(pairing))
        def _():
            part_send(turn).wait_recv()
            for a in range(2):
                for start in range(0, model, tile_d):
                    cols = slice(start, start + tile_d)
                    crecv[j, a, :, cols] = (
                        crecv[j, a, :, cols].astype(f32) + part[2, a, :, cols].astype(f32)
                    ).astype(bf16)

        @pl.when(step == 1)
        def _():
            for h in range(2):
                for copy in d_sends[h]:
                    copy.start()

        @pl.when(step == 3)
        def _():
            for copy in x_sends[0]:
                copy.start()

        @pl.when(step == 5)
        def _():
            for copy in y_sends[1]:
                copy.start()


    for h in range(2):
        j = 2 - h
        for a in range(2):
            d_sends[h][a].wait_recv()
            at = pl.ds(h * half, half)
            crecv[j, a, at, :] = (
                crecv[j, a, at, :].astype(f32) + drecv[a, at, :].astype(f32)).astype(bf16)
        for copy in (y_sends, x_sends)[h][h]:
            copy.start()
    weight_grads(0)
    weight_grads(1)
    out_copies = []
    for a, target in enumerate((out_ref, ngrad_ref)):
        for h in range(2):
            x_sends[h][a].wait_recv()
            y_sends[h][a].wait_recv()
        for n in range(model // tile_d):
            cols = slice(n * tile_d, (n + 1) * tile_d)
            if n >= 2:
                out_copies[-2].wait()
            outs[a, n % 2] = (
                crecv[0, a, :, cols].astype(f32)
                + nrecv[0, a, :, cols].astype(f32)
                + nrecv[1, a, :, cols].astype(f32)
            )
            copy = pltpu.make_async_copy(
                outs.at[a, n % 2], target.at[:, pl.ds(n * tile_d, tile_d)],
                out_sem.at[n, a])
            copy.start()
            out_copies.append(copy)
    steps = model // tile_d
    for a in range(2):
        for copy in out_copies[a * steps : (a + 1) * steps][-2:]:
            copy.wait()
    @pl.loop(0, lines)
    def _(z):
        @pl.when((o < lines - 1) & (z <= o))
        def _():
            down_pass(z, True).wait_send()

        @pl.when((o > 0) & (z >= o))
        def _():
            down_pass(z, False).wait_send()

    own_pair.wait_send()
    for h in range(2):
        own_x[h].wait_send()
        own_y[h].wait_send()
        for a in range(2):
            x_sends[h][a].wait_send()
            y_sends[h][a].wait_send()
            d_sends[h][a].wait_send()
    relay_x.wait_send()
    relay_y.wait_send()
    for j in (1, 2, 3):
        pair_of[j].wait_send()
    part_send(2).wait_send()
    part_send(3).wait_send()

    @pl.when(o > 0)
    def _():
        sum_pass(o, True).wait_recv()
        sum_add(o, 0)

    @pl.when(o < lines - 1)
    def _():
        sum_pass(o, False).wait_recv()
        sum_add(o, lines)

    keeps = [
        pltpu.make_async_copy(
            rows_of(o).at[:, pl.ds(q * width, width)], down_out.at[q], keep_sem.at[q])
        for q in range(parts)
    ]
    for copy in keeps:
        copy.start()

    @pl.when(o < lines - 1)
    def _():
        sum_pass(o + 1, True).wait_send()

    @pl.when(o > 0)
    def _():
        sum_pass(o - 1, False).wait_send()
    for copy in keeps:
        copy.wait()


def ffn_call_kernel(x_ref, w_ref, down_ref, *refs):
    ffn_kernel(x_ref, w_ref, down_ref, refs[:8], *refs[8:])


def ffn_plane(x_own, weights, down_own, c_rows):
    rows, model = x_own.shape
    lines, parts, _, quarter, width = weights.shape
    hidden = lines * quarter
    tile_w = min(256, width)
    sems = pltpu.SemaphoreType.DMA
    anywhere = pl.BlockSpec(memory_space=pl.ANY)
    return pl.pallas_call(
        ffn_call_kernel,
        out_shape=(
            jax.ShapeDtypeStruct((rows, model), f32),
            jax.ShapeDtypeStruct((rows, model), f32),
            jax.ShapeDtypeStruct(weights.shape, bf16),
            jax.ShapeDtypeStruct((parts, quarter, width), bf16),
        ),
        in_specs=[anywhere] * 11,
        out_specs=(anywhere,) * 4,
        scratch_shapes=[
            pltpu.VMEM((8, rows, model), bf16),
            pltpu.VMEM((2, rows, model), bf16),
            pltpu.VMEM((3, hidden, model), bf16),
            pltpu.VMEM((hidden, model), bf16),
            pltpu.VMEM((lines + 1, quarter, model), bf16),
            pltpu.VMEM((2, 2, rows, min(512, model)), f32),
            pltpu.VMEM((rows, hidden), bf16),
            pltpu.VMEM((rows, hidden), bf16),
            pltpu.VMEM((rows, hidden), bf16),
            pltpu.VMEM((3, hidden, 8 * rows), bf16),
            pltpu.VMEM((3, 2, rows, model), bf16),
            pltpu.VMEM((4, 2, rows, model), bf16),
            pltpu.VMEM((2, rows, model), bf16),
            pltpu.VMEM((2, 2, rows, model), bf16),
            pltpu.VMEM((2, hidden, tile_w), bf16),
            sems((10,)), sems((10,)), sems((4,)), sems((4,)), sems((12,)), sems((12,)),
            sems((2,)), sems((lines, parts)), sems((2, lines)), sems((2, 8)),
            sems((lines,)), sems((lines,)), sems((lines,)), sems((parts,)),
            sems((4, lines)), sems((parts,)), sems((4, 2)),
        ],
        compiler_params=pltpu.CompilerParams(
            collective_id=2, has_side_effects=True, vmem_limit_bytes=60 * 2**20),
        cost_estimate=pl.CostEstimate(flops=8 * 10**10, bytes_accessed=4 * 10**7, transcendentals=10**6),
        name="ffn_plane",
    )(x_own, weights, down_own, *c_rows)


def line_barrier(lines, others):
    o = lax.axis_index("z")
    barrier = pltpu.get_barrier_semaphore()
    mesh_id = pl.DeviceIdType.MESH

    @pl.when(o > 0)
    def _():
        pl.semaphore_signal(barrier, inc=1, device_id={"z": o - 1}, device_id_type=mesh_id)

    @pl.when(o < lines - 1)
    def _():
        pl.semaphore_signal(barrier, inc=1, device_id={"z": o + 1}, device_id_type=mesh_id)

    for target in others:
        pl.semaphore_signal(barrier, inc=1, device_id=target, device_id_type=mesh_id)
    peers = len(others) + (o > 0).astype(jnp.int32) + (o < lines - 1).astype(jnp.int32)
    pl.semaphore_wait(barrier, peers)


def line_copy(src, dst, send, recv, target):
    return pltpu.make_async_remote_copy(
        src_ref=src, dst_ref=dst, send_sem=send, recv_sem=recv,
        device_id=target, device_id_type=pl.DeviceIdType.MESH)


def pair_peers():
    x, core = lax.axis_index("x"), lax.axis_index("core")
    peers = [
        (x * 2 + 1 - core, {"core": 1 - core}),
        ((1 - x) * 2 + core, {"x": 1 - x}),
        ((1 - x) * 2 + 1 - core, {"x": 1 - x, "core": 1 - core}),
    ]
    return x * 2 + core, peers


class Swap:
    def __init__(self, pairs, send, recv, own):
        me, peers = pair_peers()
        self.own = [
            pltpu.make_async_copy(source.at[me], target(me), own.at[n])
            for n, (source, target) in enumerate(pairs)]
        self.away = [
            line_copy(source.at[place], target(me), send.at[n, d], recv.at[n, d], device)
            for n, (source, target) in enumerate(pairs) for d, (place, device) in enumerate(peers)]

    def start(self):
        for copy in self.away + self.own:
            copy.start()

    def wait(self):
        for copy in self.own:
            copy.wait()
        for copy in self.away:
            copy.wait_recv()
            copy.wait_send()


def gather_kernel(x_ref, o_ref, f_refs, w_refs, wb_ref, rows_ref, outs_ref, proj_refs, beta_ref,
                  pair_ref, down_ref,
                  xs, parts, stage, beta_stage, right_send, left_send, line_recv, pair_send, pair_recv,
                  part_right, part_left, part_recv, own_sem, row_sem, outs_sem, out_sem, beta_sem,
                  swap_send, swap_recv, swap_own):
    lines = xs.shape[0] // 2
    batches, rows, model = x_ref.shape
    o = lax.axis_index("z")
    i = lax.axis_index("y")
    line_barrier(lines, [other("y")] + [device for _, device in pair_peers()[1]])
    swap = Swap(
        [(f_refs[0], lambda place: pair_ref.at[place, 0]),
         (f_refs[1], lambda place: pair_ref.at[place, 1]),
         (f_refs[2], lambda place: down_ref.at[place])],
        swap_send, swap_recv, swap_own)

    def right(z, m):
        ref = xs.at[z * 2 + i, m]
        return line_copy(ref, ref, right_send.at[z, m], line_recv.at[z, m], {"z": o + 1})

    def left(z, m):
        ref = xs.at[z * 2 + i, m]
        return line_copy(ref, ref, left_send.at[z, m], line_recv.at[z, m], {"z": o - 1})

    def across(z, m):
        ref = xs.at[z * 2 + i, m]
        return line_copy(ref, ref, pair_send.at[z, m], pair_recv.at[z, m], other("y"))

    own = [
        pltpu.make_async_copy(x_ref, xs.at[o * 2 + i], own_sem.at[0]),
        pltpu.make_async_copy(o_ref, parts.at[o], own_sem.at[1]),
    ]

    def pass_part(z):
        ref = parts.at[z]
        return (line_copy(ref, ref, part_right.at[z], part_recv.at[z], {"z": o + 1}),
                line_copy(ref, ref, part_left.at[z], part_recv.at[z], {"z": o - 1}))

    for copy in own:
        copy.start()
    for copy in own:
        copy.wait()

    def outs(turn, slot):
        buffer = lax.rem(turn, 2)
        return [
            copy for m in range(batches) for copy in (
                pltpu.make_async_copy(stage.at[buffer, m], proj_refs[m].at[slot], out_sem.at[buffer, m]),
                pltpu.make_async_copy(beta_stage.at[buffer, m], beta_ref.at[m, slot], beta_sem.at[buffer, m]))
        ]

    def keep(slot, m):
        return pltpu.make_async_copy(xs.at[slot, m], rows_ref.at[m, slot], row_sem.at[slot, m])

    def keep_outs(z):
        return pltpu.make_async_copy(parts.at[z], outs_ref.at[z], outs_sem.at[z])

    def project(turn, slot):
        @pl.when(turn >= 2)
        def _():
            for copy in outs(turn, slot):
                copy.wait()
        for m in range(batches):
            keep(slot, m).start()
        x = xs[slot].reshape(batches * rows, model)
        buffer = lax.rem(turn, 2)
        width = w_refs[0].shape[1]
        for n, w_ref in enumerate(w_refs):
            stage[buffer, :, :, n * width : (n + 1) * width] = jnp.dot(
                x, w_ref[...], preferred_element_type=f32).reshape(batches, rows, width)
        beta_stage[buffer] = jnp.dot(
            x, wb_ref[...], preferred_element_type=f32).reshape(batches, rows, 128)
        for copy in outs(turn, slot):
            copy.start()

    def in_line(index):
        far = (index + 1) // 2
        side = 1 - 2 * lax.rem(index, 2)
        z = o + side * far
        return far, z, (z >= 0) & (z < lines)

    def first(index, turn):
        far, z, valid = in_line(index)

        @pl.when(valid)
        def _():
            for m in range(batches):
                @pl.when(far > 0)
                def _():
                    left(z, m).wait_recv()

                @pl.when((o < lines - 1) & (z <= o))
                def _():
                    right(z, m).start()

                @pl.when((o > 0) & (z >= o))
                def _():
                    left(z, m).start()

                across(z, m).start()
            project(turn, z * 2 + i)

        return turn + valid.astype(jnp.int32)

    swap.start()
    turn = lax.fori_loop(0, 2 * lines - 1, first, jnp.int32(0))

    def second(index, turn):
        far, z, valid = in_line(index)

        @pl.when(valid)
        def _():
            to_right, to_left = pass_part(z)

            @pl.when(far > 0)
            def _():
                to_left.wait_recv()

            @pl.when((o < lines - 1) & (z <= o))
            def _():
                to_right.start()

            @pl.when((o > 0) & (z >= o))
            def _():
                to_left.start()

            keep_outs(z).start()
            for m in range(batches):
                across(z, m).wait_recv()
            project(turn, z * 2 + 1 - i)

        return turn + valid.astype(jnp.int32)

    lax.fori_loop(0, 2 * lines - 1, second, turn)
    for turn in range(2 * lines - 2, 2 * lines):
        for copy in outs(turn, 0):
            copy.wait()

    @pl.loop(0, lines)
    def _(z):
        keep_outs(z).wait()

        @pl.when((o < lines - 1) & (z <= o))
        def _():
            pass_part(z)[0].wait_send()
            for m in range(batches):
                right(z, m).wait_send()

        @pl.when((o > 0) & (z >= o))
        def _():
            pass_part(z)[1].wait_send()
            for m in range(batches):
                left(z, m).wait_send()

        for m in range(batches):

            across(z, m).wait_send()
            for y in range(2):
                keep(z * 2 + y, m).wait()

    swap.wait()


def gather_call_kernel(x_ref, o_ref, *refs):
    gather_kernel(x_ref, o_ref, refs[:3], refs[3:7], refs[7], refs[8], refs[9], refs[10:12], *refs[12:])


def gather_project(x, w_out_part, ffn_parts, w_inner, w_beta):
    batches, rows, model = x.shape
    more = w_out_part.shape[1]
    lines = lax.axis_size("z")
    width = sum(w.shape[1] for w in w_inner)
    slots = 2 * lines
    sems = pltpu.SemaphoreType.DMA
    anywhere = pl.BlockSpec(memory_space=pl.ANY)
    pair = sems((lines, batches))
    ranks, quarter, share = ffn_parts[0].shape
    gathered, outs, *projected, beta, pair_parts, down_part = pl.pallas_call(
        gather_call_kernel,
        out_shape=(
            jax.ShapeDtypeStruct((batches, slots, rows, model), bf16),
            jax.ShapeDtypeStruct((lines, batches, more, model), bf16),
            *[jax.ShapeDtypeStruct((slots, rows, width), f32)] * batches,
            jax.ShapeDtypeStruct((batches, slots, rows, 128), f32),
            jax.ShapeDtypeStruct((ranks, 2, quarter, share), bf16),
            jax.ShapeDtypeStruct((ranks, quarter, share), bf16),
        ),
        in_specs=[anywhere] * 5 + [vmem()] * 5,
        out_specs=(anywhere,) * (5 + batches),
        scratch_shapes=[
            pltpu.VMEM((slots, batches, rows, model), bf16),
            pltpu.VMEM((lines, batches, more, model), bf16),
            pltpu.VMEM((2, batches, rows, width), f32),
            pltpu.VMEM((2, batches, rows, 128), f32),
            pair, pair, pair, pair, pair, sems((lines,)), sems((lines,)), sems((lines,)),
            sems((2,)), sems((slots, batches)), sems((lines,)), sems((2, batches)), sems((2, batches)),
            sems((3, 3)), sems((3, 3)), sems((3,)),
        ],
        compiler_params=pltpu.CompilerParams(
            collective_id=1, has_side_effects=True, vmem_limit_bytes=40 * 2**20),
        cost_estimate=pl.CostEstimate(flops=10**11, bytes_accessed=4 * 10**7, transcendentals=0),
        name="gather_project",
    )(x, w_out_part, *ffn_parts, *w_inner, w_beta)
    total = slots * rows
    return (gathered.reshape(batches, total, model), outs,
            [wide.reshape(total, width) for wide in projected],
            beta.reshape(batches, total, 128), pair_parts, down_part)


def scatter_kernel(w_refs, g_refs, gb_refs, o_refs, inner_ref, wb_ref, small_ref, gains_ref, pair_ref, down_ref,
                   out_ref, small_out, outs_ref, inner_out, pair_out, down_out,
                   gs, bs, ysend, yrecv, from_left, from_right, part_sum, part_left, part_right, outs_s, inner_s, inner_r, small_s, small_r, gains_r,
                   pair_send, pair_recv, right_send, left_send, right_recv, left_recv, g_sem,
                   sum_send, sum_recv, outs_send, outs_recv, gain_send, gain_recv, part_sems, swap_send, swap_recv, swap_own, sum_sem):
    batches = len(g_refs)
    rows, width = gs.shape[2:]
    lines = yrecv.shape[0]
    model = yrecv.shape[3]
    o = lax.axis_index("z")
    i = lax.axis_index("y")
    core = lax.axis_index("core")
    me = lax.axis_index("x") * 2 + core
    tile = min(512, model)
    diagonal = {"x": 1 - lax.axis_index("x"), "core": 1 - core}
    loads = [
        pltpu.make_async_copy(source, target.at[m], g_sem.at[n, m])
        for n, (sources, target) in enumerate(((g_refs, gs), (gb_refs, bs)))
        for m, source in enumerate(sources)]
    for copy in loads:
        copy.start()
    slots = 2 * lines
    mine = o * 2 + i
    peers = []
    for d in range(1, slots):
        place = lax.rem(mine + d, slots)
        peers.append((place, {"z": place // 2, "y": lax.rem(place, 2)}))
    barrier = pltpu.get_barrier_semaphore()
    greeted = [other("core"), other("x"), diagonal] + [device for _, device in peers]
    for device in greeted:
        pl.semaphore_signal(barrier, inc=1, device_id=device, device_id_type=pl.DeviceIdType.MESH)
    pl.semaphore_wait(barrier, len(greeted))
    gain_copies = [
        line_copy(gains_ref.at[place], gains_r.at[mine], gain_send.at[d], gain_recv.at[d], device)
        for d, (place, device) in enumerate(peers)
    ]
    for copy in gain_copies:
        copy.start()

    inner_pair = line_copy(inner_ref.at[1 - core], inner_r.at[0], sum_send.at[0], sum_recv.at[0], other("core"))
    inner_across = line_copy(inner_s, inner_r.at[1], sum_send.at[1], sum_recv.at[1], other("x"))
    inner_back = line_copy(inner_s, inner_out.at[core], sum_send.at[2], sum_recv.at[2], other("core"))
    small_pair = line_copy(small_s.at[0], small_r.at[0], sum_send.at[3], sum_recv.at[3], other("core"))
    small_across = line_copy(small_s.at[1], small_r.at[1], sum_send.at[4], sum_recv.at[4], other("x"))
    inner_own = pltpu.make_async_copy(inner_ref.at[core], inner_s, sum_sem.at[0])
    inner_keep = pltpu.make_async_copy(inner_s, inner_out.at[core], sum_sem.at[1])
    outs_keep = pltpu.make_async_copy(outs_s, outs_ref.at[me], sum_sem.at[2])
    outs_away = [
        line_copy(outs_s, outs_ref.at[me], outs_send.at[n], outs_recv.at[n], target)
        for n, target in enumerate((other("core"), other("x"), diagonal))
    ]
    swap = Swap(
        [(pair_ref, lambda place: pair_out.at[place]), (down_ref, lambda place: down_out.at[place])],
        swap_send, swap_recv, swap_own)
    swap.start()
    inner_pair.start()
    inner_own.start()
    for copy in loads:
        copy.wait()

    def add_into(target, other_ref):
        height = target.shape[0]
        step = next(size for size in range(min(128, height), 0, -16) if height % size == 0)

        @pl.loop(0, height // step)
        def _(n):
            at = pl.ds(pl.multiple_of(n * step, step), step)
            target[at, :] = (target[at, :].astype(f32) + other_ref[at, :].astype(f32)).astype(target.dtype)

    def target(index):
        far = lines - 1 - index // 2
        side = 1 - 2 * lax.rem(index, 2)
        z = o + side * far
        return far, z, (z >= 0) & (z < lines) & ((far > 0) | (side > 0))

    def partial_rows(z, y, m, store):
        g = gs[m, z * 2 + y]
        b = bs[m, z * 2 + y]
        for start in range(0, model, tile):
            cols = slice(start, start + tile)
            value = lax.dot_general(b, wb_ref[cols, :], NT, preferred_element_type=f32)
            for n, w_ref in enumerate(w_refs):
                part = g[:, n * w_ref.shape[1] : (n + 1) * w_ref.shape[1]]
                value = value + lax.dot_general(part, w_ref[cols, :], NT, preferred_element_type=f32)
            store(cols, value)

    def across(z, m):
        return line_copy(ysend.at[z, m], yrecv.at[z, m], pair_send.at[z, m], pair_recv.at[z, m], other("y"))

    def right(z, m):
        return line_copy(yrecv.at[z, m], from_left.at[z, m], right_send.at[z, m], right_recv.at[z, m], {"z": o + 1})

    def left(z, m):
        return line_copy(yrecv.at[z, m], from_right.at[z, m], left_send.at[z, m], left_recv.at[z, m], {"z": o - 1})

    def across_partial(z, m):
        def store(cols, value):
            ysend[z, m, :, cols] = value.astype(bf16)
        partial_rows(z, 1 - i, m, store)

    def pass_part(z):
        return (line_copy(part_sum.at[z], part_left.at[z], part_sems.at[0, z], part_sems.at[1, z], {"z": o + 1}),
                line_copy(part_sum.at[z], part_right.at[z], part_sems.at[2, z], part_sems.at[3, z], {"z": o - 1}))

    def part_round():
        @pl.loop(0, 2 * lines)
        def _(index):
            far, z, valid = target(index)

            @pl.when(valid & (far > 0))
            def _():
                to_right, to_left = pass_part(z)

                @pl.when((z > o) & (o > 0))
                def _():
                    to_right.wait_recv()
                    add_into(part_sum.at[z], part_left.at[z])

                @pl.when((z < o) & (o < lines - 1))
                def _():
                    to_left.wait_recv()
                    add_into(part_sum.at[z], part_right.at[z])

                @pl.when(z > o)
                def _():
                    to_right.start()

                @pl.when(z < o)
                def _():
                    to_left.start()

        to_right, to_left = pass_part(o)
        outs_s[...] = part_sum[o]

        @pl.when(o > 0)
        def _():
            to_right.wait_recv()
            add_into(outs_s, part_left.at[o])

        @pl.when(o < lines - 1)
        def _():
            to_left.wait_recv()
            add_into(outs_s, part_right.at[o])
        outs_keep.start()
        for copy in outs_away:
            copy.start()

    def side_work():
        left, left_in, right, right_in = o_refs
        column, row = lax.axis_index("y"), lax.axis_index("x")
        wide = model // 2
        for z in range(lines):
            part_sum[z, :, :wide] = (
                left[column, z].astype(f32) + left_in[z].astype(f32)).astype(bf16)
            part_sum[z, :, wide:] = (
                right[row, z].astype(f32) + right_in[z].astype(f32)).astype(bf16)
        part_round()
        inner_own.wait()
        inner_pair.wait_recv()
        add_into(inner_s, inner_r.at[0])
        inner_across.start()
        gains_r[mine] = gains_ref[mine]
        for copy in gain_copies:
            copy.wait_recv()
        tail = small_ref.shape[0]
        small_s[0, :tail] = small_ref[...]
        small_s[0, tail:] = jnp.sum(gains_r[...], axis=0)
        small_pair.start()

    total = 2 * lines * batches

    def turn(index, carry):
        before, earlier = carry
        far, z, valid = target(index // batches)
        m = lax.rem(index, batches)
        last = index >= total
        valid = valid & jnp.logical_not(last)
        moves = valid | last

        @pl.when(valid)
        def _():
            across_partial(z, m)

        @pl.when(valid)
        def _():
            across(z, m).start()

        @pl.when(moves & (before >= 0))
        def _():
            across(before // batches, lax.rem(before, batches)).wait_recv()

        @pl.when(valid & (before < 0))
        def _():
            side_work()

        @pl.when(index == (2 * lines - 2) * batches)
        def _():
            inner_across.wait_recv()
            inner_across.wait_send()
            add_into(inner_s, inner_r.at[1])
            inner_back.start()
            inner_keep.start()
            small_pair.wait_recv()
            small_s[1] = small_s[0] + small_r[0]
            small_across.start()

        @pl.when(moves & (before >= 0))
        def _():
            place, n = before // batches, lax.rem(before, batches)

            def store(cols, value):
                yrecv[place, n, :, cols] = (
                    yrecv[place, n, :, cols].astype(f32) + value).astype(bf16)
            partial_rows(place, i, n, store)

            @pl.when((place > o) & (o == 0))
            def _():
                right(place, n).start()

            @pl.when((place < o) & (o == lines - 1))
            def _():
                left(place, n).start()

        @pl.when(moves & (earlier >= 0))
        def _():
            place, n = earlier // batches, lax.rem(earlier, batches)

            @pl.when((place > o) & (o > 0))
            def _():
                right(place, n).wait_recv()
                add_into(yrecv.at[place, n], from_left.at[place, n])
                right(place, n).start()

            @pl.when((place < o) & (o < lines - 1))
            def _():
                left(place, n).wait_recv()
                add_into(yrecv.at[place, n], from_right.at[place, n])
                left(place, n).start()

        code = jnp.where(valid, z * batches + m, -1)
        return jnp.where(moves, code, before), jnp.where(moves, before, earlier)

    lax.fori_loop(0, total + 2, turn, (jnp.int32(-1), jnp.int32(-1)))


    for m in range(batches):
        out_ref[m] = yrecv[o, m].astype(f32)

        @pl.when(o > 0)
        def _():
            right(o, m).wait_recv()
            out_ref[m] += from_left[o, m].astype(f32)

        @pl.when(o < lines - 1)
        def _():
            left(o, m).wait_recv()
            out_ref[m] += from_right[o, m].astype(f32)

    @pl.loop(0, lines)
    def _(z):
        for m in range(batches):
            across(z, m).wait_send()

            @pl.when(z > o)
            def _():
                right(z, m).wait_send()

            @pl.when(z < o)
            def _():
                left(z, m).wait_send()

        @pl.when(z > o)
        def _():
            pass_part(z)[0].wait_send()

        @pl.when(z < o)
        def _():
            pass_part(z)[1].wait_send()

    small_across.wait_recv()
    small_out[...] = small_s[1] + small_r[1]
    for copy in gain_copies:
        copy.wait_send()
    inner_pair.wait_send()
    small_pair.wait_send()
    small_across.wait_send()
    inner_back.wait_recv()
    inner_back.wait_send()
    inner_keep.wait()
    outs_keep.wait()
    swap.wait()
    for copy in outs_away:
        copy.wait_recv()
        copy.wait_send()


def scatter_call_kernel(*refs):
    scatter_kernel(refs[:4], refs[4:6], refs[6:8], refs[8:12], *refs[12:])


def scatter_rows(grads, beta_grads, out_grads, inner_grads, w_inner, w_beta, small, gains,
                 pair_grads, down_grads):
    batches = len(grads)
    total, width = grads[0].shape
    model = w_inner[0].shape[0]
    lines = lax.axis_size("z")
    slots = 2 * lines
    rows = total // slots
    more = out_grads[1].shape[1]
    sems = pltpu.SemaphoreType.DMA
    anywhere = pl.BlockSpec(memory_space=pl.ANY)
    slab = pltpu.VMEM((lines, batches, rows, model), bf16)
    part = pltpu.VMEM((lines, more, model), bf16)
    half = inner_grads.shape[1:]
    flat = (small.shape[0] + gains.shape[1], 128)
    return pl.pallas_call(
        scatter_call_kernel,
        out_shape=(
            jax.ShapeDtypeStruct((batches, rows, model), f32),
            jax.ShapeDtypeStruct(flat, f32),
            jax.ShapeDtypeStruct((4, more, model), bf16),
            jax.ShapeDtypeStruct(inner_grads.shape, bf16),
            jax.ShapeDtypeStruct(pair_grads.shape, bf16),
            jax.ShapeDtypeStruct(down_grads.shape, bf16),
        ),
        in_specs=[vmem()] * 4 + [anywhere] * 4 + [vmem()] * 4
        + [anywhere, vmem(), vmem(), vmem(), anywhere, anywhere],
        out_specs=(vmem(), vmem()) + (anywhere,) * 4,
        scratch_shapes=[
            pltpu.VMEM((batches, slots, rows, width), bf16),
            pltpu.VMEM((batches, slots, rows, 128), bf16),
            slab, slab, slab, slab, part, part, part,
            pltpu.VMEM((more, model), bf16),
            pltpu.VMEM(half, bf16),
            pltpu.VMEM((2, *half), bf16),
            pltpu.VMEM((2, *flat), f32),
            pltpu.VMEM((2, *flat), f32),
            pltpu.VMEM(gains.shape, f32),
            sems((lines, batches)), sems((lines, batches)), sems((lines, batches)),
            sems((lines, batches)), sems((lines, batches)), sems((lines, batches)),
            sems((2, batches)), sems((5,)), sems((5,)), sems((3,)), sems((3,)), sems((slots,)), sems((slots,)), sems((4, lines)),
            sems((2, 3)), sems((2, 3)), sems((2,)), sems((3,)),
        ],
        compiler_params=pltpu.CompilerParams(
            collective_id=3, has_side_effects=True, vmem_limit_bytes=58 * 2**20),
        cost_estimate=pl.CostEstimate(flops=7 * 10**10, bytes_accessed=4 * 10**7, transcendentals=0),
        name="scatter_rows",
    )(*w_inner, *[grad.reshape(slots, rows, width) for grad in grads],
      *[grad.reshape(slots, rows, 128) for grad in beta_grads], *out_grads,
      inner_grads, w_beta, small, gains,
      pair_grads, down_grads)


def tensor_peers(slots):
    mine = lax.axis_index("z") * 2 + lax.axis_index("y")
    places = [lax.rem(mine + d, slots) for d in range(1, slots)]
    return mine, [(place, {"z": place // 2, "y": lax.rem(place, 2)}) for place in places]


def greet(devices):
    barrier = pltpu.get_barrier_semaphore()
    for device in devices:
        pl.semaphore_signal(barrier, inc=1, device_id=device, device_id_type=pl.DeviceIdType.MESH)
    pl.semaphore_wait(barrier, len(devices))


def attend_kernel(x_ref, low_first, low_second, gain_ref, *refs):
    pieces, refs = refs[:8], refs[8:]
    hidden_ref, normed_ref, w_ref, heads_ref, ws, heads, send, recv, sem, own_sem = refs
    slots = heads.shape[1]
    mine, peers = tensor_peers(slots)
    greet([device for _, device in peers])
    lows = (low_first, low_second)
    away = [
        line_copy(low.at[place], heads.at[m, mine], send.at[m, d], recv.at[m, d], device)
        for d, (place, device) in enumerate(peers) for m, low in enumerate(lows)
    ]
    for copy in away:
        copy.start()
    own = [pltpu.make_async_copy(low.at[mine], heads.at[m, mine], own_sem.at[m]) for m, low in enumerate(lows)]
    for copy in own:
        copy.start()
    x = lax.axis_index("x")
    core = lax.axis_index("core")
    y = lax.axis_index("y")
    copies = []
    for n, piece in enumerate(pieces):
        far_y, far_x, far_core = n // 4, n // 2 % 2, n % 2
        column = 1 - y if far_y else y
        quarter = (1 - x if far_x else x) * 2 + (1 - core if far_core else core)
        copies.append(pltpu.make_async_copy(piece, ws.at[:, column, quarter], sem.at[n]))
    for copy in copies:
        copy.start()
    for copy in copies + own:
        copy.wait()
    keep = pltpu.make_async_copy(ws, w_ref, own_sem.at[2])
    keep.start()
    for copy in away:
        copy.wait_recv()
    keep_heads = pltpu.make_async_copy(heads, heads_ref, own_sem.at[3])
    keep_heads.start()
    model = x_ref.shape[1]
    tile = min(512, model)
    width = heads.shape[3]
    squares = 0.0
    for start in range(0, model, tile):
        cols = slice(start, start + tile)
        total = x_ref[:, cols].astype(f32)
        for t in range(slots):
            left = jnp.concatenate([heads[0, t], heads[1, t]], axis=0)
            total = total + jnp.dot(
                left, ws[t // 2, t % 2, :, :, cols].reshape(width, tile), preferred_element_type=f32)
        hidden_ref[:, cols] = total
        squares = squares + jnp.sum(total * total, axis=-1, keepdims=True)
    scale = lax.rsqrt(squares / model + epsilon)
    for start in range(0, model, tile):
        cols = slice(start, start + tile)
        normed_ref[:, cols] = (hidden_ref[:, cols] * scale * gain_ref[:, cols]).astype(bf16)
    keep.wait()
    keep_heads.wait()
    for copy in away:
        copy.wait_send()


def attend(x, lows, gain, pieces):
    rows, model = x.shape
    lines, part, _ = pieces[0].shape
    full = (lines, 2, 4, part, model)
    heads = (2, *lows[0].shape)
    slots = 2 * lines
    anywhere = pl.BlockSpec(memory_space=pl.ANY)
    sems = pltpu.SemaphoreType.DMA
    return pl.pallas_call(
        attend_kernel,
        out_shape=(
            jax.ShapeDtypeStruct((rows, model), f32),
            jax.ShapeDtypeStruct((rows, model), bf16),
            jax.ShapeDtypeStruct(full, bf16),
            jax.ShapeDtypeStruct(heads, bf16),
        ),
        in_specs=[vmem(), anywhere, anywhere, vmem()] + [anywhere] * 8,
        out_specs=(vmem(), vmem(), anywhere, anywhere),
        scratch_shapes=[
            pltpu.VMEM(full, bf16), pltpu.VMEM(heads, bf16),
            sems((2, slots)), sems((2, slots)), sems((8,)), sems((4,))],
        compiler_params=pltpu.CompilerParams(
            collective_id=4, has_side_effects=True, vmem_limit_bytes=32 * 2**20),
        cost_estimate=pl.CostEstimate(flops=3 * 10**10, bytes_accessed=2 * 10**7, transcendentals=0),
        name="attend",
    )(x, *lows, gain, *pieces)


def attend_back_kernel(hidden_ref, ffn_ref, grad_ref, c_ref, gain_ref, w_ref, heads,
                       result_ref, hgrad_ref, back_first, back_second, left_mine, left_theirs,
                       right_mine, right_theirs, gain_out, low, wgrad, wrecv, backs, send, recv, sem, core_sem):
    rows, model = hidden_ref.shape
    half = rows // 2
    tile = min(512, model)
    slots = heads.shape[1]
    width = heads.shape[3]
    mine, peers = tensor_peers(slots)
    greet([device for _, device in peers] + [other("core")])
    squares, dots = 0.0, 0.0
    for start in range(0, model, tile):
        cols = slice(start, start + tile)
        hidden = hidden_ref[:, cols]
        squares = squares + jnp.sum(hidden * hidden, axis=-1, keepdims=True)
        dots = dots + jnp.sum(hidden * grad_ref[:, cols] * gain_ref[:, cols], axis=-1, keepdims=True)
    scale = lax.rsqrt(squares / model + epsilon)
    pull = scale * scale * scale * (dots / model)
    for start in range(0, model, tile):
        cols = slice(start, start + tile)
        hidden = hidden_ref[:, cols]
        grad = grad_ref[:, cols]
        result_ref[:, cols] = hidden + ffn_ref[:, cols]
        gain_out[:, cols] = jnp.sum(grad * hidden * scale, axis=0, keepdims=True)
        hgrad = c_ref[:, cols].astype(f32) + scale * (grad * gain_ref[:, cols]) - hidden * pull
        hgrad_ref[:, cols] = hgrad
        low[:, cols] = hgrad.astype(bf16)

    outs = (back_first, back_second)

    def away(m, d):
        place = lax.rem(mine + d, slots)
        return line_copy(backs.at[m, d], outs[m].at[mine], send.at[m, d], recv.at[m, d],
                         {"z": place // 2, "y": lax.rem(place, 2)})

    @pl.loop(0, slots)
    def _(step):
        d = slots - 1 - step
        place = lax.rem(mine + d, slots)
        back = lax.dot_general(
            low[...], w_ref[place // 2, lax.rem(place, 2)].reshape(width, model), NT,
            preferred_element_type=f32)
        for m in range(2):
            backs[m, d] = back[m * half : (m + 1) * half].astype(bf16)

            @pl.when(d > 0)
            def _():
                away(m, d).start()

            @pl.when(d == 0)
            def _():
                pltpu.make_async_copy(backs.at[m, 0], outs[m].at[mine], sem.at[2 + m]).start()

    for t in range(slots):
        left = jnp.concatenate([heads[0, t], heads[1, t]], axis=0)
        for start in range(0, model, tile):
            cols = slice(start, start + tile)
            value = lax.dot_general(
                left, low[:, cols], (((0,), (0,)), ((), ())), preferred_element_type=f32
            ).astype(bf16).reshape(2, 2, width // 4, tile)
            for c in range(2):
                wgrad[c, :, t % 2, t // 2, :, cols] = value[:, c]
    core = lax.axis_index("core")
    to_pair = line_copy(wgrad.at[1 - core], wrecv, core_sem.at[0], core_sem.at[1], other("core"))
    to_pair.start()
    to_pair.wait_recv()
    lines = wgrad.shape[3]
    for far_x in range(2):
        for far_y in range(2):
            @pl.loop(0, lines)
            def _(z):
                wrecv[far_x, far_y, z] = (
                    wrecv[far_x, far_y, z].astype(f32) + wgrad[core, far_x, far_y, z].astype(f32)
                ).astype(bf16)
    x, y = lax.axis_index("x"), lax.axis_index("y")
    wide = model // 2
    keeps = [
        pltpu.make_async_copy(source.at[..., pl.ds(start, wide)], target, sem.at[4 + n])
        for n, (source, start, target) in enumerate((
            (wrecv.at[x], 0, left_mine), (wrecv.at[1 - x], 0, left_theirs),
            (wrecv.at[:, y], wide, right_mine), (wrecv.at[:, 1 - y], wide, right_theirs)))
    ]
    for copy in keeps:
        copy.start()
    for copy in keeps:
        copy.wait()
    to_pair.wait_send()
    for m in range(2):
        pltpu.make_async_copy(backs.at[m, 0], outs[m].at[mine], sem.at[2 + m]).wait()
        for d in range(1, slots):
            away(m, d).wait_recv()
            away(m, d).wait_send()


def attend_back(hidden, ffn_out, normed_grad, c_rows, gain, w_full, heads):
    rows, model = hidden.shape
    wide = jax.ShapeDtypeStruct((rows, model), f32)
    lines, _, _, part, _ = w_full.shape
    share = (2, 2, lines, part, model)
    slots = 2 * lines
    back = jax.ShapeDtypeStruct(heads.shape[1:], bf16)
    anywhere = pl.BlockSpec(memory_space=pl.ANY)
    sems = pltpu.SemaphoreType.DMA
    return pl.pallas_call(
        attend_back_kernel,
        out_shape=(
            wide, wide, back, back,
            *[jax.ShapeDtypeStruct((2, lines, part, model // 2), bf16)] * 4,
            jax.ShapeDtypeStruct((1, model), f32),
        ),
        in_specs=[vmem()] * 7,
        out_specs=(vmem(),) * 2 + (anywhere,) * 6 + (vmem(),),
        scratch_shapes=[
            pltpu.VMEM((rows, model), bf16), pltpu.VMEM((2, *share), bf16), pltpu.VMEM(share, bf16),
            pltpu.VMEM(heads.shape, bf16), sems((2, slots)), sems((2, slots)), sems((8,)), sems((2,))],
        compiler_params=pltpu.CompilerParams(
            collective_id=5, has_side_effects=True, vmem_limit_bytes=48 * 2**20),
        cost_estimate=pl.CostEstimate(flops=3 * 10**10, bytes_accessed=4 * 10**7, transcendentals=0),
        name="attend_back",
    )(hidden, ffn_out, normed_grad, c_rows, gain, w_full, heads)


def inner_grads_kernel(x_ref, g_first, g_second, b_first, b_second, w0, w1, w2, w3, wb_ref,
                       low_ref, beta_ref, gain_ref):
    dims = (((0,), (0,)), ((), ()))
    beta = 0.0
    for m, b_ref in enumerate((b_first, b_second)):
        beta = beta + lax.dot_general(x_ref[m], b_ref[...], dims, preferred_element_type=f32)
    beta_ref[...] = beta
    gain = jnp.sum(beta * wb_ref[...].astype(f32), axis=1, keepdims=True)
    for n, w_ref in enumerate((w0, w1, w2, w3)):
        width = w_ref.shape[1]
        cols = slice(n * width, (n + 1) * width)
        value = 0.0
        for m, g_ref in enumerate((g_first, g_second)):
            value = value + lax.dot_general(x_ref[m], g_ref[:, cols], dims, preferred_element_type=f32)
        low_ref[:, cols] = value.astype(bf16)
        gain = gain + jnp.sum(value * w_ref[...].astype(f32), axis=1, keepdims=True)
    gain_ref[...] = jnp.broadcast_to(gain, gain_ref.shape)


def inner_grads(tokens, grads, beta_grads, w_inner, w_beta):
    _, total, model = tokens.shape
    wide = grads[0].shape[1]
    width = w_inner[0].shape[1]
    tile = 256

    def whole(columns):
        return pl.BlockSpec((total, columns), lambda n: (0, 0))

    def rows(columns):
        return pl.BlockSpec((tile, columns), lambda n: (n, 0))

    return pl.pallas_call(
        inner_grads_kernel,
        out_shape=(
            jax.ShapeDtypeStruct((model, wide), bf16),
            jax.ShapeDtypeStruct((model, 128), f32),
            jax.ShapeDtypeStruct((model, 128), f32),
        ),
        grid=(model // tile,),
        in_specs=[pl.BlockSpec((2, total, tile), lambda n: (0, 0, n))]
        + [whole(wide)] * 2 + [whole(128)] * 2 + [rows(width)] * 4 + [rows(128)],
        out_specs=(rows(wide), rows(128), rows(128)),
        compiler_params=pltpu.CompilerParams(vmem_limit_bytes=40 * 2**20),
        cost_estimate=pl.CostEstimate(flops=10**10, bytes_accessed=2 * 10**7, transcendentals=0),
        name="inner_grads",
    )(tokens, *grads, *beta_grads, *w_inner, w_beta)


def root_scale(row_values, gain_vector):
    row_scale = lax.rsqrt(jnp.mean(row_values * row_values, axis=-1, keepdims=True) + epsilon)
    return (row_values * row_scale * gain_vector, row_scale)


def norm_backward(row_values, row_scale, gain_vector, normed_grad):
    weighted = normed_grad * gain_vector
    rows_grad = row_scale * weighted - row_values * row_scale * row_scale * row_scale * jnp.mean(
        weighted * row_values, axis=-1, keepdims=True
    )
    gain_grad = jnp.sum(normed_grad * row_values * row_scale, axis=tuple(range(row_values.ndim - 1)))
    return (rows_grad, gain_grad)


DP = ("x", "core")
TP = ("z", "y")


def gather(x, axis_name, axis=0):
    return lax.all_gather(x, axis_name, axis=axis, tiled=True)


def scatter_sum(x, axis_name, axis=0):
    return lax.psum_scatter(
        x.astype(bf16), axis_name, scatter_dimension=axis, tiled=True
    ).astype(f32)


def dot(a, b):
    return jnp.dot(a, b, preferred_element_type=f32)


def dot_nt(a, b):
    return jnp.einsum("tk,nk->tn", a, b, preferred_element_type=f32)


def dot_tn(a, b):
    return jnp.einsum("tm,tn->mn", a, b, preferred_element_type=f32)


def exchange(x, axis_name, distance=1):
    size = lax.axis_size(axis_name)
    return lax.ppermute(x, axis_name, [(i, i ^ distance) for i in range(size)])


def pick(x, index, axis):
    return lax.dynamic_index_in_dim(x, index, axis, keepdims=False)


def after(x, *others):
    return lax.optimization_barrier((x, *others))[0]


def add_low(x, y):
    return (x.astype(f32) + y.astype(f32)).astype(bf16)


def halve_sum(grad, axis_name):
    me = lax.axis_index(axis_name)
    return add_low(pick(grad, me, 0), exchange(pick(grad, 1 - me, 0), axis_name))


def feed_forward_groups(normed, cotangents, w_gate, w_up, w_down):
    gate_full = gather(w_gate, DP)
    up_full = gather(w_up, DP)
    down_full = gather(w_down, DP, 1)
    outs, normed_grads, inner_rows, gate_grads, up_grads, rows, grad_rows = [], [], [], [], [], [], []
    for m in range(normed.shape[0]):
        rows.append(gather(normed[m], TP))
        grad_rows.append(gather(cotangents[m], TP))
        gate_values = dot(rows[m], gate_full)
        up_values = dot(rows[m], up_full)
        sigmoid_gate = jax.nn.sigmoid(gate_values)
        silu_gate = gate_values * sigmoid_gate
        inner = (silu_gate * up_values).astype(bf16)
        inner_grad = dot_nt(grad_rows[m], down_full)
        gate_grad = (
            inner_grad * up_values * sigmoid_gate * (1.0 + gate_values * (1.0 - sigmoid_gate))
        ).astype(bf16)
        up_grad = (inner_grad * silu_gate).astype(bf16)
        normed_grads.append(scatter_sum(dot_nt(gate_grad, gate_full) + dot_nt(up_grad, up_full), TP))
        outs.append(scatter_sum(dot(inner, down_full), TP))
        inner_rows.append(inner)
        gate_grads.append(gate_grad)
        up_grads.append(up_grad)
    grad_all = jnp.concatenate(grad_rows)
    rows_all = jnp.concatenate(rows)
    gate_share = scatter_sum(dot_tn(rows_all, jnp.concatenate(gate_grads)), DP)
    up_share = scatter_sum(dot_tn(rows_all, jnp.concatenate(up_grads)), DP)
    down_share = scatter_sum(dot_tn(jnp.concatenate(inner_rows), grad_all), DP, 1)
    return jnp.stack(outs), jnp.stack(normed_grads), (gate_share, up_share, down_share)


def per_device(
    inputs,
    lengths,
    norm_gain,
    ffn_gain,
    w_query,
    w_key,
    w_value,
    w_gate_out,
    w_beta,
    conv_weight,
    head_gain,
    w_out,
    w_gate,
    w_up,
    w_down,
    cotangent,
):
    batches = range(inputs.shape[0])
    local_width = w_query.shape[1]
    heads = w_beta.shape[1]
    devices = lax.axis_size(TP)
    planar = all(lax.axis_size(name) == 2 for name in ("x", "core", "y"))
    w_parts = (w_query, w_key, w_value, w_gate_out)
    w_inner = jnp.concatenate(w_parts, axis=1)
    w_beta_wide = jnp.pad(w_beta, ((0, 0), (0, 128 - heads)))
    taps = conv_weight.astype(f32).reshape(-1, local_width)
    gain_heads = head_gain.astype(f32)
    gains = gather(jnp.stack([norm_gain, ffn_gain]), DP, 1)
    gain_one, gain_two = gains[0].astype(f32), gains[1].astype(f32)
    rows_in = inputs.astype(f32)
    normed_one, scale_one = root_scale(rows_in, gain_one)
    normed_one = normed_one.astype(bf16)

    def run_mixer(m, wide, logits):
        low, *kept = mixer_forward(lengths[m, 0], wide, logits, taps, gain_heads, exact=False)
        return low, kept

    def back_mixer(m, wide, logits, grad, kept):
        return mixer_backward(
            lengths[m, 0], wide, logits, taps, gain_heads, grad, kept, exact=False)

    if planar:
        count = rows_in.shape[0] * rows_in.shape[1]
        model = rows_in.shape[2]
        ranks = lax.axis_size(DP)
        ffn_parts = [
            w.reshape(ranks, -1, w.shape[1]) for w in after((w_gate.T, w_up.T, w_down), gains)]
        c_rows = [None] * 8
        c_rows[0] = after(cotangent.reshape(count, model), gains)
        c_rows[4] = exchange(c_rows[0], "core")
        out_shares = pick(
            w_out.reshape(lax.axis_size(DP), len(batches), -1, model), lax.axis_index(DP), 0)
        gathered_one, out_own, projected, beta_logits, own_weights, own_down = gather_project(
            normed_one, out_shares, ffn_parts, w_parts, w_beta_wide)
        early = after(c_rows[0], gathered_one)
        c_rows[1] = exchange(early, "x")
        weights = gather(own_weights[None], "z")
        c_rows[2] = exchange(early, "y")
        out_own = out_own.reshape(out_own.shape[0], -1, model)
        out_y = exchange(out_own, "y")
        out_x = exchange(out_own, "x")
    else:
        gathered_one = jnp.stack([gather(normed_one[m], TP) for m in batches])
        projected = [dot(gathered_one[m], w_inner) for m in batches]
        beta_logits = [dot(gathered_one[m], w_beta_wide) for m in batches]
        out_full = gather(w_out, TP)
    token_heads, saved = [], []
    for m in batches:
        low, kept = run_mixer(m, projected[m], beta_logits[m])
        saved.append(kept)
        if planar and m == 0:
            out_y, c_rows[1], c_rows[2] = after((out_y, c_rows[1], c_rows[2]), low)
            out_xy = exchange(out_y, "x")
            c_rows[3] = exchange(c_rows[1], "y")
            c_rows[5] = exchange(c_rows[1], "core")
            c_rows[6] = exchange(c_rows[2], "core")
            projected[1] = after(projected[1], out_y, c_rows[2])
        low = low.reshape(devices, -1, local_width)
        if not planar:
            low = lax.all_to_all(low, TP, split_axis=0, concat_axis=0, tiled=True)
        token_heads.append(low)
    if planar:
        out_x, out_xy, c_rows[3] = after((out_x, out_xy, c_rows[3]), low)
        out_pieces = []
        for piece in (out_own, out_x, out_y, out_xy):
            out_pieces += [piece, exchange(piece, "core")]
        c_rows[7] = exchange(c_rows[3], "core")
        hidden, normed_two, out_full, token_heads = attend(
            inputs.reshape(count, model), token_heads, gain_two[None], out_pieces)
        ffn_out, normed_grad, weight_grads, down_grad = ffn_plane(normed_two, weights, own_down, c_rows)
        result_rows, hidden_grad, *mixed_grads, left, left_away, right, right_away, gain_two_sum = attend_back(
            hidden, ffn_out, normed_grad, c_rows[0], gain_two[None], out_full, token_heads)
        weight_grads = after(weight_grads, left)
        own_grads = lax.psum_scatter(weight_grads, "z", scatter_dimension=0, tiled=True)
        gain_two_sum = gain_two_sum[0]
        result_rows = result_rows.reshape(rows_in.shape)
        hidden_grad = hidden_grad.reshape(rows_in.shape)
    else:
        heads_rows = [
            block.swapaxes(0, 1).reshape(-1, devices * local_width) for block in token_heads]
        hidden = rows_in + jnp.stack([dot(rows, out_full) for rows in heads_rows])
        normed_two, scale_two = root_scale(hidden, gain_two)
        ffn_out, normed_grad, (gate_share, up_share, down_share) = feed_forward_groups(
            normed_two.astype(bf16), cotangent, w_gate, w_up, w_down)
        result_rows = hidden + ffn_out
        norm_grad, gain_two_sum = norm_backward(hidden, scale_two, gain_two, normed_grad)
        hidden_grad = cotangent.astype(f32) + norm_grad
        attended_low = hidden_grad.astype(bf16)
        mixed_grads = [
            dot_nt(attended_low[m], out_full).astype(bf16)
            .reshape(-1, devices, local_width).swapaxes(0, 1) for m in batches]
        out_grad = dot_tn(
            jnp.concatenate(heads_rows), jnp.concatenate(list(attended_low))).astype(bf16)
    if not planar:
        mixed_grads = [
            lax.all_to_all(grad, TP, split_axis=0, concat_axis=0, tiled=True)
            for grad in mixed_grads]
    mixed_grads = [grad.reshape(-1, local_width) for grad in mixed_grads]
    if planar:
        left = add_low(left, exchange(left_away, "x"))
        right = add_low(right, exchange(right_away, "y"))
    projected_low, beta_low = [], []
    taps_sum, heads_sum = 0.0, 0.0
    for m in batches:
        if planar and m > 0:
            mixed_grads[m] = after(mixed_grads[m], left, right)
        projected_grad, beta_grad, taps_part, heads_part = back_mixer(
            m, projected[m], beta_logits[m], mixed_grads[m], saved[m])
        taps_sum = taps_sum + taps_part
        heads_sum = heads_sum + heads_part
        projected_low.append(projected_grad)
        beta_low.append(beta_grad)
    if planar:
        left_in = exchange(pick(left, 1 - lax.axis_index("y"), 0), "y")
        right_in = exchange(pick(right, 1 - lax.axis_index("x"), 0), "x")
        low_sum, beta_sum, gain_rows = inner_grads(
            gathered_one, projected_low, beta_low, w_parts, w_beta_wide)
        beta_sum = beta_sum[:, :heads]
        gain_one_sum = gain_rows[:, 0] / gain_one
    else:
        tokens = gathered_one.reshape(-1, gathered_one.shape[2])
        inner_sum = dot_tn(tokens, jnp.concatenate(projected_low))
        beta_sum = dot_tn(tokens, jnp.concatenate(beta_low)[:, :heads])
        gain_one_sum = (
            jnp.sum(inner_sum * w_inner.astype(f32), axis=1)
            + jnp.sum(beta_sum * w_beta.astype(f32), axis=1)
        ) / gain_one
        low_sum = inner_sum.astype(bf16)
    gain_parts = jnp.stack([gain_one_sum, gain_two_sum])
    sums = [part.reshape(-1, 128) for part in (beta_sum.T, taps_sum, heads_sum)]
    marks = [sums[0].shape[0], sums[0].shape[0] + sums[1].shape[0], sum(part.shape[0] for part in sums)]
    small = jnp.concatenate(sums)
    if planar:
        ranks = lax.axis_size(DP)
        gain_parts = gain_parts.reshape(2, ranks, devices, -1).transpose(2, 0, 1, 3)
        chunk = gain_parts.shape[3]
        gain_parts = gain_parts.reshape(devices, -1, 128)
        gain_rows = gain_parts.shape[1]
        gain_parts = jnp.pad(gain_parts, ((0, 0), (0, -gain_rows % 8), (0, 0)))
        small = jnp.pad(small, ((0, -small.shape[0] % 8), (0, 0)))
        input_norm, flat, out_total, inner_total, pair_grads, down_grads = scatter_rows(
            projected_low, beta_low, (left, left_in, right, right_in),
            low_sum.reshape(2, -1, low_sum.shape[1]), w_parts, w_beta_wide, small, gain_parts,
            own_grads[0], down_grad)
        gate_share, up_share = (
            pair_grads[:, kind].reshape(-1, pair_grads.shape[3]).astype(f32).T for kind in range(2))
        down_share = down_grads.reshape(w_down.shape).astype(f32)
        gain_totals = pick(
            flat[small.shape[0] :][:gain_rows].reshape(2, ranks, chunk), lax.axis_index(DP), 1)
        small = flat[: small.shape[0]]
        out_total = out_total.reshape(w_out.shape).astype(f32)
        inner_total = inner_total.reshape(low_sum.shape)
    else:
        gain_totals = lax.psum_scatter(gain_parts, DP + TP, scatter_dimension=1, tiled=True)
        inner_total = lax.psum(low_sum, DP)
        small = lax.psum(small, DP)
        out_grad = lax.psum_scatter(out_grad, TP, scatter_dimension=0, tiled=True)
        out_total = lax.psum(out_grad, DP).astype(f32)
        input_norm = jnp.stack([
            scatter_sum(
                dot_nt(projected_low[m], w_inner) + dot_nt(beta_low[m], w_beta_wide), TP)
            for m in batches])
    norm_grad, _ = norm_backward(rows_in, scale_one, gain_one, input_norm)
    beta_total = small[: marks[0]].reshape(heads, -1).T
    conv_total = small[marks[0] : marks[1]].reshape(conv_weight.shape)
    heads_total = small[marks[1] : marks[2]].reshape(head_gain.shape)
    columns = [
        inner_total[:, n * local_width : (n + 1) * local_width].astype(f32) for n in range(4)]
    return (
        result_rows,
        hidden_grad + norm_grad,
        gain_totals[0],
        gain_totals[1],
        *columns,
        beta_total,
        conv_total,
        heads_total,
        out_total,
        gate_share,
        up_share,
        down_share,
    )


def solution(mesh):
    dp, tensor = mesh.shape["dp"], mesh.shape["tensor"]
    inner = 2 if tensor == 8 else 4
    axes = ("x", "core", "z", "y")
    fine = jax.sharding.Mesh(
        mesh.devices.reshape(dp // 2, 2, tensor // inner, inner), axes)
    tokens = P(None, DP + TP, None)
    in_specs = (
        tokens,
        P(None, DP, None),
        P(DP),
        P(DP),
        P(None, TP),
        P(None, TP),
        P(None, TP),
        P(None, TP),
        P(None, TP),
        P(None, None, TP),
        P(TP, None),
        P(TP, None),
        P(DP, TP),
        P(DP, TP),
        P(TP, DP),
        tokens,
    )
    out_specs = (
        tokens,
        tokens,
        P(DP + TP),
        P(DP + TP),
        P(None, TP),
        P(None, TP),
        P(None, TP),
        P(None, TP),
        P(None, TP),
        P(None, None, TP),
        P(TP, None),
        P(TP, None),
        P(DP, TP),
        P(DP, TP),
        P(TP, DP),
    )
    return jax.shard_map(
        per_device, mesh=fine, in_specs=in_specs, out_specs=out_specs, check_vma=False
    )
```

```python
from functools import partial

import jax
import jax.numpy as jnp
from jax import lax
from jax.experimental import pallas as pl
from jax.experimental.pallas import tpu as pltpu
from jax.sharding import PartitionSpec as P


CHUNK = 128
HALO = 8
epsilon = 1e-06
highest = lax.Precision.HIGHEST
f32 = jnp.float32
bf16 = jnp.bfloat16


def product(left, right, left_dim, right_dim, exact=False):
    dims = (((left_dim,), (right_dim,)), ((), ()))
    if exact:
        return lax.dot_general(left, right, dims, precision=highest, preferred_element_type=f32)
    return lax.dot_general(
        left.astype(bf16), right.astype(bf16), dims, preferred_element_type=f32
    )


def sigmoid(x):
    return 1.0 / (1.0 + jnp.exp(-x))


def segment_tools(lengths_ref):
    ends = []
    total = 0
    for i in range(lengths_ref.shape[0] - 1):
        total = total + lengths_ref[i]
        ends.append(total)

    def segment_of(pos):
        result = 0
        for end in ends:
            result = result + (pos >= end).astype(jnp.int32)
        return result

    return segment_of, len(ends)


def chunk_masks(segment_of, base, chunk):
    col = base + lax.broadcasted_iota(jnp.int32, (chunk, 1), 0)
    row = base + lax.broadcasted_iota(jnp.int32, (1, chunk), 1)
    seg_col = segment_of(col)
    seg_row = segment_of(row)
    first = segment_of(base - 1)
    last = segment_of(base + chunk - 1)
    same = seg_col == seg_row
    strict = (same & (col > row)).astype(f32)
    within = (same & (col >= row)).astype(f32)
    has_past = base > 0
    carry = ((seg_col == first) & has_past).astype(f32)
    close = (seg_col == last).astype(f32)
    keep = ((first == last) & has_past).astype(f32)
    return strict, within, carry, close, keep


def level_masks(chunk):
    row = lax.broadcasted_iota(jnp.int32, (chunk, chunk), 0)
    col = lax.broadcasted_iota(jnp.int32, (chunk, chunk), 1)
    masks = []
    width = 1
    while width < chunk:
        mask = (
            (row // (2 * width) == col // (2 * width))
            & ((row // width) % 2 == 1)
            & ((col // width) % 2 == 0)
        )
        masks.append(mask)
        width *= 2
    return masks, (row == col).astype(f32)


def conv_part(proj_ref, tap_ref, segment_of, base, part, width, chunk):
    taps = tap_ref.shape[0] // 3
    cols = pl.ds(part * width, width)
    main = proj_ref[pl.ds(base, chunk), cols]
    prev = proj_ref[pl.ds(pl.multiple_of(jnp.maximum(base - HALO, 0), HALO), HALO), cols]
    full = jnp.concatenate([prev, main], axis=0)
    col = base + lax.broadcasted_iota(jnp.int32, (chunk, 1), 0)
    seg = segment_of(col)
    total = main * tap_ref[part * taps : part * taps + 1, :]
    shifted = [main]
    for s in range(1, taps):
        valid = (segment_of(col - s) == seg) & (col >= s)
        moved = jnp.where(valid, pltpu.roll(full, s, 0)[HALO:], 0.0)
        shifted.append(moved)
        total = total + moved * tap_ref[part * taps + s : part * taps + s + 1, :]
    return total, shifted


def heads_of(x, heads):
    return [x[:, h * 128 : (h + 1) * 128] for h in range(heads)]


def unit_rows(a, scale):
    r = lax.rsqrt(jnp.sum(a * a, axis=-1, keepdims=True) + epsilon)
    return a * (r * scale)


def mixer_forward_kernel(exact, group, lengths_ref, proj_ref, beta_ref, tap_ref, gain_ref,
                         mixed_ref, heads_ref, fixed_ref, delta_ref, state_ref, inverse_ref,
                         query_s, key_s, value_s, score_s):
    rows_all = proj_ref.shape[0]
    width = proj_ref.shape[1] // 4
    heads = width // 128
    chunk = CHUNK
    count = rows_all // chunk
    segment_of, segments = segment_tools(lengths_ref)

    @pl.loop(0, count)
    def _(c):
        base = pl.multiple_of(c * chunk, chunk)
        rows = pl.ds(base, chunk)
        for part, target in enumerate((query_s, key_s, value_s)):
            pre, _ = conv_part(proj_ref, tap_ref, segment_of, base, part, width, chunk)
            act = pre * sigmoid(pre)
            if part == 2:
                target[rows, :] = act
            else:
                scale = 128 ** (-0.5) if part == 0 else 1.0
                for h, a in enumerate(heads_of(act, heads)):
                    target[rows, h * 128 : (h + 1) * 128] = unit_rows(a, scale)

    def beta_of(base, h):
        pos = base + lax.broadcasted_iota(jnp.int32, (chunk, 1), 0)
        live = (segment_of(pos) < segments).astype(f32)
        return sigmoid(beta_ref[pl.ds(base, chunk), h : h + 1]) * live

    masks, eye = level_masks(chunk)

    @pl.loop(0, count // group)
    def _(g):
        lowers, places = [], []
        for i in range(group):
            c = g * group + i
            base = pl.multiple_of(c * chunk, chunk)
            strict, within, _, _, _ = chunk_masks(segment_of, base, chunk)
            for h in range(heads):
                cols = slice(h * 128, (h + 1) * 128)
                k = key_s[pl.ds(base, chunk), cols]
                q = query_s[pl.ds(base, chunk), cols]
                lowers.append(product(k, k, 1, 1, exact) * strict * beta_of(base, h))
                score_s[c * heads + h] = (product(q, k, 1, 1, exact) * within).astype(score_s.dtype)
                places.append(c * heads + h)
        inverses = [eye - jnp.where(masks[0], lower, 0.0) for lower in lowers]
        for mask in masks[1:]:
            steps = [product(jnp.where(mask, lower, 0.0), x, 1, 0, True) for lower, x in zip(lowers, inverses)]
            inverses = [x - product(x, step, 1, 0, True) for x, step in zip(inverses, steps)]
        for place, x in zip(places, inverses):
            inverse_ref[place] = x

    def advance(c, states):
        base = pl.multiple_of(c * chunk, chunk)
        rows = pl.ds(base, chunk)
        _, _, carry, close, keep = chunk_masks(segment_of, base, chunk)
        new_states = []
        for h in range(heads):
            cols = slice(h * 128, (h + 1) * 128)
            state = states[h]
            k = key_s[rows, cols]
            q = query_s[rows, cols]
            delta = value_s[rows, cols] - carry * product(k, state, 1, 0, exact)
            fixed = product(inverse_ref[c * heads + h], beta_of(base, h) * delta, 1, 0, exact)
            out = carry * product(q, state, 1, 0, exact) + product(
                score_s[c * heads + h], fixed, 1, 0, exact)
            state_ref[c * heads + h] = state
            new_states.append(keep * state + product(k, close * fixed, 0, 0, exact))
            delta_ref[rows, cols] = delta
            fixed_ref[rows, cols] = fixed
            heads_ref[rows, cols] = out
            gate = proj_ref[rows, 3 * width + h * 128 : 3 * width + (h + 1) * 128]
            r = lax.rsqrt(jnp.mean(out * out, axis=-1, keepdims=True) + epsilon)
            mixed_ref[rows, cols] = (
                out * r * gain_ref[h : h + 1, :] * (gate * sigmoid(gate))
            ).astype(mixed_ref.dtype)
        return tuple(new_states)

    lax.fori_loop(0, count, advance, tuple(jnp.zeros((128, 128), f32) for _ in range(heads)))


def mixer_backward_kernel(exact, lengths_ref, proj_ref, beta_ref, tap_ref, gain_ref, grad_ref,
                          heads_ref, fixed_ref, delta_ref, state_ref, inverse_ref,
                          dproj_ref, dbeta_ref, dtap_ref, dgain_ref,
                          query_s, key_s, pre_s, dout_s, dpre_s):
    rows_all = proj_ref.shape[0]
    width = proj_ref.shape[1] // 4
    heads = width // 128
    chunk = CHUNK
    count = rows_all // chunk
    taps = tap_ref.shape[0] // 3
    segment_of, segments = segment_tools(lengths_ref)
    dgain_ref[...] = jnp.zeros_like(dgain_ref)
    dbeta_ref[...] = jnp.zeros_like(dbeta_ref)
    dtap_ref[...] = jnp.zeros_like(dtap_ref)

    @pl.loop(0, count)
    def _(c):
        base = pl.multiple_of(c * chunk, chunk)
        rows = pl.ds(base, chunk)
        for part in range(3):
            pre, _ = conv_part(proj_ref, tap_ref, segment_of, base, part, width, chunk)
            pre_s[rows, part * width : (part + 1) * width] = pre
            if part < 2:
                act = pre * sigmoid(pre)
                target = (query_s, key_s)[part]
                scale = 128 ** (-0.5) if part == 0 else 1.0
                for h, a in enumerate(heads_of(act, heads)):
                    target[rows, h * 128 : (h + 1) * 128] = unit_rows(a, scale)
        for h in range(heads):
            cols = slice(h * 128, (h + 1) * 128)
            gate_cols = slice(3 * width + h * 128, 3 * width + (h + 1) * 128)
            out = heads_ref[rows, cols]
            gate = proj_ref[rows, gate_cols]
            grad = grad_ref[rows, cols].astype(f32)
            gain = gain_ref[h : h + 1, :]
            sg = sigmoid(gate)
            silu = gate * sg
            r = lax.rsqrt(jnp.mean(out * out, axis=-1, keepdims=True) + epsilon)
            normed = out * r
            dgain_ref[h : h + 1, :] += jnp.sum(grad * normed * silu, axis=0, keepdims=True)
            dproj_ref[rows, gate_cols] = (
                grad * normed * gain * (sg * (1.0 + gate * (1.0 - sg)))
            ).astype(dproj_ref.dtype)
            weighted = grad * gain * silu
            dout_s[rows, cols] = r * weighted - out * (r * r * r) * jnp.mean(
                weighted * out, axis=-1, keepdims=True)

    dpre_s[rows_all : rows_all + HALO, :] = jnp.zeros((HALO, 3 * width), f32)

    def retreat(step, dstates):
        c = count - 1 - step
        base = pl.multiple_of(c * chunk, chunk)
        rows = pl.ds(base, chunk)
        strict, within, carry, close, keep = chunk_masks(segment_of, base, chunk)
        pos = base + lax.broadcasted_iota(jnp.int32, (chunk, 1), 0)
        live = (segment_of(pos) < segments).astype(f32)
        new_dstates = []
        for h in range(heads):
            cols = slice(h * 128, (h + 1) * 128)
            place = c * heads + h
            k = key_s[rows, cols]
            q = query_s[rows, cols]
            dout = dout_s[rows, cols]
            state = state_ref[place]
            inverse = inverse_ref[place]
            fixed = fixed_ref[rows, cols]
            delta = delta_ref[rows, cols]
            dstate = dstates[h]
            rate = sigmoid(beta_ref[rows, h : h + 1])
            beta = rate * live
            scores = product(q, k, 1, 1, exact) * within
            gram = product(k, k, 1, 1, exact) * strict
            dfixed = product(scores, dout, 0, 0, exact) + close * product(k, dstate, 1, 0, exact)
            drhs = product(inverse, dfixed, 0, 0, exact)
            ddelta = beta * drhs
            carried_dout = carry * dout
            carried_ddelta = carry * ddelta
            new_dstates.append(
                keep * dstate
                + product(q, carried_dout, 0, 0, exact)
                - product(k, carried_ddelta, 0, 0, exact)
            )
            dscores = product(dout, fixed, 1, 1, exact) * within
            dlower = -product(drhs, fixed, 1, 1, exact) * strict
            dgram = beta * dlower
            dq = product(carried_dout, state, 1, 1, exact) + product(dscores, k, 1, 0, exact)
            dk = (
                product(dscores, q, 0, 0, exact)
                + close * product(fixed, dstate, 1, 1, exact)
                - product(carried_ddelta, state, 1, 1, exact)
                + product(dgram, k, 1, 0, exact)
                + product(dgram, k, 0, 0, exact)
            )
            drate = live * (
                jnp.sum(drhs * delta, axis=-1, keepdims=True)
                + jnp.sum(dlower * gram, axis=-1, keepdims=True)
            )
            dbeta_ref[rows, h : h + 1] = (drate * rate * (1.0 - rate)).astype(dbeta_ref.dtype)
            for part, da in enumerate((dq, dk, ddelta)):
                part_cols = slice(part * width + h * 128, part * width + (h + 1) * 128)
                pre = pre_s[rows, part_cols]
                sg = sigmoid(pre)
                if part < 2:
                    a = pre * sg
                    scale = 128 ** (-0.5) if part == 0 else 1.0
                    r = lax.rsqrt(jnp.sum(a * a, axis=-1, keepdims=True) + epsilon)
                    da = (scale * r) * (da - a * (r * r) * jnp.sum(da * a, axis=-1, keepdims=True))
                dpre_s[rows, part_cols] = da * (sg * (1.0 + pre * (1.0 - sg)))
        return tuple(new_dstates)

    lax.fori_loop(0, count, retreat, tuple(jnp.zeros((128, 128), f32) for _ in range(heads)))

    @pl.loop(0, count)
    def _(c):
        base = pl.multiple_of(c * chunk, chunk)
        rows = pl.ds(base, chunk)
        col = base + lax.broadcasted_iota(jnp.int32, (chunk, 1), 0)
        seg = segment_of(col)
        for part in range(3):
            cols = slice(part * width, (part + 1) * width)
            _, shifted = conv_part(proj_ref, tap_ref, segment_of, base, part, width, chunk)
            full = dpre_s[pl.ds(base, chunk + HALO), cols]
            main = full[:chunk]
            total = main * tap_ref[part * taps : part * taps + 1, :]
            for s in range(taps):
                at = slice(part * taps + s, part * taps + s + 1)
                dtap_ref[at, :] += jnp.sum(main * shifted[s], axis=0, keepdims=True)
                if s > 0:
                    valid = (segment_of(col + s) == seg) & (col + s < rows_all)
                    moved = pltpu.roll(full, chunk + HALO - s, 0)[:chunk]
                    total = total + jnp.where(valid, moved, 0.0) * tap_ref[at, :]
            dproj_ref[rows, cols] = total.astype(dproj_ref.dtype)


def vmem():
    return pl.BlockSpec(memory_space=pltpu.VMEM)


def mixer_forward(lengths_row, projected, beta_logits, taps, gain, exact=True, group=4):
    rows, wide = projected.shape
    width = wide // 4
    heads = width // 128
    places = rows // CHUNK * heads
    group = min(group, rows // CHUNK)
    return pl.pallas_call(
        partial(mixer_forward_kernel, exact, group),
        out_shape=(
            jax.ShapeDtypeStruct((rows, width), bf16),
            jax.ShapeDtypeStruct((rows, width), f32),
            jax.ShapeDtypeStruct((rows, width), f32),
            jax.ShapeDtypeStruct((rows, width), f32),
            jax.ShapeDtypeStruct((places, 128, 128), f32),
            jax.ShapeDtypeStruct((places, CHUNK, CHUNK), f32),
        ),
        in_specs=[pl.BlockSpec(memory_space=pltpu.SMEM)] + [vmem()] * 4,
        out_specs=(vmem(),) * 6,
        scratch_shapes=[pltpu.VMEM((rows, width), f32)] * 3
        + [pltpu.VMEM((places, CHUNK, CHUNK), f32 if exact else bf16)],
        compiler_params=pltpu.CompilerParams(vmem_limit_bytes=48 * 2**20),
        cost_estimate=pl.CostEstimate(flops=10**10, bytes_accessed=10**7, transcendentals=10**6),
        name="mixer_forward",
    )(lengths_row, projected, beta_logits, taps, gain)


def mixer_backward(lengths_row, projected, beta_logits, taps, gain, grad, saved, exact=True):
    rows, wide = projected.shape
    width = wide // 4
    return pl.pallas_call(
        partial(mixer_backward_kernel, exact),
        out_shape=(
            jax.ShapeDtypeStruct((rows, wide), bf16),
            jax.ShapeDtypeStruct((rows, 128), bf16),
            jax.ShapeDtypeStruct(taps.shape, f32),
            jax.ShapeDtypeStruct(gain.shape, f32),
        ),
        in_specs=[pl.BlockSpec(memory_space=pltpu.SMEM)] + [vmem()] * 10,
        out_specs=(vmem(),) * 4,
        scratch_shapes=[pltpu.VMEM((rows, width), f32)] * 2
        + [pltpu.VMEM((rows, 3 * width), f32), pltpu.VMEM((rows, width), f32),
           pltpu.VMEM((rows + HALO, 3 * width), f32)],
        compiler_params=pltpu.CompilerParams(vmem_limit_bytes=56 * 2**20),
        cost_estimate=pl.CostEstimate(flops=10**10, bytes_accessed=10**7, transcendentals=10**6),
        name="mixer_backward",
    )(lengths_row, projected, beta_logits, taps, gain, grad, *saved)


NT = (((1,), (1,)), ((), ()))


def other(axis_name):
    return {axis_name: 1 - lax.axis_index(axis_name)}


def ffn_kernel(x_ref, w_ref, down_ref, c_refs, out_ref, ngrad_ref, wgrad_ref, down_out,
               xs, cs, ws, dsum, landed, outs, inner_s, gate_s, up_s, acts_t, part, crecv, drecv, nrecv, stage,
               ag_send, ag_recv, pair_send, pair_recv, rs_send, rs_recv, c_sem, w_sem, g_sem, t_sem,
               down_right, down_left, down_recv, down_sem, sum_sems, keep_sem, out_sem):
    half = xs.shape[1] // 2
    rows = 2 * half
    model = xs.shape[2]
    hidden = ws.shape[1]
    lines = w_ref.shape[0]
    parts, _, quarter, width = w_ref.shape[1:]
    tile_f = 256
    tile_d = min(512, model)
    tile_w = min(256, width)

    def remote(src, dst, send, recv, axis_name):
        return pltpu.make_async_remote_copy(
            src_ref=src, dst_ref=dst, send_sem=send, recv_sem=recv,
            device_id=other(axis_name), device_id_type=pl.DeviceIdType.MESH)

    def halves(ref, index, h):
        return ref.at[index, pl.ds(h * half, half)]

    o = lax.axis_index("z")

    def down_rows(z):
        return ws.at[2, pl.ds(pl.multiple_of(z * quarter, 16), quarter)]

    def down_pass(z, right):
        send = down_right if right else down_left
        return pltpu.make_async_remote_copy(
            src_ref=down_rows(z), dst_ref=down_rows(z), send_sem=send.at[z], recv_sem=down_recv.at[z],
            device_id={"z": o + 1 if right else o - 1}, device_id_type=pl.DeviceIdType.MESH)

    def down_forward(z, right):
        @pl.when(o < lines - 1 if right else o > 0)
        def _():
            down_pass(z, right).start()

    def down_step(far):
        for side in (-1, 1):
            z = o + side * far

            @pl.when((z >= 0) & (z < lines))
            def _():
                down_pass(z, side < 0).wait_recv()
                down_forward(z, side < 0)

    weight_copies, down_copies = [], []
    for r in range(parts):
        cols = pl.ds(r * width, width)
        for line in range(lines):
            weight_copies.append(pltpu.make_async_copy(
                w_ref.at[line, r], ws.at[pl.ds(0, 2), pl.ds(line * quarter, quarter), cols],
                w_sem.at[line, r]))
        down_copies.append(pltpu.make_async_copy(
            down_ref.at[r], down_rows(o).at[:, cols], down_sem.at[r]))
    for copy in down_copies:
        copy.start()
    for copy in weight_copies:
        copy.start()

    def pair_at(turn):
        return jnp.where(turn < 2, 3 - 2 * turn, 6 - 2 * turn)

    def slot_of(step):
        return (1 - lax.rem(step, 2)) * 4 + pair_at(step // 2)

    def c_copy(step, n):
        buffer = lax.rem(step, 2)
        return pltpu.make_async_copy(c_refs[n], cs.at[buffer], c_sem.at[buffer])

    def c_start(step):
        for n in range(8):
            @pl.when(slot_of(step) == n)
            def _():
                c_copy(step, n).start()

    c_copy(0, 7).start()
    line_barrier(lines, [other(name) for name in ("core", "x", "y")])

    own_pair = remote(x_ref, xs.at[4], ag_send.at[0], ag_recv.at[0], "core")
    own_x = [remote(x_ref.at[pl.ds(h * half, half)], halves(xs, 1, h), ag_send.at[1 + h], ag_recv.at[1 + h], "x") for h in range(2)]
    own_y = [remote(x_ref.at[pl.ds(h * half, half)], halves(xs, 2, h), ag_send.at[3 + h], ag_recv.at[3 + h], "y") for h in range(2)]
    relay_y = remote(halves(xs, 1, 0), halves(xs, 3, 0), ag_send.at[5], ag_recv.at[5], "y")
    relay_x = remote(halves(xs, 2, 1), halves(xs, 3, 1), ag_send.at[6], ag_recv.at[6], "x")
    pair_of = [None] + [remote(xs.at[j], xs.at[4 + j], ag_send.at[6 + j], ag_recv.at[6 + j], "core") for j in (1, 2, 3)]
    own_pair.start()
    own_x[0].start()
    own_y[1].start()
    own_x[1].start()
    own_y[0].start()
    for copy in down_copies:
        copy.wait()
    down_forward(o, True)
    down_forward(o, False)
    own_copy = pltpu.make_async_copy(x_ref, xs.at[0], t_sem.at[0, 0])
    own_copy.start()
    own_copy.wait()
    for copy in weight_copies:
        copy.wait()

    def part_send(turn):
        j = pair_at(turn)
        return remote(part.at[lax.rem(turn, 2)], crecv.at[j], pair_send.at[j], pair_recv.at[j], "core")

    x_sends = [[remote(crecv.at[1, a, pl.ds(h * half, half)], nrecv.at[0, a, pl.ds(h * half, half)],
                       rs_send.at[a * 2 + h], rs_recv.at[a * 2 + h], "x") for a in range(2)] for h in range(2)]
    y_sends = [[remote(crecv.at[2, a, pl.ds(h * half, half)], nrecv.at[1, a, pl.ds(h * half, half)],
                       rs_send.at[4 + a * 2 + h], rs_recv.at[4 + a * 2 + h], "y") for a in range(2)] for h in range(2)]
    d_sends = [[remote(crecv.at[3, a, pl.ds(h * half, half)], drecv.at[a, pl.ds(h * half, half)],
                       rs_send.at[8 + a * 2 + h], rs_recv.at[8 + a * 2 + h], ("x", "y")[h]) for a in range(2)] for h in range(2)]

    def gates(slot, cols):
        return [
            lax.dot_general(xs[slot], ws[kind, cols, :], NT, preferred_element_type=f32)
            for kind in range(2)]

    @pl.loop(0, 8)
    def _(early):
        slot = lax.rem(early + 1, 2) * 4 + early // 2

        @pl.when(early == 0)
        def _():
            own_pair.wait_recv()

        @pl.when(early == 2)
        def _():
            down_step(1)
            own_x[0].wait_recv()
            relay_y.start()
            own_y[1].wait_recv()
            relay_x.start()
            own_x[1].wait_recv()
            pair_of[1].start()
            own_y[0].wait_recv()
            pair_of[2].start()
            pair_of[1].wait_recv()

        @pl.when(early == 4)
        def _():
            pair_of[2].wait_recv()

        @pl.when(early == 6)
        def _():
            if lines > 2:
                down_step(2)
            relay_y.wait_recv()
            relay_x.wait_recv()
            pair_of[3].start()
            pair_of[3].wait_recv()

        places = pl.ds(pl.multiple_of(slot * rows, rows), rows)
        for start in range(0, hidden, tile_f):
            cols = slice(start, min(start + tile_f, hidden))
            gate, up = gates(slot, cols)
            acts_t[2, cols, places] = (gate * sigmoid(gate) * up).astype(bf16).T

    tiles = model // tile_w

    def c_tile(t):
        buffer = lax.rem(t, 2)
        cols = pl.ds(pl.multiple_of(t * tile_w, tile_w), tile_w)
        return [
            pltpu.make_async_copy(
                ref.at[:, cols], part.at[0, buffer, :, pl.ds(n * tile_w, tile_w)], t_sem.at[buffer, n])
            for n, ref in enumerate(c_refs)]

    def grad_copy(kind, t, line):
        return pltpu.make_async_copy(
            stage.at[lax.rem(t, 2), pl.ds(line * quarter, quarter)],
            wgrad_ref.at[line, t * tile_w // width, kind, :,
                         pl.ds(pl.multiple_of(lax.rem(t * tile_w, width), tile_w), tile_w)],
            g_sem.at[lax.rem(t, 2), line])

    def weight_grads(kind):
        @pl.loop(0, tiles)
        def _(t):
            if kind == 2:
                for copy in c_tile(t):
                    copy.wait()
                right = jnp.concatenate(
                    [part[0, lax.rem(t, 2), :, n * tile_w : (n + 1) * tile_w] for n in range(8)])
            else:
                right = xs[:, :, pl.ds(pl.multiple_of(t * tile_w, tile_w), tile_w)].reshape(8 * rows, tile_w)

            if kind < 2:
                @pl.when(t >= 2)
                def _():
                    for line in range(lines):
                        grad_copy(kind, t - 2, line).wait()

            value = jnp.dot(acts_t[kind], right, preferred_element_type=f32).astype(bf16)
            if kind == 2:
                @pl.when(t + 2 < tiles)
                def _():
                    for copy in c_tile(t + 2):
                        copy.start()
            if kind < 2:
                stage[lax.rem(t, 2)] = value
                for line in range(lines):
                    grad_copy(kind, t, line).start()
            else:
                dsum[:, pl.ds(pl.multiple_of(t * tile_w, tile_w), tile_w)] = value

        if kind == 2:
            return
        for t in range(max(tiles - 2, 0), tiles):
            for line in range(lines):
                grad_copy(kind, t, line).wait()

    mesh_id = pl.DeviceIdType.MESH

    def rows_of(z):
        return dsum.at[pl.ds(pl.multiple_of(z * quarter, 16), quarter)]

    def sum_pass(z, right):
        side = 0 if right else 2
        block = jnp.maximum(z - o - 1, 0) if right else jnp.minimum(lines - o + 1 + z, lines)
        return pltpu.make_async_remote_copy(
            src_ref=rows_of(z), dst_ref=landed.at[block],
            send_sem=sum_sems.at[side, z], recv_sem=sum_sems.at[side + 1, z],
            device_id={"z": o + 1 if right else o - 1}, device_id_type=mesh_id)

    def sum_add(z, block):
        at = pl.ds(pl.multiple_of(z * quarter, 16), quarter)
        for start in range(0, model, tile_d):
            cols = slice(start, start + tile_d)
            dsum[at, cols] = (
                dsum[at, cols].astype(f32) + landed[block, :, cols].astype(f32)).astype(bf16)

    def sum_tick(k):
        z_right = lines - 1 - k + o

        @pl.when(o <= k)
        def _():
            @pl.when(o > 0)
            def _():
                sum_pass(z_right, True).wait_recv()
                sum_add(z_right, z_right - o)

            @pl.when(o < k)
            def _():
                sum_pass(z_right + 1, True).wait_send()
            sum_pass(z_right, True).start()

        back = lines - 1 - o
        z_left = k - back

        @pl.when(back <= k)
        def _():
            @pl.when(back > 0)
            def _():
                sum_pass(z_left, False).wait_recv()
                sum_add(z_left, lines - o + z_left)

            @pl.when(back < k)
            def _():
                sum_pass(z_left - 1, False).wait_send()
            sum_pass(z_left, False).start()

    for t in range(2):
        for copy in c_tile(t):
            copy.start()
    weight_grads(2)
    sum_tick(0)
    for far in range(3, lines):
        down_step(far)

    @pl.loop(0, 8)
    def _(step):
        turn = step // 2
        j = pair_at(turn)
        slot = slot_of(step)
        pairing = lax.rem(step, 2) == 0

        @pl.when(step < 7)
        def _():
            c_start(step + 1)

        for k in range(1, lines - 1):
            @pl.when(step == min(1 + 3 * k, 7))
            def _():
                sum_tick(k)

        c_copy(step, 0).wait()

        for start in range(0, hidden, tile_f):
            size = min(tile_f, hidden - start)
            cols = slice(start, start + size)
            gate, up = gates(slot, cols)
            grad = lax.dot_general(cs[lax.rem(step, 2)], ws[2, cols, :], NT, preferred_element_type=f32)
            sg = sigmoid(gate)
            silu = gate * sg
            inner = (silu * up).astype(bf16)
            gate_grad = (grad * up * sg * (1.0 + gate * (1.0 - sg))).astype(bf16)
            up_grad = (grad * silu).astype(bf16)
            places = pl.ds(pl.multiple_of(slot * rows, rows), rows)
            for kind, (value, target) in enumerate(((gate_grad, gate_s), (up_grad, up_s), (inner, inner_s))):
                target[:, cols] = value
                if kind < 2:
                    acts_t[kind, cols, places] = value.T

        @pl.when(pairing & (step >= 4))
        def _():
            part_send(turn - 2).wait_send()

        place = jnp.where(pairing, lax.rem(turn, 2), 2)
        for start in range(0, model, tile_d):
            cols = slice(start, start + tile_d)
            part[place, 0, :, cols] = jnp.dot(
                inner_s[...], ws[2, :, cols], preferred_element_type=f32).astype(bf16)
            part[place, 1, :, cols] = (
                jnp.dot(gate_s[...], ws[0, :, cols], preferred_element_type=f32)
                + jnp.dot(up_s[...], ws[1, :, cols], preferred_element_type=f32)
            ).astype(bf16)

        @pl.when(pairing)
        def _():
            part_send(turn).start()

        @pl.when(jnp.logical_not(pairing))
        def _():
            part_send(turn).wait_recv()
            for a in range(2):
                for start in range(0, model, tile_d):
                    cols = slice(start, start + tile_d)
                    crecv[j, a, :, cols] = (
                        crecv[j, a, :, cols].astype(f32) + part[2, a, :, cols].astype(f32)
                    ).astype(bf16)

        @pl.when(step == 1)
        def _():
            for h in range(2):
                for copy in d_sends[h]:
                    copy.start()

        @pl.when(step == 3)
        def _():
            for copy in x_sends[0]:
                copy.start()

        @pl.when(step == 5)
        def _():
            for copy in y_sends[1]:
                copy.start()


    for h in range(2):
        j = 2 - h
        for a in range(2):
            d_sends[h][a].wait_recv()
            at = pl.ds(h * half, half)
            crecv[j, a, at, :] = (
                crecv[j, a, at, :].astype(f32) + drecv[a, at, :].astype(f32)).astype(bf16)
        for copy in (y_sends, x_sends)[h][h]:
            copy.start()
    weight_grads(0)
    weight_grads(1)
    out_copies = []
    for a, target in enumerate((out_ref, ngrad_ref)):
        for h in range(2):
            x_sends[h][a].wait_recv()
            y_sends[h][a].wait_recv()
        for n in range(model // tile_d):
            cols = slice(n * tile_d, (n + 1) * tile_d)
            if n >= 2:
                out_copies[-2].wait()
            outs[a, n % 2] = (
                crecv[0, a, :, cols].astype(f32)
                + nrecv[0, a, :, cols].astype(f32)
                + nrecv[1, a, :, cols].astype(f32)
            )
            copy = pltpu.make_async_copy(
                outs.at[a, n % 2], target.at[:, pl.ds(n * tile_d, tile_d)],
                out_sem.at[n, a])
            copy.start()
            out_copies.append(copy)
    steps = model // tile_d
    for a in range(2):
        for copy in out_copies[a * steps : (a + 1) * steps][-2:]:
            copy.wait()
    @pl.loop(0, lines)
    def _(z):
        @pl.when((o < lines - 1) & (z <= o))
        def _():
            down_pass(z, True).wait_send()

        @pl.when((o > 0) & (z >= o))
        def _():
            down_pass(z, False).wait_send()

    own_pair.wait_send()
    for h in range(2):
        own_x[h].wait_send()
        own_y[h].wait_send()
        for a in range(2):
            x_sends[h][a].wait_send()
            y_sends[h][a].wait_send()
            d_sends[h][a].wait_send()
    relay_x.wait_send()
    relay_y.wait_send()
    for j in (1, 2, 3):
        pair_of[j].wait_send()
    part_send(2).wait_send()
    part_send(3).wait_send()

    @pl.when(o > 0)
    def _():
        sum_pass(o, True).wait_recv()
        sum_add(o, 0)

    @pl.when(o < lines - 1)
    def _():
        sum_pass(o, False).wait_recv()
        sum_add(o, lines)

    keeps = [
        pltpu.make_async_copy(
            rows_of(o).at[:, pl.ds(q * width, width)], down_out.at[q], keep_sem.at[q])
        for q in range(parts)
    ]
    for copy in keeps:
        copy.start()

    @pl.when(o < lines - 1)
    def _():
        sum_pass(o + 1, True).wait_send()

    @pl.when(o > 0)
    def _():
        sum_pass(o - 1, False).wait_send()
    for copy in keeps:
        copy.wait()


def ffn_call_kernel(x_ref, w_ref, down_ref, *refs):
    ffn_kernel(x_ref, w_ref, down_ref, refs[:8], *refs[8:])


def ffn_plane(x_own, weights, down_own, c_rows):
    rows, model = x_own.shape
    lines, parts, _, quarter, width = weights.shape
    hidden = lines * quarter
    tile_w = min(256, width)
    sems = pltpu.SemaphoreType.DMA
    anywhere = pl.BlockSpec(memory_space=pl.ANY)
    return pl.pallas_call(
        ffn_call_kernel,
        out_shape=(
            jax.ShapeDtypeStruct((rows, model), f32),
            jax.ShapeDtypeStruct((rows, model), f32),
            jax.ShapeDtypeStruct(weights.shape, bf16),
            jax.ShapeDtypeStruct((parts, quarter, width), bf16),
        ),
        in_specs=[anywhere] * 11,
        out_specs=(anywhere,) * 4,
        scratch_shapes=[
            pltpu.VMEM((8, rows, model), bf16),
            pltpu.VMEM((2, rows, model), bf16),
            pltpu.VMEM((3, hidden, model), bf16),
            pltpu.VMEM((hidden, model), bf16),
            pltpu.VMEM((lines + 1, quarter, model), bf16),
            pltpu.VMEM((2, 2, rows, min(512, model)), f32),
            pltpu.VMEM((rows, hidden), bf16),
            pltpu.VMEM((rows, hidden), bf16),
            pltpu.VMEM((rows, hidden), bf16),
            pltpu.VMEM((3, hidden, 8 * rows), bf16),
            pltpu.VMEM((3, 2, rows, model), bf16),
            pltpu.VMEM((4, 2, rows, model), bf16),
            pltpu.VMEM((2, rows, model), bf16),
            pltpu.VMEM((2, 2, rows, model), bf16),
            pltpu.VMEM((2, hidden, tile_w), bf16),
            sems((10,)), sems((10,)), sems((4,)), sems((4,)), sems((12,)), sems((12,)),
            sems((2,)), sems((lines, parts)), sems((2, lines)), sems((2, 8)),
            sems((lines,)), sems((lines,)), sems((lines,)), sems((parts,)),
            sems((4, lines)), sems((parts,)), sems((4, 2)),
        ],
        compiler_params=pltpu.CompilerParams(
            collective_id=2, has_side_effects=True, vmem_limit_bytes=60 * 2**20),
        cost_estimate=pl.CostEstimate(flops=8 * 10**10, bytes_accessed=4 * 10**7, transcendentals=10**6),
        name="ffn_plane",
    )(x_own, weights, down_own, *c_rows)


def line_barrier(lines, others):
    o = lax.axis_index("z")
    barrier = pltpu.get_barrier_semaphore()
    mesh_id = pl.DeviceIdType.MESH

    @pl.when(o > 0)
    def _():
        pl.semaphore_signal(barrier, inc=1, device_id={"z": o - 1}, device_id_type=mesh_id)

    @pl.when(o < lines - 1)
    def _():
        pl.semaphore_signal(barrier, inc=1, device_id={"z": o + 1}, device_id_type=mesh_id)

    for target in others:
        pl.semaphore_signal(barrier, inc=1, device_id=target, device_id_type=mesh_id)
    peers = len(others) + (o > 0).astype(jnp.int32) + (o < lines - 1).astype(jnp.int32)
    pl.semaphore_wait(barrier, peers)


def line_copy(src, dst, send, recv, target):
    return pltpu.make_async_remote_copy(
        src_ref=src, dst_ref=dst, send_sem=send, recv_sem=recv,
        device_id=target, device_id_type=pl.DeviceIdType.MESH)


def pair_peers():
    x, core = lax.axis_index("x"), lax.axis_index("core")
    peers = [
        (x * 2 + 1 - core, {"core": 1 - core}),
        ((1 - x) * 2 + core, {"x": 1 - x}),
        ((1 - x) * 2 + 1 - core, {"x": 1 - x, "core": 1 - core}),
    ]
    return x * 2 + core, peers


class Swap:
    def __init__(self, pairs, send, recv, own):
        me, peers = pair_peers()
        self.own = [
            pltpu.make_async_copy(source.at[me], target(me), own.at[n])
            for n, (source, target) in enumerate(pairs)]
        self.away = [
            line_copy(source.at[place], target(me), send.at[n, d], recv.at[n, d], device)
            for n, (source, target) in enumerate(pairs) for d, (place, device) in enumerate(peers)]

    def start(self):
        for copy in self.away + self.own:
            copy.start()

    def wait(self):
        for copy in self.own:
            copy.wait()
        for copy in self.away:
            copy.wait_recv()
            copy.wait_send()


def gather_kernel(x_ref, gain_ref, o_ref, f_refs, w_refs, wb_ref, rows_ref, outs_ref, proj_refs, beta_ref,
                  pair_ref, down_ref, gain_out,
                  xs, parts, stage, beta_stage, right_send, left_send, line_recv, pair_send, pair_recv,
                  part_right, part_left, part_recv, own_sem, row_sem, outs_sem, out_sem, beta_sem,
                  swap_send, swap_recv, swap_own, gains, gain_send, gain_recv, gain_own):
    lines = xs.shape[0] // 2
    batches, rows, model = x_ref.shape
    o = lax.axis_index("z")
    i = lax.axis_index("y")
    line_barrier(lines, [other("y")] + [device for _, device in pair_peers()[1]])
    swap = Swap(
        [(f_refs[0], lambda place: pair_ref.at[place, 0]),
         (f_refs[1], lambda place: pair_ref.at[place, 1]),
         (f_refs[2], lambda place: down_ref.at[place])],
        swap_send, swap_recv, swap_own)

    def right(z, m):
        ref = xs.at[z * 2 + i, m]
        return line_copy(ref, ref, right_send.at[z, m], line_recv.at[z, m], {"z": o + 1})

    def left(z, m):
        ref = xs.at[z * 2 + i, m]
        return line_copy(ref, ref, left_send.at[z, m], line_recv.at[z, m], {"z": o - 1})

    def across(z, m):
        ref = xs.at[z * 2 + i, m]
        return line_copy(ref, ref, pair_send.at[z, m], pair_recv.at[z, m], other("y"))

    own = [
        pltpu.make_async_copy(o_ref, parts.at[o], own_sem.at[1]),
    ]

    def pass_part(z):
        ref = parts.at[z]
        return (line_copy(ref, ref, part_right.at[z], part_recv.at[z], {"z": o + 1}),
                line_copy(ref, ref, part_left.at[z], part_recv.at[z], {"z": o - 1}))

    for copy in own:
        copy.start()
    me, peers = pair_peers()
    share = gain_ref.shape[1]
    gain_place = gains.at[:, pl.ds(pl.multiple_of(me * share, 128), share)]
    gain_away = [
        line_copy(gain_ref, gain_place, gain_send.at[d], gain_recv.at[d], device)
        for d, (_, device) in enumerate(peers)]
    gain_keep = pltpu.make_async_copy(gain_ref, gain_place, gain_own.at[0])
    gain_keep.start()
    for copy in gain_away:
        copy.start()
    gain_keep.wait()
    for copy in gain_away:
        copy.wait_recv()
    for m in range(batches):
        value = x_ref[m].astype(f32)
        scale = lax.rsqrt(jnp.mean(value * value, axis=-1, keepdims=True) + epsilon)
        xs[o * 2 + i, m] = (value * scale * gains[0:1, :]).astype(bf16)
    for copy in own:
        copy.wait()

    def outs(turn, slot):
        buffer = lax.rem(turn, 2)
        return [
            copy for m in range(batches) for copy in (
                pltpu.make_async_copy(stage.at[buffer, m], proj_refs[m].at[slot], out_sem.at[buffer, m]),
                pltpu.make_async_copy(beta_stage.at[buffer, m], beta_ref.at[m, slot], beta_sem.at[buffer, m]))
        ]

    def keep(slot, m):
        return pltpu.make_async_copy(xs.at[slot, m], rows_ref.at[m, slot], row_sem.at[slot, m])

    def keep_outs(z):
        return pltpu.make_async_copy(parts.at[z], outs_ref.at[z], outs_sem.at[z])

    def project(turn, slot):
        @pl.when(turn >= 2)
        def _():
            for copy in outs(turn, slot):
                copy.wait()
        for m in range(batches):
            keep(slot, m).start()
        x = xs[slot].reshape(batches * rows, model)
        buffer = lax.rem(turn, 2)
        width = w_refs[0].shape[1]
        for n, w_ref in enumerate(w_refs):
            stage[buffer, :, :, n * width : (n + 1) * width] = jnp.dot(
                x, w_ref[...], preferred_element_type=f32).reshape(batches, rows, width)
        beta_stage[buffer] = jnp.dot(
            x, wb_ref[...], preferred_element_type=f32).reshape(batches, rows, 128)
        for copy in outs(turn, slot):
            copy.start()

    def in_line(index):
        far = (index + 1) // 2
        side = 1 - 2 * lax.rem(index, 2)
        z = o + side * far
        return far, z, (z >= 0) & (z < lines)

    def first(index, turn):
        far, z, valid = in_line(index)

        @pl.when(valid)
        def _():
            for m in range(batches):
                @pl.when(far > 0)
                def _():
                    left(z, m).wait_recv()

                @pl.when((o < lines - 1) & (z <= o))
                def _():
                    right(z, m).start()

                @pl.when((o > 0) & (z >= o))
                def _():
                    left(z, m).start()

                across(z, m).start()
            project(turn, z * 2 + i)

        return turn + valid.astype(jnp.int32)

    swap.start()
    turn = lax.fori_loop(0, 2 * lines - 1, first, jnp.int32(0))

    def second(index, turn):
        far, z, valid = in_line(index)

        @pl.when(valid)
        def _():
            to_right, to_left = pass_part(z)

            @pl.when(far > 0)
            def _():
                to_left.wait_recv()

            @pl.when((o < lines - 1) & (z <= o))
            def _():
                to_right.start()

            @pl.when((o > 0) & (z >= o))
            def _():
                to_left.start()

            keep_outs(z).start()
            for m in range(batches):
                across(z, m).wait_recv()
            project(turn, z * 2 + 1 - i)

        return turn + valid.astype(jnp.int32)

    lax.fori_loop(0, 2 * lines - 1, second, turn)
    for turn in range(2 * lines - 2, 2 * lines):
        for copy in outs(turn, 0):
            copy.wait()

    @pl.loop(0, lines)
    def _(z):
        keep_outs(z).wait()

        @pl.when((o < lines - 1) & (z <= o))
        def _():
            pass_part(z)[0].wait_send()
            for m in range(batches):
                right(z, m).wait_send()

        @pl.when((o > 0) & (z >= o))
        def _():
            pass_part(z)[1].wait_send()
            for m in range(batches):
                left(z, m).wait_send()

        for m in range(batches):

            across(z, m).wait_send()
            for y in range(2):
                keep(z * 2 + y, m).wait()

    swap.wait()
    gain_out[...] = gains[...]
    for copy in gain_away:
        copy.wait_send()


def gather_call_kernel(x_ref, gain_ref, o_ref, *refs):
    gather_kernel(x_ref, gain_ref, o_ref, refs[:3], refs[3:7], refs[7], refs[8], refs[9], refs[10:12],
                  *refs[12:])


def gather_project(x, gains, w_out_part, ffn_parts, w_inner, w_beta):
    batches, rows, model = x.shape
    more = w_out_part.shape[1]
    lines = lax.axis_size("z")
    width = sum(w.shape[1] for w in w_inner)
    slots = 2 * lines
    sems = pltpu.SemaphoreType.DMA
    anywhere = pl.BlockSpec(memory_space=pl.ANY)
    pair = sems((lines, batches))
    ranks, quarter, share = ffn_parts[0].shape
    gathered, outs, *projected, beta, pair_parts, down_part, gains_all = pl.pallas_call(
        gather_call_kernel,
        out_shape=(
            jax.ShapeDtypeStruct((batches, slots, rows, model), bf16),
            jax.ShapeDtypeStruct((lines, batches, more, model), bf16),
            *[jax.ShapeDtypeStruct((slots, rows, width), f32)] * batches,
            jax.ShapeDtypeStruct((batches, slots, rows, 128), f32),
            jax.ShapeDtypeStruct((ranks, 2, quarter, share), bf16),
            jax.ShapeDtypeStruct((ranks, quarter, share), bf16),
            jax.ShapeDtypeStruct((gains.shape[0], model), f32),
        ),
        in_specs=[vmem()] * 2 + [anywhere] * 4 + [vmem()] * 5,
        out_specs=(anywhere,) * (5 + batches) + (vmem(),),
        scratch_shapes=[
            pltpu.VMEM((slots, batches, rows, model), bf16),
            pltpu.VMEM((lines, batches, more, model), bf16),
            pltpu.VMEM((2, batches, rows, width), f32),
            pltpu.VMEM((2, batches, rows, 128), f32),
            pair, pair, pair, pair, pair, sems((lines,)), sems((lines,)), sems((lines,)),
            sems((2,)), sems((slots, batches)), sems((lines,)), sems((2, batches)), sems((2, batches)),
            sems((3, 3)), sems((3, 3)), sems((3,)),
            pltpu.VMEM((gains.shape[0], model), f32), sems((3,)), sems((3,)), sems((1,)),
        ],
        compiler_params=pltpu.CompilerParams(
            collective_id=1, has_side_effects=True, vmem_limit_bytes=40 * 2**20),
        cost_estimate=pl.CostEstimate(flops=10**11, bytes_accessed=4 * 10**7, transcendentals=0),
        name="gather_project",
    )(x, gains, w_out_part, *ffn_parts, *w_inner, w_beta)
    total = slots * rows
    return (gathered.reshape(batches, total, model), outs,
            [wide.reshape(total, width) for wide in projected],
            beta.reshape(batches, total, 128), pair_parts, down_part, gains_all)


def scatter_kernel(w_refs, g_refs, gb_refs, o_refs, inner_ref, wb_ref, small_ref, gains_ref, pair_ref, down_ref,
                   out_ref, small_out, outs_ref, inner_out, pair_out, down_out,
                   gs, bs, ysend, yrecv, from_left, from_right, part_sum, part_left, part_right, outs_s, inner_s, inner_r, small_s, small_r, gains_r,
                   pair_send, pair_recv, right_send, left_send, right_recv, left_recv, g_sem,
                   sum_send, sum_recv, outs_send, outs_recv, gain_send, gain_recv, part_sems, swap_send, swap_recv, swap_own, sum_sem):
    batches = len(g_refs)
    rows, width = gs.shape[2:]
    lines = yrecv.shape[0]
    model = yrecv.shape[3]
    o = lax.axis_index("z")
    i = lax.axis_index("y")
    core = lax.axis_index("core")
    me = lax.axis_index("x") * 2 + core
    tile = min(512, model)
    diagonal = {"x": 1 - lax.axis_index("x"), "core": 1 - core}
    loads = [
        pltpu.make_async_copy(source, target.at[m], g_sem.at[n, m])
        for n, (sources, target) in enumerate(((g_refs, gs), (gb_refs, bs)))
        for m, source in enumerate(sources)]
    for copy in loads:
        copy.start()
    slots = 2 * lines
    mine = o * 2 + i
    peers = []
    for d in range(1, slots):
        place = lax.rem(mine + d, slots)
        peers.append((place, {"z": place // 2, "y": lax.rem(place, 2)}))
    barrier = pltpu.get_barrier_semaphore()
    greeted = [other("core"), other("x"), diagonal] + [device for _, device in peers]
    for device in greeted:
        pl.semaphore_signal(barrier, inc=1, device_id=device, device_id_type=pl.DeviceIdType.MESH)
    pl.semaphore_wait(barrier, len(greeted))
    gain_copies = [
        line_copy(gains_ref.at[place], gains_r.at[mine], gain_send.at[d], gain_recv.at[d], device)
        for d, (place, device) in enumerate(peers)
    ]
    for copy in gain_copies:
        copy.start()

    inner_pair = line_copy(inner_ref.at[1 - core], inner_r.at[0], sum_send.at[0], sum_recv.at[0], other("core"))
    inner_across = line_copy(inner_s, inner_r.at[1], sum_send.at[1], sum_recv.at[1], other("x"))
    inner_back = line_copy(inner_s, inner_out.at[core], sum_send.at[2], sum_recv.at[2], other("core"))
    small_pair = line_copy(small_s.at[0], small_r.at[0], sum_send.at[3], sum_recv.at[3], other("core"))
    small_across = line_copy(small_s.at[1], small_r.at[1], sum_send.at[4], sum_recv.at[4], other("x"))
    inner_own = pltpu.make_async_copy(inner_ref.at[core], inner_s, sum_sem.at[0])
    inner_keep = pltpu.make_async_copy(inner_s, inner_out.at[core], sum_sem.at[1])
    outs_keep = pltpu.make_async_copy(outs_s, outs_ref.at[me], sum_sem.at[2])
    outs_away = [
        line_copy(outs_s, outs_ref.at[me], outs_send.at[n], outs_recv.at[n], target)
        for n, target in enumerate((other("core"), other("x"), diagonal))
    ]
    swap = Swap(
        [(pair_ref, lambda place: pair_out.at[place]), (down_ref, lambda place: down_out.at[place])],
        swap_send, swap_recv, swap_own)
    swap.start()
    inner_pair.start()
    inner_own.start()
    for copy in loads:
        copy.wait()

    def add_into(target, other_ref):
        height = target.shape[0]
        step = next(size for size in range(min(128, height), 0, -16) if height % size == 0)

        @pl.loop(0, height // step)
        def _(n):
            at = pl.ds(pl.multiple_of(n * step, step), step)
            target[at, :] = (target[at, :].astype(f32) + other_ref[at, :].astype(f32)).astype(target.dtype)

    def target(index):
        far = lines - 1 - index // 2
        side = 1 - 2 * lax.rem(index, 2)
        z = o + side * far
        return far, z, (z >= 0) & (z < lines) & ((far > 0) | (side > 0))

    def partial_rows(z, y, m, store):
        g = gs[m, z * 2 + y]
        b = bs[m, z * 2 + y]
        for start in range(0, model, tile):
            cols = slice(start, start + tile)
            value = lax.dot_general(b, wb_ref[cols, :], NT, preferred_element_type=f32)
            for n, w_ref in enumerate(w_refs):
                part = g[:, n * w_ref.shape[1] : (n + 1) * w_ref.shape[1]]
                value = value + lax.dot_general(part, w_ref[cols, :], NT, preferred_element_type=f32)
            store(cols, value)

    def across(z, m):
        return line_copy(ysend.at[z, m], yrecv.at[z, m], pair_send.at[z, m], pair_recv.at[z, m], other("y"))

    def right(z, m):
        return line_copy(yrecv.at[z, m], from_left.at[z, m], right_send.at[z, m], right_recv.at[z, m], {"z": o + 1})

    def left(z, m):
        return line_copy(yrecv.at[z, m], from_right.at[z, m], left_send.at[z, m], left_recv.at[z, m], {"z": o - 1})

    def across_partial(z, m):
        def store(cols, value):
            ysend[z, m, :, cols] = value.astype(bf16)
        partial_rows(z, 1 - i, m, store)

    def pass_part(z):
        return (line_copy(part_sum.at[z], part_left.at[z], part_sems.at[0, z], part_sems.at[1, z], {"z": o + 1}),
                line_copy(part_sum.at[z], part_right.at[z], part_sems.at[2, z], part_sems.at[3, z], {"z": o - 1}))

    def part_round():
        @pl.loop(0, 2 * lines)
        def _(index):
            far, z, valid = target(index)

            @pl.when(valid & (far > 0))
            def _():
                to_right, to_left = pass_part(z)

                @pl.when((z > o) & (o > 0))
                def _():
                    to_right.wait_recv()
                    add_into(part_sum.at[z], part_left.at[z])

                @pl.when((z < o) & (o < lines - 1))
                def _():
                    to_left.wait_recv()
                    add_into(part_sum.at[z], part_right.at[z])

                @pl.when(z > o)
                def _():
                    to_right.start()

                @pl.when(z < o)
                def _():
                    to_left.start()

        to_right, to_left = pass_part(o)
        outs_s[...] = part_sum[o]

        @pl.when(o > 0)
        def _():
            to_right.wait_recv()
            add_into(outs_s, part_left.at[o])

        @pl.when(o < lines - 1)
        def _():
            to_left.wait_recv()
            add_into(outs_s, part_right.at[o])
        outs_keep.start()
        for copy in outs_away:
            copy.start()

    def side_work():
        left, left_in, right, right_in = o_refs
        column, row = lax.axis_index("y"), lax.axis_index("x")
        wide = model // 2
        for z in range(lines):
            part_sum[z, :, :wide] = (
                left[column, z].astype(f32) + left_in[z].astype(f32)).astype(bf16)
            part_sum[z, :, wide:] = (
                right[row, z].astype(f32) + right_in[z].astype(f32)).astype(bf16)
        part_round()
        inner_own.wait()
        inner_pair.wait_recv()
        add_into(inner_s, inner_r.at[0])
        inner_across.start()
        gains_r[mine] = gains_ref[mine]
        for copy in gain_copies:
            copy.wait_recv()
        tail = small_ref.shape[0]
        small_s[0, :tail] = small_ref[...]
        small_s[0, tail:] = jnp.sum(gains_r[...], axis=0)
        small_pair.start()

    total = 2 * lines * batches

    def turn(index, carry):
        before, earlier = carry
        far, z, valid = target(index // batches)
        m = lax.rem(index, batches)
        last = index >= total
        valid = valid & jnp.logical_not(last)
        moves = valid | last

        @pl.when(valid)
        def _():
            across_partial(z, m)

        @pl.when(valid)
        def _():
            across(z, m).start()

        @pl.when(moves & (before >= 0))
        def _():
            across(before // batches, lax.rem(before, batches)).wait_recv()

        @pl.when(valid & (before < 0))
        def _():
            side_work()

        @pl.when(index == (2 * lines - 2) * batches)
        def _():
            inner_across.wait_recv()
            inner_across.wait_send()
            add_into(inner_s, inner_r.at[1])
            inner_back.start()
            inner_keep.start()
            small_pair.wait_recv()
            small_s[1] = small_s[0] + small_r[0]
            small_across.start()

        @pl.when(moves & (before >= 0))
        def _():
            place, n = before // batches, lax.rem(before, batches)

            def store(cols, value):
                yrecv[place, n, :, cols] = (
                    yrecv[place, n, :, cols].astype(f32) + value).astype(bf16)
            partial_rows(place, i, n, store)

            @pl.when((place > o) & (o == 0))
            def _():
                right(place, n).start()

            @pl.when((place < o) & (o == lines - 1))
            def _():
                left(place, n).start()

        @pl.when(moves & (earlier >= 0))
        def _():
            place, n = earlier // batches, lax.rem(earlier, batches)

            @pl.when((place > o) & (o > 0))
            def _():
                right(place, n).wait_recv()
                add_into(yrecv.at[place, n], from_left.at[place, n])
                right(place, n).start()

            @pl.when((place < o) & (o < lines - 1))
            def _():
                left(place, n).wait_recv()
                add_into(yrecv.at[place, n], from_right.at[place, n])
                left(place, n).start()

        code = jnp.where(valid, z * batches + m, -1)
        return jnp.where(moves, code, before), jnp.where(moves, before, earlier)

    lax.fori_loop(0, total + 2, turn, (jnp.int32(-1), jnp.int32(-1)))


    for m in range(batches):
        out_ref[m] = yrecv[o, m].astype(f32)

        @pl.when(o > 0)
        def _():
            right(o, m).wait_recv()
            out_ref[m] += from_left[o, m].astype(f32)

        @pl.when(o < lines - 1)
        def _():
            left(o, m).wait_recv()
            out_ref[m] += from_right[o, m].astype(f32)

    @pl.loop(0, lines)
    def _(z):
        for m in range(batches):
            across(z, m).wait_send()

            @pl.when(z > o)
            def _():
                right(z, m).wait_send()

            @pl.when(z < o)
            def _():
                left(z, m).wait_send()

        @pl.when(z > o)
        def _():
            pass_part(z)[0].wait_send()

        @pl.when(z < o)
        def _():
            pass_part(z)[1].wait_send()

    small_across.wait_recv()
    small_out[...] = small_s[1] + small_r[1]
    for copy in gain_copies:
        copy.wait_send()
    inner_pair.wait_send()
    small_pair.wait_send()
    small_across.wait_send()
    inner_back.wait_recv()
    inner_back.wait_send()
    inner_keep.wait()
    outs_keep.wait()
    swap.wait()
    for copy in outs_away:
        copy.wait_recv()
        copy.wait_send()


def scatter_call_kernel(*refs):
    scatter_kernel(refs[:4], refs[4:6], refs[6:8], refs[8:12], *refs[12:])


def scatter_rows(grads, beta_grads, out_grads, inner_grads, w_inner, w_beta, small, gains,
                 pair_grads, down_grads):
    batches = len(grads)
    total, width = grads[0].shape
    model = w_inner[0].shape[0]
    lines = lax.axis_size("z")
    slots = 2 * lines
    rows = total // slots
    more = out_grads[1].shape[1]
    sems = pltpu.SemaphoreType.DMA
    anywhere = pl.BlockSpec(memory_space=pl.ANY)
    slab = pltpu.VMEM((lines, batches, rows, model), bf16)
    part = pltpu.VMEM((lines, more, model), bf16)
    half = inner_grads.shape[1:]
    flat = (small.shape[0] + gains.shape[1], 128)
    return pl.pallas_call(
        scatter_call_kernel,
        out_shape=(
            jax.ShapeDtypeStruct((batches, rows, model), f32),
            jax.ShapeDtypeStruct(flat, f32),
            jax.ShapeDtypeStruct((4, more, model), bf16),
            jax.ShapeDtypeStruct(inner_grads.shape, bf16),
            jax.ShapeDtypeStruct(pair_grads.shape, bf16),
            jax.ShapeDtypeStruct(down_grads.shape, bf16),
        ),
        in_specs=[vmem()] * 4 + [anywhere] * 4 + [vmem()] * 4
        + [anywhere, vmem(), vmem(), vmem(), anywhere, anywhere],
        out_specs=(vmem(), vmem()) + (anywhere,) * 4,
        scratch_shapes=[
            pltpu.VMEM((batches, slots, rows, width), bf16),
            pltpu.VMEM((batches, slots, rows, 128), bf16),
            slab, slab, slab, slab, part, part, part,
            pltpu.VMEM((more, model), bf16),
            pltpu.VMEM(half, bf16),
            pltpu.VMEM((2, *half), bf16),
            pltpu.VMEM((2, *flat), f32),
            pltpu.VMEM((2, *flat), f32),
            pltpu.VMEM(gains.shape, f32),
            sems((lines, batches)), sems((lines, batches)), sems((lines, batches)),
            sems((lines, batches)), sems((lines, batches)), sems((lines, batches)),
            sems((2, batches)), sems((5,)), sems((5,)), sems((3,)), sems((3,)), sems((slots,)), sems((slots,)), sems((4, lines)),
            sems((2, 3)), sems((2, 3)), sems((2,)), sems((3,)),
        ],
        compiler_params=pltpu.CompilerParams(
            collective_id=3, has_side_effects=True, vmem_limit_bytes=58 * 2**20),
        cost_estimate=pl.CostEstimate(flops=7 * 10**10, bytes_accessed=4 * 10**7, transcendentals=0),
        name="scatter_rows",
    )(*w_inner, *[grad.reshape(slots, rows, width) for grad in grads],
      *[grad.reshape(slots, rows, 128) for grad in beta_grads], *out_grads,
      inner_grads, w_beta, small, gains,
      pair_grads, down_grads)


def tensor_peers(slots):
    mine = lax.axis_index("z") * 2 + lax.axis_index("y")
    places = [lax.rem(mine + d, slots) for d in range(1, slots)]
    return mine, [(place, {"z": place // 2, "y": lax.rem(place, 2)}) for place in places]


def greet(devices):
    barrier = pltpu.get_barrier_semaphore()
    for device in devices:
        pl.semaphore_signal(barrier, inc=1, device_id=device, device_id_type=pl.DeviceIdType.MESH)
    pl.semaphore_wait(barrier, len(devices))


def attend_kernel(x_ref, low_first, low_second, gain_ref, *refs):
    pieces, refs = refs[:8], refs[8:]
    hidden_ref, normed_ref, w_ref, heads_ref, ws, heads, send, recv, sem, own_sem = refs
    slots = heads.shape[1]
    mine, peers = tensor_peers(slots)
    greet([device for _, device in peers])
    lows = (low_first, low_second)
    away = [
        line_copy(low.at[place], heads.at[m, mine], send.at[m, d], recv.at[m, d], device)
        for d, (place, device) in enumerate(peers) for m, low in enumerate(lows)
    ]
    for copy in away:
        copy.start()
    own = [pltpu.make_async_copy(low.at[mine], heads.at[m, mine], own_sem.at[m]) for m, low in enumerate(lows)]
    for copy in own:
        copy.start()
    x = lax.axis_index("x")
    core = lax.axis_index("core")
    y = lax.axis_index("y")
    copies = []
    for n, piece in enumerate(pieces):
        far_y, far_x, far_core = n // 4, n // 2 % 2, n % 2
        column = 1 - y if far_y else y
        quarter = (1 - x if far_x else x) * 2 + (1 - core if far_core else core)
        copies.append(pltpu.make_async_copy(piece, ws.at[:, column, quarter], sem.at[n]))
    for copy in copies:
        copy.start()
    for copy in copies + own:
        copy.wait()
    keep = pltpu.make_async_copy(ws, w_ref, own_sem.at[2])
    keep.start()
    for copy in away:
        copy.wait_recv()
    keep_heads = pltpu.make_async_copy(heads, heads_ref, own_sem.at[3])
    keep_heads.start()
    model = x_ref.shape[1]
    tile = min(512, model)
    width = heads.shape[3]
    squares = 0.0
    for start in range(0, model, tile):
        cols = slice(start, start + tile)
        total = x_ref[:, cols].astype(f32)
        for t in range(slots):
            left = jnp.concatenate([heads[0, t], heads[1, t]], axis=0)
            total = total + jnp.dot(
                left, ws[t // 2, t % 2, :, :, cols].reshape(width, tile), preferred_element_type=f32)
        hidden_ref[:, cols] = total
        squares = squares + jnp.sum(total * total, axis=-1, keepdims=True)
    scale = lax.rsqrt(squares / model + epsilon)
    for start in range(0, model, tile):
        cols = slice(start, start + tile)
        normed_ref[:, cols] = (hidden_ref[:, cols] * scale * gain_ref[:, cols]).astype(bf16)
    keep.wait()
    keep_heads.wait()
    for copy in away:
        copy.wait_send()


def attend(x, lows, gain, pieces):
    rows, model = x.shape
    lines, part, _ = pieces[0].shape
    full = (lines, 2, 4, part, model)
    heads = (2, *lows[0].shape)
    slots = 2 * lines
    anywhere = pl.BlockSpec(memory_space=pl.ANY)
    sems = pltpu.SemaphoreType.DMA
    return pl.pallas_call(
        attend_kernel,
        out_shape=(
            jax.ShapeDtypeStruct((rows, model), f32),
            jax.ShapeDtypeStruct((rows, model), bf16),
            jax.ShapeDtypeStruct(full, bf16),
            jax.ShapeDtypeStruct(heads, bf16),
        ),
        in_specs=[vmem(), anywhere, anywhere, vmem()] + [anywhere] * 8,
        out_specs=(vmem(), vmem(), anywhere, anywhere),
        scratch_shapes=[
            pltpu.VMEM(full, bf16), pltpu.VMEM(heads, bf16),
            sems((2, slots)), sems((2, slots)), sems((8,)), sems((4,))],
        compiler_params=pltpu.CompilerParams(
            collective_id=4, has_side_effects=True, vmem_limit_bytes=32 * 2**20),
        cost_estimate=pl.CostEstimate(flops=3 * 10**10, bytes_accessed=2 * 10**7, transcendentals=0),
        name="attend",
    )(x, *lows, gain, *pieces)


def attend_back_kernel(hidden_ref, ffn_ref, grad_ref, c_ref, gain_ref, w_ref, heads,
                       result_ref, hgrad_ref, back_first, back_second, left_mine, left_theirs,
                       right_mine, right_theirs, gain_out, low, wgrad, wrecv, backs, send, recv, sem, core_sem):
    rows, model = hidden_ref.shape
    half = rows // 2
    tile = min(512, model)
    slots = heads.shape[1]
    width = heads.shape[3]
    mine, peers = tensor_peers(slots)
    greet([device for _, device in peers] + [other("core")])
    squares, dots = 0.0, 0.0
    for start in range(0, model, tile):
        cols = slice(start, start + tile)
        hidden = hidden_ref[:, cols]
        squares = squares + jnp.sum(hidden * hidden, axis=-1, keepdims=True)
        dots = dots + jnp.sum(hidden * grad_ref[:, cols] * gain_ref[:, cols], axis=-1, keepdims=True)
    scale = lax.rsqrt(squares / model + epsilon)
    pull = scale * scale * scale * (dots / model)
    for start in range(0, model, tile):
        cols = slice(start, start + tile)
        hidden = hidden_ref[:, cols]
        grad = grad_ref[:, cols]
        result_ref[:, cols] = hidden + ffn_ref[:, cols]
        gain_out[:, cols] = jnp.sum(grad * hidden * scale, axis=0, keepdims=True)
        hgrad = c_ref[:, cols].astype(f32) + scale * (grad * gain_ref[:, cols]) - hidden * pull
        hgrad_ref[:, cols] = hgrad
        low[:, cols] = hgrad.astype(bf16)

    outs = (back_first, back_second)

    def away(m, d):
        place = lax.rem(mine + d, slots)
        return line_copy(backs.at[m, d], outs[m].at[mine], send.at[m, d], recv.at[m, d],
                         {"z": place // 2, "y": lax.rem(place, 2)})

    @pl.loop(0, slots)
    def _(step):
        d = slots - 1 - step
        place = lax.rem(mine + d, slots)
        back = lax.dot_general(
            low[...], w_ref[place // 2, lax.rem(place, 2)].reshape(width, model), NT,
            preferred_element_type=f32)
        for m in range(2):
            backs[m, d] = back[m * half : (m + 1) * half].astype(bf16)

            @pl.when(d > 0)
            def _():
                away(m, d).start()

            @pl.when(d == 0)
            def _():
                pltpu.make_async_copy(backs.at[m, 0], outs[m].at[mine], sem.at[2 + m]).start()

    for t in range(slots):
        left = jnp.concatenate([heads[0, t], heads[1, t]], axis=0)
        for start in range(0, model, tile):
            cols = slice(start, start + tile)
            value = lax.dot_general(
                left, low[:, cols], (((0,), (0,)), ((), ())), preferred_element_type=f32
            ).astype(bf16).reshape(2, 2, width // 4, tile)
            for c in range(2):
                wgrad[c, :, t % 2, t // 2, :, cols] = value[:, c]
    core = lax.axis_index("core")
    to_pair = line_copy(wgrad.at[1 - core], wrecv, core_sem.at[0], core_sem.at[1], other("core"))
    to_pair.start()
    to_pair.wait_recv()
    lines = wgrad.shape[3]
    for far_x in range(2):
        for far_y in range(2):
            @pl.loop(0, lines)
            def _(z):
                wrecv[far_x, far_y, z] = (
                    wrecv[far_x, far_y, z].astype(f32) + wgrad[core, far_x, far_y, z].astype(f32)
                ).astype(bf16)
    x, y = lax.axis_index("x"), lax.axis_index("y")
    wide = model // 2
    keeps = [
        pltpu.make_async_copy(source.at[..., pl.ds(start, wide)], target, sem.at[4 + n])
        for n, (source, start, target) in enumerate((
            (wrecv.at[x], 0, left_mine), (wrecv.at[1 - x], 0, left_theirs),
            (wrecv.at[:, y], wide, right_mine), (wrecv.at[:, 1 - y], wide, right_theirs)))
    ]
    for copy in keeps:
        copy.start()
    for copy in keeps:
        copy.wait()
    to_pair.wait_send()
    for m in range(2):
        pltpu.make_async_copy(backs.at[m, 0], outs[m].at[mine], sem.at[2 + m]).wait()
        for d in range(1, slots):
            away(m, d).wait_recv()
            away(m, d).wait_send()


def attend_back(hidden, ffn_out, normed_grad, c_rows, gain, w_full, heads):
    rows, model = hidden.shape
    wide = jax.ShapeDtypeStruct((rows, model), f32)
    lines, _, _, part, _ = w_full.shape
    share = (2, 2, lines, part, model)
    slots = 2 * lines
    back = jax.ShapeDtypeStruct(heads.shape[1:], bf16)
    anywhere = pl.BlockSpec(memory_space=pl.ANY)
    sems = pltpu.SemaphoreType.DMA
    return pl.pallas_call(
        attend_back_kernel,
        out_shape=(
            wide, wide, back, back,
            *[jax.ShapeDtypeStruct((2, lines, part, model // 2), bf16)] * 4,
            jax.ShapeDtypeStruct((1, model), f32),
        ),
        in_specs=[vmem()] * 7,
        out_specs=(vmem(),) * 2 + (anywhere,) * 6 + (vmem(),),
        scratch_shapes=[
            pltpu.VMEM((rows, model), bf16), pltpu.VMEM((2, *share), bf16), pltpu.VMEM(share, bf16),
            pltpu.VMEM(heads.shape, bf16), sems((2, slots)), sems((2, slots)), sems((8,)), sems((2,))],
        compiler_params=pltpu.CompilerParams(
            collective_id=5, has_side_effects=True, vmem_limit_bytes=48 * 2**20),
        cost_estimate=pl.CostEstimate(flops=3 * 10**10, bytes_accessed=4 * 10**7, transcendentals=0),
        name="attend_back",
    )(hidden, ffn_out, normed_grad, c_rows, gain, w_full, heads)


def inner_grads_kernel(x_ref, g_first, g_second, b_first, b_second, w0, w1, w2, w3, wb_ref,
                       low_ref, beta_ref, gain_ref):
    dims = (((0,), (0,)), ((), ()))
    beta = 0.0
    for m, b_ref in enumerate((b_first, b_second)):
        beta = beta + lax.dot_general(x_ref[m], b_ref[...], dims, preferred_element_type=f32)
    beta_ref[...] = beta
    gain = jnp.sum(beta * wb_ref[...].astype(f32), axis=1, keepdims=True)
    for n, w_ref in enumerate((w0, w1, w2, w3)):
        width = w_ref.shape[1]
        cols = slice(n * width, (n + 1) * width)
        value = 0.0
        for m, g_ref in enumerate((g_first, g_second)):
            value = value + lax.dot_general(x_ref[m], g_ref[:, cols], dims, preferred_element_type=f32)
        low_ref[:, cols] = value.astype(bf16)
        gain = gain + jnp.sum(value * w_ref[...].astype(f32), axis=1, keepdims=True)
    gain_ref[...] = jnp.broadcast_to(gain, gain_ref.shape)


def inner_grads(tokens, grads, beta_grads, w_inner, w_beta):
    _, total, model = tokens.shape
    wide = grads[0].shape[1]
    width = w_inner[0].shape[1]
    tile = 256

    def whole(columns):
        return pl.BlockSpec((total, columns), lambda n: (0, 0))

    def rows(columns):
        return pl.BlockSpec((tile, columns), lambda n: (n, 0))

    return pl.pallas_call(
        inner_grads_kernel,
        out_shape=(
            jax.ShapeDtypeStruct((model, wide), bf16),
            jax.ShapeDtypeStruct((model, 128), f32),
            jax.ShapeDtypeStruct((model, 128), f32),
        ),
        grid=(model // tile,),
        in_specs=[pl.BlockSpec((2, total, tile), lambda n: (0, 0, n))]
        + [whole(wide)] * 2 + [whole(128)] * 2 + [rows(width)] * 4 + [rows(128)],
        out_specs=(rows(wide), rows(128), rows(128)),
        compiler_params=pltpu.CompilerParams(vmem_limit_bytes=40 * 2**20),
        cost_estimate=pl.CostEstimate(flops=10**10, bytes_accessed=2 * 10**7, transcendentals=0),
        name="inner_grads",
    )(tokens, *grads, *beta_grads, *w_inner, w_beta)


def root_scale(row_values, gain_vector):
    row_scale = lax.rsqrt(jnp.mean(row_values * row_values, axis=-1, keepdims=True) + epsilon)
    return (row_values * row_scale * gain_vector, row_scale)


def norm_backward(row_values, row_scale, gain_vector, normed_grad):
    weighted = normed_grad * gain_vector
    rows_grad = row_scale * weighted - row_values * row_scale * row_scale * row_scale * jnp.mean(
        weighted * row_values, axis=-1, keepdims=True
    )
    gain_grad = jnp.sum(normed_grad * row_values * row_scale, axis=tuple(range(row_values.ndim - 1)))
    return (rows_grad, gain_grad)


DP = ("x", "core")
TP = ("z", "y")


def gather(x, axis_name, axis=0):
    return lax.all_gather(x, axis_name, axis=axis, tiled=True)


def scatter_sum(x, axis_name, axis=0):
    return lax.psum_scatter(
        x.astype(bf16), axis_name, scatter_dimension=axis, tiled=True
    ).astype(f32)


def dot(a, b):
    return jnp.dot(a, b, preferred_element_type=f32)


def dot_nt(a, b):
    return jnp.einsum("tk,nk->tn", a, b, preferred_element_type=f32)


def dot_tn(a, b):
    return jnp.einsum("tm,tn->mn", a, b, preferred_element_type=f32)


def exchange(x, axis_name, distance=1):
    size = lax.axis_size(axis_name)
    return lax.ppermute(x, axis_name, [(i, i ^ distance) for i in range(size)])


def pick(x, index, axis):
    return lax.dynamic_index_in_dim(x, index, axis, keepdims=False)


def after(x, *others):
    return lax.optimization_barrier((x, *others))[0]


def add_low(x, y):
    return (x.astype(f32) + y.astype(f32)).astype(bf16)


def halve_sum(grad, axis_name):
    me = lax.axis_index(axis_name)
    return add_low(pick(grad, me, 0), exchange(pick(grad, 1 - me, 0), axis_name))


def feed_forward_groups(normed, cotangents, w_gate, w_up, w_down):
    gate_full = gather(w_gate, DP)
    up_full = gather(w_up, DP)
    down_full = gather(w_down, DP, 1)
    outs, normed_grads, inner_rows, gate_grads, up_grads, rows, grad_rows = [], [], [], [], [], [], []
    for m in range(normed.shape[0]):
        rows.append(gather(normed[m], TP))
        grad_rows.append(gather(cotangents[m], TP))
        gate_values = dot(rows[m], gate_full)
        up_values = dot(rows[m], up_full)
        sigmoid_gate = jax.nn.sigmoid(gate_values)
        silu_gate = gate_values * sigmoid_gate
        inner = (silu_gate * up_values).astype(bf16)
        inner_grad = dot_nt(grad_rows[m], down_full)
        gate_grad = (
            inner_grad * up_values * sigmoid_gate * (1.0 + gate_values * (1.0 - sigmoid_gate))
        ).astype(bf16)
        up_grad = (inner_grad * silu_gate).astype(bf16)
        normed_grads.append(scatter_sum(dot_nt(gate_grad, gate_full) + dot_nt(up_grad, up_full), TP))
        outs.append(scatter_sum(dot(inner, down_full), TP))
        inner_rows.append(inner)
        gate_grads.append(gate_grad)
        up_grads.append(up_grad)
    grad_all = jnp.concatenate(grad_rows)
    rows_all = jnp.concatenate(rows)
    gate_share = scatter_sum(dot_tn(rows_all, jnp.concatenate(gate_grads)), DP)
    up_share = scatter_sum(dot_tn(rows_all, jnp.concatenate(up_grads)), DP)
    down_share = scatter_sum(dot_tn(jnp.concatenate(inner_rows), grad_all), DP, 1)
    return jnp.stack(outs), jnp.stack(normed_grads), (gate_share, up_share, down_share)


def per_device(
    inputs,
    lengths,
    norm_gain,
    ffn_gain,
    w_query,
    w_key,
    w_value,
    w_gate_out,
    w_beta,
    conv_weight,
    head_gain,
    w_out,
    w_gate,
    w_up,
    w_down,
    cotangent,
):
    batches = range(inputs.shape[0])
    local_width = w_query.shape[1]
    heads = w_beta.shape[1]
    devices = lax.axis_size(TP)
    planar = all(lax.axis_size(name) == 2 for name in ("x", "core", "y"))
    w_parts = (w_query, w_key, w_value, w_gate_out)
    w_inner = jnp.concatenate(w_parts, axis=1)
    w_beta_wide = jnp.pad(w_beta, ((0, 0), (0, 128 - heads)))
    taps = conv_weight.astype(f32).reshape(-1, local_width)
    gain_heads = head_gain.astype(f32)
    gains = jnp.stack([norm_gain, ffn_gain])
    rows_in = inputs.astype(f32)

    def run_mixer(m, wide, logits):
        low, *kept = mixer_forward(lengths[m, 0], wide, logits, taps, gain_heads, exact=False)
        return low, kept

    def back_mixer(m, wide, logits, grad, kept):
        return mixer_backward(
            lengths[m, 0], wide, logits, taps, gain_heads, grad, kept, exact=False)

    if planar:
        count = rows_in.shape[0] * rows_in.shape[1]
        model = rows_in.shape[2]
        ranks = lax.axis_size(DP)
        ffn_parts = [
            w.reshape(ranks, -1, w.shape[1]) for w in (w_gate.T, w_up.T, w_down)]
        c_rows = [None] * 8
        c_rows[0] = cotangent.reshape(count, model)
        c_rows[4] = exchange(c_rows[0], "core")
        out_shares = pick(
            w_out.reshape(lax.axis_size(DP), len(batches), -1, model), lax.axis_index(DP), 0)
        gains = jnp.pad(gains.astype(f32), ((0, 6), (0, 0)))
        gathered_one, out_own, projected, beta_logits, own_weights, own_down, gains = gather_project(
            inputs, gains, out_shares, ffn_parts, w_parts, w_beta_wide)
        gain_one, gain_two = gains[0], gains[1]
        _, scale_one = root_scale(rows_in, gain_one)
        early = after(c_rows[0], gathered_one)
        c_rows[1] = exchange(early, "x")
        weights = gather(own_weights[None], "z")
        c_rows[2] = exchange(early, "y")
        out_own = out_own.reshape(out_own.shape[0], -1, model)
        out_y = exchange(out_own, "y")
        out_x = exchange(out_own, "x")
    else:
        gains = gather(gains, DP, 1).astype(f32)
        gain_one, gain_two = gains[0], gains[1]
        normed_one, scale_one = root_scale(rows_in, gain_one)
        normed_one = normed_one.astype(bf16)
        gathered_one = jnp.stack([gather(normed_one[m], TP) for m in batches])
        projected = [dot(gathered_one[m], w_inner) for m in batches]
        beta_logits = [dot(gathered_one[m], w_beta_wide) for m in batches]
        out_full = gather(w_out, TP)
    token_heads, saved = [], []
    for m in batches:
        low, kept = run_mixer(m, projected[m], beta_logits[m])
        saved.append(kept)
        if planar and m == 0:
            out_y, c_rows[1], c_rows[2] = after((out_y, c_rows[1], c_rows[2]), low)
            out_xy = exchange(out_y, "x")
            c_rows[3] = exchange(c_rows[1], "y")
            c_rows[5] = exchange(c_rows[1], "core")
            c_rows[6] = exchange(c_rows[2], "core")
            projected[1] = after(projected[1], out_y, c_rows[2])
        low = low.reshape(devices, -1, local_width)
        if not planar:
            low = lax.all_to_all(low, TP, split_axis=0, concat_axis=0, tiled=True)
        token_heads.append(low)
    if planar:
        out_x, out_xy, c_rows[3] = after((out_x, out_xy, c_rows[3]), low)
        out_pieces = []
        for piece in (out_own, out_x, out_y, out_xy):
            out_pieces += [piece, exchange(piece, "core")]
        c_rows[7] = exchange(c_rows[3], "core")
        hidden, normed_two, out_full, token_heads = attend(
            inputs.reshape(count, model), token_heads, gain_two[None], out_pieces)
        ffn_out, normed_grad, weight_grads, down_grad = ffn_plane(normed_two, weights, own_down, c_rows)
        result_rows, hidden_grad, *mixed_grads, left, left_away, right, right_away, gain_two_sum = attend_back(
            hidden, ffn_out, normed_grad, c_rows[0], gain_two[None], out_full, token_heads)
        weight_grads = after(weight_grads, left)
        own_grads = lax.psum_scatter(weight_grads, "z", scatter_dimension=0, tiled=True)
        gain_two_sum = gain_two_sum[0]
        result_rows = result_rows.reshape(rows_in.shape)
        hidden_grad = hidden_grad.reshape(rows_in.shape)
    else:
        heads_rows = [
            block.swapaxes(0, 1).reshape(-1, devices * local_width) for block in token_heads]
        hidden = rows_in + jnp.stack([dot(rows, out_full) for rows in heads_rows])
        normed_two, scale_two = root_scale(hidden, gain_two)
        ffn_out, normed_grad, (gate_share, up_share, down_share) = feed_forward_groups(
            normed_two.astype(bf16), cotangent, w_gate, w_up, w_down)
        result_rows = hidden + ffn_out
        norm_grad, gain_two_sum = norm_backward(hidden, scale_two, gain_two, normed_grad)
        hidden_grad = cotangent.astype(f32) + norm_grad
        attended_low = hidden_grad.astype(bf16)
        mixed_grads = [
            dot_nt(attended_low[m], out_full).astype(bf16)
            .reshape(-1, devices, local_width).swapaxes(0, 1) for m in batches]
        out_grad = dot_tn(
            jnp.concatenate(heads_rows), jnp.concatenate(list(attended_low))).astype(bf16)
    if not planar:
        mixed_grads = [
            lax.all_to_all(grad, TP, split_axis=0, concat_axis=0, tiled=True)
            for grad in mixed_grads]
    mixed_grads = [grad.reshape(-1, local_width) for grad in mixed_grads]
    if planar:
        left = add_low(left, exchange(left_away, "x"))
        right = add_low(right, exchange(right_away, "y"))
    projected_low, beta_low = [], []
    taps_sum, heads_sum = 0.0, 0.0
    for m in batches:
        if planar and m > 0:
            mixed_grads[m] = after(mixed_grads[m], left, right)
        projected_grad, beta_grad, taps_part, heads_part = back_mixer(
            m, projected[m], beta_logits[m], mixed_grads[m], saved[m])
        taps_sum = taps_sum + taps_part
        heads_sum = heads_sum + heads_part
        projected_low.append(projected_grad)
        beta_low.append(beta_grad)
    if planar:
        left_in = exchange(pick(left, 1 - lax.axis_index("y"), 0), "y")
        right_in = exchange(pick(right, 1 - lax.axis_index("x"), 0), "x")
        low_sum, beta_sum, gain_rows = inner_grads(
            gathered_one, projected_low, beta_low, w_parts, w_beta_wide)
        beta_sum = beta_sum[:, :heads]
        gain_one_sum = gain_rows[:, 0] / gain_one
    else:
        tokens = gathered_one.reshape(-1, gathered_one.shape[2])
        inner_sum = dot_tn(tokens, jnp.concatenate(projected_low))
        beta_sum = dot_tn(tokens, jnp.concatenate(beta_low)[:, :heads])
        gain_one_sum = (
            jnp.sum(inner_sum * w_inner.astype(f32), axis=1)
            + jnp.sum(beta_sum * w_beta.astype(f32), axis=1)
        ) / gain_one
        low_sum = inner_sum.astype(bf16)
    gain_parts = jnp.stack([gain_one_sum, gain_two_sum])
    sums = [part.reshape(-1, 128) for part in (beta_sum.T, taps_sum, heads_sum)]
    marks = [sums[0].shape[0], sums[0].shape[0] + sums[1].shape[0], sum(part.shape[0] for part in sums)]
    small = jnp.concatenate(sums)
    if planar:
        ranks = lax.axis_size(DP)
        gain_parts = gain_parts.reshape(2, ranks, devices, -1).transpose(2, 0, 1, 3)
        chunk = gain_parts.shape[3]
        gain_parts = gain_parts.reshape(devices, -1, 128)
        gain_rows = gain_parts.shape[1]
        gain_parts = jnp.pad(gain_parts, ((0, 0), (0, -gain_rows % 8), (0, 0)))
        small = jnp.pad(small, ((0, -small.shape[0] % 8), (0, 0)))
        input_norm, flat, out_total, inner_total, pair_grads, down_grads = scatter_rows(
            projected_low, beta_low, (left, left_in, right, right_in),
            low_sum.reshape(2, -1, low_sum.shape[1]), w_parts, w_beta_wide, small, gain_parts,
            own_grads[0], down_grad)
        gate_share, up_share = (
            pair_grads[:, kind].reshape(-1, pair_grads.shape[3]).astype(f32).T for kind in range(2))
        down_share = down_grads.reshape(w_down.shape).astype(f32)
        gain_totals = pick(
            flat[small.shape[0] :][:gain_rows].reshape(2, ranks, chunk), lax.axis_index(DP), 1)
        small = flat[: small.shape[0]]
        out_total = out_total.reshape(w_out.shape).astype(f32)
        inner_total = inner_total.reshape(low_sum.shape)
    else:
        gain_totals = lax.psum_scatter(gain_parts, DP + TP, scatter_dimension=1, tiled=True)
        inner_total = lax.psum(low_sum, DP)
        small = lax.psum(small, DP)
        out_grad = lax.psum_scatter(out_grad, TP, scatter_dimension=0, tiled=True)
        out_total = lax.psum(out_grad, DP).astype(f32)
        input_norm = jnp.stack([
            scatter_sum(
                dot_nt(projected_low[m], w_inner) + dot_nt(beta_low[m], w_beta_wide), TP)
            for m in batches])
    norm_grad, _ = norm_backward(rows_in, scale_one, gain_one, input_norm)
    beta_total = small[: marks[0]].reshape(heads, -1).T
    conv_total = small[marks[0] : marks[1]].reshape(conv_weight.shape)
    heads_total = small[marks[1] : marks[2]].reshape(head_gain.shape)
    columns = [
        inner_total[:, n * local_width : (n + 1) * local_width].astype(f32) for n in range(4)]
    return (
        result_rows,
        hidden_grad + norm_grad,
        gain_totals[0],
        gain_totals[1],
        *columns,
        beta_total,
        conv_total,
        heads_total,
        out_total,
        gate_share,
        up_share,
        down_share,
    )


def solution(mesh):
    dp, tensor = mesh.shape["dp"], mesh.shape["tensor"]
    inner = 2 if tensor == 8 else 4
    axes = ("x", "core", "z", "y")
    fine = jax.sharding.Mesh(
        mesh.devices.reshape(dp // 2, 2, tensor // inner, inner), axes)
    tokens = P(None, DP + TP, None)
    in_specs = (
        tokens,
        P(None, DP, None),
        P(DP),
        P(DP),
        P(None, TP),
        P(None, TP),
        P(None, TP),
        P(None, TP),
        P(None, TP),
        P(None, None, TP),
        P(TP, None),
        P(TP, None),
        P(DP, TP),
        P(DP, TP),
        P(TP, DP),
        tokens,
    )
    out_specs = (
        tokens,
        tokens,
        P(DP + TP),
        P(DP + TP),
        P(None, TP),
        P(None, TP),
        P(None, TP),
        P(None, TP),
        P(None, TP),
        P(None, None, TP),
        P(TP, None),
        P(TP, None),
        P(DP, TP),
        P(DP, TP),
        P(TP, DP),
    )
    return jax.shard_map(
        per_device, mesh=fine, in_specs=in_specs, out_specs=out_specs, check_vma=False
    )
```

```python
from functools import partial

import jax
import jax.numpy as jnp
from jax import lax
from jax.experimental import pallas as pl
from jax.experimental.pallas import tpu as pltpu
from jax.sharding import PartitionSpec as P


CHUNK = 128
HALO = 8
epsilon = 1e-06
highest = lax.Precision.HIGHEST
f32 = jnp.float32
bf16 = jnp.bfloat16


def product(left, right, left_dim, right_dim, exact=False):
    dims = (((left_dim,), (right_dim,)), ((), ()))
    if exact:
        return lax.dot_general(left, right, dims, precision=highest, preferred_element_type=f32)
    return lax.dot_general(
        left.astype(bf16), right.astype(bf16), dims, preferred_element_type=f32
    )


def sigmoid(x):
    return 1.0 / (1.0 + jnp.exp(-x))


def segment_tools(lengths_ref):
    ends = []
    total = 0
    for i in range(lengths_ref.shape[0] - 1):
        total = total + lengths_ref[i]
        ends.append(total)

    def segment_of(pos):
        result = 0
        for end in ends:
            result = result + (pos >= end).astype(jnp.int32)
        return result

    return segment_of, len(ends)


def chunk_masks(segment_of, base, chunk):
    col = base + lax.broadcasted_iota(jnp.int32, (chunk, 1), 0)
    row = base + lax.broadcasted_iota(jnp.int32, (1, chunk), 1)
    seg_col = segment_of(col)
    seg_row = segment_of(row)
    first = segment_of(base - 1)
    last = segment_of(base + chunk - 1)
    same = seg_col == seg_row
    strict = (same & (col > row)).astype(f32)
    within = (same & (col >= row)).astype(f32)
    has_past = base > 0
    carry = ((seg_col == first) & has_past).astype(f32)
    close = (seg_col == last).astype(f32)
    keep = ((first == last) & has_past).astype(f32)
    return strict, within, carry, close, keep


def level_masks(chunk):
    row = lax.broadcasted_iota(jnp.int32, (chunk, chunk), 0)
    col = lax.broadcasted_iota(jnp.int32, (chunk, chunk), 1)
    masks = []
    width = 1
    while width < chunk:
        mask = (
            (row // (2 * width) == col // (2 * width))
            & ((row // width) % 2 == 1)
            & ((col // width) % 2 == 0)
        )
        masks.append(mask)
        width *= 2
    return masks, (row == col).astype(f32)


def conv_part(proj_ref, tap_ref, segment_of, base, part, width, chunk):
    taps = tap_ref.shape[0] // 3
    cols = pl.ds(part * width, width)
    main = proj_ref[pl.ds(base, chunk), cols]
    prev = proj_ref[pl.ds(pl.multiple_of(jnp.maximum(base - HALO, 0), HALO), HALO), cols]
    full = jnp.concatenate([prev, main], axis=0)
    col = base + lax.broadcasted_iota(jnp.int32, (chunk, 1), 0)
    seg = segment_of(col)
    total = main * tap_ref[part * taps : part * taps + 1, :]
    shifted = [main]
    for s in range(1, taps):
        valid = (segment_of(col - s) == seg) & (col >= s)
        moved = jnp.where(valid, pltpu.roll(full, s, 0)[HALO:], 0.0)
        shifted.append(moved)
        total = total + moved * tap_ref[part * taps + s : part * taps + s + 1, :]
    return total, shifted


def heads_of(x, heads):
    return [x[:, h * 128 : (h + 1) * 128] for h in range(heads)]


def unit_rows(a, scale):
    r = lax.rsqrt(jnp.sum(a * a, axis=-1, keepdims=True) + epsilon)
    return a * (r * scale)


def mixer_forward_kernel(exact, group, lengths_ref, proj_ref, beta_ref, tap_ref, gain_ref,
                         mixed_ref, heads_ref, fixed_ref, delta_ref, state_ref, inverse_ref,
                         query_s, key_s, value_s, score_s):
    rows_all = proj_ref.shape[0]
    width = proj_ref.shape[1] // 4
    heads = width // 128
    chunk = CHUNK
    count = rows_all // chunk
    segment_of, segments = segment_tools(lengths_ref)

    @pl.loop(0, count)
    def _(c):
        base = pl.multiple_of(c * chunk, chunk)
        rows = pl.ds(base, chunk)
        for part, target in enumerate((query_s, key_s, value_s)):
            pre, _ = conv_part(proj_ref, tap_ref, segment_of, base, part, width, chunk)
            act = pre * sigmoid(pre)
            if part == 2:
                target[rows, :] = act
            else:
                scale = 128 ** (-0.5) if part == 0 else 1.0
                for h, a in enumerate(heads_of(act, heads)):
                    target[rows, h * 128 : (h + 1) * 128] = unit_rows(a, scale)

    def beta_of(base, h):
        pos = base + lax.broadcasted_iota(jnp.int32, (chunk, 1), 0)
        live = (segment_of(pos) < segments).astype(f32)
        return sigmoid(beta_ref[pl.ds(base, chunk), h : h + 1]) * live

    masks, eye = level_masks(chunk)

    @pl.loop(0, count // group)
    def _(g):
        lowers, places = [], []
        for i in range(group):
            c = g * group + i
            base = pl.multiple_of(c * chunk, chunk)
            strict, within, _, _, _ = chunk_masks(segment_of, base, chunk)
            for h in range(heads):
                cols = slice(h * 128, (h + 1) * 128)
                k = key_s[pl.ds(base, chunk), cols]
                q = query_s[pl.ds(base, chunk), cols]
                lowers.append(product(k, k, 1, 1, exact) * strict * beta_of(base, h))
                score_s[c * heads + h] = (product(q, k, 1, 1, exact) * within).astype(score_s.dtype)
                places.append(c * heads + h)
        inverses = [eye - jnp.where(masks[0], lower, 0.0) for lower in lowers]
        for mask in masks[1:]:
            steps = [product(jnp.where(mask, lower, 0.0), x, 1, 0, True) for lower, x in zip(lowers, inverses)]
            inverses = [x - product(x, step, 1, 0, True) for x, step in zip(inverses, steps)]
        for place, x in zip(places, inverses):
            inverse_ref[place] = x

    def advance(c, states):
        base = pl.multiple_of(c * chunk, chunk)
        rows = pl.ds(base, chunk)
        _, _, carry, close, keep = chunk_masks(segment_of, base, chunk)
        new_states = []
        for h in range(heads):
            cols = slice(h * 128, (h + 1) * 128)
            state = states[h]
            k = key_s[rows, cols]
            q = query_s[rows, cols]
            delta = value_s[rows, cols] - carry * product(k, state, 1, 0, exact)
            fixed = product(inverse_ref[c * heads + h], beta_of(base, h) * delta, 1, 0, exact)
            out = carry * product(q, state, 1, 0, exact) + product(
                score_s[c * heads + h], fixed, 1, 0, exact)
            state_ref[c * heads + h] = state
            new_states.append(keep * state + product(k, close * fixed, 0, 0, exact))
            delta_ref[rows, cols] = delta
            fixed_ref[rows, cols] = fixed
            heads_ref[rows, cols] = out
            gate = proj_ref[rows, 3 * width + h * 128 : 3 * width + (h + 1) * 128]
            r = lax.rsqrt(jnp.mean(out * out, axis=-1, keepdims=True) + epsilon)
            mixed_ref[rows, cols] = (
                out * r * gain_ref[h : h + 1, :] * (gate * sigmoid(gate))
            ).astype(mixed_ref.dtype)
        return tuple(new_states)

    lax.fori_loop(0, count, advance, tuple(jnp.zeros((128, 128), f32) for _ in range(heads)))


def mixer_backward_kernel(exact, lengths_ref, proj_ref, beta_ref, tap_ref, gain_ref, grad_ref,
                          heads_ref, fixed_ref, delta_ref, state_ref, inverse_ref,
                          dproj_ref, dbeta_ref, dtap_ref, dgain_ref,
                          query_s, key_s, pre_s, dout_s, dpre_s):
    rows_all = proj_ref.shape[0]
    width = proj_ref.shape[1] // 4
    heads = width // 128
    chunk = CHUNK
    count = rows_all // chunk
    taps = tap_ref.shape[0] // 3
    segment_of, segments = segment_tools(lengths_ref)
    dgain_ref[...] = jnp.zeros_like(dgain_ref)
    dbeta_ref[...] = jnp.zeros_like(dbeta_ref)
    dtap_ref[...] = jnp.zeros_like(dtap_ref)

    @pl.loop(0, count)
    def _(c):
        base = pl.multiple_of(c * chunk, chunk)
        rows = pl.ds(base, chunk)
        for part in range(3):
            pre, _ = conv_part(proj_ref, tap_ref, segment_of, base, part, width, chunk)
            pre_s[rows, part * width : (part + 1) * width] = pre
            if part < 2:
                act = pre * sigmoid(pre)
                target = (query_s, key_s)[part]
                scale = 128 ** (-0.5) if part == 0 else 1.0
                for h, a in enumerate(heads_of(act, heads)):
                    target[rows, h * 128 : (h + 1) * 128] = unit_rows(a, scale)
        for h in range(heads):
            cols = slice(h * 128, (h + 1) * 128)
            gate_cols = slice(3 * width + h * 128, 3 * width + (h + 1) * 128)
            out = heads_ref[rows, cols]
            gate = proj_ref[rows, gate_cols]
            grad = grad_ref[rows, cols].astype(f32)
            gain = gain_ref[h : h + 1, :]
            sg = sigmoid(gate)
            silu = gate * sg
            r = lax.rsqrt(jnp.mean(out * out, axis=-1, keepdims=True) + epsilon)
            normed = out * r
            dgain_ref[h : h + 1, :] += jnp.sum(grad * normed * silu, axis=0, keepdims=True)
            dproj_ref[rows, gate_cols] = (
                grad * normed * gain * (sg * (1.0 + gate * (1.0 - sg)))
            ).astype(dproj_ref.dtype)
            weighted = grad * gain * silu
            dout_s[rows, cols] = r * weighted - out * (r * r * r) * jnp.mean(
                weighted * out, axis=-1, keepdims=True)

    dpre_s[rows_all : rows_all + HALO, :] = jnp.zeros((HALO, 3 * width), f32)

    def retreat(step, dstates):
        c = count - 1 - step
        base = pl.multiple_of(c * chunk, chunk)
        rows = pl.ds(base, chunk)
        strict, within, carry, close, keep = chunk_masks(segment_of, base, chunk)
        pos = base + lax.broadcasted_iota(jnp.int32, (chunk, 1), 0)
        live = (segment_of(pos) < segments).astype(f32)
        new_dstates = []
        for h in range(heads):
            cols = slice(h * 128, (h + 1) * 128)
            place = c * heads + h
            k = key_s[rows, cols]
            q = query_s[rows, cols]
            dout = dout_s[rows, cols]
            state = state_ref[place]
            inverse = inverse_ref[place]
            fixed = fixed_ref[rows, cols]
            delta = delta_ref[rows, cols]
            dstate = dstates[h]
            rate = sigmoid(beta_ref[rows, h : h + 1])
            beta = rate * live
            scores = product(q, k, 1, 1, exact) * within
            gram = product(k, k, 1, 1, exact) * strict
            dfixed = product(scores, dout, 0, 0, exact) + close * product(k, dstate, 1, 0, exact)
            drhs = product(inverse, dfixed, 0, 0, exact)
            ddelta = beta * drhs
            carried_dout = carry * dout
            carried_ddelta = carry * ddelta
            new_dstates.append(
                keep * dstate
                + product(q, carried_dout, 0, 0, exact)
                - product(k, carried_ddelta, 0, 0, exact)
            )
            dscores = product(dout, fixed, 1, 1, exact) * within
            dlower = -product(drhs, fixed, 1, 1, exact) * strict
            dgram = beta * dlower
            dq = product(carried_dout, state, 1, 1, exact) + product(dscores, k, 1, 0, exact)
            dk = (
                product(dscores, q, 0, 0, exact)
                + close * product(fixed, dstate, 1, 1, exact)
                - product(carried_ddelta, state, 1, 1, exact)
                + product(dgram, k, 1, 0, exact)
                + product(dgram, k, 0, 0, exact)
            )
            drate = live * (
                jnp.sum(drhs * delta, axis=-1, keepdims=True)
                + jnp.sum(dlower * gram, axis=-1, keepdims=True)
            )
            dbeta_ref[rows, h : h + 1] = (drate * rate * (1.0 - rate)).astype(dbeta_ref.dtype)
            for part, da in enumerate((dq, dk, ddelta)):
                part_cols = slice(part * width + h * 128, part * width + (h + 1) * 128)
                pre = pre_s[rows, part_cols]
                sg = sigmoid(pre)
                if part < 2:
                    a = pre * sg
                    scale = 128 ** (-0.5) if part == 0 else 1.0
                    r = lax.rsqrt(jnp.sum(a * a, axis=-1, keepdims=True) + epsilon)
                    da = (scale * r) * (da - a * (r * r) * jnp.sum(da * a, axis=-1, keepdims=True))
                dpre_s[rows, part_cols] = da * (sg * (1.0 + pre * (1.0 - sg)))
        return tuple(new_dstates)

    lax.fori_loop(0, count, retreat, tuple(jnp.zeros((128, 128), f32) for _ in range(heads)))

    @pl.loop(0, count)
    def _(c):
        base = pl.multiple_of(c * chunk, chunk)
        rows = pl.ds(base, chunk)
        col = base + lax.broadcasted_iota(jnp.int32, (chunk, 1), 0)
        seg = segment_of(col)
        for part in range(3):
            cols = slice(part * width, (part + 1) * width)
            _, shifted = conv_part(proj_ref, tap_ref, segment_of, base, part, width, chunk)
            full = dpre_s[pl.ds(base, chunk + HALO), cols]
            main = full[:chunk]
            total = main * tap_ref[part * taps : part * taps + 1, :]
            for s in range(taps):
                at = slice(part * taps + s, part * taps + s + 1)
                dtap_ref[at, :] += jnp.sum(main * shifted[s], axis=0, keepdims=True)
                if s > 0:
                    valid = (segment_of(col + s) == seg) & (col + s < rows_all)
                    moved = pltpu.roll(full, chunk + HALO - s, 0)[:chunk]
                    total = total + jnp.where(valid, moved, 0.0) * tap_ref[at, :]
            dproj_ref[rows, cols] = total.astype(dproj_ref.dtype)


def vmem():
    return pl.BlockSpec(memory_space=pltpu.VMEM)


def mixer_forward(lengths_row, projected, beta_logits, taps, gain, exact=True, group=4):
    rows, wide = projected.shape
    width = wide // 4
    heads = width // 128
    places = rows // CHUNK * heads
    group = min(group, rows // CHUNK)
    return pl.pallas_call(
        partial(mixer_forward_kernel, exact, group),
        out_shape=(
            jax.ShapeDtypeStruct((rows, width), bf16),
            jax.ShapeDtypeStruct((rows, width), f32),
            jax.ShapeDtypeStruct((rows, width), f32),
            jax.ShapeDtypeStruct((rows, width), f32),
            jax.ShapeDtypeStruct((places, 128, 128), f32),
            jax.ShapeDtypeStruct((places, CHUNK, CHUNK), f32),
        ),
        in_specs=[pl.BlockSpec(memory_space=pltpu.SMEM)] + [vmem()] * 4,
        out_specs=(vmem(),) * 6,
        scratch_shapes=[pltpu.VMEM((rows, width), f32)] * 3
        + [pltpu.VMEM((places, CHUNK, CHUNK), f32 if exact else bf16)],
        compiler_params=pltpu.CompilerParams(vmem_limit_bytes=48 * 2**20),
        cost_estimate=pl.CostEstimate(flops=10**10, bytes_accessed=10**7, transcendentals=10**6),
        name="mixer_forward",
    )(lengths_row, projected, beta_logits, taps, gain)


def mixer_backward(lengths_row, projected, beta_logits, taps, gain, grad, saved, exact=True):
    rows, wide = projected.shape
    width = wide // 4
    return pl.pallas_call(
        partial(mixer_backward_kernel, exact),
        out_shape=(
            jax.ShapeDtypeStruct((rows, wide), bf16),
            jax.ShapeDtypeStruct((rows, 128), bf16),
            jax.ShapeDtypeStruct(taps.shape, f32),
            jax.ShapeDtypeStruct(gain.shape, f32),
        ),
        in_specs=[pl.BlockSpec(memory_space=pltpu.SMEM)] + [vmem()] * 10,
        out_specs=(vmem(),) * 4,
        scratch_shapes=[pltpu.VMEM((rows, width), f32)] * 2
        + [pltpu.VMEM((rows, 3 * width), f32), pltpu.VMEM((rows, width), f32),
           pltpu.VMEM((rows + HALO, 3 * width), f32)],
        compiler_params=pltpu.CompilerParams(vmem_limit_bytes=56 * 2**20),
        cost_estimate=pl.CostEstimate(flops=10**10, bytes_accessed=10**7, transcendentals=10**6),
        name="mixer_backward",
    )(lengths_row, projected, beta_logits, taps, gain, grad, *saved)


NT = (((1,), (1,)), ((), ()))


def other(axis_name):
    return {axis_name: 1 - lax.axis_index(axis_name)}


def ffn_kernel(x_ref, w_ref, down_ref, c_refs, out_ref, ngrad_ref, wgrad_ref, down_out,
               xs, cs, ws, dsum, landed, outs, inner_s, gate_s, up_s, acts_t, part, crecv, drecv, nrecv, stage,
               ag_send, ag_recv, pair_send, pair_recv, rs_send, rs_recv, c_sem, w_sem, g_sem, t_sem,
               down_right, down_left, down_recv, down_sem, sum_sems, keep_sem, out_sem):
    half = xs.shape[1] // 2
    rows = 2 * half
    model = xs.shape[2]
    hidden = ws.shape[1]
    lines = w_ref.shape[0]
    parts, _, quarter, width = w_ref.shape[1:]
    tile_f = 256
    tile_d = min(512, model)
    tile_w = min(256, width)

    def remote(src, dst, send, recv, axis_name):
        return pltpu.make_async_remote_copy(
            src_ref=src, dst_ref=dst, send_sem=send, recv_sem=recv,
            device_id=other(axis_name), device_id_type=pl.DeviceIdType.MESH)

    def halves(ref, index, h):
        return ref.at[index, pl.ds(h * half, half)]

    o = lax.axis_index("z")

    def down_rows(z):
        return ws.at[2, pl.ds(pl.multiple_of(z * quarter, 16), quarter)]

    def down_pass(z, right):
        send = down_right if right else down_left
        return pltpu.make_async_remote_copy(
            src_ref=down_rows(z), dst_ref=down_rows(z), send_sem=send.at[z], recv_sem=down_recv.at[z],
            device_id={"z": o + 1 if right else o - 1}, device_id_type=pl.DeviceIdType.MESH)

    def down_forward(z, right):
        @pl.when(o < lines - 1 if right else o > 0)
        def _():
            down_pass(z, right).start()

    def down_step(far):
        for side in (-1, 1):
            z = o + side * far

            @pl.when((z >= 0) & (z < lines))
            def _():
                down_pass(z, side < 0).wait_recv()
                down_forward(z, side < 0)

    weight_copies, down_copies = [], []
    for r in range(parts):
        cols = pl.ds(r * width, width)
        for line in range(lines):
            weight_copies.append(pltpu.make_async_copy(
                w_ref.at[line, r], ws.at[pl.ds(0, 2), pl.ds(line * quarter, quarter), cols],
                w_sem.at[line, r]))
        down_copies.append(pltpu.make_async_copy(
            down_ref.at[r], down_rows(o).at[:, cols], down_sem.at[r]))
    for copy in down_copies:
        copy.start()
    for copy in weight_copies:
        copy.start()

    def pair_at(turn):
        return jnp.where(turn < 2, 3 - 2 * turn, 6 - 2 * turn)

    def slot_of(step):
        return (1 - lax.rem(step, 2)) * 4 + pair_at(step // 2)

    def c_copy(step, n):
        buffer = lax.rem(step, 2)
        return pltpu.make_async_copy(c_refs[n], cs.at[buffer], c_sem.at[buffer])

    def c_start(step):
        for n in range(8):
            @pl.when(slot_of(step) == n)
            def _():
                c_copy(step, n).start()

    c_copy(0, 7).start()
    line_barrier(lines, [other(name) for name in ("core", "x", "y")])

    own_pair = remote(x_ref, xs.at[4], ag_send.at[0], ag_recv.at[0], "core")
    own_x = [remote(x_ref.at[pl.ds(h * half, half)], halves(xs, 1, h), ag_send.at[1 + h], ag_recv.at[1 + h], "x") for h in range(2)]
    own_y = [remote(x_ref.at[pl.ds(h * half, half)], halves(xs, 2, h), ag_send.at[3 + h], ag_recv.at[3 + h], "y") for h in range(2)]
    relay_y = remote(halves(xs, 1, 0), halves(xs, 3, 0), ag_send.at[5], ag_recv.at[5], "y")
    relay_x = remote(halves(xs, 2, 1), halves(xs, 3, 1), ag_send.at[6], ag_recv.at[6], "x")
    pair_of = [None] + [remote(xs.at[j], xs.at[4 + j], ag_send.at[6 + j], ag_recv.at[6 + j], "core") for j in (1, 2, 3)]
    own_pair.start()
    own_x[0].start()
    own_y[1].start()
    own_x[1].start()
    own_y[0].start()
    for copy in down_copies:
        copy.wait()
    down_forward(o, True)
    down_forward(o, False)
    own_copy = pltpu.make_async_copy(x_ref, xs.at[0], t_sem.at[0, 0])
    own_copy.start()
    own_copy.wait()
    for copy in weight_copies:
        copy.wait()

    def part_send(turn):
        j = pair_at(turn)
        return remote(part.at[lax.rem(turn, 2)], crecv.at[j], pair_send.at[j], pair_recv.at[j], "core")

    x_sends = [[remote(crecv.at[1, a, pl.ds(h * half, half)], nrecv.at[0, a, pl.ds(h * half, half)],
                       rs_send.at[a * 2 + h], rs_recv.at[a * 2 + h], "x") for a in range(2)] for h in range(2)]
    y_sends = [[remote(crecv.at[2, a, pl.ds(h * half, half)], nrecv.at[1, a, pl.ds(h * half, half)],
                       rs_send.at[4 + a * 2 + h], rs_recv.at[4 + a * 2 + h], "y") for a in range(2)] for h in range(2)]
    d_sends = [[remote(crecv.at[3, a, pl.ds(h * half, half)], drecv.at[a, pl.ds(h * half, half)],
                       rs_send.at[8 + a * 2 + h], rs_recv.at[8 + a * 2 + h], ("x", "y")[h]) for a in range(2)] for h in range(2)]

    def gates(slot, cols):
        return [
            lax.dot_general(xs[slot], ws[kind, cols, :], NT, preferred_element_type=f32)
            for kind in range(2)]

    @pl.loop(0, 8)
    def _(early):
        slot = lax.rem(early + 1, 2) * 4 + early // 2

        @pl.when(early == 0)
        def _():
            own_pair.wait_recv()

        @pl.when(early == 2)
        def _():
            down_step(1)
            own_x[0].wait_recv()
            relay_y.start()
            own_y[1].wait_recv()
            relay_x.start()
            own_x[1].wait_recv()
            pair_of[1].start()
            own_y[0].wait_recv()
            pair_of[2].start()
            pair_of[1].wait_recv()

        @pl.when(early == 4)
        def _():
            pair_of[2].wait_recv()

        @pl.when(early == 6)
        def _():
            if lines > 2:
                down_step(2)
            relay_y.wait_recv()
            relay_x.wait_recv()
            pair_of[3].start()
            pair_of[3].wait_recv()

        places = pl.ds(pl.multiple_of(slot * rows, rows), rows)
        for start in range(0, hidden, tile_f):
            cols = slice(start, min(start + tile_f, hidden))
            gate, up = gates(slot, cols)
            acts_t[2, cols, places] = (gate * sigmoid(gate) * up).astype(bf16).T

    tiles = model // tile_w

    def c_tile(t):
        buffer = lax.rem(t, 2)
        cols = pl.ds(pl.multiple_of(t * tile_w, tile_w), tile_w)
        return [
            pltpu.make_async_copy(
                ref.at[:, cols], part.at[0, buffer, :, pl.ds(n * tile_w, tile_w)], t_sem.at[buffer, n])
            for n, ref in enumerate(c_refs)]

    def grad_copy(kind, t, line):
        return pltpu.make_async_copy(
            stage.at[lax.rem(t, 2), pl.ds(line * quarter, quarter)],
            wgrad_ref.at[line, t * tile_w // width, kind, :,
                         pl.ds(pl.multiple_of(lax.rem(t * tile_w, width), tile_w), tile_w)],
            g_sem.at[lax.rem(t, 2), line])

    def weight_grads(kind):
        @pl.loop(0, tiles)
        def _(t):
            if kind == 2:
                for copy in c_tile(t):
                    copy.wait()
                right = jnp.concatenate(
                    [part[0, lax.rem(t, 2), :, n * tile_w : (n + 1) * tile_w] for n in range(8)])
            else:
                right = xs[:, :, pl.ds(pl.multiple_of(t * tile_w, tile_w), tile_w)].reshape(8 * rows, tile_w)

            if kind < 2:
                @pl.when(t >= 2)
                def _():
                    for line in range(lines):
                        grad_copy(kind, t - 2, line).wait()

            value = jnp.dot(acts_t[kind], right, preferred_element_type=f32).astype(bf16)
            if kind == 2:
                @pl.when(t + 2 < tiles)
                def _():
                    for copy in c_tile(t + 2):
                        copy.start()
            if kind < 2:
                stage[lax.rem(t, 2)] = value
                for line in range(lines):
                    grad_copy(kind, t, line).start()
            else:
                dsum[:, pl.ds(pl.multiple_of(t * tile_w, tile_w), tile_w)] = value

        if kind == 2:
            return
        for t in range(max(tiles - 2, 0), tiles):
            for line in range(lines):
                grad_copy(kind, t, line).wait()

    mesh_id = pl.DeviceIdType.MESH

    def rows_of(z):
        return dsum.at[pl.ds(pl.multiple_of(z * quarter, 16), quarter)]

    def sum_pass(z, right):
        side = 0 if right else 2
        block = jnp.maximum(z - o - 1, 0) if right else jnp.minimum(lines - o + 1 + z, lines)
        return pltpu.make_async_remote_copy(
            src_ref=rows_of(z), dst_ref=landed.at[block],
            send_sem=sum_sems.at[side, z], recv_sem=sum_sems.at[side + 1, z],
            device_id={"z": o + 1 if right else o - 1}, device_id_type=mesh_id)

    def sum_add(z, block):
        at = pl.ds(pl.multiple_of(z * quarter, 16), quarter)
        for start in range(0, model, tile_d):
            cols = slice(start, start + tile_d)
            dsum[at, cols] = (
                dsum[at, cols].astype(f32) + landed[block, :, cols].astype(f32)).astype(bf16)

    def sum_tick(k):
        z_right = lines - 1 - k + o

        @pl.when(o <= k)
        def _():
            @pl.when(o > 0)
            def _():
                sum_pass(z_right, True).wait_recv()
                sum_add(z_right, z_right - o)

            @pl.when(o < k)
            def _():
                sum_pass(z_right + 1, True).wait_send()
            sum_pass(z_right, True).start()

        back = lines - 1 - o
        z_left = k - back

        @pl.when(back <= k)
        def _():
            @pl.when(back > 0)
            def _():
                sum_pass(z_left, False).wait_recv()
                sum_add(z_left, lines - o + z_left)

            @pl.when(back < k)
            def _():
                sum_pass(z_left - 1, False).wait_send()
            sum_pass(z_left, False).start()

    for t in range(2):
        for copy in c_tile(t):
            copy.start()
    weight_grads(2)
    sum_tick(0)
    for far in range(3, lines):
        down_step(far)

    @pl.loop(0, 8)
    def _(step):
        turn = step // 2
        j = pair_at(turn)
        slot = slot_of(step)
        pairing = lax.rem(step, 2) == 0

        @pl.when(step < 7)
        def _():
            c_start(step + 1)

        for k in range(1, lines - 1):
            @pl.when(step == min(1 + 3 * k, 7))
            def _():
                sum_tick(k)

        @pl.when(step == 7)
        def _():
            for h in range(2):
                n = 2 - h
                for a in range(2):
                    d_sends[h][a].wait_recv()
                    at = pl.ds(h * half, half)
                    crecv[n, a, at, :] = (
                        crecv[n, a, at, :].astype(f32) + drecv[a, at, :].astype(f32)).astype(bf16)
                for copy in (y_sends, x_sends)[h][h]:
                    copy.start()

        c_copy(step, 0).wait()

        for start in range(0, hidden, tile_f):
            size = min(tile_f, hidden - start)
            cols = slice(start, start + size)
            gate, up = gates(slot, cols)
            grad = lax.dot_general(cs[lax.rem(step, 2)], ws[2, cols, :], NT, preferred_element_type=f32)
            sg = sigmoid(gate)
            silu = gate * sg
            inner = (silu * up).astype(bf16)
            gate_grad = (grad * up * sg * (1.0 + gate * (1.0 - sg))).astype(bf16)
            up_grad = (grad * silu).astype(bf16)
            places = pl.ds(pl.multiple_of(slot * rows, rows), rows)
            for kind, (value, target) in enumerate(((gate_grad, gate_s), (up_grad, up_s), (inner, inner_s))):
                target[:, cols] = value
                if kind < 2:
                    acts_t[kind, cols, places] = value.T

        @pl.when(pairing & (step >= 4))
        def _():
            part_send(turn - 2).wait_send()

        place = jnp.where(pairing, lax.rem(turn, 2), 2)
        for start in range(0, model, tile_d):
            cols = slice(start, start + tile_d)
            part[place, 0, :, cols] = jnp.dot(
                inner_s[...], ws[2, :, cols], preferred_element_type=f32).astype(bf16)
            part[place, 1, :, cols] = (
                jnp.dot(gate_s[...], ws[0, :, cols], preferred_element_type=f32)
                + jnp.dot(up_s[...], ws[1, :, cols], preferred_element_type=f32)
            ).astype(bf16)

        @pl.when(pairing)
        def _():
            part_send(turn).start()

        @pl.when(jnp.logical_not(pairing))
        def _():
            part_send(turn).wait_recv()
            for a in range(2):
                for start in range(0, model, tile_d):
                    cols = slice(start, start + tile_d)
                    crecv[j, a, :, cols] = (
                        crecv[j, a, :, cols].astype(f32) + part[2, a, :, cols].astype(f32)
                    ).astype(bf16)

        @pl.when(step == 1)
        def _():
            for h in range(2):
                for copy in d_sends[h]:
                    copy.start()

        @pl.when(step == 3)
        def _():
            for copy in x_sends[0]:
                copy.start()

        @pl.when(step == 5)
        def _():
            for copy in y_sends[1]:
                copy.start()


    weight_grads(0)
    weight_grads(1)
    out_copies = []
    for a, target in enumerate((out_ref, ngrad_ref)):
        for h in range(2):
            x_sends[h][a].wait_recv()
            y_sends[h][a].wait_recv()
        for n in range(model // tile_d):
            cols = slice(n * tile_d, (n + 1) * tile_d)
            if n >= 2:
                out_copies[-2].wait()
            outs[a, n % 2] = (
                crecv[0, a, :, cols].astype(f32)
                + nrecv[0, a, :, cols].astype(f32)
                + nrecv[1, a, :, cols].astype(f32)
            )
            copy = pltpu.make_async_copy(
                outs.at[a, n % 2], target.at[:, pl.ds(n * tile_d, tile_d)],
                out_sem.at[n, a])
            copy.start()
            out_copies.append(copy)
    steps = model // tile_d
    for a in range(2):
        for copy in out_copies[a * steps : (a + 1) * steps][-2:]:
            copy.wait()
    @pl.loop(0, lines)
    def _(z):
        @pl.when((o < lines - 1) & (z <= o))
        def _():
            down_pass(z, True).wait_send()

        @pl.when((o > 0) & (z >= o))
        def _():
            down_pass(z, False).wait_send()

    own_pair.wait_send()
    for h in range(2):
        own_x[h].wait_send()
        own_y[h].wait_send()
        for a in range(2):
            x_sends[h][a].wait_send()
            y_sends[h][a].wait_send()
            d_sends[h][a].wait_send()
    relay_x.wait_send()
    relay_y.wait_send()
    for j in (1, 2, 3):
        pair_of[j].wait_send()
    part_send(2).wait_send()
    part_send(3).wait_send()

    @pl.when(o > 0)
    def _():
        sum_pass(o, True).wait_recv()
        sum_add(o, 0)

    @pl.when(o < lines - 1)
    def _():
        sum_pass(o, False).wait_recv()
        sum_add(o, lines)

    keeps = [
        pltpu.make_async_copy(
            rows_of(o).at[:, pl.ds(q * width, width)], down_out.at[q], keep_sem.at[q])
        for q in range(parts)
    ]
    for copy in keeps:
        copy.start()

    @pl.when(o < lines - 1)
    def _():
        sum_pass(o + 1, True).wait_send()

    @pl.when(o > 0)
    def _():
        sum_pass(o - 1, False).wait_send()
    for copy in keeps:
        copy.wait()


def ffn_call_kernel(x_ref, w_ref, down_ref, *refs):
    ffn_kernel(x_ref, w_ref, down_ref, refs[:8], *refs[8:])


def ffn_plane(x_own, weights, down_own, c_rows):
    rows, model = x_own.shape
    lines, parts, _, quarter, width = weights.shape
    hidden = lines * quarter
    tile_w = min(256, width)
    sems = pltpu.SemaphoreType.DMA
    anywhere = pl.BlockSpec(memory_space=pl.ANY)
    return pl.pallas_call(
        ffn_call_kernel,
        out_shape=(
            jax.ShapeDtypeStruct((rows, model), f32),
            jax.ShapeDtypeStruct((rows, model), f32),
            jax.ShapeDtypeStruct(weights.shape, bf16),
            jax.ShapeDtypeStruct((parts, quarter, width), bf16),
        ),
        in_specs=[anywhere] * 11,
        out_specs=(anywhere,) * 4,
        scratch_shapes=[
            pltpu.VMEM((8, rows, model), bf16),
            pltpu.VMEM((2, rows, model), bf16),
            pltpu.VMEM((3, hidden, model), bf16),
            pltpu.VMEM((hidden, model), bf16),
            pltpu.VMEM((lines + 1, quarter, model), bf16),
            pltpu.VMEM((2, 2, rows, min(512, model)), f32),
            pltpu.VMEM((rows, hidden), bf16),
            pltpu.VMEM((rows, hidden), bf16),
            pltpu.VMEM((rows, hidden), bf16),
            pltpu.VMEM((3, hidden, 8 * rows), bf16),
            pltpu.VMEM((3, 2, rows, model), bf16),
            pltpu.VMEM((4, 2, rows, model), bf16),
            pltpu.VMEM((2, rows, model), bf16),
            pltpu.VMEM((2, 2, rows, model), bf16),
            pltpu.VMEM((2, hidden, tile_w), bf16),
            sems((10,)), sems((10,)), sems((4,)), sems((4,)), sems((12,)), sems((12,)),
            sems((2,)), sems((lines, parts)), sems((2, lines)), sems((2, 8)),
            sems((lines,)), sems((lines,)), sems((lines,)), sems((parts,)),
            sems((4, lines)), sems((parts,)), sems((4, 2)),
        ],
        compiler_params=pltpu.CompilerParams(
            collective_id=2, has_side_effects=True, vmem_limit_bytes=60 * 2**20),
        cost_estimate=pl.CostEstimate(flops=8 * 10**10, bytes_accessed=4 * 10**7, transcendentals=10**6),
        name="ffn_plane",
    )(x_own, weights, down_own, *c_rows)


def line_barrier(lines, others):
    o = lax.axis_index("z")
    barrier = pltpu.get_barrier_semaphore()
    mesh_id = pl.DeviceIdType.MESH

    @pl.when(o > 0)
    def _():
        pl.semaphore_signal(barrier, inc=1, device_id={"z": o - 1}, device_id_type=mesh_id)

    @pl.when(o < lines - 1)
    def _():
        pl.semaphore_signal(barrier, inc=1, device_id={"z": o + 1}, device_id_type=mesh_id)

    for target in others:
        pl.semaphore_signal(barrier, inc=1, device_id=target, device_id_type=mesh_id)
    peers = len(others) + (o > 0).astype(jnp.int32) + (o < lines - 1).astype(jnp.int32)
    pl.semaphore_wait(barrier, peers)


def line_copy(src, dst, send, recv, target):
    return pltpu.make_async_remote_copy(
        src_ref=src, dst_ref=dst, send_sem=send, recv_sem=recv,
        device_id=target, device_id_type=pl.DeviceIdType.MESH)


def pair_peers():
    x, core = lax.axis_index("x"), lax.axis_index("core")
    peers = [
        (x * 2 + 1 - core, {"core": 1 - core}),
        ((1 - x) * 2 + core, {"x": 1 - x}),
        ((1 - x) * 2 + 1 - core, {"x": 1 - x, "core": 1 - core}),
    ]
    return x * 2 + core, peers


class Swap:
    def __init__(self, pairs, send, recv, own):
        me, peers = pair_peers()
        self.own = [
            pltpu.make_async_copy(source.at[me], target(me), own.at[n])
            for n, (source, target) in enumerate(pairs)]
        self.away = [
            line_copy(source.at[place], target(me), send.at[n, d], recv.at[n, d], device)
            for n, (source, target) in enumerate(pairs) for d, (place, device) in enumerate(peers)]

    def start(self):
        for copy in self.away + self.own:
            copy.start()

    def wait(self):
        for copy in self.own:
            copy.wait()
        for copy in self.away:
            copy.wait_recv()
            copy.wait_send()


def gather_kernel(x_ref, gain_ref, o_ref, f_refs, w_refs, wb_ref, rows_ref, outs_ref, proj_refs, beta_ref,
                  pair_ref, down_ref, gain_out,
                  xs, parts, stage, beta_stage, right_send, left_send, line_recv, pair_send, pair_recv,
                  part_right, part_left, part_recv, own_sem, row_sem, outs_sem, out_sem, beta_sem,
                  swap_send, swap_recv, swap_own, gains, gain_send, gain_recv, gain_own):
    lines = xs.shape[0] // 2
    batches, rows, model = x_ref.shape
    o = lax.axis_index("z")
    i = lax.axis_index("y")
    line_barrier(lines, [other("y")] + [device for _, device in pair_peers()[1]])
    swap = Swap(
        [(f_refs[0], lambda place: pair_ref.at[place, 0]),
         (f_refs[1], lambda place: pair_ref.at[place, 1]),
         (f_refs[2], lambda place: down_ref.at[place])],
        swap_send, swap_recv, swap_own)

    def right(z, m):
        ref = xs.at[z * 2 + i, m]
        return line_copy(ref, ref, right_send.at[z, m], line_recv.at[z, m], {"z": o + 1})

    def left(z, m):
        ref = xs.at[z * 2 + i, m]
        return line_copy(ref, ref, left_send.at[z, m], line_recv.at[z, m], {"z": o - 1})

    def across(z, m):
        ref = xs.at[z * 2 + i, m]
        return line_copy(ref, ref, pair_send.at[z, m], pair_recv.at[z, m], other("y"))

    own = [
        pltpu.make_async_copy(o_ref, parts.at[o], own_sem.at[1]),
    ]

    def pass_part(z):
        ref = parts.at[z]
        return (line_copy(ref, ref, part_right.at[z], part_recv.at[z], {"z": o + 1}),
                line_copy(ref, ref, part_left.at[z], part_recv.at[z], {"z": o - 1}))

    for copy in own:
        copy.start()
    me, peers = pair_peers()
    share = gain_ref.shape[1]
    gain_place = gains.at[:, pl.ds(pl.multiple_of(me * share, 128), share)]
    gain_away = [
        line_copy(gain_ref, gain_place, gain_send.at[d], gain_recv.at[d], device)
        for d, (_, device) in enumerate(peers)]
    gain_keep = pltpu.make_async_copy(gain_ref, gain_place, gain_own.at[0])
    gain_keep.start()
    for copy in gain_away:
        copy.start()
    gain_keep.wait()
    for copy in gain_away:
        copy.wait_recv()
    for m in range(batches):
        value = x_ref[m].astype(f32)
        scale = lax.rsqrt(jnp.mean(value * value, axis=-1, keepdims=True) + epsilon)
        xs[o * 2 + i, m] = (value * scale * gains[0:1, :]).astype(bf16)
    for copy in own:
        copy.wait()

    def outs(turn, slot):
        buffer = lax.rem(turn, 2)
        return [
            copy for m in range(batches) for copy in (
                pltpu.make_async_copy(stage.at[buffer, m], proj_refs[m].at[slot], out_sem.at[buffer, m]),
                pltpu.make_async_copy(beta_stage.at[buffer, m], beta_ref.at[m, slot], beta_sem.at[buffer, m]))
        ]

    def keep(slot, m):
        return pltpu.make_async_copy(xs.at[slot, m], rows_ref.at[m, slot], row_sem.at[slot, m])

    def keep_outs(z):
        return pltpu.make_async_copy(parts.at[z], outs_ref.at[z], outs_sem.at[z])

    def project(turn, slot):
        @pl.when(turn >= 2)
        def _():
            for copy in outs(turn, slot):
                copy.wait()
        for m in range(batches):
            keep(slot, m).start()
        x = xs[slot].reshape(batches * rows, model)
        buffer = lax.rem(turn, 2)
        width = w_refs[0].shape[1]
        for n, w_ref in enumerate(w_refs):
            stage[buffer, :, :, n * width : (n + 1) * width] = jnp.dot(
                x, w_ref[...], preferred_element_type=f32).reshape(batches, rows, width)
        beta_stage[buffer] = jnp.dot(
            x, wb_ref[...], preferred_element_type=f32).reshape(batches, rows, 128)
        for copy in outs(turn, slot):
            copy.start()

    def in_line(index):
        far = (index + 1) // 2
        side = 1 - 2 * lax.rem(index, 2)
        z = o + side * far
        return far, z, (z >= 0) & (z < lines)

    def first(index, turn):
        far, z, valid = in_line(index)

        @pl.when(valid)
        def _():
            for m in range(batches):
                @pl.when(far > 0)
                def _():
                    left(z, m).wait_recv()

                @pl.when((o < lines - 1) & (z <= o))
                def _():
                    right(z, m).start()

                @pl.when((o > 0) & (z >= o))
                def _():
                    left(z, m).start()

                across(z, m).start()
            project(turn, z * 2 + i)

        return turn + valid.astype(jnp.int32)

    swap.start()
    turn = lax.fori_loop(0, 2 * lines - 1, first, jnp.int32(0))

    def second(index, turn):
        far, z, valid = in_line(index)

        @pl.when(valid)
        def _():
            to_right, to_left = pass_part(z)

            @pl.when(far > 0)
            def _():
                to_left.wait_recv()

            @pl.when((o < lines - 1) & (z <= o))
            def _():
                to_right.start()

            @pl.when((o > 0) & (z >= o))
            def _():
                to_left.start()

            keep_outs(z).start()
            for m in range(batches):
                across(z, m).wait_recv()
            project(turn, z * 2 + 1 - i)

        return turn + valid.astype(jnp.int32)

    lax.fori_loop(0, 2 * lines - 1, second, turn)
    for turn in range(2 * lines - 2, 2 * lines):
        for copy in outs(turn, 0):
            copy.wait()

    @pl.loop(0, lines)
    def _(z):
        keep_outs(z).wait()

        @pl.when((o < lines - 1) & (z <= o))
        def _():
            pass_part(z)[0].wait_send()
            for m in range(batches):
                right(z, m).wait_send()

        @pl.when((o > 0) & (z >= o))
        def _():
            pass_part(z)[1].wait_send()
            for m in range(batches):
                left(z, m).wait_send()

        for m in range(batches):

            across(z, m).wait_send()
            for y in range(2):
                keep(z * 2 + y, m).wait()

    swap.wait()
    gain_out[...] = gains[...]
    for copy in gain_away:
        copy.wait_send()


def gather_call_kernel(x_ref, gain_ref, o_ref, *refs):
    gather_kernel(x_ref, gain_ref, o_ref, refs[:3], refs[3:7], refs[7], refs[8], refs[9], refs[10:12],
                  *refs[12:])


def gather_project(x, gains, w_out_part, ffn_parts, w_inner, w_beta):
    batches, rows, model = x.shape
    more = w_out_part.shape[1]
    lines = lax.axis_size("z")
    width = sum(w.shape[1] for w in w_inner)
    slots = 2 * lines
    sems = pltpu.SemaphoreType.DMA
    anywhere = pl.BlockSpec(memory_space=pl.ANY)
    pair = sems((lines, batches))
    ranks, quarter, share = ffn_parts[0].shape
    gathered, outs, *projected, beta, pair_parts, down_part, gains_all = pl.pallas_call(
        gather_call_kernel,
        out_shape=(
            jax.ShapeDtypeStruct((batches, slots, rows, model), bf16),
            jax.ShapeDtypeStruct((lines, batches, more, model), bf16),
            *[jax.ShapeDtypeStruct((slots, rows, width), f32)] * batches,
            jax.ShapeDtypeStruct((batches, slots, rows, 128), f32),
            jax.ShapeDtypeStruct((ranks, 2, quarter, share), bf16),
            jax.ShapeDtypeStruct((ranks, quarter, share), bf16),
            jax.ShapeDtypeStruct((gains.shape[0], model), f32),
        ),
        in_specs=[vmem()] * 2 + [anywhere] * 4 + [vmem()] * 5,
        out_specs=(anywhere,) * (5 + batches) + (vmem(),),
        scratch_shapes=[
            pltpu.VMEM((slots, batches, rows, model), bf16),
            pltpu.VMEM((lines, batches, more, model), bf16),
            pltpu.VMEM((2, batches, rows, width), f32),
            pltpu.VMEM((2, batches, rows, 128), f32),
            pair, pair, pair, pair, pair, sems((lines,)), sems((lines,)), sems((lines,)),
            sems((2,)), sems((slots, batches)), sems((lines,)), sems((2, batches)), sems((2, batches)),
            sems((3, 3)), sems((3, 3)), sems((3,)),
            pltpu.VMEM((gains.shape[0], model), f32), sems((3,)), sems((3,)), sems((1,)),
        ],
        compiler_params=pltpu.CompilerParams(
            collective_id=1, has_side_effects=True, vmem_limit_bytes=40 * 2**20),
        cost_estimate=pl.CostEstimate(flops=10**11, bytes_accessed=4 * 10**7, transcendentals=0),
        name="gather_project",
    )(x, gains, w_out_part, *ffn_parts, *w_inner, w_beta)
    total = slots * rows
    return (gathered.reshape(batches, total, model), outs,
            [wide.reshape(total, width) for wide in projected],
            beta.reshape(batches, total, 128), pair_parts, down_part, gains_all)


def scatter_kernel(w_refs, g_refs, gb_refs, o_refs, inner_ref, wb_ref, small_ref, gains_ref, pair_ref, down_ref,
                   out_ref, small_out, outs_ref, inner_out, pair_out, down_out,
                   gs, bs, ysend, yrecv, from_left, from_right, part_sum, part_left, part_right, outs_s, inner_s, inner_r, small_s, small_r, gains_r,
                   pair_send, pair_recv, right_send, left_send, right_recv, left_recv, g_sem,
                   sum_send, sum_recv, outs_send, outs_recv, gain_send, gain_recv, part_sems, swap_send, swap_recv, swap_own, sum_sem):
    batches = len(g_refs)
    rows, width = gs.shape[2:]
    lines = yrecv.shape[0]
    model = yrecv.shape[3]
    o = lax.axis_index("z")
    i = lax.axis_index("y")
    core = lax.axis_index("core")
    me = lax.axis_index("x") * 2 + core
    tile = min(512, model)
    diagonal = {"x": 1 - lax.axis_index("x"), "core": 1 - core}
    loads = [
        pltpu.make_async_copy(source, target.at[m], g_sem.at[n, m])
        for n, (sources, target) in enumerate(((g_refs, gs), (gb_refs, bs)))
        for m, source in enumerate(sources)]
    for copy in loads:
        copy.start()
    slots = 2 * lines
    mine = o * 2 + i
    peers = []
    for d in range(1, slots):
        place = lax.rem(mine + d, slots)
        peers.append((place, {"z": place // 2, "y": lax.rem(place, 2)}))
    barrier = pltpu.get_barrier_semaphore()
    greeted = [other("core"), other("x"), diagonal] + [device for _, device in peers]
    for device in greeted:
        pl.semaphore_signal(barrier, inc=1, device_id=device, device_id_type=pl.DeviceIdType.MESH)
    pl.semaphore_wait(barrier, len(greeted))
    gain_copies = [
        line_copy(gains_ref.at[place], gains_r.at[mine], gain_send.at[d], gain_recv.at[d], device)
        for d, (place, device) in enumerate(peers)
    ]
    for copy in gain_copies:
        copy.start()

    inner_pair = line_copy(inner_ref.at[1 - core], inner_r.at[0], sum_send.at[0], sum_recv.at[0], other("core"))
    inner_across = line_copy(inner_s, inner_r.at[1], sum_send.at[1], sum_recv.at[1], other("x"))
    inner_back = line_copy(inner_s, inner_out.at[core], sum_send.at[2], sum_recv.at[2], other("core"))
    small_pair = line_copy(small_s.at[0], small_r.at[0], sum_send.at[3], sum_recv.at[3], other("core"))
    small_across = line_copy(small_s.at[1], small_r.at[1], sum_send.at[4], sum_recv.at[4], other("x"))
    inner_own = pltpu.make_async_copy(inner_ref.at[core], inner_s, sum_sem.at[0])
    inner_keep = pltpu.make_async_copy(inner_s, inner_out.at[core], sum_sem.at[1])
    outs_keep = pltpu.make_async_copy(outs_s, outs_ref.at[me], sum_sem.at[2])
    outs_away = [
        line_copy(outs_s, outs_ref.at[me], outs_send.at[n], outs_recv.at[n], target)
        for n, target in enumerate((other("core"), other("x"), diagonal))
    ]
    swap = Swap(
        [(pair_ref, lambda place: pair_out.at[place]), (down_ref, lambda place: down_out.at[place])],
        swap_send, swap_recv, swap_own)
    swap.start()
    inner_pair.start()
    inner_own.start()
    for copy in loads:
        copy.wait()

    def add_into(target, other_ref):
        height = target.shape[0]
        step = next(size for size in range(min(128, height), 0, -16) if height % size == 0)

        @pl.loop(0, height // step)
        def _(n):
            at = pl.ds(pl.multiple_of(n * step, step), step)
            target[at, :] = (target[at, :].astype(f32) + other_ref[at, :].astype(f32)).astype(target.dtype)

    def target(index):
        far = lines - 1 - index // 2
        side = 1 - 2 * lax.rem(index, 2)
        z = o + side * far
        return far, z, (z >= 0) & (z < lines) & ((far > 0) | (side > 0))

    def partial_rows(z, y, m, store):
        g = gs[m, z * 2 + y]
        b = bs[m, z * 2 + y]
        for start in range(0, model, tile):
            cols = slice(start, start + tile)
            value = lax.dot_general(b, wb_ref[cols, :], NT, preferred_element_type=f32)
            for n, w_ref in enumerate(w_refs):
                part = g[:, n * w_ref.shape[1] : (n + 1) * w_ref.shape[1]]
                value = value + lax.dot_general(part, w_ref[cols, :], NT, preferred_element_type=f32)
            store(cols, value)

    def across(z, m):
        return line_copy(ysend.at[z, m], yrecv.at[z, m], pair_send.at[z, m], pair_recv.at[z, m], other("y"))

    def right(z, m):
        return line_copy(yrecv.at[z, m], from_left.at[z, m], right_send.at[z, m], right_recv.at[z, m], {"z": o + 1})

    def left(z, m):
        return line_copy(yrecv.at[z, m], from_right.at[z, m], left_send.at[z, m], left_recv.at[z, m], {"z": o - 1})

    def across_partial(z, m):
        def store(cols, value):
            ysend[z, m, :, cols] = value.astype(bf16)
        partial_rows(z, 1 - i, m, store)

    def pass_part(z):
        return (line_copy(part_sum.at[z], part_left.at[z], part_sems.at[0, z], part_sems.at[1, z], {"z": o + 1}),
                line_copy(part_sum.at[z], part_right.at[z], part_sems.at[2, z], part_sems.at[3, z], {"z": o - 1}))

    def part_round():
        @pl.loop(0, 2 * lines)
        def _(index):
            far, z, valid = target(index)

            @pl.when(valid & (far > 0))
            def _():
                to_right, to_left = pass_part(z)

                @pl.when((z > o) & (o > 0))
                def _():
                    to_right.wait_recv()
                    add_into(part_sum.at[z], part_left.at[z])

                @pl.when((z < o) & (o < lines - 1))
                def _():
                    to_left.wait_recv()
                    add_into(part_sum.at[z], part_right.at[z])

                @pl.when(z > o)
                def _():
                    to_right.start()

                @pl.when(z < o)
                def _():
                    to_left.start()

        to_right, to_left = pass_part(o)
        outs_s[...] = part_sum[o]

        @pl.when(o > 0)
        def _():
            to_right.wait_recv()
            add_into(outs_s, part_left.at[o])

        @pl.when(o < lines - 1)
        def _():
            to_left.wait_recv()
            add_into(outs_s, part_right.at[o])
        outs_keep.start()
        for copy in outs_away:
            copy.start()

    def side_work():
        left, left_in, right, right_in = o_refs
        column, row = lax.axis_index("y"), lax.axis_index("x")
        wide = model // 2
        for z in range(lines):
            part_sum[z, :, :wide] = (
                left[column, z].astype(f32) + left_in[z].astype(f32)).astype(bf16)
            part_sum[z, :, wide:] = (
                right[row, z].astype(f32) + right_in[z].astype(f32)).astype(bf16)
        part_round()
        inner_own.wait()
        inner_pair.wait_recv()
        add_into(inner_s, inner_r.at[0])
        inner_across.start()
        gains_r[mine] = gains_ref[mine]
        for copy in gain_copies:
            copy.wait_recv()
        tail = small_ref.shape[0]
        small_s[0, :tail] = small_ref[...]
        small_s[0, tail:] = jnp.sum(gains_r[...], axis=0)
        small_pair.start()

    total = 2 * lines * batches

    def turn(index, carry):
        before, earlier = carry
        far, z, valid = target(index // batches)
        m = lax.rem(index, batches)
        last = index >= total
        valid = valid & jnp.logical_not(last)
        moves = valid | last

        @pl.when(valid)
        def _():
            across_partial(z, m)

        @pl.when(valid)
        def _():
            across(z, m).start()

        @pl.when(moves & (before >= 0))
        def _():
            across(before // batches, lax.rem(before, batches)).wait_recv()

        @pl.when(valid & (before < 0))
        def _():
            side_work()

        @pl.when(index == (2 * lines - 2) * batches)
        def _():
            inner_across.wait_recv()
            inner_across.wait_send()
            add_into(inner_s, inner_r.at[1])
            inner_back.start()
            inner_keep.start()
            small_pair.wait_recv()
            small_s[1] = small_s[0] + small_r[0]
            small_across.start()

        @pl.when(moves & (before >= 0))
        def _():
            place, n = before // batches, lax.rem(before, batches)

            def store(cols, value):
                yrecv[place, n, :, cols] = (
                    yrecv[place, n, :, cols].astype(f32) + value).astype(bf16)
            partial_rows(place, i, n, store)

            @pl.when((place > o) & (o == 0))
            def _():
                right(place, n).start()

            @pl.when((place < o) & (o == lines - 1))
            def _():
                left(place, n).start()

        @pl.when(moves & (earlier >= 0))
        def _():
            place, n = earlier // batches, lax.rem(earlier, batches)

            @pl.when((place > o) & (o > 0))
            def _():
                right(place, n).wait_recv()
                add_into(yrecv.at[place, n], from_left.at[place, n])
                right(place, n).start()

            @pl.when((place < o) & (o < lines - 1))
            def _():
                left(place, n).wait_recv()
                add_into(yrecv.at[place, n], from_right.at[place, n])
                left(place, n).start()

        code = jnp.where(valid, z * batches + m, -1)
        return jnp.where(moves, code, before), jnp.where(moves, before, earlier)

    lax.fori_loop(0, total + 2, turn, (jnp.int32(-1), jnp.int32(-1)))


    for m in range(batches):
        out_ref[m] = yrecv[o, m].astype(f32)

        @pl.when(o > 0)
        def _():
            right(o, m).wait_recv()
            out_ref[m] += from_left[o, m].astype(f32)

        @pl.when(o < lines - 1)
        def _():
            left(o, m).wait_recv()
            out_ref[m] += from_right[o, m].astype(f32)

    @pl.loop(0, lines)
    def _(z):
        for m in range(batches):
            across(z, m).wait_send()

            @pl.when(z > o)
            def _():
                right(z, m).wait_send()

            @pl.when(z < o)
            def _():
                left(z, m).wait_send()

        @pl.when(z > o)
        def _():
            pass_part(z)[0].wait_send()

        @pl.when(z < o)
        def _():
            pass_part(z)[1].wait_send()

    small_across.wait_recv()
    small_out[...] = small_s[1] + small_r[1]
    for copy in gain_copies:
        copy.wait_send()
    inner_pair.wait_send()
    small_pair.wait_send()
    small_across.wait_send()
    inner_back.wait_recv()
    inner_back.wait_send()
    inner_keep.wait()
    outs_keep.wait()
    swap.wait()
    for copy in outs_away:
        copy.wait_recv()
        copy.wait_send()


def scatter_call_kernel(*refs):
    scatter_kernel(refs[:4], refs[4:6], refs[6:8], refs[8:12], *refs[12:])


def scatter_rows(grads, beta_grads, out_grads, inner_grads, w_inner, w_beta, small, gains,
                 pair_grads, down_grads):
    batches = len(grads)
    total, width = grads[0].shape
    model = w_inner[0].shape[0]
    lines = lax.axis_size("z")
    slots = 2 * lines
    rows = total // slots
    more = out_grads[1].shape[1]
    sems = pltpu.SemaphoreType.DMA
    anywhere = pl.BlockSpec(memory_space=pl.ANY)
    slab = pltpu.VMEM((lines, batches, rows, model), bf16)
    part = pltpu.VMEM((lines, more, model), bf16)
    half = inner_grads.shape[1:]
    flat = (small.shape[0] + gains.shape[1], 128)
    return pl.pallas_call(
        scatter_call_kernel,
        out_shape=(
            jax.ShapeDtypeStruct((batches, rows, model), f32),
            jax.ShapeDtypeStruct(flat, f32),
            jax.ShapeDtypeStruct((4, more, model), bf16),
            jax.ShapeDtypeStruct(inner_grads.shape, bf16),
            jax.ShapeDtypeStruct(pair_grads.shape, bf16),
            jax.ShapeDtypeStruct(down_grads.shape, bf16),
        ),
        in_specs=[vmem()] * 4 + [anywhere] * 4 + [vmem()] * 4
        + [anywhere, vmem(), vmem(), vmem(), anywhere, anywhere],
        out_specs=(vmem(), vmem()) + (anywhere,) * 4,
        scratch_shapes=[
            pltpu.VMEM((batches, slots, rows, width), bf16),
            pltpu.VMEM((batches, slots, rows, 128), bf16),
            slab, slab, slab, slab, part, part, part,
            pltpu.VMEM((more, model), bf16),
            pltpu.VMEM(half, bf16),
            pltpu.VMEM((2, *half), bf16),
            pltpu.VMEM((2, *flat), f32),
            pltpu.VMEM((2, *flat), f32),
            pltpu.VMEM(gains.shape, f32),
            sems((lines, batches)), sems((lines, batches)), sems((lines, batches)),
            sems((lines, batches)), sems((lines, batches)), sems((lines, batches)),
            sems((2, batches)), sems((5,)), sems((5,)), sems((3,)), sems((3,)), sems((slots,)), sems((slots,)), sems((4, lines)),
            sems((2, 3)), sems((2, 3)), sems((2,)), sems((3,)),
        ],
        compiler_params=pltpu.CompilerParams(
            collective_id=3, has_side_effects=True, vmem_limit_bytes=58 * 2**20),
        cost_estimate=pl.CostEstimate(flops=7 * 10**10, bytes_accessed=4 * 10**7, transcendentals=0),
        name="scatter_rows",
    )(*w_inner, *[grad.reshape(slots, rows, width) for grad in grads],
      *[grad.reshape(slots, rows, 128) for grad in beta_grads], *out_grads,
      inner_grads, w_beta, small, gains,
      pair_grads, down_grads)


def tensor_peers(slots):
    mine = lax.axis_index("z") * 2 + lax.axis_index("y")
    places = [lax.rem(mine + d, slots) for d in range(1, slots)]
    return mine, [(place, {"z": place // 2, "y": lax.rem(place, 2)}) for place in places]


def greet(devices):
    barrier = pltpu.get_barrier_semaphore()
    for device in devices:
        pl.semaphore_signal(barrier, inc=1, device_id=device, device_id_type=pl.DeviceIdType.MESH)
    pl.semaphore_wait(barrier, len(devices))


def attend_kernel(x_ref, low_first, low_second, gain_ref, *refs):
    pieces, refs = refs[:8], refs[8:]
    hidden_ref, normed_ref, w_ref, heads_ref, ws, heads, send, recv, sem, own_sem = refs
    slots = heads.shape[1]
    mine, peers = tensor_peers(slots)
    greet([device for _, device in peers])
    lows = (low_first, low_second)
    away = [
        line_copy(low.at[place], heads.at[m, mine], send.at[m, d], recv.at[m, d], device)
        for d, (place, device) in enumerate(peers) for m, low in enumerate(lows)
    ]
    for copy in away:
        copy.start()
    own = [pltpu.make_async_copy(low.at[mine], heads.at[m, mine], own_sem.at[m]) for m, low in enumerate(lows)]
    for copy in own:
        copy.start()
    x = lax.axis_index("x")
    core = lax.axis_index("core")
    y = lax.axis_index("y")
    copies = []
    for n, piece in enumerate(pieces):
        far_y, far_x, far_core = n // 4, n // 2 % 2, n % 2
        column = 1 - y if far_y else y
        quarter = (1 - x if far_x else x) * 2 + (1 - core if far_core else core)
        copies.append(pltpu.make_async_copy(piece, ws.at[:, column, quarter], sem.at[n]))
    for copy in copies:
        copy.start()
    for copy in copies + own:
        copy.wait()
    keep = pltpu.make_async_copy(ws, w_ref, own_sem.at[2])
    keep.start()
    for copy in away:
        copy.wait_recv()
    keep_heads = pltpu.make_async_copy(heads, heads_ref, own_sem.at[3])
    keep_heads.start()
    model = x_ref.shape[1]
    tile = min(512, model)
    width = heads.shape[3]
    squares = 0.0
    for start in range(0, model, tile):
        cols = slice(start, start + tile)
        total = x_ref[:, cols].astype(f32)
        for t in range(slots):
            left = jnp.concatenate([heads[0, t], heads[1, t]], axis=0)
            total = total + jnp.dot(
                left, ws[t // 2, t % 2, :, :, cols].reshape(width, tile), preferred_element_type=f32)
        hidden_ref[:, cols] = total
        squares = squares + jnp.sum(total * total, axis=-1, keepdims=True)
    scale = lax.rsqrt(squares / model + epsilon)
    for start in range(0, model, tile):
        cols = slice(start, start + tile)
        normed_ref[:, cols] = (hidden_ref[:, cols] * scale * gain_ref[:, cols]).astype(bf16)
    keep.wait()
    keep_heads.wait()
    for copy in away:
        copy.wait_send()


def attend(x, lows, gain, pieces):
    rows, model = x.shape
    lines, part, _ = pieces[0].shape
    full = (lines, 2, 4, part, model)
    heads = (2, *lows[0].shape)
    slots = 2 * lines
    anywhere = pl.BlockSpec(memory_space=pl.ANY)
    sems = pltpu.SemaphoreType.DMA
    return pl.pallas_call(
        attend_kernel,
        out_shape=(
            jax.ShapeDtypeStruct((rows, model), f32),
            jax.ShapeDtypeStruct((rows, model), bf16),
            jax.ShapeDtypeStruct(full, bf16),
            jax.ShapeDtypeStruct(heads, bf16),
        ),
        in_specs=[vmem(), anywhere, anywhere, vmem()] + [anywhere] * 8,
        out_specs=(vmem(), vmem(), anywhere, anywhere),
        scratch_shapes=[
            pltpu.VMEM(full, bf16), pltpu.VMEM(heads, bf16),
            sems((2, slots)), sems((2, slots)), sems((8,)), sems((4,))],
        compiler_params=pltpu.CompilerParams(
            collective_id=4, has_side_effects=True, vmem_limit_bytes=32 * 2**20),
        cost_estimate=pl.CostEstimate(flops=3 * 10**10, bytes_accessed=2 * 10**7, transcendentals=0),
        name="attend",
    )(x, *lows, gain, *pieces)


def attend_back_kernel(hidden_ref, ffn_ref, grad_ref, c_ref, gain_ref, w_ref, heads,
                       result_ref, hgrad_ref, back_first, back_second, left_mine, left_theirs,
                       right_mine, right_theirs, gain_out, low, wgrad, wrecv, backs, send, recv, sem, core_sem):
    rows, model = hidden_ref.shape
    half = rows // 2
    tile = min(512, model)
    slots = heads.shape[1]
    width = heads.shape[3]
    mine, peers = tensor_peers(slots)
    greet([device for _, device in peers] + [other("core")])
    squares, dots = 0.0, 0.0
    for start in range(0, model, tile):
        cols = slice(start, start + tile)
        hidden = hidden_ref[:, cols]
        squares = squares + jnp.sum(hidden * hidden, axis=-1, keepdims=True)
        dots = dots + jnp.sum(hidden * grad_ref[:, cols] * gain_ref[:, cols], axis=-1, keepdims=True)
    scale = lax.rsqrt(squares / model + epsilon)
    pull = scale * scale * scale * (dots / model)
    for start in range(0, model, tile):
        cols = slice(start, start + tile)
        hidden = hidden_ref[:, cols]
        grad = grad_ref[:, cols]
        result_ref[:, cols] = hidden + ffn_ref[:, cols]
        gain_out[:, cols] = jnp.sum(grad * hidden * scale, axis=0, keepdims=True)
        hgrad = c_ref[:, cols].astype(f32) + scale * (grad * gain_ref[:, cols]) - hidden * pull
        hgrad_ref[:, cols] = hgrad
        low[:, cols] = hgrad.astype(bf16)

    outs = (back_first, back_second)

    def away(m, d):
        place = lax.rem(mine + d, slots)
        return line_copy(backs.at[m, d], outs[m].at[mine], send.at[m, d], recv.at[m, d],
                         {"z": place // 2, "y": lax.rem(place, 2)})

    @pl.loop(0, slots)
    def _(step):
        d = slots - 1 - step
        place = lax.rem(mine + d, slots)
        back = lax.dot_general(
            low[...], w_ref[place // 2, lax.rem(place, 2)].reshape(width, model), NT,
            preferred_element_type=f32)
        for m in range(2):
            backs[m, d] = back[m * half : (m + 1) * half].astype(bf16)

            @pl.when(d > 0)
            def _():
                away(m, d).start()

            @pl.when(d == 0)
            def _():
                pltpu.make_async_copy(backs.at[m, 0], outs[m].at[mine], sem.at[2 + m]).start()

    for t in range(slots):
        left = jnp.concatenate([heads[0, t], heads[1, t]], axis=0)
        for start in range(0, model, tile):
            cols = slice(start, start + tile)
            value = lax.dot_general(
                left, low[:, cols], (((0,), (0,)), ((), ())), preferred_element_type=f32
            ).astype(bf16).reshape(2, 2, width // 4, tile)
            for c in range(2):
                wgrad[c, :, t % 2, t // 2, :, cols] = value[:, c]
    core = lax.axis_index("core")
    to_pair = line_copy(wgrad.at[1 - core], wrecv, core_sem.at[0], core_sem.at[1], other("core"))
    to_pair.start()
    to_pair.wait_recv()
    lines = wgrad.shape[3]
    for far_x in range(2):
        for far_y in range(2):
            @pl.loop(0, lines)
            def _(z):
                wrecv[far_x, far_y, z] = (
                    wrecv[far_x, far_y, z].astype(f32) + wgrad[core, far_x, far_y, z].astype(f32)
                ).astype(bf16)
    x, y = lax.axis_index("x"), lax.axis_index("y")
    wide = model // 2
    keeps = [
        pltpu.make_async_copy(source.at[..., pl.ds(start, wide)], target, sem.at[4 + n])
        for n, (source, start, target) in enumerate((
            (wrecv.at[x], 0, left_mine), (wrecv.at[1 - x], 0, left_theirs),
            (wrecv.at[:, y], wide, right_mine), (wrecv.at[:, 1 - y], wide, right_theirs)))
    ]
    for copy in keeps:
        copy.start()
    for copy in keeps:
        copy.wait()
    to_pair.wait_send()
    for m in range(2):
        pltpu.make_async_copy(backs.at[m, 0], outs[m].at[mine], sem.at[2 + m]).wait()
        for d in range(1, slots):
            away(m, d).wait_recv()
            away(m, d).wait_send()


def attend_back(hidden, ffn_out, normed_grad, c_rows, gain, w_full, heads):
    rows, model = hidden.shape
    wide = jax.ShapeDtypeStruct((rows, model), f32)
    lines, _, _, part, _ = w_full.shape
    share = (2, 2, lines, part, model)
    slots = 2 * lines
    back = jax.ShapeDtypeStruct(heads.shape[1:], bf16)
    anywhere = pl.BlockSpec(memory_space=pl.ANY)
    sems = pltpu.SemaphoreType.DMA
    return pl.pallas_call(
        attend_back_kernel,
        out_shape=(
            wide, wide, back, back,
            *[jax.ShapeDtypeStruct((2, lines, part, model // 2), bf16)] * 4,
            jax.ShapeDtypeStruct((1, model), f32),
        ),
        in_specs=[vmem()] * 7,
        out_specs=(vmem(),) * 2 + (anywhere,) * 6 + (vmem(),),
        scratch_shapes=[
            pltpu.VMEM((rows, model), bf16), pltpu.VMEM((2, *share), bf16), pltpu.VMEM(share, bf16),
            pltpu.VMEM(heads.shape, bf16), sems((2, slots)), sems((2, slots)), sems((8,)), sems((2,))],
        compiler_params=pltpu.CompilerParams(
            collective_id=5, has_side_effects=True, vmem_limit_bytes=48 * 2**20),
        cost_estimate=pl.CostEstimate(flops=3 * 10**10, bytes_accessed=4 * 10**7, transcendentals=0),
        name="attend_back",
    )(hidden, ffn_out, normed_grad, c_rows, gain, w_full, heads)


def inner_grads_kernel(x_ref, g_first, g_second, b_first, b_second, w0, w1, w2, w3, wb_ref,
                       low_ref, beta_ref, gain_ref):
    dims = (((0,), (0,)), ((), ()))
    beta = 0.0
    for m, b_ref in enumerate((b_first, b_second)):
        beta = beta + lax.dot_general(x_ref[m], b_ref[...], dims, preferred_element_type=f32)
    beta_ref[...] = beta
    gain = jnp.sum(beta * wb_ref[...].astype(f32), axis=1, keepdims=True)
    for n, w_ref in enumerate((w0, w1, w2, w3)):
        width = w_ref.shape[1]
        cols = slice(n * width, (n + 1) * width)
        value = 0.0
        for m, g_ref in enumerate((g_first, g_second)):
            value = value + lax.dot_general(x_ref[m], g_ref[:, cols], dims, preferred_element_type=f32)
        low_ref[:, cols] = value.astype(bf16)
        gain = gain + jnp.sum(value * w_ref[...].astype(f32), axis=1, keepdims=True)
    gain_ref[...] = jnp.broadcast_to(gain, gain_ref.shape)


def inner_grads(tokens, grads, beta_grads, w_inner, w_beta):
    _, total, model = tokens.shape
    wide = grads[0].shape[1]
    width = w_inner[0].shape[1]
    tile = 256

    def whole(columns):
        return pl.BlockSpec((total, columns), lambda n: (0, 0))

    def rows(columns):
        return pl.BlockSpec((tile, columns), lambda n: (n, 0))

    return pl.pallas_call(
        inner_grads_kernel,
        out_shape=(
            jax.ShapeDtypeStruct((model, wide), bf16),
            jax.ShapeDtypeStruct((model, 128), f32),
            jax.ShapeDtypeStruct((model, 128), f32),
        ),
        grid=(model // tile,),
        in_specs=[pl.BlockSpec((2, total, tile), lambda n: (0, 0, n))]
        + [whole(wide)] * 2 + [whole(128)] * 2 + [rows(width)] * 4 + [rows(128)],
        out_specs=(rows(wide), rows(128), rows(128)),
        compiler_params=pltpu.CompilerParams(vmem_limit_bytes=40 * 2**20),
        cost_estimate=pl.CostEstimate(flops=10**10, bytes_accessed=2 * 10**7, transcendentals=0),
        name="inner_grads",
    )(tokens, *grads, *beta_grads, *w_inner, w_beta)


def root_scale(row_values, gain_vector):
    row_scale = lax.rsqrt(jnp.mean(row_values * row_values, axis=-1, keepdims=True) + epsilon)
    return (row_values * row_scale * gain_vector, row_scale)


def norm_backward(row_values, row_scale, gain_vector, normed_grad):
    weighted = normed_grad * gain_vector
    rows_grad = row_scale * weighted - row_values * row_scale * row_scale * row_scale * jnp.mean(
        weighted * row_values, axis=-1, keepdims=True
    )
    gain_grad = jnp.sum(normed_grad * row_values * row_scale, axis=tuple(range(row_values.ndim - 1)))
    return (rows_grad, gain_grad)


DP = ("x", "core")
TP = ("z", "y")


def gather(x, axis_name, axis=0):
    return lax.all_gather(x, axis_name, axis=axis, tiled=True)


def scatter_sum(x, axis_name, axis=0):
    return lax.psum_scatter(
        x.astype(bf16), axis_name, scatter_dimension=axis, tiled=True
    ).astype(f32)


def dot(a, b):
    return jnp.dot(a, b, preferred_element_type=f32)


def dot_nt(a, b):
    return jnp.einsum("tk,nk->tn", a, b, preferred_element_type=f32)


def dot_tn(a, b):
    return jnp.einsum("tm,tn->mn", a, b, preferred_element_type=f32)


def exchange(x, axis_name, distance=1):
    size = lax.axis_size(axis_name)
    return lax.ppermute(x, axis_name, [(i, i ^ distance) for i in range(size)])


def pick(x, index, axis):
    return lax.dynamic_index_in_dim(x, index, axis, keepdims=False)


def after(x, *others):
    return lax.optimization_barrier((x, *others))[0]


def add_low(x, y):
    return (x.astype(f32) + y.astype(f32)).astype(bf16)


def halve_sum(grad, axis_name):
    me = lax.axis_index(axis_name)
    return add_low(pick(grad, me, 0), exchange(pick(grad, 1 - me, 0), axis_name))


def feed_forward_groups(normed, cotangents, w_gate, w_up, w_down):
    gate_full = gather(w_gate, DP)
    up_full = gather(w_up, DP)
    down_full = gather(w_down, DP, 1)
    outs, normed_grads, inner_rows, gate_grads, up_grads, rows, grad_rows = [], [], [], [], [], [], []
    for m in range(normed.shape[0]):
        rows.append(gather(normed[m], TP))
        grad_rows.append(gather(cotangents[m], TP))
        gate_values = dot(rows[m], gate_full)
        up_values = dot(rows[m], up_full)
        sigmoid_gate = jax.nn.sigmoid(gate_values)
        silu_gate = gate_values * sigmoid_gate
        inner = (silu_gate * up_values).astype(bf16)
        inner_grad = dot_nt(grad_rows[m], down_full)
        gate_grad = (
            inner_grad * up_values * sigmoid_gate * (1.0 + gate_values * (1.0 - sigmoid_gate))
        ).astype(bf16)
        up_grad = (inner_grad * silu_gate).astype(bf16)
        normed_grads.append(scatter_sum(dot_nt(gate_grad, gate_full) + dot_nt(up_grad, up_full), TP))
        outs.append(scatter_sum(dot(inner, down_full), TP))
        inner_rows.append(inner)
        gate_grads.append(gate_grad)
        up_grads.append(up_grad)
    grad_all = jnp.concatenate(grad_rows)
    rows_all = jnp.concatenate(rows)
    gate_share = scatter_sum(dot_tn(rows_all, jnp.concatenate(gate_grads)), DP)
    up_share = scatter_sum(dot_tn(rows_all, jnp.concatenate(up_grads)), DP)
    down_share = scatter_sum(dot_tn(jnp.concatenate(inner_rows), grad_all), DP, 1)
    return jnp.stack(outs), jnp.stack(normed_grads), (gate_share, up_share, down_share)


def per_device(
    inputs,
    lengths,
    norm_gain,
    ffn_gain,
    w_query,
    w_key,
    w_value,
    w_gate_out,
    w_beta,
    conv_weight,
    head_gain,
    w_out,
    w_gate,
    w_up,
    w_down,
    cotangent,
):
    batches = range(inputs.shape[0])
    local_width = w_query.shape[1]
    heads = w_beta.shape[1]
    devices = lax.axis_size(TP)
    planar = all(lax.axis_size(name) == 2 for name in ("x", "core", "y"))
    w_parts = (w_query, w_key, w_value, w_gate_out)
    w_inner = jnp.concatenate(w_parts, axis=1)
    w_beta_wide = jnp.pad(w_beta, ((0, 0), (0, 128 - heads)))
    taps = conv_weight.astype(f32).reshape(-1, local_width)
    gain_heads = head_gain.astype(f32)
    gains = jnp.stack([norm_gain, ffn_gain])
    rows_in = inputs.astype(f32)

    def run_mixer(m, wide, logits):
        low, *kept = mixer_forward(lengths[m, 0], wide, logits, taps, gain_heads, exact=False)
        return low, kept

    def back_mixer(m, wide, logits, grad, kept):
        return mixer_backward(
            lengths[m, 0], wide, logits, taps, gain_heads, grad, kept, exact=False)

    if planar:
        count = rows_in.shape[0] * rows_in.shape[1]
        model = rows_in.shape[2]
        ranks = lax.axis_size(DP)
        ffn_parts = [
            w.reshape(ranks, -1, w.shape[1]) for w in (w_gate.T, w_up.T, w_down)]
        c_rows = [None] * 8
        c_rows[0] = cotangent.reshape(count, model)
        c_rows[4] = exchange(c_rows[0], "core")
        out_shares = pick(
            w_out.reshape(lax.axis_size(DP), len(batches), -1, model), lax.axis_index(DP), 0)
        gains = jnp.pad(gains.astype(f32), ((0, 6), (0, 0)))
        gathered_one, out_own, projected, beta_logits, own_weights, own_down, gains = gather_project(
            inputs, gains, out_shares, ffn_parts, w_parts, w_beta_wide)
        gain_one, gain_two = gains[0], gains[1]
        _, scale_one = root_scale(rows_in, gain_one)
        early = after(c_rows[0], gathered_one)
        c_rows[1] = exchange(early, "x")
        weights = gather(own_weights[None], "z")
        c_rows[2] = exchange(early, "y")
        out_own = out_own.reshape(out_own.shape[0], -1, model)
        out_y = exchange(out_own, "y")
        out_x = exchange(out_own, "x")
    else:
        gains = gather(gains, DP, 1).astype(f32)
        gain_one, gain_two = gains[0], gains[1]
        normed_one, scale_one = root_scale(rows_in, gain_one)
        normed_one = normed_one.astype(bf16)
        gathered_one = jnp.stack([gather(normed_one[m], TP) for m in batches])
        projected = [dot(gathered_one[m], w_inner) for m in batches]
        beta_logits = [dot(gathered_one[m], w_beta_wide) for m in batches]
        out_full = gather(w_out, TP)
    token_heads, saved = [], []
    for m in batches:
        low, kept = run_mixer(m, projected[m], beta_logits[m])
        saved.append(kept)
        if planar and m == 0:
            out_y, c_rows[1], c_rows[2] = after((out_y, c_rows[1], c_rows[2]), low)
            out_xy = exchange(out_y, "x")
            c_rows[3] = exchange(c_rows[1], "y")
            c_rows[5] = exchange(c_rows[1], "core")
            c_rows[6] = exchange(c_rows[2], "core")
            projected[1] = after(projected[1], out_y, c_rows[2])
        low = low.reshape(devices, -1, local_width)
        if not planar:
            low = lax.all_to_all(low, TP, split_axis=0, concat_axis=0, tiled=True)
        token_heads.append(low)
    if planar:
        out_x, out_xy, c_rows[3] = after((out_x, out_xy, c_rows[3]), low)
        out_pieces = []
        for piece in (out_own, out_x, out_y, out_xy):
            out_pieces += [piece, exchange(piece, "core")]
        c_rows[7] = exchange(c_rows[3], "core")
        hidden, normed_two, out_full, token_heads = attend(
            inputs.reshape(count, model), token_heads, gain_two[None], out_pieces)
        ffn_out, normed_grad, weight_grads, down_grad = ffn_plane(normed_two, weights, own_down, c_rows)
        result_rows, hidden_grad, *mixed_grads, left, left_away, right, right_away, gain_two_sum = attend_back(
            hidden, ffn_out, normed_grad, c_rows[0], gain_two[None], out_full, token_heads)
        weight_grads = after(weight_grads, left)
        own_grads = lax.psum_scatter(weight_grads, "z", scatter_dimension=0, tiled=True)
        gain_two_sum = gain_two_sum[0]
        result_rows = result_rows.reshape(rows_in.shape)
        hidden_grad = hidden_grad.reshape(rows_in.shape)
    else:
        heads_rows = [
            block.swapaxes(0, 1).reshape(-1, devices * local_width) for block in token_heads]
        hidden = rows_in + jnp.stack([dot(rows, out_full) for rows in heads_rows])
        normed_two, scale_two = root_scale(hidden, gain_two)
        ffn_out, normed_grad, (gate_share, up_share, down_share) = feed_forward_groups(
            normed_two.astype(bf16), cotangent, w_gate, w_up, w_down)
        result_rows = hidden + ffn_out
        norm_grad, gain_two_sum = norm_backward(hidden, scale_two, gain_two, normed_grad)
        hidden_grad = cotangent.astype(f32) + norm_grad
        attended_low = hidden_grad.astype(bf16)
        mixed_grads = [
            dot_nt(attended_low[m], out_full).astype(bf16)
            .reshape(-1, devices, local_width).swapaxes(0, 1) for m in batches]
        out_grad = dot_tn(
            jnp.concatenate(heads_rows), jnp.concatenate(list(attended_low))).astype(bf16)
    if not planar:
        mixed_grads = [
            lax.all_to_all(grad, TP, split_axis=0, concat_axis=0, tiled=True)
            for grad in mixed_grads]
    mixed_grads = [grad.reshape(-1, local_width) for grad in mixed_grads]
    if planar:
        left = add_low(left, exchange(left_away, "x"))
        right = add_low(right, exchange(right_away, "y"))
    projected_low, beta_low = [], []
    taps_sum, heads_sum = 0.0, 0.0
    for m in batches:
        if planar and m > 0:
            mixed_grads[m] = after(mixed_grads[m], left, right)
        projected_grad, beta_grad, taps_part, heads_part = back_mixer(
            m, projected[m], beta_logits[m], mixed_grads[m], saved[m])
        taps_sum = taps_sum + taps_part
        heads_sum = heads_sum + heads_part
        projected_low.append(projected_grad)
        beta_low.append(beta_grad)
    if planar:
        left_in = exchange(pick(left, 1 - lax.axis_index("y"), 0), "y")
        right_in = exchange(pick(right, 1 - lax.axis_index("x"), 0), "x")
        low_sum, beta_sum, gain_rows = inner_grads(
            gathered_one, projected_low, beta_low, w_parts, w_beta_wide)
        beta_sum = beta_sum[:, :heads]
        gain_one_sum = gain_rows[:, 0] / gain_one
    else:
        tokens = gathered_one.reshape(-1, gathered_one.shape[2])
        inner_sum = dot_tn(tokens, jnp.concatenate(projected_low))
        beta_sum = dot_tn(tokens, jnp.concatenate(beta_low)[:, :heads])
        gain_one_sum = (
            jnp.sum(inner_sum * w_inner.astype(f32), axis=1)
            + jnp.sum(beta_sum * w_beta.astype(f32), axis=1)
        ) / gain_one
        low_sum = inner_sum.astype(bf16)
    gain_parts = jnp.stack([gain_one_sum, gain_two_sum])
    sums = [part.reshape(-1, 128) for part in (beta_sum.T, taps_sum, heads_sum)]
    marks = [sums[0].shape[0], sums[0].shape[0] + sums[1].shape[0], sum(part.shape[0] for part in sums)]
    small = jnp.concatenate(sums)
    if planar:
        ranks = lax.axis_size(DP)
        gain_parts = gain_parts.reshape(2, ranks, devices, -1).transpose(2, 0, 1, 3)
        chunk = gain_parts.shape[3]
        gain_parts = gain_parts.reshape(devices, -1, 128)
        gain_rows = gain_parts.shape[1]
        gain_parts = jnp.pad(gain_parts, ((0, 0), (0, -gain_rows % 8), (0, 0)))
        small = jnp.pad(small, ((0, -small.shape[0] % 8), (0, 0)))
        input_norm, flat, out_total, inner_total, pair_grads, down_grads = scatter_rows(
            projected_low, beta_low, (left, left_in, right, right_in),
            low_sum.reshape(2, -1, low_sum.shape[1]), w_parts, w_beta_wide, small, gain_parts,
            own_grads[0], down_grad)
        gate_share, up_share = (
            pair_grads[:, kind].reshape(-1, pair_grads.shape[3]).astype(f32).T for kind in range(2))
        down_share = down_grads.reshape(w_down.shape).astype(f32)
        gain_totals = pick(
            flat[small.shape[0] :][:gain_rows].reshape(2, ranks, chunk), lax.axis_index(DP), 1)
        small = flat[: small.shape[0]]
        out_total = out_total.reshape(w_out.shape).astype(f32)
        inner_total = inner_total.reshape(low_sum.shape)
    else:
        gain_totals = lax.psum_scatter(gain_parts, DP + TP, scatter_dimension=1, tiled=True)
        inner_total = lax.psum(low_sum, DP)
        small = lax.psum(small, DP)
        out_grad = lax.psum_scatter(out_grad, TP, scatter_dimension=0, tiled=True)
        out_total = lax.psum(out_grad, DP).astype(f32)
        input_norm = jnp.stack([
            scatter_sum(
                dot_nt(projected_low[m], w_inner) + dot_nt(beta_low[m], w_beta_wide), TP)
            for m in batches])
    norm_grad, _ = norm_backward(rows_in, scale_one, gain_one, input_norm)
    beta_total = small[: marks[0]].reshape(heads, -1).T
    conv_total = small[marks[0] : marks[1]].reshape(conv_weight.shape)
    heads_total = small[marks[1] : marks[2]].reshape(head_gain.shape)
    columns = [
        inner_total[:, n * local_width : (n + 1) * local_width].astype(f32) for n in range(4)]
    return (
        result_rows,
        hidden_grad + norm_grad,
        gain_totals[0],
        gain_totals[1],
        *columns,
        beta_total,
        conv_total,
        heads_total,
        out_total,
        gate_share,
        up_share,
        down_share,
    )


def solution(mesh):
    dp, tensor = mesh.shape["dp"], mesh.shape["tensor"]
    inner = 2 if tensor == 8 else 4
    axes = ("x", "core", "z", "y")
    fine = jax.sharding.Mesh(
        mesh.devices.reshape(dp // 2, 2, tensor // inner, inner), axes)
    tokens = P(None, DP + TP, None)
    in_specs = (
        tokens,
        P(None, DP, None),
        P(DP),
        P(DP),
        P(None, TP),
        P(None, TP),
        P(None, TP),
        P(None, TP),
        P(None, TP),
        P(None, None, TP),
        P(TP, None),
        P(TP, None),
        P(DP, TP),
        P(DP, TP),
        P(TP, DP),
        tokens,
    )
    out_specs = (
        tokens,
        tokens,
        P(DP + TP),
        P(DP + TP),
        P(None, TP),
        P(None, TP),
        P(None, TP),
        P(None, TP),
        P(None, TP),
        P(None, None, TP),
        P(TP, None),
        P(TP, None),
        P(DP, TP),
        P(DP, TP),
        P(TP, DP),
    )
    return jax.shard_map(
        per_device, mesh=fine, in_specs=in_specs, out_specs=out_specs, check_vma=False
    )
```
